32 devices in a mesh: ctx: 8 (over y, x, core), head: 4 (over z).
Axes of the slice: x: 2, y: 2, z: 4, core: 2. Of those that a mesh axis runs over, the one named last changes fastest.
Arguments:
- query: bfloat16 [3072, 1024], P('ctx', 'head'), may hold values from -140 to 140
- key: bfloat16 [3072, 1024], P('ctx', 'head'), may hold values from -6 to 6
- value: bfloat16 [3072, 1024], P('ctx', 'head'), may hold values from -6 to 6
- block_mask: int32 [24, 3], P('ctx'), may hold values 0 or 1
- out_weight: bfloat16 [1024, 4096], P('head'), may hold values from -0.1875 to 0.1875
- cotangent: bfloat16 [3072, 4096], P(('ctx', 'head')), may hold values from -6 to 6
Outputs:
- mixed: bfloat16 [3072, 4096], P(('ctx', 'head'))
- grad_query: bfloat16 [3072, 1024], P('ctx', 'head')
- grad_key: bfloat16 [3072, 1024], P('ctx', 'head')
- grad_value: bfloat16 [3072, 1024], P('ctx', 'head')
The draws below stay inside these ranges and needn't reach their ends.
All inputs are finite; a program needn't handle non-finite values. No bound on the sum of `block_mask` on one device may be relied on, other than what follows from the above.
Results may differ from the reference program's by a relative error of at most 0.006.
Values may be sent and summed in bfloat16 or wider, within the bound.
No kernel may reach another device: no remote copies, remote signals or barrier semaphores. Data moves between devices by JAX's collectives and lax.ppermute only.
A program may use at most 64 MiB of HBM per device.

```python
import math
import jax
import jax.numpy as jnp
from jax import lax

D = 4096
DH = 128
BLK = 128
TOK_DEV = 384
HEADS = 8
LENGTH = 3072


def pair_draw(key):
    width = HEADS * DH
    query_base = jnp.clip(jax.random.normal(jax.random.fold_in(key, 11), (LENGTH, width), jnp.float32), -6.0, 6.0)
    key_offset = jnp.clip(jax.random.normal(jax.random.fold_in(key, 12), (LENGTH, width), jnp.float32), -6.0, 6.0)
    return (query_base, key_offset)


def draw_query(key, part):
    return pair_draw(key)[0].astype(jnp.bfloat16)


def draw_key(key, part):
    return pair_draw(key)[1].astype(jnp.bfloat16)


def touch_ends(result, rng, low, top_value):
    longest = result.shape.index(max(result.shape))
    spots = []
    for shift in (0, 1):
        where = [jax.random.randint(jax.random.fold_in(rng, axis), (), 0, length) for axis, length in enumerate(result.shape)]
        where[longest] = (where[longest] + shift) % result.shape[longest]
        spots.append(tuple(where))
    return result.at[spots[0]].set(low).at[spots[1]].set(top_value)


def shard_levels(stream_key, dims, split, low, high):
    level = 1.0
    for dim, parts in split:
        heights = jax.random.uniform(jax.random.fold_in(jax.random.fold_in(stream_key, 6), dim), (parts,), jnp.float32, low / len(split), high / len(split))
        level = level * jnp.repeat(jnp.exp(heights), dims[dim] // parts).reshape((-1,) + (1,) * (len(dims) - 1 - dim))
    return level


def centred(key, shape, scale, most, pieces=(), dtype=jnp.bfloat16):
    array = jax.random.normal(key, shape, jnp.float32) * scale
    if len(pieces) > 0:
        array = shard_levels(key, shape, pieces, -0.22, 0.18) * array
    return jnp.clip(array, min=-most, max=most).astype(dtype)


def setup_inputs(seed: int = 0) -> dict:
    key_of = jax.random.split(jax.random.key(seed), 7)
    return {
        "query": draw_query(jax.random.fold_in(key_of[6], 71), 0),
        "key": draw_key(jax.random.fold_in(key_of[6], 71), 0),
        "value": centred(key_of[2], (LENGTH, HEADS * DH), 1.0, 6.0, ((0, 8), (1, 4))),
        "block_mask": touch_ends((jax.random.randint(key_of[3], (LENGTH // BLK, TOK_DEV // BLK), 0, 2) < 1).astype(jnp.int32), jax.random.fold_in(key_of[3], 1), 0, 1),
        "out_weight": centred(key_of[4], (HEADS * DH, D), (HEADS * DH) ** -0.5, 0.1875, ((0, 4),)),
        "cotangent": centred(key_of[5], (LENGTH, D), 1.0, 6.0, ((0, 32),)),
    }


def keep_table(mask, rows):
    blk = rows // mask.shape[0]
    full = jnp.repeat(jnp.repeat(mask, blk, axis=0), blk, axis=1) > 0
    pos = jnp.arange(rows)
    same = pos[:, None] // blk == pos[None, :] // blk
    causal = pos[:, None] >= pos[None, :]
    return (causal & (full | same), causal)

def f32(x):
    return x.astype(jnp.float32)

def shard_work(q3, k3, v3, g3, mask, linear_state, grad_state, scale):
    rows = q3.shape[0]
    keep, causal = keep_table(mask, rows)
    inv_root = 1.0 / math.sqrt(DH)
    raw = jnp.einsum('ihd,jhd->hij', f32(q3), f32(k3))
    s = jnp.where(keep[None], raw * inv_root, -1e+30)
    top = lax.optimization_barrier(jnp.max(s, -1, keepdims=True))
    ex = jnp.exp(s - top)
    probs = (ex / lax.optimization_barrier(jnp.sum(ex, -1, keepdims=True))).astype(jnp.bfloat16)
    soft = jnp.einsum('hij,jhd->ihd', f32(probs), f32(v3))
    inner = jnp.where(causal[None], raw, 0.0).astype(jnp.bfloat16)
    intra = jnp.einsum('hij,jhd->ihd', f32(inner), f32(v3))
    inter = jnp.einsum('ihd,hde->ihe', f32(q3), linear_state, precision=lax.Precision.HIGHEST)
    attn = (soft + scale * (intra + inter)).astype(jnp.bfloat16)
    dprod = jnp.einsum('ihd,jhd->hij', f32(g3), f32(v3))
    delta = lax.optimization_barrier(jnp.sum(f32(g3) * soft, -1)).T
    dscore = (f32(probs) * (dprod - delta[:, :, None]) * inv_root).astype(jnp.bfloat16)
    dinner = jnp.where(causal[None], dprod, 0.0).astype(jnp.bfloat16)
    grad_q = jnp.einsum('hij,jhd->ihd', f32(dscore), f32(k3)) + scale * (jnp.einsum('hij,jhd->ihd', f32(dinner), f32(k3)) + jnp.einsum('ihb,hab->iha', f32(g3), linear_state, precision=lax.Precision.HIGHEST))
    grad_k = jnp.einsum('hij,ihd->jhd', f32(dscore), f32(q3)) + scale * jnp.einsum('hij,ihd->jhd', f32(dinner), f32(q3)) + jnp.einsum('jhb,hab->jha', f32(v3), grad_state, precision=lax.Precision.HIGHEST)
    value_gradient = jnp.einsum('hij,ihd->jhd', f32(probs), f32(g3)) + scale * jnp.einsum('hij,ihd->jhd', f32(inner), f32(g3)) + jnp.einsum('jha,hab->jhb', f32(k3), grad_state, precision=lax.Precision.HIGHEST)
    width = q3.shape[1] * q3.shape[2]
    return (attn.reshape(rows, width), grad_q.astype(jnp.bfloat16).reshape(rows, width), grad_k.astype(jnp.bfloat16).reshape(rows, width), value_gradient.astype(jnp.bfloat16).reshape(rows, width))

def reference(query, key, value, block_mask, out_weight, cotangent):
    total_rows = query.shape[0]
    rows = TOK_DEV
    shards = total_rows // rows
    heads = query.shape[1] // DH
    scale = 1.0 / math.sqrt(DH * total_rows)
    grad_attn = jnp.dot(cotangent, out_weight.T, preferred_element_type=jnp.float32).astype(jnp.bfloat16)

    def shaped(x):
        return x.reshape(shards, rows, heads, DH)
    qs, ks, vs, gs = (shaped(query), shaped(key), shaped(value), shaped(grad_attn))
    masks = block_mask.reshape(shards, rows // BLK, rows // BLK)
    own = lax.map(lambda a: jnp.einsum('jhd,jhe->hde', f32(a[0]), f32(a[1])), (ks, vs))
    own_grad = lax.map(lambda a: scale * jnp.einsum('ihd,ihe->hde', f32(a[0]), f32(a[1])), (qs, gs))
    zero = jnp.zeros_like(own[:1])
    prefix = jnp.concatenate([zero, jnp.cumsum(own, 0)[:-1]], 0)
    trailing_part = jnp.concatenate([jnp.cumsum(own_grad[::-1], 0)[::-1][1:], zero], 0)
    attn, grad_q, grad_k, value_gradient = lax.map(lambda a: shard_work(a[0], a[1], a[2], a[3], a[4], a[5], a[6], scale), (qs, ks, vs, gs, masks, prefix, trailing_part))
    width = heads * DH
    attn = attn.reshape(total_rows, width)
    mixed = jnp.dot(attn, out_weight, preferred_element_type=jnp.float32).astype(jnp.bfloat16)
    return (mixed, grad_q.reshape(total_rows, width), grad_k.reshape(total_rows, width), value_gradient.reshape(total_rows, width))
```

```python
import math

import jax
import jax.numpy as jnp
from jax import lax
from jax.sharding import PartitionSpec as P

DH = 128


def carried_in(part, axis, reverse):
    count = lax.axis_size(axis)
    place = lax.axis_index(axis)
    total = part
    carried = jnp.zeros_like(part)
    step = 1
    while step < count:
        other = lax.ppermute(total, axis, [(i, i ^ step) for i in range(count)])
        upper = (place & step) > 0
        carried = carried + jnp.where(upper ^ reverse, other, 0.0)
        total = total + other
        step *= 2
    return carried


def keep_table(mask, rows):
    count = mask.shape[0]
    blk = rows // count
    full = jnp.broadcast_to((mask > 0)[:, None, :, None], (count, blk, count, blk)).reshape(
        rows, rows
    )
    pos = jnp.arange(rows)
    same = pos[:, None] // blk == pos[None, :] // blk
    causal = pos[:, None] >= pos[None, :]
    return (causal & (full | same), causal)


def on_device(query, key, value, block_mask, out_weight, cotangent):
    rows = query.shape[0]
    heads = query.shape[1] // DH
    width = heads * DH
    length = rows * lax.axis_size("ctx")
    scale = 1.0 / math.sqrt(DH * length)
    inv_root = 1.0 / math.sqrt(DH)
    single_float_type = jnp.float32
    upper_limit = lax.Precision.HIGHEST
    qh = query.reshape(rows, heads, DH).transpose(1, 0, 2)
    kh = key.reshape(rows, heads, DH).transpose(1, 0, 2)
    vh = value.reshape(rows, heads, DH).transpose(1, 0, 2)
    keep, causal = keep_table(block_mask, rows)
    shards = lax.axis_size("ctx")
    piece = width // shards
    part = lax.dynamic_slice_in_dim(out_weight, lax.axis_index("ctx") * piece, piece, 0)
    weight = lax.all_gather(part, ("head", "ctx"), axis=0, tiled=True)
    grad_own = jnp.einsum(
        "rn,kn->rk", cotangent, weight, preferred_element_type=single_float_type
    ).astype(jnp.bfloat16)
    grad_attn = lax.all_to_all(grad_own, "head", 1, 0, tiled=True)
    gradient_heads = grad_attn.reshape(rows, heads, DH).transpose(1, 0, 2)
    own_state = jnp.einsum("hjd,hje->hde", kh, vh, preferred_element_type=single_float_type)
    own_grad = scale * jnp.einsum(
        "hid,hie->hde", qh, gradient_heads, preferred_element_type=single_float_type
    )
    linear_state = carried_in(own_state, "ctx", False)
    grad_state = carried_in(own_grad, "ctx", True)
    raw = jnp.einsum("hid,hjd->hij", qh, kh, preferred_element_type=single_float_type)
    scores = jnp.where(keep[None], raw * inv_root, -1e30)
    top = jnp.max(scores, -1, keepdims=True)
    expo = jnp.exp(scores - top)
    probs = (expo / jnp.sum(expo, -1, keepdims=True)).astype(jnp.bfloat16)
    soft = jnp.einsum("hij,hjd->hid", probs, vh, preferred_element_type=single_float_type)
    inner = jnp.where(causal[None], raw, 0.0).astype(jnp.bfloat16)
    intra = jnp.einsum("hij,hjd->hid", inner, vh, preferred_element_type=single_float_type)
    inter = jnp.einsum(
        "hid,hde->hie", qh.astype(single_float_type), linear_state, precision=upper_limit
    )
    attn_heads = (soft + scale * (intra + inter)).astype(jnp.bfloat16)
    attn = attn_heads.transpose(1, 0, 2).reshape(rows, width)
    attn_own = lax.all_to_all(attn, "head", 0, 1, tiled=True)
    mixed = jnp.dot(attn_own, weight, preferred_element_type=single_float_type).astype(jnp.bfloat16)
    dprod = jnp.einsum("hid,hjd->hij", gradient_heads, vh, preferred_element_type=single_float_type)
    delta = jnp.sum(gradient_heads.astype(single_float_type) * soft, -1)
    dscore = (probs.astype(single_float_type) * (dprod - delta[:, :, None]) * inv_root).astype(
        jnp.bfloat16
    )
    dinner = jnp.where(causal[None], dprod, 0.0).astype(jnp.bfloat16)
    grad_q = jnp.einsum(
        "hij,hjd->hid", dscore, kh, preferred_element_type=single_float_type
    ) + scale * (
        jnp.einsum("hij,hjd->hid", dinner, kh, preferred_element_type=single_float_type)
        + jnp.einsum(
            "ykd,yod->yko",
            gradient_heads.astype(single_float_type),
            linear_state,
            precision=upper_limit,
        )
    )
    grad_k = (
        jnp.einsum("hij,hid->hjd", dscore, qh, preferred_element_type=single_float_type)
        + scale * jnp.einsum("hij,hid->hjd", dinner, qh, preferred_element_type=single_float_type)
        + jnp.einsum(
            "hjb,hab->hja", vh.astype(single_float_type), grad_state, precision=upper_limit
        )
    )
    value_gradient = (
        jnp.einsum("hij,hid->hjd", probs, gradient_heads, preferred_element_type=single_float_type)
        + scale
        * jnp.einsum(
            "hij,hid->hjd", inner, gradient_heads, preferred_element_type=single_float_type
        )
        + jnp.einsum(
            "hja,hab->hjb", kh.astype(single_float_type), grad_state, precision=upper_limit
        )
    )

    def flat(x):
        return x.astype(jnp.bfloat16).transpose(1, 0, 2).reshape(rows, width)

    return (mixed, flat(grad_q), flat(grad_k), flat(value_gradient))


def solution(mesh):
    return jax.shard_map(
        on_device,
        mesh=mesh,
        in_specs=(
            P("ctx", "head"),
            P("ctx", "head"),
            P("ctx", "head"),
            P("ctx", None),
            P("head", None),
            P(("ctx", "head"), None),
        ),
        out_specs=(P(("ctx", "head"), None), P("ctx", "head"), P("ctx", "head"), P("ctx", "head")),
        check_vma=False,
    )
```

```python
import functools
import math

import jax
import jax.numpy as jnp
from jax import lax
from jax.experimental import pallas as pl
from jax.experimental.pallas import tpu as pltpu
from jax.sharding import PartitionSpec as P

DH = 128
F32 = jnp.float32
BF16 = jnp.bfloat16
NN = ((1,), (0,))
NT = ((1,), (1,))
TN = ((0,), (0,))
MIB = 1 << 20


def dot(a, b, dims):
    return lax.dot_general(a, b, (dims, ((), ())), preferred_element_type=F32)


def dot_wide(a, b, dims):
    high = b.astype(BF16)
    low = (b - high.astype(F32)).astype(BF16)
    return dot(a, high, dims) + dot(a, low, dims)


def call(body, outs, args, flops, smem=(), scratch=()):
    moved = sum(a.size * a.dtype.itemsize for a in args)
    moved += sum(math.prod(s) * jnp.dtype(t).itemsize for s, t in outs)
    return pl.pallas_call(
        body,
        out_shape=[jax.ShapeDtypeStruct(s, t) for s, t in outs],
        in_specs=[pl.BlockSpec(memory_space=pltpu.SMEM) for _ in smem]
        + [pl.BlockSpec(memory_space=pltpu.VMEM) for _ in args],
        out_specs=[pl.BlockSpec(memory_space=pltpu.VMEM) for _ in outs],
        scratch_shapes=list(scratch),
        compiler_params=pltpu.CompilerParams(vmem_limit_bytes=40 * MIB),
        cost_estimate=pl.CostEstimate(
            flops=int(flops), bytes_accessed=int(moved), transcendentals=0
        ),
    )(*smem, *args)


def lower_triangle(blk):
    return lax.broadcasted_iota(jnp.int32, (blk, blk), 0) >= lax.broadcasted_iota(
        jnp.int32, (blk, blk), 1
    )


def forward_kernel(scale, mask, q_ref, k_ref, v_ref, probs_ref, inner_ref, soft_ref, pre_ref):
    rows, width = q_ref.shape
    count = mask.shape[0]
    blk = rows // count
    inv_root = 1.0 / math.sqrt(DH)
    triangle = lower_triangle(blk)
    for h in range(width // DH):
        cols = slice(h * DH, (h + 1) * DH)
        for i in range(count):
            here = slice(i * blk, (i + 1) * blk)
            upto = slice(0, (i + 1) * blk)
            raw = dot(q_ref[here, cols], k_ref[upto, cols], NT)
            scores, inner = [], []
            for j in range(i + 1):
                part = raw[:, j * blk : (j + 1) * blk]
                keep = triangle if j == i else mask[i, j] > 0
                scores.append(jnp.where(keep, part * inv_root, -1e30))
                inner.append(jnp.where(triangle, part, 0.0) if j == i else part)
            scores = jnp.concatenate(scores, 1)
            inner = jnp.concatenate(inner, 1).astype(BF16)
            expo = jnp.exp(scores - jnp.max(scores, -1, keepdims=True))
            probs = (expo / jnp.sum(expo, -1, keepdims=True)).astype(BF16)
            v = v_ref[upto, cols]
            soft = dot(probs, v, NN)
            probs_ref[h, here, upto] = probs
            inner_ref[h, here, upto] = inner
            soft_ref[here, cols] = soft
            pre_ref[here, cols] = soft + scale * dot(inner, v, NN)


def attn_kernel(scale, place, q_ref, pre_ref, state_ref, *out_refs):
    count = len(out_refs)
    own = out_refs[0].shape[0]
    for s in range(count):
        block = lax.rem(place[0] + s, count)
        here = pl.ds(pl.multiple_of(block * own, own), own)
        for h in range(q_ref.shape[1] // DH):
            cols = slice(h * DH, (h + 1) * DH)
            inter = dot_wide(q_ref[here, cols], state_ref[h], NN)
            out_refs[s][:, cols] = (pre_ref[here, cols] + scale * inter).astype(BF16)


def grad_kernel(places, mine_ref, mate_ref, *refs):
    chunks, (own_ref, other_ref) = refs[:-2], refs[-2:]
    own = mine_ref.shape[0]
    total = None
    for j, chunk in enumerate(chunks):
        cols = pl.ds(pl.multiple_of(places[j], DH), chunk.shape[1])
        left = jnp.concatenate([mine_ref[:, cols], mate_ref[:, cols]], 0)
        part = dot(left, chunk[...], NT)
        total = part if total is None else total + part
    total = total.astype(BF16)
    own_ref[...] = total[:own]
    other_ref[...] = total[own:]


def mixed_kernel(count, places, core, *refs):
    own_out, mate_out = refs[-2:]
    attn, mate, weight = refs[:count], refs[count], refs[count + 1]
    chunks = refs[count + 2 : -2]
    each = len(chunks) // (count - 1)
    own = own_out.shape[0]
    cols = pl.ds(pl.multiple_of(core[0] * DH, DH), DH)
    left = jnp.concatenate(
        [jnp.concatenate([attn[s][:, cols], mate[s]], 0) for s in range(count)], 1
    )
    for j in range(each):
        wide = chunks[j].shape[1]
        there = pl.ds(pl.multiple_of(places[j], DH), wide)
        right = jnp.concatenate(
            [weight[:, there]] + [chunks[s * each + j][...] for s in range(count - 1)], 0
        )
        part = dot(left, right, NN)
        own_out[:, there] = part[:own]
        mate_out[:, there] = part[own:]


def collect_kernel(scale, where, q_ref, *refs):
    g_ref, state_ref = refs[-2:]
    count = (len(refs) - 2) // 2
    own = refs[0].shape[0]
    place, core = where[0], where[1]
    mine = pl.ds(pl.multiple_of(core * DH, DH), DH)
    mate = pl.ds(pl.multiple_of((1 - core) * DH, DH), DH)
    for s in range(count):
        block = lax.rem(place + s, count)
        here = pl.ds(pl.multiple_of(block * own, own), own)
        g_ref[here, mine] = refs[s][...]
        g_ref[here, mate] = refs[count + s][...]
    for h in range(q_ref.shape[1] // DH):
        cols = slice(h * DH, (h + 1) * DH)
        state_ref[h] = scale * dot(q_ref[:, cols], g_ref[:, cols], TN)


def backward_kernel(
    scale,
    count,
    q_ref,
    k_ref,
    v_ref,
    g_ref,
    probs_ref,
    inner_ref,
    soft_ref,
    state_ref,
    dq_ref,
    dk_ref,
    dv_ref,
):
    rows, width = q_ref.shape
    blk = rows // count
    inv_root = 1.0 / math.sqrt(DH)
    triangle = lower_triangle(blk)
    for h in range(width // DH):
        cols = slice(h * DH, (h + 1) * DH)
        for i in reversed(range(count)):
            here = slice(i * blk, (i + 1) * blk)
            upto = slice(0, (i + 1) * blk)
            q, g = q_ref[here, cols], g_ref[here, cols]
            k = k_ref[upto, cols]
            probs = probs_ref[h, here, upto]
            dprod = dot(g, v_ref[upto, cols], NT)
            delta = jnp.sum(g.astype(F32) * soft_ref[here, cols], -1, keepdims=True)
            dscore = (probs.astype(F32) * (dprod - delta) * inv_root).astype(BF16)
            last = jnp.where(triangle, dprod[:, i * blk :], 0.0)
            dinner = jnp.concatenate([dprod[:, : i * blk], last], 1) if i else last
            dinner = dinner.astype(BF16)
            dq_ref[here, cols] = (
                dot(dscore, k, NN)
                + scale * (dot(dinner, k, NN) + dot_wide(g, state_ref[h], NT))
            ).astype(BF16)
            dk = dot(dscore, q, TN) + scale * dot(dinner, q, TN)
            dv = dot(probs, g, TN) + scale * dot(inner_ref[h, here, upto], g, TN)
            if i == count - 1:
                dk_ref[upto, cols] = dk
                dv_ref[upto, cols] = dv
            else:
                dk_ref[upto, cols] += dk
                dv_ref[upto, cols] += dv


def close_kernel(k_ref, v_ref, dk_ref, dv_ref, state_ref, gk_ref, gv_ref):
    for h in range(k_ref.shape[1] // DH):
        cols = slice(h * DH, (h + 1) * DH)
        state = state_ref[h]
        gk_ref[:, cols] = (dk_ref[:, cols] + dot_wide(v_ref[:, cols], state, NT)).astype(BF16)
        gv_ref[:, cols] = (dv_ref[:, cols] + dot_wide(k_ref[:, cols], state, NN)).astype(BF16)


def send(x, flip, shift):
    shards, heads = lax.axis_size("ctx"), lax.axis_size("head")
    pairs = [
        (c * heads + z, (c ^ flip) * heads + (z + shift) % heads)
        for c in range(shards)
        for z in range(heads)
    ]
    return lax.ppermute(x, ("ctx", "head"), pairs)


def carried_in(part, reverse):
    place = lax.axis_index("ctx")
    total = part
    carried = jnp.zeros_like(part)
    step = 1
    while step < lax.axis_size("ctx"):
        other = send(total, step, 0)
        upper = (place & step) > 0
        carried = carried + jnp.where(upper ^ reverse, other, 0.0)
        total = total + other
        step *= 2
    return carried


def spread(piece, chip, chips):
    wide = piece.shape[1]
    if chips != 4:
        shards = lax.axis_size("ctx")
        groups = [list(range(core, shards, 2)) for core in range(2)]
        whole = lax.all_gather(piece, "ctx", axis=1, tiled=True, axis_index_groups=groups)
        return [whole], [jnp.int32(0)]
    half = wide // 2
    along_x, along_y = send(piece, 2, 0), send(piece, 4, 0)
    first, second = send(along_x[:, :half], 4, 0), send(along_y[:, half:], 2, 0)
    far = (chip ^ 3) * wide
    return (
        [piece, along_x, along_y, first, second],
        [chip * wide, (chip ^ 1) * wide, (chip ^ 2) * wide, far, far + half],
    )


def on_device(query, key, value, block_mask, out_weight, cotangent):
    rows, width = query.shape
    heads = width // DH
    shards, count = lax.axis_size("ctx"), lax.axis_size("head")
    model = out_weight.shape[1]
    own = rows // count
    scale = 1.0 / math.sqrt(DH * rows * shards)
    blocks = block_mask.shape[0]
    ctx, place = lax.axis_index("ctx"), lax.axis_index("head")
    core, chip, chips = ctx & 1, ctx >> 1, shards // 2
    place1, core1 = place.reshape(1), core.reshape(1)
    square = rows * rows * DH * heads

    weight = lax.dynamic_slice_in_dim(out_weight, core * DH, DH, 0)
    wide = model // chips
    piece = lax.dynamic_slice_in_dim(weight, chip * wide, wide, 1)
    shifts = sorted(range(1, count), key=lambda s: min(s, count - s))
    arrived = {s: send(piece, 0, s) for s in shifts}
    mate_cotangent = send(cotangent, 1, 0)

    own_state = jnp.einsum(
        "jhd,jhe->hde",
        key.reshape(rows, heads, DH),
        value.reshape(rows, heads, DH),
        preferred_element_type=F32,
    )
    linear_state = carried_in(own_state, False)
    probs, inner, soft, pre = call(
        functools.partial(forward_kernel, scale),
        [((heads, rows, rows), BF16)] * 2 + [((rows, width), F32)] * 2,
        [query, key, value],
        6 * square,
        [block_mask],
    )

    def grads(chunks, places):
        return call(
            grad_kernel,
            [((own, DH), BF16)] * 2,
            [cotangent, mate_cotangent, *chunks],
            4 * own * DH * model,
            [jnp.stack(places)],
        )

    chunks = {}
    mine, mate = [None] * count, [None] * count
    mine[0], other = grads([weight], [jnp.int32(0)])
    mate[0] = send(other, 1, 0)
    for s in shifts:
        chunks[s], places = spread(arrived[s], chip, chips)
        here, other = grads(chunks[s], places)
        mine[s], mate[s] = send(here, 0, -s), send(other, 1, -s)

    attn = call(
        functools.partial(attn_kernel, scale),
        [((own, width), BF16)] * count,
        [query, pre, linear_state],
        4 * rows * width * DH,
        [place1],
    )
    attn = [attn[0]] + [send(attn[s], 0, s) for s in range(1, count)]
    across = jnp.stack([lax.dynamic_slice_in_dim(a, (1 - core) * DH, DH, 1) for a in attn])
    across = send(across, 1, 0)
    part, mate_part = call(
        functools.partial(mixed_kernel, count),
        [((own, model), F32)] * 2,
        [*attn, across, weight, *(a for s in range(1, count) for a in chunks[s])],
        4 * own * DH * count * model,
        [jnp.stack(places), core1],
    )
    mixed = (part + send(mate_part, 1, 0)).astype(BF16)

    g, own_grad = call(
        functools.partial(collect_kernel, scale),
        [((rows, width), BF16), ((heads, DH, DH), F32)],
        [query, *mine, *mate],
        2 * rows * width * DH,
        [jnp.stack([place, core])],
    )
    grad_state = carried_in(own_grad, True)
    grad_query, dk, dv = call(
        functools.partial(backward_kernel, scale, blocks),
        [((rows, width), BF16)] + [((rows, width), F32)] * 2,
        [query, key, value, g, probs, inner, soft, linear_state],
        14 * square,
    )
    grad_key, grad_value = call(
        close_kernel,
        [((rows, width), BF16)] * 2,
        [key, value, dk, dv, grad_state],
        8 * rows * width * DH,
    )
    return mixed, grad_query, grad_key, grad_value


def solution(mesh):
    return jax.shard_map(
        on_device,
        mesh=mesh,
        in_specs=(
            P("ctx", "head"),
            P("ctx", "head"),
            P("ctx", "head"),
            P("ctx", None),
            P("head", None),
            P(("ctx", "head"), None),
        ),
        out_specs=(P(("ctx", "head"), None), P("ctx", "head"), P("ctx", "head"), P("ctx", "head")),
        check_vma=False,
    )
```

```python
import functools
import math

import jax
import jax.numpy as jnp
from jax import lax
from jax.experimental import pallas as pl
from jax.experimental.pallas import tpu as pltpu
from jax.sharding import PartitionSpec as P

DH = 128
F32 = jnp.float32
BF16 = jnp.bfloat16
NN = ((1,), (0,))
NT = ((1,), (1,))
TN = ((0,), (0,))
MIB = 1 << 20


def dot(a, b, dims):
    return lax.dot_general(a, b, (dims, ((), ())), preferred_element_type=F32)


def dot_wide(a, b, dims):
    high = b.astype(BF16)
    low = (b - high.astype(F32)).astype(BF16)
    return dot(a, high, dims) + dot(a, low, dims)


def call(body, outs, args, smem=(), after=(), room=8):
    def kernel(*refs):
        first = len(smem) + len(args)
        body(*refs[:first], *refs[first + len(after) :])

    return pl.pallas_call(
        kernel,
        out_shape=[jax.ShapeDtypeStruct(s, t) for s, t in outs],
        in_specs=[pl.BlockSpec(memory_space=pltpu.SMEM) for _ in smem]
        + [pl.BlockSpec(memory_space=pltpu.VMEM) for _ in args]
        + [pl.BlockSpec(memory_space=pl.ANY) for _ in after],
        out_specs=[pl.BlockSpec(memory_space=pltpu.VMEM) for _ in outs],
        compiler_params=pltpu.CompilerParams(vmem_limit_bytes=room * MIB),
        cost_estimate=pl.CostEstimate(flops=1, bytes_accessed=1, transcendentals=0),
    )(*smem, *args, *after)


def lower_triangle(blk):
    return lax.broadcasted_iota(jnp.int32, (blk, blk), 0) >= lax.broadcasted_iota(
        jnp.int32, (blk, blk), 1
    )


def forward_kernel(scale, mask, q_ref, k_ref, v_ref, probs_ref, inner_ref, soft_ref, pre_ref):
    rows, width = q_ref.shape
    count = mask.shape[0]
    blk = rows // count
    inv_root = 1.0 / math.sqrt(DH)
    triangle = lower_triangle(blk)
    for h in range(width // DH):
        cols = slice(h * DH, (h + 1) * DH)
        for i in range(count):
            here = slice(i * blk, (i + 1) * blk)
            upto = slice(0, (i + 1) * blk)
            raw = dot(q_ref[here, cols], k_ref[upto, cols], NT)
            scores, inner = [], []
            for j in range(i + 1):
                part = raw[:, j * blk : (j + 1) * blk]
                keep = triangle if j == i else mask[i, j] > 0
                scores.append(jnp.where(keep, part * inv_root, -1e30))
                inner.append(jnp.where(triangle, part, 0.0) if j == i else part)
            scores = jnp.concatenate(scores, 1)
            inner = jnp.concatenate(inner, 1).astype(BF16)
            expo = jnp.exp(scores - jnp.max(scores, -1, keepdims=True))
            probs = (expo / jnp.sum(expo, -1, keepdims=True)).astype(BF16)
            v = v_ref[upto, cols]
            soft = dot(probs, v, NN)
            probs_ref[h, here, upto] = probs
            inner_ref[h, here, upto] = inner
            soft_ref[here, cols] = soft
            pre_ref[here, cols] = soft + scale * dot(inner, v, NN)


def state_kernel(k_ref, v_ref, state_ref):
    for h in range(k_ref.shape[1] // DH):
        cols = slice(h * DH, (h + 1) * DH)
        state_ref[h] = dot(k_ref[:, cols], v_ref[:, cols], TN)


def attn_kernel(scale, where, q_ref, pre_ref, states_ref, *refs):
    out_refs, state_ref = refs[:-1], refs[-1]
    place, ctx = where[0], where[1]
    count = len(out_refs)
    own = out_refs[0].shape[0]
    total = jnp.zeros(state_ref.shape, F32)
    for c in range(states_ref.shape[0] - 1):
        total = total + jnp.where(c < ctx, states_ref[c], 0.0)
    state_ref[...] = total
    for s in range(count):
        block = lax.rem(place + s, count)
        here = pl.ds(pl.multiple_of(block * own, own), own)
        for h in range(q_ref.shape[1] // DH):
            cols = slice(h * DH, (h + 1) * DH)
            inter = dot_wide(q_ref[here, cols], state_ref[h], NN)
            out_refs[s][:, cols] = (pre_ref[here, cols] + scale * inter).astype(BF16)


def grad_kernel(whole, places, mine_ref, mate_ref, *refs):
    chunks, outs = refs[:-2], refs[-2:]
    own = mine_ref.shape[0]
    total = None
    for j, chunk in enumerate(chunks):
        cols = slice(None) if whole else pl.ds(pl.multiple_of(places[j], DH), chunk.shape[1])
        left = jnp.concatenate([mine_ref[:, cols], mate_ref[:, cols]], 0)
        part = dot(left, chunk[...], NT)
        total = part if total is None else total + part
    total = total.astype(BF16)
    outs[0][...] = total[:own]
    outs[1][...] = total[own:]


def mixed_kernel(count, each, places, where, *refs):
    own_out, mate_out = refs[-2:]
    attn, mate, weight = refs[:count], refs[count], refs[count + 1]
    chunks = list(refs[count + 2 : -2])
    sets = [[chunks.pop(0)[...] for _ in range(n)] for n in each]
    own = own_out.shape[0]
    cols = pl.ds(pl.multiple_of(where[2] * DH, DH), DH)
    left = jnp.concatenate(
        [jnp.concatenate([attn[s][:, cols], mate[s]], 0) for s in range(count)], 1
    )
    few = min(each)
    sets = [
        some[: few - 1] + [jnp.concatenate(some[few - 1 :], 1) if len(some) > few else some[-1]]
        for some in sets
    ]
    for j in range(few):
        there = pl.ds(pl.multiple_of(places[j], DH), sets[0][j].shape[1])
        right = jnp.concatenate([weight[:, there]] + [some[j] for some in sets], 0)
        part = dot(left, right, NN)
        own_out[:, there] = part[:own]
        mate_out[:, there] = part[own:]


def collect_kernel(scale, shifts, where, q_ref, *refs):
    g_ref, state_ref = refs[-2:]
    count = len(shifts)
    direct, across, last = refs[:count], refs[count], refs[count + 1]
    own = g_ref.shape[0] // count
    place, core = where[0], where[2]
    mine = pl.ds(pl.multiple_of(core * DH, DH), DH)
    mate = pl.ds(pl.multiple_of((1 - core) * DH, DH), DH)
    for n, s in enumerate(shifts):
        block = lax.rem(place + s, count)
        here = pl.ds(pl.multiple_of(block * own, own), own)
        g_ref[here, mine] = direct[n][:own]
        g_ref[here, mate] = across[n] if n < count - 1 else last[...]
    for h in range(q_ref.shape[1] // DH):
        cols = slice(h * DH, (h + 1) * DH)
        state_ref[h] = scale * dot(q_ref[:, cols], g_ref[:, cols], TN)


def backward_kernel(
    scale,
    count,
    q_ref,
    k_ref,
    v_ref,
    g_ref,
    probs_ref,
    inner_ref,
    soft_ref,
    state_ref,
    dq_ref,
    dk_ref,
    dv_ref,
):
    rows, width = q_ref.shape
    blk = rows // count
    inv_root = 1.0 / math.sqrt(DH)
    triangle = lower_triangle(blk)
    for h in range(width // DH):
        cols = slice(h * DH, (h + 1) * DH)
        for i in reversed(range(count)):
            here = slice(i * blk, (i + 1) * blk)
            upto = slice(0, (i + 1) * blk)
            q, g = q_ref[here, cols], g_ref[here, cols]
            k = k_ref[upto, cols]
            probs = probs_ref[h, here, upto]
            dprod = dot(g, v_ref[upto, cols], NT)
            delta = jnp.sum(g.astype(F32) * soft_ref[here, cols], -1, keepdims=True)
            dscore = (probs.astype(F32) * (dprod - delta) * inv_root).astype(BF16)
            last = jnp.where(triangle, dprod[:, i * blk :], 0.0)
            dinner = jnp.concatenate([dprod[:, : i * blk], last], 1) if i else last
            dinner = dinner.astype(BF16)
            dq_ref[here, cols] = (
                dot(dscore, k, NN)
                + scale * (dot(dinner, k, NN) + dot_wide(g, state_ref[h], NT))
            ).astype(BF16)
            dk = dot(dscore, q, TN) + scale * dot(dinner, q, TN)
            dv = dot(probs, g, TN) + scale * dot(inner_ref[h, here, upto], g, TN)
            if i == count - 1:
                dk_ref[upto, cols] = dk
                dv_ref[upto, cols] = dv
            else:
                dk_ref[upto, cols] += dk
                dv_ref[upto, cols] += dv


def close_kernel(k_ref, v_ref, dk_ref, dv_ref, state_ref, gk_ref, gv_ref):
    for h in range(k_ref.shape[1] // DH):
        cols = slice(h * DH, (h + 1) * DH)
        state = state_ref[h]
        gk_ref[:, cols] = (dk_ref[:, cols] + dot_wide(v_ref[:, cols], state, NT)).astype(BF16)
        gv_ref[:, cols] = (dv_ref[:, cols] + dot_wide(k_ref[:, cols], state, NN)).astype(BF16)


def send(x, flip, shift):
    shards, heads = lax.axis_size("ctx"), lax.axis_size("head")
    pairs = [
        (c * heads + z, (c ^ flip) * heads + (z + shift) % heads)
        for c in range(shards)
        for z in range(heads)
    ]
    return lax.ppermute(x, ("ctx", "head"), pairs)


def later_chips(total, chip, chips):
    carried = jnp.zeros_like(total)
    if chips == 4:
        for flip in (3, 2, 1):
            there = send(total, 2 * flip, 0)
            carried = carried + jnp.where((chip ^ flip) > chip, there, 0.0)
        return carried, there
    step = 1
    while step < chips:
        there = send(total, 2 * step, 0)
        carried = carried + jnp.where((chip & step) == 0, there, 0.0)
        total = total + there
        step *= 2
    return carried, there


def spread(piece, chip, chips, way):
    wide = piece.shape[1]
    if chips != 4:
        shards = lax.axis_size("ctx")
        groups = [list(range(core, shards, 2)) for core in range(2)]
        whole = lax.all_gather(piece, "ctx", axis=1, tiled=True, axis_index_groups=groups)
        return [whole], [jnp.int32(0)]
    far = (chip ^ 3) * wide
    if way == 0:
        along_x = send(piece, 2, 0)
        along_y = send(piece, 4, 0)
        ends = [send(along_x, 4, 0)]
    elif way == 1:
        along_y = send(piece, 4, 0)
        along_x = send(piece, 2, 0)
        ends = [send(along_y, 2, 0)]
    else:
        half = wide // 2
        along_x, along_y = send(piece, 2, 0), send(piece, 4, 0)
        ends = [send(along_x[:, :half], 4, 0), send(along_y[:, half:], 2, 0)]
    places = [chip * wide, (chip ^ 1) * wide, (chip ^ 2) * wide, far, far + wide // 2]
    arrays = [piece, along_x, along_y, *ends]
    return arrays, places[: len(arrays)]


def on_device(query, key, value, block_mask, out_weight, cotangent):
    rows, width = query.shape
    heads = width // DH
    shards, count = lax.axis_size("ctx"), lax.axis_size("head")
    model = out_weight.shape[1]
    own = rows // count
    scale = 1.0 / math.sqrt(DH * rows * shards)
    blocks = block_mask.shape[0]
    ctx, place = lax.axis_index("ctx"), lax.axis_index("head")
    core, chip, chips = ctx & 1, ctx >> 1, shards // 2
    where = jnp.stack([place, ctx, core])
    flat, states = (rows, width), (heads, DH, DH)

    wide = model // chips
    piece = lax.dynamic_slice(out_weight, (core * DH, chip * wide), (DH, wide))
    weight = lax.dynamic_slice_in_dim(out_weight, core * DH, DH, 0)
    shifts = sorted(range(1, count), key=lambda s: min(s, count - s))
    arrived = {0: piece}
    for s in shifts:
        step = 1 if s <= count // 2 else -1
        arrived[s] = send(arrived[(s - step) % count], 0, step)
    mate_cotangent = send(cotangent, 1, 0)

    (own_state,) = call(state_kernel, [(states, F32)], [key, value], after=[piece])
    every_state = lax.all_gather(own_state, "ctx")
    probs, inner, soft, pre = call(
        functools.partial(forward_kernel, scale),
        [((heads, rows, rows), BF16)] * 2 + [(flat, F32)] * 2,
        [query, key, value],
        [block_mask],
    )

    chunks, places = {}, None
    for n, s in enumerate(shifts):
        chunks[s], starts = spread(arrived[s], chip, chips, min(n, 2))
        if places is None or len(starts) > len(places):
            places = starts
    places = jnp.stack(places)

    def grads(some, whole=False, after=()):
        return call(
            functools.partial(grad_kernel, whole),
            [((own, DH), BF16)] * 2,
            [cotangent, mate_cotangent, *some],
            [places],
            after,
        )

    direct, across = [], []
    for s in [0] + shifts[:-1]:
        both = grads(chunks[s]) if s else grads([weight], True)
        both = send(jnp.concatenate(both, 0), 0, -s) if s else jnp.concatenate(both, 0)
        direct.append(both)
        across.append(both[own:])
    across = send(jnp.stack(across), 1, 0)
    *attn, linear_state = call(
        functools.partial(attn_kernel, scale),
        [((own, width), BF16)] * count + [(states, F32)],
        [query, pre, every_state],
        [where],
    )
    attn = [attn[0]] + [send(attn[s], 0, s) for s in range(1, count)]
    for_mate = jnp.stack([lax.dynamic_slice_in_dim(a, (1 - core) * DH, DH, 1) for a in attn])
    for_mate = send(for_mate, 1, 0)

    mine, other = grads(chunks[shifts[-1]], after=[for_mate])
    direct.append(send(mine, 0, -shifts[-1]))
    last = send(other, 1, -shifts[-1])

    g, own_grad = call(
        functools.partial(collect_kernel, scale, [0] + shifts),
        [(flat, BF16), (states, F32)],
        [query, *direct, across, last],
        [where],
    )
    here = jnp.where(core == 0, own_grad[0], own_grad[1])
    got = send(jnp.where(core == 0, own_grad[1], own_grad[0]), 1, 0)
    total = here + got
    later, neighbour = later_chips(total, chip, chips)
    part, mate_part = call(
        functools.partial(
            mixed_kernel, count, [len(chunks[s]) for s in range(1, count)]
        ),
        [((own, model), F32)] * 2,
        [*attn, for_mate, weight, *(a for s in range(1, count) for a in chunks[s])],
        [places, where],
        after=[neighbour],
        room=16,
    )
    mixed = (part + send(mate_part, 1, 0)).astype(BF16)
    back = send(jnp.where(core == 0, later, later + here), 1, 0)
    keep = jnp.where(core == 0, later + got, later)
    grad_state = jnp.stack([jnp.where(core == 0, keep, back), jnp.where(core == 0, back, keep)])

    grad_query, dk, dv = call(
        functools.partial(backward_kernel, scale, blocks),
        [(flat, BF16)] + [(flat, F32)] * 2,
        [query, key, value, g, probs, inner, soft, linear_state],
        after=[total],
    )
    grad_key, grad_value = call(
        close_kernel, [(flat, BF16)] * 2, [key, value, dk, dv, grad_state]
    )
    return mixed, grad_query, grad_key, grad_value


def solution(mesh):
    return jax.shard_map(
        on_device,
        mesh=mesh,
        in_specs=(
            P("ctx", "head"),
            P("ctx", "head"),
            P("ctx", "head"),
            P("ctx", None),
            P("head", None),
            P(("ctx", "head"), None),
        ),
        out_specs=(P(("ctx", "head"), None), P("ctx", "head"), P("ctx", "head"), P("ctx", "head")),
        check_vma=False,
    )
```

```python
import functools
import math

import jax
import jax.numpy as jnp
from jax import lax
from jax.experimental import pallas as pl
from jax.experimental.pallas import tpu as pltpu
from jax.sharding import PartitionSpec as P

DH = 128
F32 = jnp.float32
BF16 = jnp.bfloat16
NN = ((1,), (0,))
NT = ((1,), (1,))
TN = ((0,), (0,))
MIB = 1 << 20


def dot(a, b, dims):
    return lax.dot_general(a, b, (dims, ((), ())), preferred_element_type=F32)


def dot_wide(a, b, dims):
    high = b.astype(BF16)
    low = (b - high.astype(F32)).astype(BF16)
    return dot(a, high, dims) + dot(a, low, dims)


def whole_block(shape):
    return pl.BlockSpec(shape, lambda i: (0,) * len(shape))


def call(body, outs, args, smem=(), after=(), steps=1, specs=None, scratch=(), room=16, flops=1):
    ins, results = specs or ([whole_block(a.shape) for a in args], [whole_block(o) for o, _ in outs])

    def kernel(*refs):
        first = len(smem) + len(args)
        body(*refs[:first], *refs[first + len(after) :])

    moved = sum(a.size * a.dtype.itemsize for a in args)
    moved += sum(math.prod(s) * jnp.dtype(t).itemsize for s, t in outs)
    return pl.pallas_call(
        kernel,
        grid=(steps,),
        out_shape=[jax.ShapeDtypeStruct(s, t) for s, t in outs],
        in_specs=[pl.BlockSpec(memory_space=pltpu.SMEM) for _ in smem]
        + list(ins)
        + [pl.BlockSpec(memory_space=pl.ANY) for _ in after],
        out_specs=list(results),
        scratch_shapes=list(scratch),
        compiler_params=pltpu.CompilerParams(vmem_limit_bytes=room * MIB),
        cost_estimate=pl.CostEstimate(
            flops=int(flops), bytes_accessed=int(moved), transcendentals=0
        ),
    )(*smem, *args, *after)


def lower_triangle(blk):
    return lax.broadcasted_iota(jnp.int32, (blk, blk), 0) >= lax.broadcasted_iota(
        jnp.int32, (blk, blk), 1
    )


def forward_kernel(scale, mask, q_ref, k_ref, v_ref, probs_ref, inner_ref, soft_ref, pre_ref):
    rows, width = q_ref.shape
    count = mask.shape[0]
    blk = rows // count
    inv_root = 1.0 / math.sqrt(DH)
    triangle = lower_triangle(blk)
    for h in range(width // DH):
        cols = slice(h * DH, (h + 1) * DH)
        for i in range(count):
            here = slice(i * blk, (i + 1) * blk)
            upto = slice(0, (i + 1) * blk)
            raw = dot(q_ref[here, cols], k_ref[upto, cols], NT)
            scores, inner = [], []
            for j in range(i + 1):
                part = raw[:, j * blk : (j + 1) * blk]
                keep = triangle if j == i else mask[i, j] > 0
                scores.append(jnp.where(keep, part * inv_root, -1e30))
                inner.append(jnp.where(triangle, part, 0.0) if j == i else part)
            scores = jnp.concatenate(scores, 1)
            inner = jnp.concatenate(inner, 1).astype(BF16)
            expo = jnp.exp(scores - jnp.max(scores, -1, keepdims=True))
            probs = (expo / jnp.sum(expo, -1, keepdims=True)).astype(BF16)
            v = v_ref[upto, cols]
            soft = dot(probs, v, NN)
            probs_ref[h, here, upto] = probs
            inner_ref[h, here, upto] = inner
            soft_ref[here, cols] = soft
            pre_ref[here, cols] = soft + scale * dot(inner, v, NN)


def split_heads(core, parts, mine_ref, other_ref):
    mine_ref[...] = jnp.where(core == 0, parts[0], parts[1])
    other_ref[...] = jnp.where(core == 0, parts[1], parts[0])


def both_heads(core, mine_ref, other_ref):
    mine, other = mine_ref[...], other_ref[...]
    return jnp.where(core == 0, mine, other), jnp.where(core == 0, other, mine)


def state_kernel(where, k_ref, v_ref, mine_ref, other_ref):
    heads = [slice(h * DH, (h + 1) * DH) for h in range(2)]
    parts = [dot(k_ref[:, cols], v_ref[:, cols], TN) for cols in heads]
    split_heads(where[2], parts, mine_ref, other_ref)


def carry_kernel(flags, here_ref, got_ref, *refs):
    totals, (keep_ref, back_ref) = refs[:-2], refs[-2:]
    carried = jnp.zeros(here_ref.shape, F32)
    for n, total in enumerate(totals):
        carried = carried + jnp.where(flags[n] > 0, total[...], 0.0)
    counts = flags[len(totals)] > 0
    keep_ref[...] = carried + jnp.where(counts, got_ref[...], 0.0)
    back_ref[...] = carried + jnp.where(counts, 0.0, here_ref[...])


def attn_kernel(scale, where, q_ref, pre_ref, mine_ref, other_ref, *out_refs):
    count = len(out_refs)
    states = both_heads(where[2], mine_ref, other_ref)
    own = out_refs[0].shape[0]
    for s in range(count):
        block = lax.rem(where[0] + s, count)
        here = pl.ds(pl.multiple_of(block * own, own), own)
        for h in range(q_ref.shape[1] // DH):
            cols = slice(h * DH, (h + 1) * DH)
            inter = dot_wide(q_ref[here, cols], states[h], NN)
            out_refs[s][:, cols] = (pre_ref[here, cols] + scale * inter).astype(BF16)


def grad_kernel(count, where, mine_ref, mate_ref, weight_ref, *refs):
    outs, total_ref = refs[:-1], refs[-1]
    own = mine_ref.shape[0]
    step = pl.program_id(0)
    part = dot(jnp.concatenate([mine_ref[...], mate_ref[...]], 0), weight_ref[0], NT)

    @pl.when(step == 0)
    def _():
        total_ref[...] = part

    @pl.when(step > 0)
    def _():
        total_ref[...] += part

    @pl.when(step == pl.num_programs(0) - 1)
    def _():
        for s in range(count):
            z = lax.rem(where[0] + s, count)
            block = total_ref[:, pl.ds(pl.multiple_of(z * DH, DH), DH)].astype(BF16)
            outs[s][...] = block


def mixed_kernel(count, where, *refs):
    attn, mate = refs[:count], refs[count : 2 * count]
    weight_ref, own_out, *mate_outs, left_ref = refs[2 * count :]
    step = pl.program_id(0)
    each = pl.num_programs(0) // len(mate_outs)
    own = own_out.shape[0]

    @pl.when(step == 0)
    def _():
        cols = pl.ds(pl.multiple_of(where[2] * DH, DH), DH)
        for s in range(count):
            z = lax.rem(where[0] - s + count, count)
            there = pl.ds(pl.multiple_of(z * DH, DH), DH)
            left_ref[:own, there] = attn[s][:, cols]
            left_ref[own:, there] = mate[s][:, cols]

    part = dot(left_ref[...], weight_ref[0], NN)
    own_out[...] = part[:own]
    for n, mate_out in enumerate(mate_outs):

        @pl.when(step // each == n)
        def _():
            mate_out[...] = part[own:]


def collect_kernel(scale, count, where, q_ref, *refs):
    direct, across = refs[:count], refs[count : 2 * count]
    g_ref, mine_ref, other_ref = refs[2 * count :]
    own = g_ref.shape[0] // count
    mine = pl.ds(pl.multiple_of(where[2] * DH, DH), DH)
    mate = pl.ds(pl.multiple_of((1 - where[2]) * DH, DH), DH)
    for s in range(count):
        block = lax.rem(where[0] - s + count, count)
        here = pl.ds(pl.multiple_of(block * own, own), own)
        g_ref[here, mine] = direct[s][:own]
        g_ref[here, mate] = across[s][own:]
    heads = [slice(h * DH, (h + 1) * DH) for h in range(2)]
    parts = [scale * dot(q_ref[:, cols], g_ref[:, cols], TN) for cols in heads]
    split_heads(where[2], parts, mine_ref, other_ref)


def backward_kernel(
    scale,
    count,
    where,
    q_ref,
    k_ref,
    v_ref,
    g_ref,
    probs_ref,
    inner_ref,
    soft_ref,
    mine_ref,
    other_ref,
    dq_ref,
    dk_ref,
    dv_ref,
):
    rows, width = q_ref.shape
    blk = rows // count
    inv_root = 1.0 / math.sqrt(DH)
    triangle = lower_triangle(blk)
    states = both_heads(where[2], mine_ref, other_ref)
    for h in range(width // DH):
        cols = slice(h * DH, (h + 1) * DH)
        for i in reversed(range(count)):
            here = slice(i * blk, (i + 1) * blk)
            upto = slice(0, (i + 1) * blk)
            q, g = q_ref[here, cols], g_ref[here, cols]
            k = k_ref[upto, cols]
            probs = probs_ref[h, here, upto]
            dprod = dot(g, v_ref[upto, cols], NT)
            delta = jnp.sum(g.astype(F32) * soft_ref[here, cols], -1, keepdims=True)
            dscore = (probs.astype(F32) * (dprod - delta) * inv_root).astype(BF16)
            last = jnp.where(triangle, dprod[:, i * blk :], 0.0)
            dinner = jnp.concatenate([dprod[:, : i * blk], last], 1) if i else last
            dinner = dinner.astype(BF16)
            dq_ref[here, cols] = (
                dot(dscore, k, NN)
                + scale * (dot(dinner, k, NN) + dot_wide(g, states[h], NT))
            ).astype(BF16)
            dk = dot(dscore, q, TN) + scale * dot(dinner, q, TN)
            dv = dot(probs, g, TN) + scale * dot(inner_ref[h, here, upto], g, TN)
            if i == count - 1:
                dk_ref[upto, cols] = dk
                dv_ref[upto, cols] = dv
            else:
                dk_ref[upto, cols] += dk
                dv_ref[upto, cols] += dv


def close_kernel(where, k_ref, v_ref, dk_ref, dv_ref, mine_ref, other_ref, gk_ref, gv_ref):
    states = both_heads(where[2], mine_ref, other_ref)
    for h in range(k_ref.shape[1] // DH):
        cols = slice(h * DH, (h + 1) * DH)
        state = states[h]
        gk_ref[:, cols] = (dk_ref[:, cols] + dot_wide(v_ref[:, cols], state, NT)).astype(BF16)
        gv_ref[:, cols] = (dv_ref[:, cols] + dot_wide(k_ref[:, cols], state, NN)).astype(BF16)


def send(x, flip, shift):
    shards, heads = lax.axis_size("ctx"), lax.axis_size("head")
    pairs = [
        (c * heads + z, (c ^ flip) * heads + (z + shift) % heads)
        for c in range(shards)
        for z in range(heads)
    ]
    return lax.ppermute(x, ("ctx", "head"), pairs)


def exchange(mine, other, core, chip, chips, later):
    got = send(other, 1, 0)
    total = mine + got
    totals, flags = [], []
    if chips == 4:
        for flip in (1, 2, 3):
            totals.append(send(total, 2 * flip, 0))
            flags.append(((chip ^ flip) > chip) == later)
    else:
        step = 1
        while step < chips:
            totals.append(send(total, 2 * step, 0))
            flags.append(((chip & step) == 0) == later)
            total = total + totals[-1]
            step *= 2
    flags.append((core == 0) == later)
    return jnp.stack(flags).astype(jnp.int32), [mine, got, *totals]


def on_device(query, key, value, block_mask, out_weight, cotangent):
    rows, width = query.shape
    heads = width // DH
    shards, count = lax.axis_size("ctx"), lax.axis_size("head")
    model = out_weight.shape[1]
    own = rows // count
    scale = 1.0 / math.sqrt(DH * rows * shards)
    blocks = block_mask.shape[0]
    ctx, place = lax.axis_index("ctx"), lax.axis_index("head")
    core, chip, chips = ctx & 1, ctx >> 1, shards // 2
    where = jnp.stack([place, ctx, core])
    flat, square = (rows, width), rows * rows * DH * heads
    pair = [((DH, DH), F32)] * 2

    wide = model // chips
    piece = lax.dynamic_slice(out_weight, (core * DH, chip * wide), (DH, wide))
    groups = [[c * count + z for c in range(k, shards, 2) for z in range(count)] for k in range(2)]
    weight = lax.all_gather(piece, ("ctx", "head"), axis_index_groups=groups)
    weight = weight.reshape(chips, count * DH, wide)
    mate_cotangent = send(cotangent, 1, 0)

    mine, other = call(state_kernel, pair, [key, value], [where], [piece])
    flags, parts = exchange(mine, other, core, chip, chips, False)
    keep, back = call(carry_kernel, pair, parts, [flags])
    linear = [keep, send(back, 1, 0)]
    probs, inner, soft, pre = call(
        functools.partial(forward_kernel, scale),
        [((heads, rows, rows), BF16)] * 2 + [(flat, F32)] * 2,
        [query, key, value],
        [block_mask],
        flops=6 * square,
    )
    attn = call(
        functools.partial(attn_kernel, scale),
        [((own, width), BF16)] * count,
        [query, pre, *linear],
        [where],
    )
    attn = [attn[0]] + [send(attn[s], 0, s) for s in range(1, count)]
    mate_attn = [send(a, 1, 0) for a in attn]

    part_of = pl.BlockSpec((own, wide), lambda i: (0, i))
    weight_of = pl.BlockSpec((1, count * DH, wide), lambda i: (i, 0, 0))
    both = call(
        functools.partial(grad_kernel, count),
        [((2 * own, DH), BF16)] * count,
        [cotangent, mate_cotangent, weight],
        [where],
        mate_attn,
        chips,
        ([part_of, part_of, weight_of], [whole_block((2 * own, DH))] * count),
        [pltpu.VMEM((2 * own, count * DH), F32)],
        flops=4 * own * count * DH * model,
    )
    both = [both[0]] + [send(both[s], 0, s) for s in range(1, count)]
    across = [send(b, 1, 0) for b in both]
    cut = 2
    each = chips // cut
    cuts = [
        pl.BlockSpec((own, wide), lambda i, n=n: (0, jnp.clip(i - n * each, 0, each - 1)))
        for n in range(cut)
    ]
    part, *mate_parts = call(
        functools.partial(mixed_kernel, count),
        [((own, model), F32)] + [((own, model // cut), F32)] * cut,
        [*attn, *mate_attn, weight],
        [where],
        both[1:],
        chips,
        ([whole_block((own, width))] * (2 * count) + [weight_of], [part_of, *cuts]),
        [pltpu.VMEM((2 * own, count * DH), BF16)],
        flops=4 * own * count * DH * model,
    )
    g, mine, other = call(
        functools.partial(collect_kernel, scale, count),
        [(flat, BF16), *pair],
        [query, *both, *across],
        [where],
        [part],
    )
    flags, parts = exchange(mine, other, core, chip, chips, True)

    mate_part = jnp.concatenate([send(p, 1, 0) for p in mate_parts], 1)

    grad_query, dk, dv = call(
        functools.partial(backward_kernel, scale, blocks),
        [(flat, BF16)] + [(flat, F32)] * 2,
        [query, key, value, g, probs, inner, soft, *linear],
        [where],
        flops=14 * square,
    )
    keep, back = call(carry_kernel, pair, parts, [flags], [dk])
    grad_key, grad_value = call(
        close_kernel, [(flat, BF16)] * 2, [key, value, dk, dv, keep, send(back, 1, 0)], [where]
    )
    mixed = (part + mate_part).astype(BF16)
    return mixed, grad_query, grad_key, grad_value


def solution(mesh):
    return jax.shard_map(
        on_device,
        mesh=mesh,
        in_specs=(
            P("ctx", "head"),
            P("ctx", "head"),
            P("ctx", "head"),
            P("ctx", None),
            P("head", None),
            P(("ctx", "head"), None),
        ),
        out_specs=(P(("ctx", "head"), None), P("ctx", "head"), P("ctx", "head"), P("ctx", "head")),
        check_vma=False,
    )
```

```python
import functools
import math

import jax
import jax.numpy as jnp
from jax import lax
from jax.experimental import pallas as pl
from jax.experimental.pallas import tpu as pltpu
from jax.sharding import PartitionSpec as P

DH = 128
F32 = jnp.float32
BF16 = jnp.bfloat16
NN = ((1,), (0,))
NT = ((1,), (1,))
TN = ((0,), (0,))
MIB = 1 << 20


def dot(a, b, dims):
    return lax.dot_general(a, b, (dims, ((), ())), preferred_element_type=F32)


def dot_wide(a, b, dims):
    high = b.astype(BF16)
    low = (b - high.astype(F32)).astype(BF16)
    return dot(a, high, dims) + dot(a, low, dims)


def call(body, outs, args, smem=(), after=(), room=8, flops=1):
    def kernel(*refs):
        first = len(smem) + len(args)
        body(*refs[:first], *refs[first + len(after) :])

    moved = sum(a.size * a.dtype.itemsize for a in args)
    moved += sum(math.prod(s) * jnp.dtype(t).itemsize for s, t in outs)
    return pl.pallas_call(
        kernel,
        out_shape=[jax.ShapeDtypeStruct(s, t) for s, t in outs],
        in_specs=[pl.BlockSpec(memory_space=pltpu.SMEM) for _ in smem]
        + [pl.BlockSpec(memory_space=pltpu.VMEM) for _ in args]
        + [pl.BlockSpec(memory_space=pl.ANY) for _ in after],
        out_specs=[pl.BlockSpec(memory_space=pltpu.VMEM) for _ in outs],
        compiler_params=pltpu.CompilerParams(vmem_limit_bytes=room * MIB),
        cost_estimate=pl.CostEstimate(
            flops=int(flops), bytes_accessed=int(moved), transcendentals=0
        ),
    )(*smem, *args, *after)


def lower_triangle(blk):
    return lax.broadcasted_iota(jnp.int32, (blk, blk), 0) >= lax.broadcasted_iota(
        jnp.int32, (blk, blk), 1
    )


def forward_kernel(scale, mask, q_ref, k_ref, v_ref, probs_ref, inner_ref, soft_ref, pre_ref):
    rows, width = q_ref.shape
    count = mask.shape[0]
    blk = rows // count
    inv_root = 1.0 / math.sqrt(DH)
    triangle = lower_triangle(blk)
    for h in range(width // DH):
        cols = slice(h * DH, (h + 1) * DH)
        for i in range(count):
            here = slice(i * blk, (i + 1) * blk)
            upto = slice(0, (i + 1) * blk)
            raw = dot(q_ref[here, cols], k_ref[upto, cols], NT)
            scores, inner = [], []
            for j in range(i + 1):
                part = raw[:, j * blk : (j + 1) * blk]
                keep = triangle if j == i else mask[i, j] > 0
                scores.append(jnp.where(keep, part * inv_root, -1e30))
                inner.append(jnp.where(triangle, part, 0.0) if j == i else part)
            scores = jnp.concatenate(scores, 1)
            inner = jnp.concatenate(inner, 1).astype(BF16)
            expo = jnp.exp(scores - jnp.max(scores, -1, keepdims=True))
            probs = (expo / jnp.sum(expo, -1, keepdims=True)).astype(BF16)
            v = v_ref[upto, cols]
            soft = dot(probs, v, NN)
            probs_ref[h, here, upto] = probs
            inner_ref[h, here, upto] = inner
            soft_ref[here, cols] = soft
            pre_ref[here, cols] = soft + scale * dot(inner, v, NN)


def split_heads(core, parts, mine_ref, other_ref):
    mine_ref[...] = jnp.where(core == 0, parts[0], parts[1])
    other_ref[...] = jnp.where(core == 0, parts[1], parts[0])


def both_heads(core, mine_ref, other_ref):
    mine, other = mine_ref[...], other_ref[...]
    return jnp.where(core == 0, mine, other), jnp.where(core == 0, other, mine)


def state_kernel(where, k_ref, v_ref, mine_ref, other_ref):
    heads = [slice(h * DH, (h + 1) * DH) for h in range(2)]
    parts = [dot(k_ref[:, cols], v_ref[:, cols], TN) for cols in heads]
    split_heads(where[2], parts, mine_ref, other_ref)


def carry_kernel(flags, here_ref, got_ref, *refs):
    totals, (keep_ref, back_ref) = refs[:-2], refs[-2:]
    carried = jnp.zeros(here_ref.shape, F32)
    for n, total in enumerate(totals):
        carried = carried + jnp.where(flags[n] > 0, total[...], 0.0)
    counts = flags[len(totals)] > 0
    keep_ref[...] = carried + jnp.where(counts, got_ref[...], 0.0)
    back_ref[...] = carried + jnp.where(counts, 0.0, here_ref[...])


def attn_kernel(scale, where, q_ref, pre_ref, mine_ref, other_ref, *out_refs):
    count = len(out_refs)
    states = both_heads(where[2], mine_ref, other_ref)
    own = out_refs[0].shape[0]
    for s in range(count):
        block = lax.rem(where[0] + s, count)
        here = pl.ds(pl.multiple_of(block * own, own), own)
        for h in range(q_ref.shape[1] // DH):
            cols = slice(h * DH, (h + 1) * DH)
            inter = dot_wide(q_ref[here, cols], states[h], NN)
            out_refs[s][:, cols] = (pre_ref[here, cols] + scale * inter).astype(BF16)


def cut_kernel(piece_ref, *out_refs):
    wide = out_refs[0].shape[1]
    for n, out_ref in enumerate(out_refs):
        out_ref[...] = piece_ref[:, n * wide : (n + 1) * wide]


def grad_kernel(whole, added, places, mine_ref, mate_ref, *refs):
    chunks, out_ref = refs[added:-1], refs[-1]
    total = refs[0][...] if added else None
    for j, chunk in enumerate(chunks):
        cols = slice(None) if whole else pl.ds(pl.multiple_of(places[j], DH), chunk.shape[1])
        left = jnp.concatenate([mine_ref[:, cols], mate_ref[:, cols]], 0)
        part = dot(left, chunk[...], NT)
        total = part if total is None else total + part
    out_ref[...] = total.astype(out_ref.dtype)


def mixed_kernel(count, each, places, where, *refs):
    attn, mate, weight = refs[:count], refs[count : 2 * count], refs[2 * count]
    chunks, (own_out, mate_out) = list(refs[2 * count + 1 : -2]), refs[-2:]
    own = own_out.shape[0]
    cols = pl.ds(pl.multiple_of(where[2] * DH, DH), DH)
    left = jnp.concatenate(
        [jnp.concatenate([attn[s][:, cols], mate[s][:, cols]], 0) for s in range(count)], 1
    )
    right = [weight[:, pl.ds(pl.multiple_of(places[0], DH), own_out.shape[1])]]
    for n in each:
        parts = [chunks.pop(0)[...] for _ in range(n)]
        right.append(jnp.concatenate(parts, 1) if n > 1 else parts[0])
    part = dot(left, jnp.concatenate(right, 0), NN)
    own_out[...] = part[:own]
    mate_out[...] = part[own:]


def join_kernel(places, *refs):
    out_ref = refs[-1]
    for n in range(len(refs) // 2):
        wide = refs[2 * n].shape[1]
        there = pl.ds(pl.multiple_of(places[n], DH), wide)
        out_ref[:, there] = (refs[2 * n][...] + refs[2 * n + 1][...]).astype(BF16)


def collect_kernel(scale, count, where, q_ref, *refs):
    direct, across = refs[:count], refs[count : 2 * count]
    g_ref, mine_ref, other_ref = refs[2 * count :]
    own = g_ref.shape[0] // count
    mine = pl.ds(pl.multiple_of(where[2] * DH, DH), DH)
    mate = pl.ds(pl.multiple_of((1 - where[2]) * DH, DH), DH)
    for s in range(count):
        block = lax.rem(where[0] + s, count)
        here = pl.ds(pl.multiple_of(block * own, own), own)
        g_ref[here, mine] = direct[s][:own]
        g_ref[here, mate] = across[s][own:]
    heads = [slice(h * DH, (h + 1) * DH) for h in range(2)]
    parts = [scale * dot(q_ref[:, cols], g_ref[:, cols], TN) for cols in heads]
    split_heads(where[2], parts, mine_ref, other_ref)


def backward_kernel(
    scale,
    count,
    where,
    q_ref,
    k_ref,
    v_ref,
    g_ref,
    probs_ref,
    inner_ref,
    soft_ref,
    mine_ref,
    other_ref,
    dq_ref,
    dk_ref,
    dv_ref,
):
    rows, width = q_ref.shape
    blk = rows // count
    inv_root = 1.0 / math.sqrt(DH)
    triangle = lower_triangle(blk)
    states = both_heads(where[2], mine_ref, other_ref)
    for h in range(width // DH):
        cols = slice(h * DH, (h + 1) * DH)
        for i in reversed(range(count)):
            here = slice(i * blk, (i + 1) * blk)
            upto = slice(0, (i + 1) * blk)
            q, g = q_ref[here, cols], g_ref[here, cols]
            k = k_ref[upto, cols]
            probs = probs_ref[h, here, upto]
            dprod = dot(g, v_ref[upto, cols], NT)
            delta = jnp.sum(g.astype(F32) * soft_ref[here, cols], -1, keepdims=True)
            dscore = (probs.astype(F32) * (dprod - delta) * inv_root).astype(BF16)
            last = jnp.where(triangle, dprod[:, i * blk :], 0.0)
            dinner = jnp.concatenate([dprod[:, : i * blk], last], 1) if i else last
            dinner = dinner.astype(BF16)
            dq_ref[here, cols] = (
                dot(dscore, k, NN)
                + scale * (dot(dinner, k, NN) + dot_wide(g, states[h], NT))
            ).astype(BF16)
            dk = dot(dscore, q, TN) + scale * dot(dinner, q, TN)
            dv = dot(probs, g, TN) + scale * dot(inner_ref[h, here, upto], g, TN)
            if i == count - 1:
                dk_ref[upto, cols] = dk
                dv_ref[upto, cols] = dv
            else:
                dk_ref[upto, cols] += dk
                dv_ref[upto, cols] += dv


def close_kernel(where, k_ref, v_ref, dk_ref, dv_ref, mine_ref, other_ref, gk_ref, gv_ref):
    states = both_heads(where[2], mine_ref, other_ref)
    for h in range(k_ref.shape[1] // DH):
        cols = slice(h * DH, (h + 1) * DH)
        state = states[h]
        gk_ref[:, cols] = (dk_ref[:, cols] + dot_wide(v_ref[:, cols], state, NT)).astype(BF16)
        gv_ref[:, cols] = (dv_ref[:, cols] + dot_wide(k_ref[:, cols], state, NN)).astype(BF16)


def send(x, flip, shift):
    shards, heads = lax.axis_size("ctx"), lax.axis_size("head")
    pairs = [
        (c * heads + z, (c ^ flip) * heads + (z + shift) % heads)
        for c in range(shards)
        for z in range(heads)
    ]
    return lax.ppermute(x, ("ctx", "head"), pairs)


def exchange(mine, other, core, chip, chips, later):
    got = send(other, 1, 0)
    total = mine + got
    totals, flags = [], []
    if chips == 4:
        for flip in (1, 2, 3):
            totals.append(send(total, 2 * flip, 0))
            flags.append(((chip ^ flip) > chip) == later)
    else:
        step = 1
        while step < chips:
            totals.append(send(total, 2 * step, 0))
            flags.append(((chip & step) == 0) == later)
            total = total + totals[-1]
            step *= 2
    flags.append((core == 0) == later)
    return jnp.stack(flags).astype(jnp.int32), [mine, got, *totals]


def on_device(query, key, value, block_mask, out_weight, cotangent):
    rows, width = query.shape
    heads = width // DH
    shards, count = lax.axis_size("ctx"), lax.axis_size("head")
    model = out_weight.shape[1]
    own = rows // count
    scale = 1.0 / math.sqrt(DH * rows * shards)
    blocks = block_mask.shape[0]
    ctx, place = lax.axis_index("ctx"), lax.axis_index("head")
    core, chip, chips = ctx & 1, ctx >> 1, shards // 2
    where = jnp.stack([place, ctx, core])
    flat, square = (rows, width), rows * rows * DH * heads
    pair = [((DH, DH), F32)] * 2
    product = 4 * own * DH * model

    board = chips == 4
    wide = model // (2 if board else chips)
    colour = (chip & 1) ^ (chip >> 1) if board else chip
    piece = lax.dynamic_slice(out_weight, (core * DH, colour * wide), (DH, wide))
    weight = lax.dynamic_slice_in_dim(out_weight, core * DH, DH, 0)
    near = (colour * wide if board else jnp.int32(0)).reshape(1)
    far = jnp.stack([(1 - colour) * wide, (1 - colour) * wide + wide // 2])
    shifts = sorted(range(1, count), key=lambda s: min(s, count - s))
    arrived = {0: piece}
    for s in shifts:
        step = 1 if s <= count // 2 else -1
        arrived[s] = send(arrived[(s - step) % count], 0, step)
    mate_cotangent = send(cotangent, 1, 0)

    mine, other = call(state_kernel, pair, [key, value], [where], [piece])
    flags, parts = exchange(mine, other, core, chip, chips, False)
    keep, back = call(carry_kernel, pair, parts, [flags])
    linear = [keep, send(back, 1, 0)]
    probs, inner, soft, pre = call(
        functools.partial(forward_kernel, scale),
        [((heads, rows, rows), BF16)] * 2 + [(flat, F32)] * 2,
        [query, key, value],
        [block_mask],
        flops=6 * square,
    )
    attn = call(
        functools.partial(attn_kernel, scale),
        [((own, width), BF16)] * count,
        [query, pre, *linear],
        [where],
    )
    attn = [attn[0]] + [send(attn[s], 0, s) for s in range(1, count)]
    mate_attn = [send(a, 1, 0) for a in attn]

    first, second = {}, {}
    for n, s in enumerate(shifts):
        if not board:
            groups = [list(range(k, shards, 2)) for k in range(2)]
            whole = lax.all_gather(arrived[s], "ctx", axis=1, tiled=True, axis_index_groups=groups)
            first[s], second[s] = whole, []
        elif n < 2:
            first[s], second[s] = arrived[s], [send(arrived[s], 2 + 2 * n, 0)]
        else:
            cut = [((DH, wide // 2), BF16)] * 2
            left, right = call(cut_kernel, cut, [arrived[s]], after=mate_attn)
            first[s], second[s] = arrived[s], [send(left, 2, 0), send(right, 4, 0)]

    def grads(some, places, whole=False, earlier=(), last=True, after=()):
        (both,) = call(
            functools.partial(grad_kernel, whole, len(earlier)),
            [((2 * own, DH), BF16 if last else F32)],
            [cotangent, mate_cotangent, *earlier, *some],
            [places],
            after,
            flops=product,
        )
        return both

    def mix(each, places, after=()):
        wide = sum(a.shape[1] for a in each[0])
        return call(
            functools.partial(mixed_kernel, count, [len(some) for some in each]),
            [((own, wide), F32)] * 2,
            [*attn, *mate_attn, weight, *(a for some in each for a in some)],
            [places, where],
            after,
            room=16,
            flops=count * product,
        )

    both = {0: grads([weight], near, True)}
    end = shifts[-1]
    for s in shifts[:-1]:
        half = [grads([first[s]], near, last=False)] if board else []
        some, places = (second[s], far) if board else ([first[s]], near)
        both[s] = send(grads(some, places, earlier=half), 0, -s)
    half = [grads([first[end]], near, last=False)] if board else []
    part, mate_part = mix([[first[s]] for s in range(1, count)], near)
    joins, starts = [part, send(mate_part, 1, 0)], [near]
    some, places = (second[end], far) if board else ([first[end]], near)
    early = [part, *(both[s] for s in [0] + shifts[:-1])]
    both[end] = send(grads(some, places, earlier=half, after=early), 0, -end)
    across = [send(both[s], 1, 0) for s in range(count)]
    if board:
        part, mate_part = mix([second[s] for s in range(1, count)], far, [both[end]])
        joins, starts = [*joins, part, send(mate_part, 1, 0)], [near, far[:1]]

    g, mine, other = call(
        functools.partial(collect_kernel, scale, count),
        [(flat, BF16), *pair],
        [query, *(both[s] for s in range(count)), *across],
        [where],
        [part],
    )
    flags, parts = exchange(mine, other, core, chip, chips, True)
    grad_query, dk, dv = call(
        functools.partial(backward_kernel, scale, blocks),
        [(flat, BF16)] + [(flat, F32)] * 2,
        [query, key, value, g, probs, inner, soft, *linear],
        [where],
        flops=14 * square,
    )
    keep, back = call(carry_kernel, pair, parts, [flags], [dk])
    grad_key, grad_value = call(
        close_kernel, [(flat, BF16)] * 2, [key, value, dk, dv, keep, send(back, 1, 0)], [where]
    )
    (mixed,) = call(join_kernel, [((own, model), BF16)], joins, [jnp.concatenate(starts)])
    return mixed, grad_query, grad_key, grad_value


def solution(mesh):
    return jax.shard_map(
        on_device,
        mesh=mesh,
        in_specs=(
            P("ctx", "head"),
            P("ctx", "head"),
            P("ctx", "head"),
            P("ctx", None),
            P("head", None),
            P(("ctx", "head"), None),
        ),
        out_specs=(P(("ctx", "head"), None), P("ctx", "head"), P("ctx", "head"), P("ctx", "head")),
        check_vma=False,
    )
```

```python
import functools
import math

import jax
import jax.numpy as jnp
from jax import lax
from jax.experimental import pallas as pl
from jax.experimental.pallas import tpu as pltpu
from jax.sharding import PartitionSpec as P

DH = 128
F32 = jnp.float32
BF16 = jnp.bfloat16
NN = ((1,), (0,))
NT = ((1,), (1,))
TN = ((0,), (0,))
MIB = 1 << 20


def dot(a, b, dims):
    return lax.dot_general(a, b, (dims, ((), ())), preferred_element_type=F32)


def dot_wide(a, b, dims):
    high = b.astype(BF16)
    low = (b - high.astype(F32)).astype(BF16)
    return dot(a, high, dims) + dot(a, low, dims)


def call(body, outs, args, smem=(), after=(), room=8, flops=1):
    def kernel(*refs):
        first = len(smem) + len(args)
        body(*refs[:first], *refs[first + len(after) :])

    moved = sum(a.size * a.dtype.itemsize for a in args)
    moved += sum(math.prod(s) * jnp.dtype(t).itemsize for s, t in outs)
    return pl.pallas_call(
        kernel,
        out_shape=[jax.ShapeDtypeStruct(s, t) for s, t in outs],
        in_specs=[pl.BlockSpec(memory_space=pltpu.SMEM) for _ in smem]
        + [pl.BlockSpec(memory_space=pltpu.VMEM) for _ in args]
        + [pl.BlockSpec(memory_space=pl.ANY) for _ in after],
        out_specs=[pl.BlockSpec(memory_space=pltpu.VMEM) for _ in outs],
        compiler_params=pltpu.CompilerParams(vmem_limit_bytes=room * MIB),
        cost_estimate=pl.CostEstimate(
            flops=int(flops), bytes_accessed=int(moved), transcendentals=0
        ),
    )(*smem, *args, *after)


def lower_triangle(blk):
    return lax.broadcasted_iota(jnp.int32, (blk, blk), 0) >= lax.broadcasted_iota(
        jnp.int32, (blk, blk), 1
    )


def forward_kernel(scale, mask, q_ref, k_ref, v_ref, probs_ref, inner_ref, soft_ref, pre_ref):
    rows, width = q_ref.shape
    count = mask.shape[0]
    blk = rows // count
    inv_root = 1.0 / math.sqrt(DH)
    triangle = lower_triangle(blk)
    for h in range(width // DH):
        cols = slice(h * DH, (h + 1) * DH)
        for i in range(count):
            here = slice(i * blk, (i + 1) * blk)
            upto = slice(0, (i + 1) * blk)
            raw = dot(q_ref[here, cols], k_ref[upto, cols], NT)
            scores, inner = [], []
            for j in range(i + 1):
                part = raw[:, j * blk : (j + 1) * blk]
                keep = triangle if j == i else mask[i, j] > 0
                scores.append(jnp.where(keep, part * inv_root, -1e30))
                inner.append(jnp.where(triangle, part, 0.0) if j == i else part)
            scores = jnp.concatenate(scores, 1)
            inner = jnp.concatenate(inner, 1).astype(BF16)
            expo = jnp.exp(scores - jnp.max(scores, -1, keepdims=True))
            probs = (expo / jnp.sum(expo, -1, keepdims=True)).astype(BF16)
            v = v_ref[upto, cols]
            soft = dot(probs, v, NN)
            probs_ref[h, here, upto] = probs
            inner_ref[h, here, upto] = inner
            soft_ref[here, cols] = soft
            pre_ref[here, cols] = soft + scale * dot(inner, v, NN)


def split_heads(core, parts, mine_ref, other_ref):
    mine_ref[...] = jnp.where(core == 0, parts[0], parts[1])
    other_ref[...] = jnp.where(core == 0, parts[1], parts[0])


def both_heads(core, mine_ref, other_ref):
    mine, other = mine_ref[...], other_ref[...]
    return jnp.where(core == 0, mine, other), jnp.where(core == 0, other, mine)


def state_kernel(where, k_ref, v_ref, mine_ref, other_ref):
    heads = [slice(h * DH, (h + 1) * DH) for h in range(2)]
    parts = [dot(k_ref[:, cols], v_ref[:, cols], TN) for cols in heads]
    split_heads(where[2], parts, mine_ref, other_ref)


def carry_kernel(flags, here_ref, got_ref, *refs):
    totals, (keep_ref, back_ref) = refs[:-2], refs[-2:]
    carried = jnp.zeros(here_ref.shape, F32)
    for n, total in enumerate(totals):
        carried = carried + jnp.where(flags[n] > 0, total[...], 0.0)
    counts = flags[len(totals)] > 0
    keep_ref[...] = carried + jnp.where(counts, got_ref[...], 0.0)
    back_ref[...] = carried + jnp.where(counts, 0.0, here_ref[...])


def attn_kernel(scale, where, q_ref, pre_ref, mine_ref, other_ref, *out_refs):
    states = both_heads(where[2], mine_ref, other_ref)
    parts = []
    for h in range(2):
        cols = slice(h * DH, (h + 1) * DH)
        inter = dot_wide(q_ref[:, cols], states[h], NN)
        parts.append((pre_ref[:, cols] + scale * inter).astype(BF16))
    split_heads(where[2], parts, *out_refs)


def pack_kernel(where, mine_ref, got_ref, *out_refs):
    count = len(out_refs)
    own = mine_ref.shape[0] // count
    for s, out_ref in enumerate(out_refs):
        block = lax.rem(where[0] + s, count)
        here = pl.ds(pl.multiple_of(block * own, own), own)
        out_ref[:own] = mine_ref[here]
        out_ref[own:] = got_ref[here]


def cut_kernel(left_ref, right_ref, *out_refs):
    wide = out_refs[0].shape[1]
    out_refs[0][...] = left_ref[:, :wide]
    out_refs[1][...] = right_ref[:, wide:]


def copy_kernel(*refs):
    count = len(refs) // 2
    for source, target in zip(refs[:count], refs[count:]):
        target[...] = source[...]


def grad_kernel(whole, added, places, mine_ref, mate_ref, *refs):
    chunks, out_ref = refs[added:-1], refs[-1]
    total = refs[0][...] if added else None
    for j, chunk in enumerate(chunks):
        cols = slice(None) if whole else pl.ds(pl.multiple_of(places[j], DH), chunk.shape[1])
        left = jnp.concatenate([mine_ref[:, cols], mate_ref[:, cols]], 0)
        part = dot(left, chunk[...], NT)
        total = part if total is None else total + part
    out_ref[...] = total.astype(out_ref.dtype)


def mixed_kernel(count, each, places, *refs):
    attn, weight = refs[:count], refs[count]
    chunks, (own_out, mate_out) = list(refs[count + 1 : -2]), refs[-2:]
    own = own_out.shape[0]
    left = jnp.concatenate([a[...] for a in attn], 1)
    right = [weight[:, pl.ds(pl.multiple_of(places[0], DH), own_out.shape[1])]]
    for n in each:
        parts = [chunks.pop(0)[...] for _ in range(n)]
        right.append(jnp.concatenate(parts, 1) if n > 1 else parts[0])
    part = dot(left, jnp.concatenate(right, 0), NN)
    own_out[...] = part[:own]
    mate_out[...] = part[own:]


def join_kernel(places, *refs):
    out_ref = refs[-1]
    for n in range(len(refs) // 2):
        wide = refs[2 * n].shape[1]
        there = pl.ds(pl.multiple_of(places[n], DH), wide)
        out_ref[:, there] = (refs[2 * n][...] + refs[2 * n + 1][...]).astype(BF16)


def collect_kernel(scale, count, where, q_ref, *refs):
    direct, across = refs[:count], refs[count : 2 * count]
    g_ref, mine_ref, other_ref = refs[2 * count :]
    own = g_ref.shape[0] // count
    mine = pl.ds(pl.multiple_of(where[2] * DH, DH), DH)
    mate = pl.ds(pl.multiple_of((1 - where[2]) * DH, DH), DH)
    for s in range(count):
        block = lax.rem(where[0] + s, count)
        here = pl.ds(pl.multiple_of(block * own, own), own)
        g_ref[here, mine] = direct[s][:own]
        g_ref[here, mate] = across[s][own:]
    heads = [slice(h * DH, (h + 1) * DH) for h in range(2)]
    parts = [scale * dot(q_ref[:, cols], g_ref[:, cols], TN) for cols in heads]
    split_heads(where[2], parts, mine_ref, other_ref)


def backward_kernel(
    scale,
    count,
    where,
    q_ref,
    k_ref,
    v_ref,
    g_ref,
    probs_ref,
    inner_ref,
    soft_ref,
    mine_ref,
    other_ref,
    dq_ref,
    dk_ref,
    dv_ref,
):
    rows, width = q_ref.shape
    blk = rows // count
    inv_root = 1.0 / math.sqrt(DH)
    triangle = lower_triangle(blk)
    states = both_heads(where[2], mine_ref, other_ref)
    for h in range(width // DH):
        cols = slice(h * DH, (h + 1) * DH)
        for i in reversed(range(count)):
            here = slice(i * blk, (i + 1) * blk)
            upto = slice(0, (i + 1) * blk)
            q, g = q_ref[here, cols], g_ref[here, cols]
            k = k_ref[upto, cols]
            probs = probs_ref[h, here, upto]
            dprod = dot(g, v_ref[upto, cols], NT)
            delta = jnp.sum(g.astype(F32) * soft_ref[here, cols], -1, keepdims=True)
            dscore = (probs.astype(F32) * (dprod - delta) * inv_root).astype(BF16)
            last = jnp.where(triangle, dprod[:, i * blk :], 0.0)
            dinner = jnp.concatenate([dprod[:, : i * blk], last], 1) if i else last
            dinner = dinner.astype(BF16)
            dq_ref[here, cols] = (
                dot(dscore, k, NN)
                + scale * (dot(dinner, k, NN) + dot_wide(g, states[h], NT))
            ).astype(BF16)
            dk = dot(dscore, q, TN) + scale * dot(dinner, q, TN)
            dv = dot(probs, g, TN) + scale * dot(inner_ref[h, here, upto], g, TN)
            if i == count - 1:
                dk_ref[upto, cols] = dk
                dv_ref[upto, cols] = dv
            else:
                dk_ref[upto, cols] += dk
                dv_ref[upto, cols] += dv


def close_kernel(where, k_ref, v_ref, dk_ref, dv_ref, mine_ref, other_ref, gk_ref, gv_ref):
    states = both_heads(where[2], mine_ref, other_ref)
    for h in range(k_ref.shape[1] // DH):
        cols = slice(h * DH, (h + 1) * DH)
        state = states[h]
        gk_ref[:, cols] = (dk_ref[:, cols] + dot_wide(v_ref[:, cols], state, NT)).astype(BF16)
        gv_ref[:, cols] = (dv_ref[:, cols] + dot_wide(k_ref[:, cols], state, NN)).astype(BF16)


def send(x, flip, shift):
    shards, heads = lax.axis_size("ctx"), lax.axis_size("head")
    pairs = [
        (c * heads + z, (c ^ flip) * heads + (z + shift) % heads)
        for c in range(shards)
        for z in range(heads)
    ]
    return lax.ppermute(x, ("ctx", "head"), pairs)


def exchange(mine, other, core, chip, chips, later):
    got = send(other, 1, 0)
    total = mine + got
    totals, flags = [], []
    if chips == 4:
        for flip in (1, 2, 3):
            totals.append(send(total, 2 * flip, 0))
            flags.append(((chip ^ flip) > chip) == later)
    else:
        step = 1
        while step < chips:
            totals.append(send(total, 2 * step, 0))
            flags.append(((chip & step) == 0) == later)
            total = total + totals[-1]
            step *= 2
    flags.append((core == 0) == later)
    return jnp.stack(flags).astype(jnp.int32), [mine, got, *totals]


def on_device(query, key, value, block_mask, out_weight, cotangent):
    rows, width = query.shape
    heads = width // DH
    shards, count = lax.axis_size("ctx"), lax.axis_size("head")
    model = out_weight.shape[1]
    own = rows // count
    scale = 1.0 / math.sqrt(DH * rows * shards)
    blocks = block_mask.shape[0]
    ctx, place = lax.axis_index("ctx"), lax.axis_index("head")
    core, chip, chips = ctx & 1, ctx >> 1, shards // 2
    where = jnp.stack([place, ctx, core])
    flat, square = (rows, width), rows * rows * DH * heads
    pair = [((DH, DH), F32)] * 2
    product = 4 * own * DH * model

    board = chips == 4 and count == 4
    wide = model // (2 if board else chips)
    colour = (chip & 1) ^ (chip >> 1) if board else chip
    piece = lax.dynamic_slice(out_weight, (core * DH, colour * wide), (DH, wide))
    weight = lax.dynamic_slice_in_dim(out_weight, core * DH, DH, 0)
    start, other = colour * wide, (1 - colour) * wide
    near = jnp.stack([start, start + wide // 2]) if board else jnp.zeros((1,), jnp.int32)
    far = jnp.stack([other, other + wide // 2])
    arrived = {1: send(piece, 0, 1), count - 1: send(piece, 0, -1)}
    mate_cotangent = send(cotangent, 1, 0)

    mine, other = call(state_kernel, pair, [key, value], [where], [piece, mate_cotangent])
    flags, parts = exchange(mine, other, core, chip, chips, False)
    probs, inner, soft, pre = call(
        functools.partial(forward_kernel, scale),
        [((heads, rows, rows), BF16)] * 2 + [(flat, F32)] * 2,
        [query, key, value],
        [block_mask],
        flops=6 * square,
    )
    keep, back = call(carry_kernel, pair, parts, [flags], [pre])
    linear = [keep, send(back, 1, 0)]
    mine, other = call(
        functools.partial(attn_kernel, scale),
        [((rows, DH), BF16)] * 2,
        [query, pre, *linear],
        [where],
    )
    attn = call(pack_kernel, [((2 * own, DH), BF16)] * count, [mine, send(other, 1, 0)], [where])
    attn = [attn[0]] + [send(attn[s], 0, s) for s in range(1, count)]

    def grads(some, places, whole=False, earlier=(), last=True, after=()):
        (both,) = call(
            functools.partial(grad_kernel, whole, len(earlier)),
            [((2 * own, DH), BF16 if last else F32)],
            [cotangent, mate_cotangent, *earlier, *some],
            [places],
            after,
            flops=product,
        )
        return both

    def mix(each, places, after=()):
        wide = sum(a.shape[1] for a in each[0])
        return call(
            functools.partial(mixed_kernel, count, [len(some) for some in each]),
            [((own, wide), F32)] * 2,
            [*attn, weight, *(a for some in each for a in some)],
            [places],
            after,
            room=16,
            flops=count * product,
        )

    end = count // 2
    if board:
        cut = [((DH, wide // 2), BF16)] * 2
        left, right = call(cut_kernel, cut, [arrived[1], arrived[3]], after=attn[1:])
        left, right = send(left, 0, 1), send(right, 0, -1)
        first = {1: [arrived[1]], 2: [left, right], 3: [arrived[3]]}
        second = {1: [send(arrived[1], 2, 0)], 3: [send(arrived[3], 4, 0)]}
    else:
        groups = [list(range(k, shards, 2)) for k in range(2)]
        for s in range(2, count - 1):
            arrived[s] = send(arrived[s - 1], 0, 1)
        first = {
            s: [lax.all_gather(a, "ctx", axis=1, tiled=True, axis_index_groups=groups)]
            for s, a in arrived.items()
        }
    shifts = [s for s in range(1, count) if s != end] + [end]

    both = {0: grads([weight], near, True)}
    across = {0: send(both[0], 1, 0)}
    half = {s: [grads(first[s], near, last=False)] if board else [] for s in shifts}
    if board:
        before = [both[0], *half[1], *half[3], *second[1], *second[3]]
        left, right = call(copy_kernel, cut, [left, right], after=before)
        second[2] = [send(left, 2, 0), send(right, 4, 0)]
    some, places = (second, far) if board else (first, near)
    for s in shifts[:-1]:
        both[s] = send(grads(some[s], places, earlier=half[s]), 0, -s)
        across[s] = send(both[s], 1, 0)
    ahead = [across[s] for s in across]
    joins, starts = [], []
    if board:
        part, mate_part = mix([first[s] for s in range(1, count)], near)
        joins, starts = [part, send(mate_part, 1, 0)], [near[:1]]
        ahead += joins
    both[end] = send(grads(some[end], places, earlier=half[end], after=ahead), 0, -end)
    across[end] = send(both[end], 1, 0)
    part, mate_part = mix([some[s] for s in range(1, count)], places, [both[end]])
    joins, starts = [*joins, part, send(mate_part, 1, 0)], [*starts, places[:1]]

    g, mine, other = call(
        functools.partial(collect_kernel, scale, count),
        [(flat, BF16), *pair],
        [query, *(both[s] for s in range(count)), *(across[s] for s in range(count))],
        [where],
        [part],
    )
    flags, parts = exchange(mine, other, core, chip, chips, True)
    grad_query, dk, dv = call(
        functools.partial(backward_kernel, scale, blocks),
        [(flat, BF16)] + [(flat, F32)] * 2,
        [query, key, value, g, probs, inner, soft, *linear],
        [where],
        flops=14 * square,
    )
    keep, back = call(carry_kernel, pair, parts, [flags], [dk])
    grad_key, grad_value = call(
        close_kernel, [(flat, BF16)] * 2, [key, value, dk, dv, keep, send(back, 1, 0)], [where]
    )
    (mixed,) = call(join_kernel, [((own, model), BF16)], joins, [jnp.concatenate(starts)])
    return mixed, grad_query, grad_key, grad_value


def solution(mesh):
    return jax.shard_map(
        on_device,
        mesh=mesh,
        in_specs=(
            P("ctx", "head"),
            P("ctx", "head"),
            P("ctx", "head"),
            P("ctx", None),
            P("head", None),
            P(("ctx", "head"), None),
        ),
        out_specs=(P(("ctx", "head"), None), P("ctx", "head"), P("ctx", "head"), P("ctx", "head")),
        check_vma=False,
    )
```

```python
import functools
import math

import jax
import jax.numpy as jnp
from jax import lax
from jax.experimental import pallas as pl
from jax.experimental.pallas import tpu as pltpu
from jax.sharding import PartitionSpec as P

DH = 128
F32 = jnp.float32
BF16 = jnp.bfloat16
NN = ((1,), (0,))
NT = ((1,), (1,))
TN = ((0,), (0,))
MIB = 1 << 20


def dot(a, b, dims):
    return lax.dot_general(a, b, (dims, ((), ())), preferred_element_type=F32)


def dot_wide(a, b, dims):
    high = b.astype(BF16)
    low = (b - high.astype(F32)).astype(BF16)
    return dot(a, high, dims) + dot(a, low, dims)


def fetch(shape, *parts):
    return (shape, parts)


def all_of(ref, *_):
    return ref


def columns(spot, wide, rows=slice(None)):
    def view(ref, spots, *_):
        return ref.at[rows, pl.ds(pl.multiple_of(spots[spot], DH), wide)]

    return view


def rows_at(first, count):
    return lambda ref, *_: ref.at[first : first + count]


def columns_at(first, count):
    return lambda ref, *_: ref.at[:, first : first + count]


def call(body, outs, args, smem=(), after=(), room=8, flops=1):
    arrays, specs, scratch = [], [], []
    for arg in args:
        if isinstance(arg, tuple):
            arrays += [part[0] for part in arg[1]]
            specs += [pl.BlockSpec(memory_space=pltpu.HBM) for _ in arg[1]]
            scratch.append(pltpu.VMEM(arg[0], arg[1][0][0].dtype))
        else:
            arrays.append(arg)
            specs.append(pl.BlockSpec(memory_space=pltpu.VMEM))
    copies = sum(len(arg[1]) for arg in args if isinstance(arg, tuple))
    held = len(scratch)
    if copies:
        scratch.append(pltpu.SemaphoreType.DMA((copies,)))

    def kernel(*refs):
        scalars, refs = refs[: len(smem)], list(refs[len(smem) :])
        ins, refs = refs[: len(arrays)], refs[len(arrays) + len(after) :]
        results, slots = refs[: len(outs)], refs[len(outs) :]
        given, started, slot = [], [], 0
        for arg in args:
            if not isinstance(arg, tuple):
                given.append(ins.pop(0))
                continue
            for _, source, target in arg[1]:
                copy = pltpu.make_async_copy(
                    source(ins.pop(0), *scalars),
                    target(slots[slot], *scalars),
                    slots[held].at[len(started)],
                )
                copy.start()
                started.append(copy)
            given.append(slots[slot])
            slot += 1
        for copy in started:
            copy.wait()
        body(*scalars, *given, *results)

    moved = sum(a.size * a.dtype.itemsize for a in arrays)
    moved += sum(math.prod(s) * jnp.dtype(t).itemsize for s, t in outs)
    return pl.pallas_call(
        kernel,
        out_shape=[jax.ShapeDtypeStruct(s, t) for s, t in outs],
        in_specs=[pl.BlockSpec(memory_space=pltpu.SMEM) for _ in smem]
        + specs
        + [pl.BlockSpec(memory_space=pl.ANY) for _ in after],
        out_specs=[pl.BlockSpec(memory_space=pltpu.VMEM) for _ in outs],
        scratch_shapes=scratch,
        compiler_params=pltpu.CompilerParams(vmem_limit_bytes=room * MIB),
        cost_estimate=pl.CostEstimate(
            flops=int(flops), bytes_accessed=int(moved), transcendentals=0
        ),
    )(*smem, *arrays, *after)


def hold(arrays, after):
    held = len(arrays)
    return pl.pallas_call(
        lambda *refs: None,
        out_shape=[jax.ShapeDtypeStruct(a.shape, a.dtype) for a in arrays],
        in_specs=[pl.BlockSpec(memory_space=pl.ANY) for _ in (*arrays, *after)],
        out_specs=[pl.BlockSpec(memory_space=pl.ANY) for _ in arrays],
        input_output_aliases={n: n for n in range(held)},
        cost_estimate=pl.CostEstimate(flops=1, bytes_accessed=1, transcendentals=0),
    )(*arrays, *after)


def lower_triangle(blk):
    return lax.broadcasted_iota(jnp.int32, (blk, blk), 0) >= lax.broadcasted_iota(
        jnp.int32, (blk, blk), 1
    )


def forward_kernel(
    scale,
    mask,
    where,
    q_ref,
    k_ref,
    v_ref,
    probs_ref,
    inner_ref,
    soft_ref,
    mine_ref,
    other_ref,
    far_ref,
):
    rows, width = q_ref.shape
    count = mask.shape[0]
    blk = rows // count
    inv_root = 1.0 / math.sqrt(DH)
    triangle = lower_triangle(blk)
    for i in range(count):
        here = slice(i * blk, (i + 1) * blk)
        upto = slice(0, (i + 1) * blk)
        sums = []
        for h in range(2):
            cols = slice(h * DH, (h + 1) * DH)
            raw = dot(q_ref[here, cols], k_ref[upto, cols], NT)
            scores, inner = [], []
            for j in range(i + 1):
                part = raw[:, j * blk : (j + 1) * blk]
                keep = triangle if j == i else mask[i, j] > 0
                scores.append(jnp.where(keep, part * inv_root, -1e30))
                inner.append(jnp.where(triangle, part, 0.0) if j == i else part)
            scores = jnp.concatenate(scores, 1)
            inner = jnp.concatenate(inner, 1).astype(BF16)
            expo = jnp.exp(scores - jnp.max(scores, -1, keepdims=True))
            probs = (expo / jnp.sum(expo, -1, keepdims=True)).astype(BF16)
            v = v_ref[upto, cols]
            soft = dot(probs, v, NN)
            probs_ref[h, here, upto] = probs
            inner_ref[h, here, upto] = inner
            soft_ref[here, cols] = soft
            sums.append(soft + scale * dot(inner, v, NN))
        mine_ref[here], other_ref[here] = pick(where[2], sums)
    far_ref[...] = q_ref[:, pl.ds(pl.multiple_of((1 - where[2]) * DH, DH), DH)]


def pick(core, parts):
    return jnp.where(core == 0, parts[0], parts[1]), jnp.where(core == 0, parts[1], parts[0])


def both_heads(core, mine_ref, other_ref):
    mine, other = mine_ref[...], other_ref[...]
    return jnp.where(core == 0, mine, other), jnp.where(core == 0, other, mine)


def state_kernel(where, k_ref, v_ref, mine_ref, other_ref):
    heads = [slice(h * DH, (h + 1) * DH) for h in range(2)]
    parts = [dot(k_ref[:, cols], v_ref[:, cols], TN) for cols in heads]
    mine_ref[...], other_ref[...] = pick(where[2], parts)


def carry(flags, here_ref, got_ref, totals):
    carried = jnp.zeros(here_ref.shape, F32)
    for n, total in enumerate(totals):
        carried = carried + jnp.where(flags[n] > 0, total[...], 0.0)
    counts = flags[len(totals)] > 0
    keep = carried + jnp.where(counts, got_ref[...], 0.0)
    return keep, carried + jnp.where(counts, 0.0, here_ref[...])


def carry_kernel(flags, here_ref, got_ref, *refs):
    totals, (keep_ref, back_ref) = refs[:-2], refs[-2:]
    keep_ref[...], back_ref[...] = carry(flags, here_ref, got_ref, totals)


def attn_kernel(scale, count, flags, where, here_ref, got_ref, *refs):
    totals, refs = refs[: -count - 6], refs[-count - 6 :]
    q_ref, far_ref, pre_ref, far_pre_ref = refs[:4]
    out_refs, (keep_ref, back_ref) = refs[4:-2], refs[-2:]
    keep, back = carry(flags, here_ref, got_ref, totals)
    keep_ref[...], back_ref[...] = keep, back
    own = pre_ref.shape[0] // count
    cols = pl.ds(pl.multiple_of(where[2] * DH, DH), DH)
    for s, out_ref in enumerate(out_refs):
        block = lax.rem(where[0] + s, count)
        here = pl.ds(pl.multiple_of(block * own, own), own)
        mine = pre_ref[here] + scale * dot_wide(q_ref[here, cols], keep, NN)
        mate = far_pre_ref[here] + scale * dot_wide(far_ref[here], back, NN)
        out_ref[:own] = mine.astype(BF16)
        out_ref[own:] = mate.astype(BF16)


def first_kernel(spots, left_ref, weight_ref, right_ref, own_ref, half_ref):
    own_ref[...] = dot(left_ref[...], weight_ref[...], NT).astype(BF16)
    near = left_ref[:, pl.ds(pl.multiple_of(spots[0], DH), right_ref.shape[1])]
    half_ref[...] = dot(near, right_ref[...], NT)


def second_kernel(spots, left_ref, right_ref, half_ref, piece_ref, one_ref, three_ref, *cut_refs):
    wide = cut_refs[0].shape[1]
    for n, cut_ref in enumerate(cut_refs):
        cut_ref[...] = piece_ref[:, n * wide : (n + 1) * wide]
    total = (half_ref[...] + dot(left_ref[...], right_ref[...], NT)).astype(BF16)
    one_ref[...], three_ref[...] = total[:, :DH], total[:, DH:]


def last_kernel(spots, left_ref, right_ref, half_ref, out_ref):
    out_ref[...] = (half_ref[...] + dot(left_ref[...], right_ref[...], NT)).astype(BF16)


def near_kernel(spots, left_ref, right_ref, *refs):
    attn, (half_ref, own_out, mate_out) = refs[:-3], refs[-3:]
    half_ref[...] = dot(left_ref[...], right_ref[2 * DH : 3 * DH], NT)
    far_kernel(spots, right_ref, *attn, own_out, mate_out)


def far_kernel(spots, right_ref, *refs):
    attn, (own_out, mate_out) = refs[:-2], refs[-2:]
    own = own_out.shape[0]
    part = dot(jnp.concatenate([a[...] for a in attn], 1), right_ref[...], NN)
    own_out[...] = part[:own]
    mate_out[...] = part[own:]


def grad_kernel(whole, added, places, mine_ref, mate_ref, *refs):
    chunks, out_ref = refs[added:-1], refs[-1]
    total = refs[0][...] if added else None
    for j, chunk in enumerate(chunks):
        cols = slice(None) if whole else pl.ds(pl.multiple_of(places[j], DH), chunk.shape[1])
        left = jnp.concatenate([mine_ref[:, cols], mate_ref[:, cols]], 0)
        part = dot(left, chunk[...], NT)
        total = part if total is None else total + part
    out_ref[...] = total.astype(out_ref.dtype)


def mixed_kernel(count, each, places, *refs):
    attn, weight = refs[:count], refs[count]
    chunks, (own_out, mate_out) = list(refs[count + 1 : -2]), refs[-2:]
    own = own_out.shape[0]
    left = jnp.concatenate([a[...] for a in attn], 1)
    right = [weight[:, pl.ds(pl.multiple_of(places[0], DH), own_out.shape[1])]]
    for n in each:
        parts = [chunks.pop(0)[...] for _ in range(n)]
        right.append(jnp.concatenate(parts, 1) if n > 1 else parts[0])
    part = dot(left, jnp.concatenate(right, 0), NN)
    own_out[...] = part[:own]
    mate_out[...] = part[own:]


def join_kernel(places, *refs):
    out_ref, done_ref = refs[-2:]
    done_ref[...] = jnp.zeros(done_ref.shape, F32)
    for n in range(len(refs) // 2 - 1):
        wide = refs[2 * n].shape[1]
        there = pl.ds(pl.multiple_of(places[n], DH), wide)
        out_ref[:, there] = (refs[2 * n][...] + refs[2 * n + 1][...]).astype(BF16)


def collect_kernel(scale, count, where, q_ref, *refs):
    direct, across = refs[:count], refs[count : 2 * count]
    g_ref, mine_ref, other_ref = refs[2 * count :]
    own = g_ref.shape[0] // count
    mine = pl.ds(pl.multiple_of(where[2] * DH, DH), DH)
    mate = pl.ds(pl.multiple_of((1 - where[2]) * DH, DH), DH)
    for s in range(count):
        block = lax.rem(where[0] + s, count)
        here = pl.ds(pl.multiple_of(block * own, own), own)
        g_ref[here, mine] = direct[s][:own]
        g_ref[here, mate] = across[s][own:]
    heads = [slice(h * DH, (h + 1) * DH) for h in range(2)]
    parts = [scale * dot(q_ref[:, cols], g_ref[:, cols], TN) for cols in heads]
    mine_ref[...], other_ref[...] = pick(where[2], parts)


def backward_kernel(
    scale,
    count,
    where,
    q_ref,
    k_ref,
    v_ref,
    g_ref,
    probs_ref,
    inner_ref,
    soft_ref,
    mine_ref,
    other_ref,
    dq_ref,
    dk_ref,
    dv_ref,
):
    rows, width = q_ref.shape
    blk = rows // count
    inv_root = 1.0 / math.sqrt(DH)
    triangle = lower_triangle(blk)
    states = both_heads(where[2], mine_ref, other_ref)
    for h in range(width // DH):
        cols = slice(h * DH, (h + 1) * DH)
        for i in reversed(range(count)):
            here = slice(i * blk, (i + 1) * blk)
            upto = slice(0, (i + 1) * blk)
            q, g = q_ref[here, cols], g_ref[here, cols]
            k = k_ref[upto, cols]
            probs = probs_ref[h, here, upto]
            dprod = dot(g, v_ref[upto, cols], NT)
            delta = jnp.sum(g.astype(F32) * soft_ref[here, cols], -1, keepdims=True)
            dscore = (probs.astype(F32) * (dprod - delta) * inv_root).astype(BF16)
            last = jnp.where(triangle, dprod[:, i * blk :], 0.0)
            dinner = jnp.concatenate([dprod[:, : i * blk], last], 1) if i else last
            dinner = dinner.astype(BF16)
            dq_ref[here, cols] = (
                dot(dscore, k, NN)
                + scale * (dot(dinner, k, NN) + dot_wide(g, states[h], NT))
            ).astype(BF16)
            dk = dot(dscore, q, TN) + scale * dot(dinner, q, TN)
            dv = dot(probs, g, TN) + scale * dot(inner_ref[h, here, upto], g, TN)
            if i == count - 1:
                dk_ref[upto, cols] = dk
                dv_ref[upto, cols] = dv
            else:
                dk_ref[upto, cols] += dk
                dv_ref[upto, cols] += dv


def close_kernel(where, k_ref, v_ref, dk_ref, dv_ref, mine_ref, other_ref, gk_ref, gv_ref):
    states = both_heads(where[2], mine_ref, other_ref)
    for h in range(k_ref.shape[1] // DH):
        cols = slice(h * DH, (h + 1) * DH)
        state = states[h]
        gk_ref[:, cols] = (dk_ref[:, cols] + dot_wide(v_ref[:, cols], state, NT)).astype(BF16)
        gv_ref[:, cols] = (dv_ref[:, cols] + dot_wide(k_ref[:, cols], state, NN)).astype(BF16)


def send(x, flip, shift):
    shards, heads = lax.axis_size("ctx"), lax.axis_size("head")
    pairs = [
        (c * heads + z, (c ^ flip) * heads + (z + shift) % heads)
        for c in range(shards)
        for z in range(heads)
    ]
    return lax.ppermute(x, ("ctx", "head"), pairs)


def exchange(mine, other, core, chip, chips, later):
    got = send(other, 1, 0)
    own = total = mine + got
    totals, flags = [], []
    if chips == 4:
        for flip in (1, 2, 3):
            totals.append(send(total, 2 * flip, 0))
            flags.append(((chip ^ flip) > chip) == later)
    else:
        step = 1
        while step < chips:
            totals.append(send(total, 2 * step, 0))
            flags.append(((chip & step) == 0) == later)
            total = total + totals[-1]
            step *= 2
    flags.append((core == 0) == later)
    return jnp.stack(flags).astype(jnp.int32), [mine, got, *totals], own


def on_device(query, key, value, block_mask, out_weight, cotangent):
    rows, width = query.shape
    heads = width // DH
    shards, count = lax.axis_size("ctx"), lax.axis_size("head")
    model = out_weight.shape[1]
    own = rows // count
    scale = 1.0 / math.sqrt(DH * rows * shards)
    blocks = block_mask.shape[0]
    ctx, place = lax.axis_index("ctx"), lax.axis_index("head")
    core, chip, chips = ctx & 1, ctx >> 1, shards // 2
    where = jnp.stack([place, ctx, core])
    flat, square = (rows, width), rows * rows * DH * heads
    pair = [((DH, DH), F32)] * 2
    tokens = ((2 * own, DH), BF16)
    product = 4 * own * DH * model

    board = chips == 4 and count == 4
    wide = model // (2 if board else chips)
    colour = (chip & 1) ^ (chip >> 1) if board else chip
    piece = lax.dynamic_slice(out_weight, (core * DH, colour * wide), (DH, wide))
    arrived = {1: send(piece, 0, 1), count - 1: send(piece, 0, -1)}
    mate_cotangent = send(cotangent, 1, 0)

    mine, other = call(
        state_kernel,
        pair,
        [fetch(flat, (a, all_of, all_of)) for a in (key, value)],
        [where],
        [mate_cotangent],
    )
    flags, parts, total = exchange(mine, other, core, chip, chips, False)
    probs, inner, soft, pre, other, far = call(
        functools.partial(forward_kernel, scale),
        [((heads, rows, rows), BF16)] * 2
        + [(flat, F32)]
        + [((rows, DH), F32)] * 2
        + [((rows, DH), BF16)],
        [query, key, value],
        [block_mask, where],
        [total],
        flops=6 * square,
    )
    *attn, keep, back = call(
        functools.partial(attn_kernel, scale, count),
        [tokens] * count + pair,
        [*parts, query, send(far, 1, 0), pre, send(other, 1, 0)],
        [flags, where],
    )
    linear = [keep, send(back, 1, 0)]
    attn = [attn[0]] + [send(attn[s], 0, s) for s in range(1, count)]

    work = near_and_far if board else by_gathers
    both, across, joins, starts = work(
        attn, arrived, cotangent, mate_cotangent, out_weight, core, chip, colour, product
    )
    mixed, done = call(
        join_kernel, [((own, model), BF16), ((8, DH), F32)], joins, [jnp.stack(starts)]
    )

    g, mine, other = call(
        functools.partial(collect_kernel, scale, count),
        [(flat, BF16), *pair],
        [query, *both, *across],
        [where],
    )
    flags, parts, total = exchange(mine, other, core, chip, chips, True)
    grad_query, dk, dv = call(
        functools.partial(backward_kernel, scale, blocks),
        [(flat, BF16)] + [(flat, F32)] * 2,
        [query, key, value, g, probs, inner, soft, *linear],
        [where],
        [total],
        flops=14 * square,
    )
    keep, back = call(carry_kernel, pair, parts, [flags], [dk])
    grad_key, grad_value = call(
        close_kernel,
        [(flat, BF16)] * 2,
        [key, value, dk, dv, keep, send(back, 1, 0)],
        [where],
        [done],
    )
    return mixed, grad_query, grad_key, grad_value


def near_and_far(attn, arrived, cotangent, mate_cotangent, weight, core, chip, colour, product):
    own, model = cotangent.shape
    wide = model // 2
    spots = jnp.stack([colour * wide, (1 - colour) * wide, core * DH])
    tokens = ((2 * own, DH), BF16)
    parts = [((own, wide), F32)] * 2
    all_arrays = [(cotangent, all_of, rows_at(0, own)), (mate_cotangent, all_of, rows_at(own, own))]
    whole = fetch((2 * own, model), *all_arrays)
    left = [
        fetch((2 * own, wide), *((a, columns(n, wide), put) for a, _, put in all_arrays))
        for n in range(2)
    ]

    def own_rows(ref, spots, *_):
        return ref.at[pl.ds(pl.multiple_of(spots[2], DH), DH)]

    def own_columns(n):
        return lambda ref, spots, *_: ref.at[
            pl.ds(pl.multiple_of(spots[2], DH), DH), pl.ds(pl.multiple_of(spots[n], DH), wide)
        ]

    def stacked(*arrays):
        return [(a, all_of, rows_at(n * DH, DH)) for n, a in enumerate(arrays)]

    arrived[1], arrived[3] = hold([arrived[1], arrived[3]], attn[1:])
    arrived[2] = send(arrived[1], 0, 1)
    second = {1: send(arrived[1], 2, 0), 3: send(arrived[3], 4, 0)}
    mine, half = call(
        first_kernel,
        [tokens, ((2 * own, 2 * DH), F32)],
        [
            whole,
            fetch((DH, model), (weight, own_rows, all_of)),
            fetch((2 * DH, wide), *stacked(arrived[1], arrived[3])),
        ],
        [spots],
        room=24,
        flops=2 * product,
    )
    one, three, *cuts = call(
        second_kernel,
        [tokens] * 2 + [((DH, wide // 2), BF16)] * 2,
        [
            left[1],
            fetch((2 * DH, wide), *stacked(second[1], second[3])),
            half,
            fetch((DH, wide), (arrived[2], all_of, all_of)),
        ],
        [spots],
        room=16,
        flops=product,
    )
    second[2] = [send(cuts[0], 2, 0), send(cuts[1], 4, 0)]
    both = {0: mine, 1: send(one, 0, -1), 3: send(three, 0, -3)}
    across = {s: send(both[s], 1, 0) for s in (0, 1, 3)}
    half, part, mate_part = call(
        near_kernel,
        [((2 * own, DH), F32), *parts],
        [
            left[0],
            fetch(
                (4 * DH, wide),
                (weight, own_columns(0), rows_at(0, DH)),
                *((arrived[s], all_of, rows_at(s * DH, DH)) for s in (1, 2, 3)),
            ),
            *attn,
        ],
        [spots],
        room=24,
        flops=2 * product,
    )
    joins = [part, send(mate_part, 1, 0)]
    quarters = [(a, all_of, columns_at(n * wide // 2, wide // 2)) for n, a in enumerate(second[2])]
    (two,) = call(
        last_kernel,
        [tokens],
        [left[1], fetch((DH, wide), *quarters), half],
        [spots],
        [across[0], across[1], across[3]],
        room=16,
        flops=product // 2,
    )
    both[2] = send(two, 0, -2)

    def quarter(n):
        return lambda ref, *_: ref.at[2 * DH : 3 * DH, n * wide // 2 : (n + 1) * wide // 2]

    part, mate_part = call(
        far_kernel,
        parts,
        [
            fetch(
                (4 * DH, wide),
                (weight, own_columns(1), rows_at(0, DH)),
                (second[1], all_of, rows_at(DH, DH)),
                (second[3], all_of, rows_at(3 * DH, DH)),
                *((a, all_of, quarter(n)) for n, a in enumerate(second[2])),
            ),
            *attn,
        ],
        [spots],
        [both[2]],
        room=24,
        flops=2 * product,
    )
    joins += [part, send(mate_part, 1, 0)]
    across[2] = send(both[2], 1, 0)
    return [both[s] for s in range(4)], [across[s] for s in range(4)], joins, [spots[0], spots[1]]


def by_gathers(attn, arrived, cotangent, mate_cotangent, out_weight, core, chip, colour, product):
    own, model = cotangent.shape
    shards, count = lax.axis_size("ctx"), lax.axis_size("head")
    weight = lax.dynamic_slice_in_dim(out_weight, core * DH, DH, 0)
    zero = jnp.zeros((1,), jnp.int32)
    groups = [list(range(k, shards, 2)) for k in range(2)]
    for s in range(2, count - 1):
        arrived[s] = send(arrived[s - 1], 0, 1)
    chunks = [weight] + [
        lax.all_gather(arrived[s], "ctx", axis=1, tiled=True, axis_index_groups=groups)
        for s in range(1, count)
    ]
    both = []
    for s in range(count):
        (block,) = call(
            functools.partial(grad_kernel, True, 0),
            [((2 * own, DH), BF16)],
            [cotangent, mate_cotangent, chunks[s]],
            [zero],
            flops=product,
        )
        both.append(send(block, 0, -s) if s else block)
    part, mate_part = call(
        functools.partial(mixed_kernel, count, [1] * (count - 1)),
        [((own, model), F32)] * 2,
        [*attn, *chunks],
        [zero],
        room=16,
        flops=count * product,
    )
    return both, [send(b, 1, 0) for b in both], [part, send(mate_part, 1, 0)], [jnp.int32(0)]


def solution(mesh):
    return jax.shard_map(
        on_device,
        mesh=mesh,
        in_specs=(
            P("ctx", "head"),
            P("ctx", "head"),
            P("ctx", "head"),
            P("ctx", None),
            P("head", None),
            P(("ctx", "head"), None),
        ),
        out_specs=(P(("ctx", "head"), None), P("ctx", "head"), P("ctx", "head"), P("ctx", "head")),
        check_vma=False,
    )
```

```python
import functools
import math

import jax
import jax.numpy as jnp
from jax import lax
from jax.experimental import pallas as pl
from jax.experimental.pallas import tpu as pltpu
from jax.sharding import PartitionSpec as P

DH = 128
F32 = jnp.float32
BF16 = jnp.bfloat16
NN = ((1,), (0,))
NT = ((1,), (1,))
TN = ((0,), (0,))
MIB = 1 << 20


def dot(a, b, dims):
    return lax.dot_general(a, b, (dims, ((), ())), preferred_element_type=F32)


def dot_wide(a, b, dims):
    high = b.astype(BF16)
    low = (b - high.astype(F32)).astype(BF16)
    return dot(a, high, dims) + dot(a, low, dims)


def fetch(shape, *parts):
    return (shape, parts)


def all_of(ref, *_):
    return ref


def columns(spot, wide, rows=slice(None)):
    def view(ref, spots, *_):
        return ref.at[rows, pl.ds(pl.multiple_of(spots[spot], DH), wide)]

    return view


def rows_at(first, count):
    return lambda ref, *_: ref.at[first : first + count]


def columns_at(first, count):
    return lambda ref, *_: ref.at[:, first : first + count]


def here(*arrays):
    return [fetch(a.shape, (a, all_of, all_of)) for a in arrays]


def call(body, outs, args, smem=(), after=(), room=12):
    arrays, specs, scratch = [], [], []
    for arg in args:
        if isinstance(arg, tuple):
            arrays += [part[0] for part in arg[1]]
            specs += [pl.BlockSpec(memory_space=pl.ANY) for _ in arg[1]]
            scratch.append(pltpu.VMEM(arg[0], arg[1][0][0].dtype))
        else:
            arrays.append(arg)
            specs.append(pl.BlockSpec(memory_space=pltpu.VMEM))
    stored = [len(out) == 3 for out in outs]
    fetched = len(scratch)
    scratch += [pltpu.VMEM(out[0], out[1]) for out in outs if len(out) == 3]
    copies = sum(len(arg[1]) for arg in args if isinstance(arg, tuple)) + sum(stored)
    held = len(scratch)
    if copies:
        scratch.append(pltpu.SemaphoreType.DMA((copies,)))

    def kernel(*refs):
        scalars, refs = refs[: len(smem)], list(refs[len(smem) :])
        ins, refs = refs[: len(arrays)], refs[len(arrays) + len(after) :]
        results, slots = refs[: len(outs)], refs[len(outs) :]
        given, started, slot = [], [], 0
        for arg in args:
            if not isinstance(arg, tuple):
                given.append(ins.pop(0))
                continue
            for _, source, target in arg[1]:
                copy = pltpu.make_async_copy(
                    source(ins.pop(0), *scalars),
                    target(slots[slot], *scalars),
                    slots[held].at[len(started)],
                )
                copy.start()
                started.append(copy)
            given.append(slots[slot])
            slot += 1
        for copy in started:
            copy.wait()
        used, slot, targets = len(started), fetched, []
        for ref, mark in zip(results, stored):
            targets.append(slots[slot] if mark else ref)
            slot += mark
        body(*scalars, *given, *targets)
        started = []
        for ref, target, mark in zip(results, targets, stored):
            if mark:
                copy = pltpu.make_async_copy(target, ref, slots[held].at[used + len(started)])
                copy.start()
                started.append(copy)
        for copy in started:
            copy.wait()

    return pl.pallas_call(
        kernel,
        out_shape=[jax.ShapeDtypeStruct(out[0], out[1]) for out in outs],
        in_specs=[pl.BlockSpec(memory_space=pltpu.SMEM) for _ in smem]
        + specs
        + [pl.BlockSpec(memory_space=pl.ANY) for _ in after],
        out_specs=[pl.BlockSpec(memory_space=pl.ANY if m else pltpu.VMEM) for m in stored],
        scratch_shapes=scratch,
        compiler_params=pltpu.CompilerParams(vmem_limit_bytes=room * MIB),
        cost_estimate=pl.CostEstimate(flops=1, bytes_accessed=1, transcendentals=0),
    )(*smem, *arrays, *after)


def hold(arrays, after):
    held = len(arrays)
    return pl.pallas_call(
        lambda *refs: None,
        out_shape=[jax.ShapeDtypeStruct(a.shape, a.dtype) for a in arrays],
        in_specs=[pl.BlockSpec(memory_space=pl.ANY) for _ in (*arrays, *after)],
        out_specs=[pl.BlockSpec(memory_space=pl.ANY) for _ in arrays],
        input_output_aliases={n: n for n in range(held)},
        cost_estimate=pl.CostEstimate(flops=1, bytes_accessed=1, transcendentals=0),
    )(*arrays, *after)


def lower_triangle(blk):
    return lax.broadcasted_iota(jnp.int32, (blk, blk), 0) >= lax.broadcasted_iota(
        jnp.int32, (blk, blk), 1
    )


def forward_kernel(
    scale,
    mask,
    where,
    q_ref,
    k_ref,
    v_ref,
    probs_ref,
    inner_ref,
    soft_ref,
    mine_ref,
    other_ref,
    far_ref,
):
    rows, width = q_ref.shape
    count = mask.shape[0]
    blk = rows // count
    inv_root = 1.0 / math.sqrt(DH)
    triangle = lower_triangle(blk)
    for i in range(count):
        here = slice(i * blk, (i + 1) * blk)
        upto = slice(0, (i + 1) * blk)
        sums = []
        for h in range(2):
            cols = slice(h * DH, (h + 1) * DH)
            raw = dot(q_ref[here, cols], k_ref[upto, cols], NT)
            scores, inner = [], []
            for j in range(i + 1):
                part = raw[:, j * blk : (j + 1) * blk]
                keep = triangle if j == i else mask[i, j] > 0
                scores.append(jnp.where(keep, part * inv_root, -1e30))
                inner.append(jnp.where(triangle, part, 0.0) if j == i else part)
            scores = jnp.concatenate(scores, 1)
            inner = jnp.concatenate(inner, 1).astype(BF16)
            expo = jnp.exp(scores - jnp.max(scores, -1, keepdims=True))
            probs = (expo / jnp.sum(expo, -1, keepdims=True)).astype(BF16)
            v = v_ref[upto, cols]
            soft = dot(probs, v, NN)
            probs_ref[h, here, upto] = probs
            inner_ref[h, here, upto] = inner
            soft_ref[here, cols] = soft
            sums.append(soft + scale * dot(inner, v, NN))
        mine_ref[here], other_ref[here] = pick(where[2], sums)
    far_ref[...] = q_ref[:, pl.ds(pl.multiple_of((1 - where[2]) * DH, DH), DH)]


def pick(core, parts):
    return jnp.where(core == 0, parts[0], parts[1]), jnp.where(core == 0, parts[1], parts[0])


def both_heads(core, mine_ref, other_ref):
    mine, other = mine_ref[...], other_ref[...]
    return jnp.where(core == 0, mine, other), jnp.where(core == 0, other, mine)


def state_kernel(where, k_ref, v_ref, mine_ref, other_ref):
    heads = [slice(h * DH, (h + 1) * DH) for h in range(2)]
    parts = [dot(k_ref[:, cols], v_ref[:, cols], TN) for cols in heads]
    mine_ref[...], other_ref[...] = pick(where[2], parts)


def carry(flags, here_ref, got_ref, totals):
    carried = jnp.zeros(here_ref.shape, F32)
    for n, total in enumerate(totals):
        carried = carried + jnp.where(flags[n] > 0, total[...], 0.0)
    counts = flags[len(totals)] > 0
    keep = carried + jnp.where(counts, got_ref[...], 0.0)
    return keep, carried + jnp.where(counts, 0.0, here_ref[...])


def carry_kernel(flags, here_ref, got_ref, *refs):
    totals, (keep_ref, back_ref) = refs[:-2], refs[-2:]
    keep_ref[...], back_ref[...] = carry(flags, here_ref, got_ref, totals)


def attn_kernel(scale, count, flags, where, here_ref, got_ref, *refs):
    totals, refs = refs[: -count - 6], refs[-count - 6 :]
    q_ref, far_ref, pre_ref, far_pre_ref = refs[:4]
    out_refs, (keep_ref, back_ref) = refs[4:-2], refs[-2:]
    keep, back = carry(flags, here_ref, got_ref, totals)
    keep_ref[...], back_ref[...] = keep, back
    own = pre_ref.shape[0] // count
    cols = pl.ds(pl.multiple_of(where[2] * DH, DH), DH)
    for s, out_ref in enumerate(out_refs):
        block = lax.rem(where[0] + s, count)
        here = pl.ds(pl.multiple_of(block * own, own), own)
        mine = pre_ref[here] + scale * dot_wide(q_ref[here, cols], keep, NN)
        mate = far_pre_ref[here] + scale * dot_wide(far_ref[here], back, NN)
        out_ref[:own] = mine.astype(BF16)
        out_ref[own:] = mate.astype(BF16)


def first_kernel(spots, left_ref, weight_ref, right_ref, own_ref, half_ref):
    own_ref[...] = dot(left_ref[...], weight_ref[...], NT).astype(BF16)
    near = left_ref[:, pl.ds(pl.multiple_of(spots[0], DH), right_ref.shape[1])]
    half_ref[...] = dot(near, right_ref[...], NT)


def second_kernel(spots, left_ref, right_ref, half_ref, piece_ref, one_ref, three_ref, *cut_refs):
    wide = cut_refs[0].shape[1]
    for n, cut_ref in enumerate(cut_refs):
        cut_ref[...] = piece_ref[:, n * wide : (n + 1) * wide]
    total = (half_ref[...] + dot(left_ref[...], right_ref[...], NT)).astype(BF16)
    one_ref[...], three_ref[...] = total[:, :DH], total[:, DH:]


def last_kernel(spots, left_ref, right_ref, half_ref, out_ref):
    out_ref[...] = (half_ref[...] + dot(left_ref[...], right_ref[...], NT)).astype(BF16)


def near_kernel(spots, left_ref, right_ref, *refs):
    attn, (half_ref, own_out, mate_out) = refs[:-3], refs[-3:]
    half_ref[...] = dot(left_ref[...], right_ref[2 * DH : 3 * DH], NT)
    far_kernel(spots, right_ref, *attn, own_out, mate_out)


def far_kernel(spots, right_ref, *refs):
    attn, (own_out, mate_out) = refs[:-2], refs[-2:]
    own = own_out.shape[0]
    part = dot(jnp.concatenate([a[...] for a in attn], 1), right_ref[...], NN)
    own_out[...] = part[:own]
    mate_out[...] = part[own:]


def grad_kernel(whole, added, places, mine_ref, mate_ref, *refs):
    chunks, out_ref = refs[added:-1], refs[-1]
    total = refs[0][...] if added else None
    for j, chunk in enumerate(chunks):
        cols = slice(None) if whole else pl.ds(pl.multiple_of(places[j], DH), chunk.shape[1])
        left = jnp.concatenate([mine_ref[:, cols], mate_ref[:, cols]], 0)
        part = dot(left, chunk[...], NT)
        total = part if total is None else total + part
    out_ref[...] = total.astype(out_ref.dtype)


def mixed_kernel(count, each, places, *refs):
    attn, weight = refs[:count], refs[count]
    chunks, (own_out, mate_out) = list(refs[count + 1 : -2]), refs[-2:]
    own = own_out.shape[0]
    left = jnp.concatenate([a[...] for a in attn], 1)
    right = [weight[:, pl.ds(pl.multiple_of(places[0], DH), own_out.shape[1])]]
    for n in each:
        parts = [chunks.pop(0)[...] for _ in range(n)]
        right.append(jnp.concatenate(parts, 1) if n > 1 else parts[0])
    part = dot(left, jnp.concatenate(right, 0), NN)
    own_out[...] = part[:own]
    mate_out[...] = part[own:]


def join_kernel(places, *refs):
    out_ref, done_ref = refs[-2:]
    done_ref[...] = jnp.zeros(done_ref.shape, F32)
    for n in range(len(refs) // 2 - 1):
        wide = refs[2 * n].shape[1]
        there = pl.ds(pl.multiple_of(places[n], DH), wide)
        out_ref[:, there] = (refs[2 * n][...] + refs[2 * n + 1][...]).astype(BF16)


def collect_kernel(scale, count, where, q_ref, *refs):
    direct, across = refs[:count], refs[count : 2 * count]
    g_ref, mine_ref, other_ref = refs[2 * count :]
    own = g_ref.shape[0] // count
    mine = pl.ds(pl.multiple_of(where[2] * DH, DH), DH)
    mate = pl.ds(pl.multiple_of((1 - where[2]) * DH, DH), DH)
    for s in range(count):
        block = lax.rem(where[0] + s, count)
        here = pl.ds(pl.multiple_of(block * own, own), own)
        g_ref[here, mine] = direct[s][:own]
        g_ref[here, mate] = across[s][own:]
    heads = [slice(h * DH, (h + 1) * DH) for h in range(2)]
    parts = [scale * dot(q_ref[:, cols], g_ref[:, cols], TN) for cols in heads]
    mine_ref[...], other_ref[...] = pick(where[2], parts)


def backward_kernel(
    scale,
    count,
    where,
    q_ref,
    k_ref,
    v_ref,
    g_ref,
    probs_ref,
    inner_ref,
    soft_ref,
    mine_ref,
    other_ref,
    dq_ref,
    dk_ref,
    dv_ref,
):
    rows, width = q_ref.shape
    blk = rows // count
    inv_root = 1.0 / math.sqrt(DH)
    triangle = lower_triangle(blk)
    states = both_heads(where[2], mine_ref, other_ref)
    for h in range(width // DH):
        cols = slice(h * DH, (h + 1) * DH)
        for i in reversed(range(count)):
            here = slice(i * blk, (i + 1) * blk)
            upto = slice(0, (i + 1) * blk)
            q, g = q_ref[here, cols], g_ref[here, cols]
            k = k_ref[upto, cols]
            probs = probs_ref[h, here, upto]
            dprod = dot(g, v_ref[upto, cols], NT)
            delta = jnp.sum(g.astype(F32) * soft_ref[here, cols], -1, keepdims=True)
            dscore = (probs.astype(F32) * (dprod - delta) * inv_root).astype(BF16)
            last = jnp.where(triangle, dprod[:, i * blk :], 0.0)
            dinner = jnp.concatenate([dprod[:, : i * blk], last], 1) if i else last
            dinner = dinner.astype(BF16)
            dq_ref[here, cols] = (
                dot(dscore, k, NN)
                + scale * (dot(dinner, k, NN) + dot_wide(g, states[h], NT))
            ).astype(BF16)
            dk = dot(dscore, q, TN) + scale * dot(dinner, q, TN)
            dv = dot(probs, g, TN) + scale * dot(inner_ref[h, here, upto], g, TN)
            if i == count - 1:
                dk_ref[upto, cols] = dk
                dv_ref[upto, cols] = dv
            else:
                dk_ref[upto, cols] += dk
                dv_ref[upto, cols] += dv


def close_kernel(where, k_ref, v_ref, dk_ref, dv_ref, mine_ref, other_ref, gk_ref, gv_ref):
    states = both_heads(where[2], mine_ref, other_ref)
    for h in range(k_ref.shape[1] // DH):
        cols = slice(h * DH, (h + 1) * DH)
        state = states[h]
        gk_ref[:, cols] = (dk_ref[:, cols] + dot_wide(v_ref[:, cols], state, NT)).astype(BF16)
        gv_ref[:, cols] = (dv_ref[:, cols] + dot_wide(k_ref[:, cols], state, NN)).astype(BF16)


def send(x, flip, shift):
    shards, heads = lax.axis_size("ctx"), lax.axis_size("head")
    pairs = [
        (c * heads + z, (c ^ flip) * heads + (z + shift) % heads)
        for c in range(shards)
        for z in range(heads)
    ]
    return lax.ppermute(x, ("ctx", "head"), pairs)


def exchange(mine, other, core, chip, chips, later):
    got = send(other, 1, 0)
    own = total = mine + got
    totals, flags = [], []
    if chips == 4:
        for flip in (1, 2, 3):
            totals.append(send(total, 2 * flip, 0))
            flags.append(((chip ^ flip) > chip) == later)
    else:
        step = 1
        while step < chips:
            totals.append(send(total, 2 * step, 0))
            flags.append(((chip & step) == 0) == later)
            total = total + totals[-1]
            step *= 2
    flags.append((core == 0) == later)
    return jnp.stack(flags).astype(jnp.int32), [mine, got, *totals], own


def on_device(query, key, value, block_mask, out_weight, cotangent):
    rows, width = query.shape
    heads = width // DH
    shards, count = lax.axis_size("ctx"), lax.axis_size("head")
    model = out_weight.shape[1]
    own = rows // count
    scale = 1.0 / math.sqrt(DH * rows * shards)
    blocks = block_mask.shape[0]
    ctx, place = lax.axis_index("ctx"), lax.axis_index("head")
    core, chip, chips = ctx & 1, ctx >> 1, shards // 2
    where = jnp.stack([place, ctx, core])
    flat = (rows, width)
    pair = [((DH, DH), F32)] * 2
    tokens = ((2 * own, DH), BF16)

    board = chips == 4 and count == 4
    wide = model // (2 if board else chips)
    colour = (chip & 1) ^ (chip >> 1) if board else chip
    piece = lax.dynamic_slice(out_weight, (core * DH, colour * wide), (DH, wide))
    arrived = {1: send(piece, 0, 1), count - 1: send(piece, 0, -1)}
    mate_cotangent = send(cotangent, 1, 0)

    mine, other = call(
        state_kernel,
        pair,
        [*here(key, value)],
        [where],
        [mate_cotangent],
    )
    flags, parts, total = exchange(mine, other, core, chip, chips, False)
    probs, inner, soft, pre, other, far = call(
        functools.partial(forward_kernel, scale),
        [((heads, rows, rows), BF16, True)] * 2
        + [(flat, F32, True)]
        + [((rows, DH), F32, True)] * 2
        + [((rows, DH), BF16, True)],
        here(query, key, value),
        [block_mask, where],
        [total],
    )
    *attn, keep, back = call(
        functools.partial(attn_kernel, scale, count),
        [(*tokens, True)] + [tokens] * (count - 1) + [(*kept, True) for kept in pair],
        [*parts, *here(query, send(far, 1, 0), pre, send(other, 1, 0))],
        [flags, where],
    )
    linear = [keep, send(back, 1, 0)]
    attn = [attn[0]] + [send(attn[s], 0, s) for s in range(1, count)]

    work = near_and_far if board else by_gathers
    both, across, joins, starts = work(
        attn, arrived, cotangent, mate_cotangent, out_weight, core, chip, colour
    )
    mixed, done = call(
        join_kernel, [((own, model), BF16, True), ((8, DH), F32)], here(*joins), [jnp.stack(starts)]
    )

    g, mine, other = call(
        functools.partial(collect_kernel, scale, count),
        [(flat, BF16), *pair],
        [*here(query, *both, *across)],
        [where],
    )
    flags, parts, total = exchange(mine, other, core, chip, chips, True)
    grad_query, dk, dv = call(
        functools.partial(backward_kernel, scale, blocks),
        [(flat, BF16, True)] + [(flat, F32)] * 2,
        [*here(query, key, value), g, *here(probs, inner, soft, *linear)],
        [where],
        [total],
    )
    keep, back = call(carry_kernel, pair, parts, [flags], [dk])
    grad_key, grad_value = call(
        close_kernel,
        [(flat, BF16, True)] * 2,
        [*here(key, value), dk, dv, keep, send(back, 1, 0)],
        [where],
        [done],
    )
    return mixed, grad_query, grad_key, grad_value


def near_and_far(attn, arrived, cotangent, mate_cotangent, weight, core, chip, colour):
    own, model = cotangent.shape
    wide = model // 2
    spots = jnp.stack([colour * wide, (1 - colour) * wide, core * DH])
    tokens = ((2 * own, DH), BF16)
    parts = [((own, wide), F32, True)] * 2
    all_arrays = [(cotangent, all_of, rows_at(0, own)), (mate_cotangent, all_of, rows_at(own, own))]
    whole = fetch((2 * own, model), *all_arrays)
    left = [
        fetch((2 * own, wide), *((a, columns(n, wide), put) for a, _, put in all_arrays))
        for n in range(2)
    ]

    def own_rows(ref, spots, *_):
        return ref.at[pl.ds(pl.multiple_of(spots[2], DH), DH)]

    def own_columns(n):
        return lambda ref, spots, *_: ref.at[
            pl.ds(pl.multiple_of(spots[2], DH), DH), pl.ds(pl.multiple_of(spots[n], DH), wide)
        ]

    def stacked(*arrays):
        return [(a, all_of, rows_at(n * DH, DH)) for n, a in enumerate(arrays)]

    arrived[1], arrived[3] = hold([arrived[1], arrived[3]], attn[1:])
    arrived[2] = send(arrived[1], 0, 1)
    second = {1: send(arrived[1], 2, 0), 3: send(arrived[3], 4, 0)}
    mine, half = call(
        first_kernel,
        [(*tokens, True), ((2 * own, 2 * DH), F32, True)],
        [
            whole,
            fetch((DH, model), (weight, own_rows, all_of)),
            fetch((2 * DH, wide), *stacked(arrived[1], arrived[3])),
        ],
        [spots],
    )
    one, three, *cuts = call(
        second_kernel,
        [tokens] * 2 + [((DH, wide // 2), BF16)] * 2,
        [
            left[1],
            fetch((2 * DH, wide), *stacked(second[1], second[3])),
            *here(half),
            fetch((DH, wide), (arrived[2], all_of, all_of)),
        ],
        [spots],
    )
    second[2] = [send(cuts[0], 2, 0), send(cuts[1], 4, 0)]
    both = {0: mine, 1: send(one, 0, -1), 3: send(three, 0, -3)}
    across = {s: send(both[s], 1, 0) for s in (0, 1, 3)}
    half, part, mate_part = call(
        near_kernel,
        [((2 * own, DH), F32), *parts],
        [
            left[0],
            fetch(
                (4 * DH, wide),
                (weight, own_columns(0), rows_at(0, DH)),
                *((arrived[s], all_of, rows_at(s * DH, DH)) for s in (1, 2, 3)),
            ),
            *here(*attn),
        ],
        [spots],
    )
    joins = [part, send(mate_part, 1, 0)]
    quarters = [(a, all_of, columns_at(n * wide // 2, wide // 2)) for n, a in enumerate(second[2])]
    (two,) = call(
        last_kernel,
        [tokens],
        [left[1], fetch((DH, wide), *quarters), half],
        [spots],
        [across[0], across[1], across[3]],
    )
    both[2] = send(two, 0, -2)

    def quarter(n):
        return lambda ref, *_: ref.at[2 * DH : 3 * DH, n * wide // 2 : (n + 1) * wide // 2]

    part, mate_part = call(
        far_kernel,
        parts,
        [
            fetch(
                (4 * DH, wide),
                (weight, own_columns(1), rows_at(0, DH)),
                (second[1], all_of, rows_at(DH, DH)),
                (second[3], all_of, rows_at(3 * DH, DH)),
                *((a, all_of, quarter(n)) for n, a in enumerate(second[2])),
            ),
            *here(*attn),
        ],
        [spots],
        [both[2]],
    )
    joins += [part, send(mate_part, 1, 0)]
    across[2] = send(both[2], 1, 0)
    return [both[s] for s in range(4)], [across[s] for s in range(4)], joins, [spots[0], spots[1]]


def by_gathers(attn, arrived, cotangent, mate_cotangent, out_weight, core, chip, colour):
    own, model = cotangent.shape
    shards, count = lax.axis_size("ctx"), lax.axis_size("head")
    weight = lax.dynamic_slice_in_dim(out_weight, core * DH, DH, 0)
    zero = jnp.zeros((1,), jnp.int32)
    groups = [list(range(k, shards, 2)) for k in range(2)]
    for s in range(2, count - 1):
        arrived[s] = send(arrived[s - 1], 0, 1)
    chunks = [weight] + [
        lax.all_gather(arrived[s], "ctx", axis=1, tiled=True, axis_index_groups=groups)
        for s in range(1, count)
    ]
    both = []
    for s in range(count):
        (block,) = call(
            functools.partial(grad_kernel, True, 0),
            [((2 * own, DH), BF16)],
            here(cotangent, mate_cotangent, chunks[s]),
            [zero],
            )
        both.append(send(block, 0, -s) if s else block)
    part, mate_part = call(
        functools.partial(mixed_kernel, count, [1] * (count - 1)),
        [((own, model), F32, True)] * 2,
        here(*attn, *chunks),
        [zero],
        room=40,
    )
    return both, [send(b, 1, 0) for b in both], [part, send(mate_part, 1, 0)], [jnp.int32(0)]


def solution(mesh):
    return jax.shard_map(
        on_device,
        mesh=mesh,
        in_specs=(
            P("ctx", "head"),
            P("ctx", "head"),
            P("ctx", "head"),
            P("ctx", None),
            P("head", None),
            P(("ctx", "head"), None),
        ),
        out_specs=(P(("ctx", "head"), None), P("ctx", "head"), P("ctx", "head"), P("ctx", "head")),
        check_vma=False,
    )
```

```python
import functools
import math

import jax
import jax.numpy as jnp
from jax import lax
from jax.experimental import pallas as pl
from jax.experimental.pallas import tpu as pltpu
from jax.sharding import PartitionSpec as P

DH = 128
F32 = jnp.float32
BF16 = jnp.bfloat16
NN = ((1,), (0,))
NT = ((1,), (1,))
TN = ((0,), (0,))
MIB = 1 << 20


def dot(a, b, dims):
    return lax.dot_general(a, b, (dims, ((), ())), preferred_element_type=F32)


def dot_wide(a, b, dims):
    high = b.astype(BF16)
    low = (b - high.astype(F32)).astype(BF16)
    return dot(a, high, dims) + dot(a, low, dims)


def fetch(shape, *parts):
    return (shape, parts)


def all_of(ref, *_):
    return ref


def columns(spot, wide, rows=slice(None)):
    def view(ref, spots, *_):
        return ref.at[rows, pl.ds(pl.multiple_of(spots[spot], DH), wide)]

    return view


def rows_at(first, count):
    return lambda ref, *_: ref.at[first : first + count]


def columns_at(first, count):
    return lambda ref, *_: ref.at[:, first : first + count]


def call(body, outs, args, smem=(), after=(), room=8, flops=1):
    arrays, specs, scratch = [], [], []
    for arg in args:
        if isinstance(arg, tuple):
            arrays += [part[0] for part in arg[1]]
            specs += [pl.BlockSpec(memory_space=pltpu.HBM) for _ in arg[1]]
            scratch.append(pltpu.VMEM(arg[0], arg[1][0][0].dtype))
        else:
            arrays.append(arg)
            specs.append(pl.BlockSpec(memory_space=pltpu.VMEM))
    copies = sum(len(arg[1]) for arg in args if isinstance(arg, tuple))
    held = len(scratch)
    if copies:
        scratch.append(pltpu.SemaphoreType.DMA((copies,)))

    def kernel(*refs):
        scalars, refs = refs[: len(smem)], list(refs[len(smem) :])
        ins, refs = refs[: len(arrays)], refs[len(arrays) + len(after) :]
        results, slots = refs[: len(outs)], refs[len(outs) :]
        given, started, slot = [], [], 0
        for arg in args:
            if not isinstance(arg, tuple):
                given.append(ins.pop(0))
                continue
            for _, source, target in arg[1]:
                copy = pltpu.make_async_copy(
                    source(ins.pop(0), *scalars),
                    target(slots[slot], *scalars),
                    slots[held].at[len(started)],
                )
                copy.start()
                started.append(copy)
            given.append(slots[slot])
            slot += 1
        for copy in started:
            copy.wait()
        body(*scalars, *given, *results)

    moved = sum(a.size * a.dtype.itemsize for a in arrays)
    moved += sum(math.prod(s) * jnp.dtype(t).itemsize for s, t in outs)
    return pl.pallas_call(
        kernel,
        out_shape=[jax.ShapeDtypeStruct(s, t) for s, t in outs],
        in_specs=[pl.BlockSpec(memory_space=pltpu.SMEM) for _ in smem]
        + specs
        + [pl.BlockSpec(memory_space=pl.ANY) for _ in after],
        out_specs=[pl.BlockSpec(memory_space=pltpu.VMEM) for _ in outs],
        scratch_shapes=scratch,
        compiler_params=pltpu.CompilerParams(vmem_limit_bytes=room * MIB),
        cost_estimate=pl.CostEstimate(
            flops=int(flops), bytes_accessed=int(moved), transcendentals=0
        ),
    )(*smem, *arrays, *after)


def hold(arrays, after):
    held = len(arrays)
    return pl.pallas_call(
        lambda *refs: None,
        out_shape=[jax.ShapeDtypeStruct(a.shape, a.dtype) for a in arrays],
        in_specs=[pl.BlockSpec(memory_space=pl.ANY) for _ in (*arrays, *after)],
        out_specs=[pl.BlockSpec(memory_space=pl.ANY) for _ in arrays],
        input_output_aliases={n: n for n in range(held)},
        cost_estimate=pl.CostEstimate(flops=1, bytes_accessed=1, transcendentals=0),
    )(*arrays, *after)


def lower_triangle(blk):
    return lax.broadcasted_iota(jnp.int32, (blk, blk), 0) >= lax.broadcasted_iota(
        jnp.int32, (blk, blk), 1
    )


def forward_kernel(
    scale,
    mask,
    where,
    q_ref,
    k_ref,
    v_ref,
    probs_ref,
    inner_ref,
    soft_ref,
    mine_ref,
    other_ref,
    far_ref,
    mine_state_ref,
    other_state_ref,
):
    heads = [slice(h * DH, (h + 1) * DH) for h in range(2)]
    states = [dot(k_ref[:, cols], v_ref[:, cols], TN) for cols in heads]
    mine_state_ref[...], other_state_ref[...] = pick(where[2], states)
    rows, width = q_ref.shape
    count = mask.shape[0]
    blk = rows // count
    inv_root = 1.0 / math.sqrt(DH)
    triangle = lower_triangle(blk)
    for i in range(count):
        here = slice(i * blk, (i + 1) * blk)
        upto = slice(0, (i + 1) * blk)
        sums = []
        for h in range(2):
            cols = slice(h * DH, (h + 1) * DH)
            raw = dot(q_ref[here, cols], k_ref[upto, cols], NT)
            scores, inner = [], []
            for j in range(i + 1):
                part = raw[:, j * blk : (j + 1) * blk]
                keep = triangle if j == i else mask[i, j] > 0
                scores.append(jnp.where(keep, part * inv_root, -1e30))
                inner.append(jnp.where(triangle, part, 0.0) if j == i else part)
            scores = jnp.concatenate(scores, 1)
            inner = jnp.concatenate(inner, 1).astype(BF16)
            expo = jnp.exp(scores - jnp.max(scores, -1, keepdims=True))
            probs = (expo / jnp.sum(expo, -1, keepdims=True)).astype(BF16)
            v = v_ref[upto, cols]
            soft = dot(probs, v, NN)
            probs_ref[h, here, upto] = probs
            inner_ref[h, here, upto] = inner
            soft_ref[here, cols] = soft
            sums.append(soft + scale * dot(inner, v, NN))
        mine_ref[here], other_ref[here] = pick(where[2], sums)
    far_ref[...] = q_ref[:, pl.ds(pl.multiple_of((1 - where[2]) * DH, DH), DH)]


def pick(core, parts):
    return jnp.where(core == 0, parts[0], parts[1]), jnp.where(core == 0, parts[1], parts[0])


def both_heads(core, mine_ref, other_ref):
    mine, other = mine_ref[...], other_ref[...]
    return jnp.where(core == 0, mine, other), jnp.where(core == 0, other, mine)


def carry(flags, here_ref, got_ref, totals):
    carried = jnp.zeros(here_ref.shape, F32)
    for n, total in enumerate(totals):
        carried = carried + jnp.where(flags[n] > 0, total[...], 0.0)
    counts = flags[len(totals)] > 0
    keep = carried + jnp.where(counts, got_ref[...], 0.0)
    return keep, carried + jnp.where(counts, 0.0, here_ref[...])


def carry_kernel(flags, here_ref, got_ref, *refs):
    totals, (keep_ref, back_ref) = refs[:-2], refs[-2:]
    keep_ref[...], back_ref[...] = carry(flags, here_ref, got_ref, totals)


def attn_kernel(scale, count, flags, where, here_ref, got_ref, *refs):
    totals, refs = refs[: -count - 6], refs[-count - 6 :]
    q_ref, far_ref, pre_ref, far_pre_ref = refs[:4]
    out_refs, (keep_ref, back_ref) = refs[4:-2], refs[-2:]
    keep, back = carry(flags, here_ref, got_ref, totals)
    keep_ref[...], back_ref[...] = keep, back
    own = pre_ref.shape[0] // count
    cols = pl.ds(pl.multiple_of(where[2] * DH, DH), DH)
    for s, out_ref in enumerate(out_refs):
        block = lax.rem(where[0] + s, count)
        here = pl.ds(pl.multiple_of(block * own, own), own)
        mine = pre_ref[here] + scale * dot_wide(q_ref[here, cols], keep, NN)
        mate = far_pre_ref[here] + scale * dot_wide(far_ref[here], back, NN)
        out_ref[:own] = mine.astype(BF16)
        out_ref[own:] = mate.astype(BF16)


def first_kernel(spots, left_ref, weight_ref, right_ref, own_ref, half_ref):
    own_ref[...] = dot(left_ref[...], weight_ref[...], NT).astype(BF16)
    near = left_ref[:, pl.ds(pl.multiple_of(spots[0], DH), right_ref.shape[1])]
    half_ref[...] = dot(near, right_ref[...], NT)


def second_kernel(spots, left_ref, right_ref, half_ref, piece_ref, one_ref, three_ref, *cut_refs):
    wide = cut_refs[0].shape[1]
    for n, cut_ref in enumerate(cut_refs):
        cut_ref[...] = piece_ref[:, n * wide : (n + 1) * wide]
    total = (half_ref[...] + dot(left_ref[...], right_ref[...], NT)).astype(BF16)
    one_ref[...], three_ref[...] = total[:, :DH], total[:, DH:]


def last_kernel(spots, left_ref, right_ref, half_ref, out_ref):
    out_ref[...] = (half_ref[...] + dot(left_ref[...], right_ref[...], NT)).astype(BF16)


def near_kernel(spots, left_ref, right_ref, *refs):
    attn, (half_ref, own_out, mate_out) = refs[:-3], refs[-3:]
    half_ref[...] = dot(left_ref[...], right_ref[2 * DH : 3 * DH], NT)
    far_kernel(spots, right_ref, *attn, own_out, mate_out)


def far_kernel(spots, right_ref, *refs):
    attn, (own_out, mate_out) = refs[:-2], refs[-2:]
    own = own_out.shape[0]
    part = dot(jnp.concatenate([a[...] for a in attn], 1), right_ref[...], NN)
    own_out[...] = part[:own]
    mate_out[...] = part[own:]


def grad_kernel(whole, added, places, mine_ref, mate_ref, *refs):
    chunks, out_ref = refs[added:-1], refs[-1]
    total = refs[0][...] if added else None
    for j, chunk in enumerate(chunks):
        cols = slice(None) if whole else pl.ds(pl.multiple_of(places[j], DH), chunk.shape[1])
        left = jnp.concatenate([mine_ref[:, cols], mate_ref[:, cols]], 0)
        part = dot(left, chunk[...], NT)
        total = part if total is None else total + part
    out_ref[...] = total.astype(out_ref.dtype)


def mixed_kernel(count, each, places, *refs):
    attn, weight = refs[:count], refs[count]
    chunks, (own_out, mate_out) = list(refs[count + 1 : -2]), refs[-2:]
    own = own_out.shape[0]
    left = jnp.concatenate([a[...] for a in attn], 1)
    right = [weight[:, pl.ds(pl.multiple_of(places[0], DH), own_out.shape[1])]]
    for n in each:
        parts = [chunks.pop(0)[...] for _ in range(n)]
        right.append(jnp.concatenate(parts, 1) if n > 1 else parts[0])
    part = dot(left, jnp.concatenate(right, 0), NN)
    own_out[...] = part[:own]
    mate_out[...] = part[own:]


def join_kernel(places, *refs):
    out_ref, done_ref = refs[-2:]
    done_ref[...] = jnp.zeros(done_ref.shape, F32)
    for n in range(len(refs) // 2 - 1):
        wide = refs[2 * n].shape[1]
        there = pl.ds(pl.multiple_of(places[n], DH), wide)
        out_ref[:, there] = (refs[2 * n][...] + refs[2 * n + 1][...]).astype(BF16)


def collect_kernel(scale, count, where, q_ref, *refs):
    direct, across = refs[:count], refs[count : 2 * count]
    g_ref, mine_ref, other_ref = refs[2 * count :]
    own = g_ref.shape[0] // count
    mine = pl.ds(pl.multiple_of(where[2] * DH, DH), DH)
    mate = pl.ds(pl.multiple_of((1 - where[2]) * DH, DH), DH)
    for s in range(count):
        block = lax.rem(where[0] + s, count)
        here = pl.ds(pl.multiple_of(block * own, own), own)
        g_ref[here, mine] = direct[s][:own]
        g_ref[here, mate] = across[s][own:]
    heads = [slice(h * DH, (h + 1) * DH) for h in range(2)]
    parts = [scale * dot(q_ref[:, cols], g_ref[:, cols], TN) for cols in heads]
    mine_ref[...], other_ref[...] = pick(where[2], parts)


def backward_kernel(
    scale,
    count,
    where,
    q_ref,
    k_ref,
    v_ref,
    g_ref,
    probs_ref,
    inner_ref,
    soft_ref,
    mine_ref,
    other_ref,
    dq_ref,
    dk_ref,
    dv_ref,
):
    rows, width = q_ref.shape
    blk = rows // count
    inv_root = 1.0 / math.sqrt(DH)
    triangle = lower_triangle(blk)
    states = both_heads(where[2], mine_ref, other_ref)
    for h in range(width // DH):
        cols = slice(h * DH, (h + 1) * DH)
        for i in reversed(range(count)):
            here = slice(i * blk, (i + 1) * blk)
            upto = slice(0, (i + 1) * blk)
            q, g = q_ref[here, cols], g_ref[here, cols]
            k = k_ref[upto, cols]
            probs = probs_ref[h, here, upto]
            dprod = dot(g, v_ref[upto, cols], NT)
            delta = jnp.sum(g.astype(F32) * soft_ref[here, cols], -1, keepdims=True)
            dscore = (probs.astype(F32) * (dprod - delta) * inv_root).astype(BF16)
            last = jnp.where(triangle, dprod[:, i * blk :], 0.0)
            dinner = jnp.concatenate([dprod[:, : i * blk], last], 1) if i else last
            dinner = dinner.astype(BF16)
            dq_ref[here, cols] = (
                dot(dscore, k, NN)
                + scale * (dot(dinner, k, NN) + dot_wide(g, states[h], NT))
            ).astype(BF16)
            dk = dot(dscore, q, TN) + scale * dot(dinner, q, TN)
            dv = dot(probs, g, TN) + scale * dot(inner_ref[h, here, upto], g, TN)
            if i == count - 1:
                dk_ref[upto, cols] = dk
                dv_ref[upto, cols] = dv
            else:
                dk_ref[upto, cols] += dk
                dv_ref[upto, cols] += dv


def close_kernel(where, k_ref, v_ref, dk_ref, dv_ref, mine_ref, other_ref, gk_ref, gv_ref):
    states = both_heads(where[2], mine_ref, other_ref)
    for h in range(k_ref.shape[1] // DH):
        cols = slice(h * DH, (h + 1) * DH)
        state = states[h]
        gk_ref[:, cols] = (dk_ref[:, cols] + dot_wide(v_ref[:, cols], state, NT)).astype(BF16)
        gv_ref[:, cols] = (dv_ref[:, cols] + dot_wide(k_ref[:, cols], state, NN)).astype(BF16)


def send(x, flip, shift):
    shards, heads = lax.axis_size("ctx"), lax.axis_size("head")
    pairs = [
        (c * heads + z, (c ^ flip) * heads + (z + shift) % heads)
        for c in range(shards)
        for z in range(heads)
    ]
    return lax.ppermute(x, ("ctx", "head"), pairs)


def exchange(mine, other, core, chip, chips, later):
    got = send(other, 1, 0)
    own = total = mine + got
    totals, flags = [], []
    if chips == 4:
        for flip in (1, 2, 3):
            totals.append(send(total, 2 * flip, 0))
            flags.append(((chip ^ flip) > chip) == later)
    else:
        step = 1
        while step < chips:
            totals.append(send(total, 2 * step, 0))
            flags.append(((chip & step) == 0) == later)
            total = total + totals[-1]
            step *= 2
    flags.append((core == 0) == later)
    return jnp.stack(flags).astype(jnp.int32), [mine, got, *totals], own


def on_device(query, key, value, block_mask, out_weight, cotangent):
    rows, width = query.shape
    heads = width // DH
    shards, count = lax.axis_size("ctx"), lax.axis_size("head")
    model = out_weight.shape[1]
    own = rows // count
    scale = 1.0 / math.sqrt(DH * rows * shards)
    blocks = block_mask.shape[0]
    ctx, place = lax.axis_index("ctx"), lax.axis_index("head")
    core, chip, chips = ctx & 1, ctx >> 1, shards // 2
    where = jnp.stack([place, ctx, core])
    flat, square = (rows, width), rows * rows * DH * heads
    pair = [((DH, DH), F32)] * 2
    tokens = ((2 * own, DH), BF16)
    product = 4 * own * DH * model

    board = chips == 4 and count == 4
    wide = model // (2 if board else chips)
    colour = (chip & 1) ^ (chip >> 1) if board else chip
    piece = lax.dynamic_slice(out_weight, (core * DH, colour * wide), (DH, wide))
    arrived = {1: send(piece, 0, 1), count - 1: send(piece, 0, -1)}
    mate_cotangent = send(cotangent, 1, 0)

    probs, inner, soft, pre, other_pre, far, mine, other = call(
        functools.partial(forward_kernel, scale),
        [((heads, rows, rows), BF16)] * 2
        + [(flat, F32)]
        + [((rows, DH), F32)] * 2
        + [((rows, DH), BF16)]
        + pair,
        [query, key, value],
        [block_mask, where],
        [mate_cotangent],
        flops=7 * square,
    )
    flags, parts, total = exchange(mine, other, core, chip, chips, False)
    *attn, keep, back = call(
        functools.partial(attn_kernel, scale, count),
        [tokens] * count + pair,
        [*parts, query, send(far, 1, 0), pre, send(other_pre, 1, 0)],
        [flags, where],
    )
    linear = [keep, send(back, 1, 0)]
    attn = [attn[0]] + [send(attn[s], 0, s) for s in range(1, count)]

    work = near_and_far if board else by_gathers
    both, across, joins, starts = work(
        attn, arrived, cotangent, mate_cotangent, out_weight, core, chip, colour, product
    )
    mixed, done = call(
        join_kernel, [((own, model), BF16), ((8, DH), F32)], joins, [jnp.stack(starts)]
    )

    g, mine, other = call(
        functools.partial(collect_kernel, scale, count),
        [(flat, BF16), *pair],
        [query, *both, *across],
        [where],
    )
    flags, parts, total = exchange(mine, other, core, chip, chips, True)
    grad_query, dk, dv = call(
        functools.partial(backward_kernel, scale, blocks),
        [(flat, BF16)] + [(flat, F32)] * 2,
        [query, key, value, g, probs, inner, soft, *linear],
        [where],
        [total],
        flops=14 * square,
    )
    keep, back = call(carry_kernel, pair, parts, [flags], [dk])
    grad_key, grad_value = call(
        close_kernel,
        [(flat, BF16)] * 2,
        [key, value, dk, dv, keep, send(back, 1, 0)],
        [where],
        [done],
    )
    return mixed, grad_query, grad_key, grad_value


def near_and_far(attn, arrived, cotangent, mate_cotangent, weight, core, chip, colour, product):
    own, model = cotangent.shape
    wide = model // 2
    spots = jnp.stack([colour * wide, (1 - colour) * wide, core * DH])
    tokens = ((2 * own, DH), BF16)
    parts = [((own, wide), F32)] * 2
    all_arrays = [(cotangent, all_of, rows_at(0, own)), (mate_cotangent, all_of, rows_at(own, own))]
    whole = fetch((2 * own, model), *all_arrays)
    left = [
        fetch((2 * own, wide), *((a, columns(n, wide), put) for a, _, put in all_arrays))
        for n in range(2)
    ]

    def own_rows(ref, spots, *_):
        return ref.at[pl.ds(pl.multiple_of(spots[2], DH), DH)]

    def own_columns(n):
        return lambda ref, spots, *_: ref.at[
            pl.ds(pl.multiple_of(spots[2], DH), DH), pl.ds(pl.multiple_of(spots[n], DH), wide)
        ]

    def stacked(*arrays):
        return [(a, all_of, rows_at(n * DH, DH)) for n, a in enumerate(arrays)]

    arrived[1], arrived[3] = hold([arrived[1], arrived[3]], attn[:1])
    arrived[2] = send(arrived[1], 0, 1)
    second = {1: send(arrived[1], 2, 0), 3: send(arrived[3], 4, 0)}
    mine, half = call(
        first_kernel,
        [tokens, ((2 * own, 2 * DH), F32)],
        [
            whole,
            fetch((DH, model), (weight, own_rows, all_of)),
            fetch((2 * DH, wide), *stacked(arrived[1], arrived[3])),
        ],
        [spots],
        room=24,
        flops=2 * product,
    )
    one, three, *cuts = call(
        second_kernel,
        [tokens] * 2 + [((DH, wide // 2), BF16)] * 2,
        [
            left[1],
            fetch((2 * DH, wide), *stacked(second[1], second[3])),
            half,
            fetch((DH, wide), (arrived[2], all_of, all_of)),
        ],
        [spots],
        attn[1:],
        room=16,
        flops=product,
    )
    second[2] = [send(cuts[0], 2, 0), send(cuts[1], 4, 0)]
    both = {0: mine, 1: send(one, 0, -1), 3: send(three, 0, -3)}
    across = {s: send(both[s], 1, 0) for s in (0, 1, 3)}
    half, part, mate_part = call(
        near_kernel,
        [((2 * own, DH), F32), *parts],
        [
            left[0],
            fetch(
                (4 * DH, wide),
                (weight, own_columns(0), rows_at(0, DH)),
                *((arrived[s], all_of, rows_at(s * DH, DH)) for s in (1, 2, 3)),
            ),
            *attn,
        ],
        [spots],
        room=24,
        flops=2 * product,
    )
    joins = [part, send(mate_part, 1, 0)]
    quarters = [(a, all_of, columns_at(n * wide // 2, wide // 2)) for n, a in enumerate(second[2])]
    (two,) = call(
        last_kernel,
        [tokens],
        [left[1], fetch((DH, wide), *quarters), half],
        [spots],
        [both[1], both[3]],
        room=16,
        flops=product // 2,
    )
    both[2] = send(two, 0, -2)

    def quarter(n):
        return lambda ref, *_: ref.at[2 * DH : 3 * DH, n * wide // 2 : (n + 1) * wide // 2]

    part, mate_part = call(
        far_kernel,
        parts,
        [
            fetch(
                (4 * DH, wide),
                (weight, own_columns(1), rows_at(0, DH)),
                (second[1], all_of, rows_at(DH, DH)),
                (second[3], all_of, rows_at(3 * DH, DH)),
                *((a, all_of, quarter(n)) for n, a in enumerate(second[2])),
            ),
            *attn,
        ],
        [spots],
        [both[2], across[0], across[1], across[3]],
        room=24,
        flops=2 * product,
    )
    joins += [part, send(mate_part, 1, 0)]
    across[2] = send(both[2], 1, 0)
    return [both[s] for s in range(4)], [across[s] for s in range(4)], joins, [spots[0], spots[1]]


def by_gathers(attn, arrived, cotangent, mate_cotangent, out_weight, core, chip, colour, product):
    own, model = cotangent.shape
    shards, count = lax.axis_size("ctx"), lax.axis_size("head")
    weight = lax.dynamic_slice_in_dim(out_weight, core * DH, DH, 0)
    zero = jnp.zeros((1,), jnp.int32)
    groups = [list(range(k, shards, 2)) for k in range(2)]
    for s in range(2, count - 1):
        arrived[s] = send(arrived[s - 1], 0, 1)
    chunks = [weight] + [
        lax.all_gather(arrived[s], "ctx", axis=1, tiled=True, axis_index_groups=groups)
        for s in range(1, count)
    ]
    both = []
    for s in range(count):
        (block,) = call(
            functools.partial(grad_kernel, True, 0),
            [((2 * own, DH), BF16)],
            [cotangent, mate_cotangent, chunks[s]],
            [zero],
            flops=product,
        )
        both.append(send(block, 0, -s) if s else block)
    part, mate_part = call(
        functools.partial(mixed_kernel, count, [1] * (count - 1)),
        [((own, model), F32)] * 2,
        [*attn, *chunks],
        [zero],
        room=16,
        flops=count * product,
    )
    return both, [send(b, 1, 0) for b in both], [part, send(mate_part, 1, 0)], [jnp.int32(0)]


def solution(mesh):
    return jax.shard_map(
        on_device,
        mesh=mesh,
        in_specs=(
            P("ctx", "head"),
            P("ctx", "head"),
            P("ctx", "head"),
            P("ctx", None),
            P("head", None),
            P(("ctx", "head"), None),
        ),
        out_specs=(P(("ctx", "head"), None), P("ctx", "head"), P("ctx", "head"), P("ctx", "head")),
        check_vma=False,
    )
```

```python
import functools
import math

import jax
import jax.numpy as jnp
from jax import lax
from jax.experimental import pallas as pl
from jax.experimental.pallas import tpu as pltpu
from jax.sharding import PartitionSpec as P

DH = 128
F32 = jnp.float32
BF16 = jnp.bfloat16
NN = ((1,), (0,))
NT = ((1,), (1,))
TN = ((0,), (0,))
MIB = 1 << 20


def dot(a, b, dims):
    return lax.dot_general(a, b, (dims, ((), ())), preferred_element_type=F32)


def dot_wide(a, b, dims):
    high = b.astype(BF16)
    low = (b - high.astype(F32)).astype(BF16)
    return dot(a, high, dims) + dot(a, low, dims)


def fetch(shape, *parts):
    return (shape, parts)


def all_of(ref, *_):
    return ref


def columns(spot, wide, rows=slice(None)):
    def view(ref, spots, *_):
        return ref.at[rows, pl.ds(pl.multiple_of(spots[spot], DH), wide)]

    return view


def rows_at(first, count):
    return lambda ref, *_: ref.at[first : first + count]


def columns_at(first, count):
    return lambda ref, *_: ref.at[:, first : first + count]


def call(body, outs, args, smem=(), after=(), room=8, flops=1):
    arrays, specs, scratch = [], [], []
    for arg in args:
        if isinstance(arg, tuple):
            arrays += [part[0] for part in arg[1]]
            specs += [pl.BlockSpec(memory_space=pltpu.HBM) for _ in arg[1]]
            scratch.append(pltpu.VMEM(arg[0], arg[1][0][0].dtype))
        else:
            arrays.append(arg)
            specs.append(pl.BlockSpec(memory_space=pltpu.VMEM))
    copies = sum(len(arg[1]) for arg in args if isinstance(arg, tuple))
    held = len(scratch)
    if copies:
        scratch.append(pltpu.SemaphoreType.DMA((copies,)))

    def kernel(*refs):
        scalars, refs = refs[: len(smem)], list(refs[len(smem) :])
        ins, refs = refs[: len(arrays)], refs[len(arrays) + len(after) :]
        results, slots = refs[: len(outs)], refs[len(outs) :]
        given, started, slot = [], [], 0
        for arg in args:
            if not isinstance(arg, tuple):
                given.append(ins.pop(0))
                continue
            for _, source, target in arg[1]:
                copy = pltpu.make_async_copy(
                    source(ins.pop(0), *scalars),
                    target(slots[slot], *scalars),
                    slots[held].at[len(started)],
                )
                copy.start()
                started.append(copy)
            given.append(slots[slot])
            slot += 1
        for copy in started:
            copy.wait()
        body(*scalars, *given, *results)

    moved = sum(a.size * a.dtype.itemsize for a in arrays)
    moved += sum(math.prod(s) * jnp.dtype(t).itemsize for s, t in outs)
    return pl.pallas_call(
        kernel,
        out_shape=[jax.ShapeDtypeStruct(s, t) for s, t in outs],
        in_specs=[pl.BlockSpec(memory_space=pltpu.SMEM) for _ in smem]
        + specs
        + [pl.BlockSpec(memory_space=pl.ANY) for _ in after],
        out_specs=[pl.BlockSpec(memory_space=pltpu.VMEM) for _ in outs],
        scratch_shapes=scratch,
        compiler_params=pltpu.CompilerParams(vmem_limit_bytes=room * MIB),
        cost_estimate=pl.CostEstimate(
            flops=int(flops), bytes_accessed=int(moved), transcendentals=0
        ),
    )(*smem, *arrays, *after)


def hold(arrays, after):
    held = len(arrays)
    return pl.pallas_call(
        lambda *refs: None,
        out_shape=[jax.ShapeDtypeStruct(a.shape, a.dtype) for a in arrays],
        in_specs=[pl.BlockSpec(memory_space=pl.ANY) for _ in (*arrays, *after)],
        out_specs=[pl.BlockSpec(memory_space=pl.ANY) for _ in arrays],
        input_output_aliases={n: n for n in range(held)},
        cost_estimate=pl.CostEstimate(flops=1, bytes_accessed=1, transcendentals=0),
    )(*arrays, *after)


def lower_triangle(blk):
    return lax.broadcasted_iota(jnp.int32, (blk, blk), 0) >= lax.broadcasted_iota(
        jnp.int32, (blk, blk), 1
    )


def forward_kernel(
    scale,
    mask,
    where,
    q_ref,
    k_ref,
    v_ref,
    probs_ref,
    inner_ref,
    soft_ref,
    mine_ref,
    other_ref,
    far_ref,
    mine_state_ref,
    other_state_ref,
):
    heads = [slice(h * DH, (h + 1) * DH) for h in range(2)]
    states = [dot(k_ref[:, cols], v_ref[:, cols], TN) for cols in heads]
    mine_state_ref[...], other_state_ref[...] = pick(where[2], states)
    rows, width = q_ref.shape
    count = mask.shape[0]
    blk = rows // count
    inv_root = 1.0 / math.sqrt(DH)
    triangle = lower_triangle(blk)
    for i in range(count):
        here = slice(i * blk, (i + 1) * blk)
        upto = slice(0, (i + 1) * blk)
        sums = []
        for h in range(2):
            cols = slice(h * DH, (h + 1) * DH)
            raw = dot(q_ref[here, cols], k_ref[upto, cols], NT)
            scores, inner = [], []
            for j in range(i + 1):
                part = raw[:, j * blk : (j + 1) * blk]
                keep = triangle if j == i else mask[i, j] > 0
                scores.append(jnp.where(keep, part * inv_root, -1e30))
                inner.append(jnp.where(triangle, part, 0.0) if j == i else part)
            scores = jnp.concatenate(scores, 1)
            inner = jnp.concatenate(inner, 1).astype(BF16)
            expo = jnp.exp(scores - jnp.max(scores, -1, keepdims=True))
            probs = (expo / jnp.sum(expo, -1, keepdims=True)).astype(BF16)
            v = v_ref[upto, cols]
            soft = dot(probs, v, NN)
            probs_ref[h, here, upto] = probs
            inner_ref[h, here, upto] = inner
            soft_ref[here, cols] = soft
            sums.append(soft + scale * dot(inner, v, NN))
        mine_ref[here], other_ref[here] = pick(where[2], sums)
    far_ref[...] = q_ref[:, pl.ds(pl.multiple_of((1 - where[2]) * DH, DH), DH)]


def pick(core, parts):
    return jnp.where(core == 0, parts[0], parts[1]), jnp.where(core == 0, parts[1], parts[0])


def both_heads(core, mine_ref, other_ref):
    mine, other = mine_ref[...], other_ref[...]
    return jnp.where(core == 0, mine, other), jnp.where(core == 0, other, mine)


def carry(flags, here_ref, got_ref, totals):
    carried = jnp.zeros(here_ref.shape, F32)
    for n, total in enumerate(totals):
        carried = carried + jnp.where(flags[n] > 0, total[...], 0.0)
    counts = flags[len(totals)] > 0
    keep = carried + jnp.where(counts, got_ref[...], 0.0)
    return keep, carried + jnp.where(counts, 0.0, here_ref[...])


def carry_kernel(flags, here_ref, got_ref, *refs):
    totals, (keep_ref, back_ref) = refs[:-2], refs[-2:]
    keep_ref[...], back_ref[...] = carry(flags, here_ref, got_ref, totals)


def attn_kernel(scale, count, flags, where, here_ref, got_ref, *refs):
    totals, refs = refs[: -count - 6], refs[-count - 6 :]
    q_ref, far_ref, pre_ref, far_pre_ref = refs[:4]
    out_refs, (keep_ref, back_ref) = refs[4:-2], refs[-2:]
    keep, back = carry(flags, here_ref, got_ref, totals)
    keep_ref[...], back_ref[...] = keep, back
    own = pre_ref.shape[0] // count
    cols = pl.ds(pl.multiple_of(where[2] * DH, DH), DH)
    for s, out_ref in enumerate(out_refs):
        block = lax.rem(where[0] + s, count)
        here = pl.ds(pl.multiple_of(block * own, own), own)
        mine = pre_ref[here] + scale * dot_wide(q_ref[here, cols], keep, NN)
        mate = far_pre_ref[here] + scale * dot_wide(far_ref[here], back, NN)
        out_ref[:own] = mine.astype(BF16)
        out_ref[own:] = mate.astype(BF16)


def first_kernel(spots, left_ref, weight_ref, right_ref, own_ref, half_ref):
    own_ref[...] = dot(left_ref[...], weight_ref[...], NT).astype(BF16)
    near = left_ref[:, pl.ds(pl.multiple_of(spots[0], DH), right_ref.shape[1])]
    half_ref[...] = dot(near, right_ref[...], NT)


def second_kernel(spots, left_ref, right_ref, half_ref, piece_ref, one_ref, three_ref, *cut_refs):
    wide = cut_refs[0].shape[1]
    for n, cut_ref in enumerate(cut_refs):
        cut_ref[...] = piece_ref[:, n * wide : (n + 1) * wide]
    total = (half_ref[...] + dot(left_ref[...], right_ref[...], NT)).astype(BF16)
    one_ref[...], three_ref[...] = total[:, :DH], total[:, DH:]


def last_kernel(spots, left_ref, right_ref, half_ref, out_ref):
    out_ref[...] = (half_ref[...] + dot(left_ref[...], right_ref[...], NT)).astype(BF16)


def near_kernel(spots, left_ref, right_ref, *refs):
    attn, (half_ref, own_out, mate_out) = refs[:-3], refs[-3:]
    half_ref[...] = dot(left_ref[...], right_ref[2 * DH : 3 * DH], NT)
    far_kernel(spots, right_ref, *attn, own_out, mate_out)


def far_kernel(spots, right_ref, *refs):
    attn, (own_out, mate_out) = refs[:-2], refs[-2:]
    own = own_out.shape[0]
    part = dot(jnp.concatenate([a[...] for a in attn], 1), right_ref[...], NN)
    own_out[...] = part[:own]
    mate_out[...] = part[own:]


def grad_kernel(whole, added, places, mine_ref, mate_ref, *refs):
    chunks, out_ref = refs[added:-1], refs[-1]
    total = refs[0][...] if added else None
    for j, chunk in enumerate(chunks):
        cols = slice(None) if whole else pl.ds(pl.multiple_of(places[j], DH), chunk.shape[1])
        left = jnp.concatenate([mine_ref[:, cols], mate_ref[:, cols]], 0)
        part = dot(left, chunk[...], NT)
        total = part if total is None else total + part
    out_ref[...] = total.astype(out_ref.dtype)


def mixed_kernel(count, each, places, *refs):
    attn, weight = refs[:count], refs[count]
    chunks, (own_out, mate_out) = list(refs[count + 1 : -2]), refs[-2:]
    own = own_out.shape[0]
    left = jnp.concatenate([a[...] for a in attn], 1)
    right = [weight[:, pl.ds(pl.multiple_of(places[0], DH), own_out.shape[1])]]
    for n in each:
        parts = [chunks.pop(0)[...] for _ in range(n)]
        right.append(jnp.concatenate(parts, 1) if n > 1 else parts[0])
    part = dot(left, jnp.concatenate(right, 0), NN)
    own_out[...] = part[:own]
    mate_out[...] = part[own:]


def join_kernel(places, *refs):
    out_ref, done_ref = refs[-2:]
    done_ref[...] = jnp.zeros(done_ref.shape, F32)
    for n in range(len(refs) // 2 - 1):
        wide = refs[2 * n].shape[1]
        there = pl.ds(pl.multiple_of(places[n], DH), wide)
        out_ref[:, there] = (refs[2 * n][...] + refs[2 * n + 1][...]).astype(BF16)


def collect_kernel(scale, count, where, q_ref, *refs):
    direct, across = refs[:count], refs[count : 2 * count]
    g_ref, mine_ref, other_ref = refs[2 * count :]
    own = g_ref.shape[0] // count
    mine = pl.ds(pl.multiple_of(where[2] * DH, DH), DH)
    mate = pl.ds(pl.multiple_of((1 - where[2]) * DH, DH), DH)
    for s in range(count):
        block = lax.rem(where[0] + s, count)
        here = pl.ds(pl.multiple_of(block * own, own), own)
        g_ref[here, mine] = direct[s][:own]
        g_ref[here, mate] = across[s][own:]
    heads = [slice(h * DH, (h + 1) * DH) for h in range(2)]
    parts = [scale * dot(q_ref[:, cols], g_ref[:, cols], TN) for cols in heads]
    mine_ref[...], other_ref[...] = pick(where[2], parts)


def backward_kernel(
    scale,
    count,
    where,
    q_ref,
    k_ref,
    v_ref,
    g_ref,
    probs_ref,
    inner_ref,
    soft_ref,
    mine_ref,
    other_ref,
    dq_ref,
    dk_ref,
    dv_ref,
):
    rows, width = q_ref.shape
    blk = rows // count
    inv_root = 1.0 / math.sqrt(DH)
    triangle = lower_triangle(blk)
    states = both_heads(where[2], mine_ref, other_ref)
    for h in range(width // DH):
        cols = slice(h * DH, (h + 1) * DH)
        for i in reversed(range(count)):
            here = slice(i * blk, (i + 1) * blk)
            upto = slice(0, (i + 1) * blk)
            q, g = q_ref[here, cols], g_ref[here, cols]
            k = k_ref[upto, cols]
            probs = probs_ref[h, here, upto]
            dprod = dot(g, v_ref[upto, cols], NT)
            delta = jnp.sum(g.astype(F32) * soft_ref[here, cols], -1, keepdims=True)
            dscore = (probs.astype(F32) * (dprod - delta) * inv_root).astype(BF16)
            last = jnp.where(triangle, dprod[:, i * blk :], 0.0)
            dinner = jnp.concatenate([dprod[:, : i * blk], last], 1) if i else last
            dinner = dinner.astype(BF16)
            dq_ref[here, cols] = (
                dot(dscore, k, NN)
                + scale * (dot(dinner, k, NN) + dot_wide(g, states[h], NT))
            ).astype(BF16)
            dk = dot(dscore, q, TN) + scale * dot(dinner, q, TN)
            dv = dot(probs, g, TN) + scale * dot(inner_ref[h, here, upto], g, TN)
            if i == count - 1:
                dk_ref[upto, cols] = dk
                dv_ref[upto, cols] = dv
            else:
                dk_ref[upto, cols] += dk
                dv_ref[upto, cols] += dv


def close_kernel(where, k_ref, v_ref, dk_ref, dv_ref, mine_ref, other_ref, gk_ref, gv_ref):
    states = both_heads(where[2], mine_ref, other_ref)
    for h in range(k_ref.shape[1] // DH):
        cols = slice(h * DH, (h + 1) * DH)
        state = states[h]
        gk_ref[:, cols] = (dk_ref[:, cols] + dot_wide(v_ref[:, cols], state, NT)).astype(BF16)
        gv_ref[:, cols] = (dv_ref[:, cols] + dot_wide(k_ref[:, cols], state, NN)).astype(BF16)


def send(x, flip, shift):
    shards, heads = lax.axis_size("ctx"), lax.axis_size("head")
    pairs = [
        (c * heads + z, (c ^ flip) * heads + (z + shift) % heads)
        for c in range(shards)
        for z in range(heads)
    ]
    return lax.ppermute(x, ("ctx", "head"), pairs)


def exchange(mine, other, core, chip, chips, later):
    got = send(other, 1, 0)
    own = total = mine + got
    totals, flags = [], []
    if chips == 4:
        for flip in (1, 2, 3):
            totals.append(send(total, 2 * flip, 0))
            flags.append(((chip ^ flip) > chip) == later)
    else:
        step = 1
        while step < chips:
            totals.append(send(total, 2 * step, 0))
            flags.append(((chip & step) == 0) == later)
            total = total + totals[-1]
            step *= 2
    flags.append((core == 0) == later)
    return jnp.stack(flags).astype(jnp.int32), [mine, got, *totals], own


def on_device(query, key, value, block_mask, out_weight, cotangent):
    rows, width = query.shape
    heads = width // DH
    shards, count = lax.axis_size("ctx"), lax.axis_size("head")
    model = out_weight.shape[1]
    own = rows // count
    scale = 1.0 / math.sqrt(DH * rows * shards)
    blocks = block_mask.shape[0]
    ctx, place = lax.axis_index("ctx"), lax.axis_index("head")
    core, chip, chips = ctx & 1, ctx >> 1, shards // 2
    where = jnp.stack([place, ctx, core])
    flat, square = (rows, width), rows * rows * DH * heads
    pair = [((DH, DH), F32)] * 2
    tokens = ((2 * own, DH), BF16)
    product = 4 * own * DH * model

    board = chips == 4 and count == 4
    wide = model // (2 if board else chips)
    colour = (chip & 1) ^ (chip >> 1) if board else chip
    piece = lax.dynamic_slice(out_weight, (core * DH, colour * wide), (DH, wide))
    arrived = {1: send(piece, 0, 1), count - 1: send(piece, 0, -1)}
    mate_cotangent = send(cotangent, 1, 0)

    probs, inner, soft, pre, other_pre, far, mine, other = call(
        functools.partial(forward_kernel, scale),
        [((heads, rows, rows), BF16)] * 2
        + [(flat, F32)]
        + [((rows, DH), F32)] * 2
        + [((rows, DH), BF16)]
        + pair,
        [query, key, value],
        [block_mask, where],
        [mate_cotangent],
        flops=7 * square,
    )
    flags, parts, total = exchange(mine, other, core, chip, chips, False)
    if board:
        arrived[1], arrived[3], parts[1] = hold([arrived[1], arrived[3], parts[1]], parts[2:])
    *attn, keep, back = call(
        functools.partial(attn_kernel, scale, count),
        [tokens] * count + pair,
        [*parts, query, send(far, 1, 0), pre, send(other_pre, 1, 0)],
        [flags, where],
    )
    linear = [keep, send(back, 1, 0)]
    attn = [attn[0]] + [send(attn[s], 0, s) for s in range(1, count)]

    work = near_and_far if board else by_gathers
    both, across, joins, starts = work(
        attn, arrived, cotangent, mate_cotangent, out_weight, core, chip, colour, product
    )
    mixed, done = call(
        join_kernel, [((own, model), BF16), ((8, DH), F32)], joins, [jnp.stack(starts)]
    )

    g, mine, other = call(
        functools.partial(collect_kernel, scale, count),
        [(flat, BF16), *pair],
        [query, *both, *across],
        [where],
    )
    flags, parts, total = exchange(mine, other, core, chip, chips, True)
    grad_query, dk, dv = call(
        functools.partial(backward_kernel, scale, blocks),
        [(flat, BF16)] + [(flat, F32)] * 2,
        [query, key, value, g, probs, inner, soft, *linear],
        [where],
        [total],
        flops=14 * square,
    )
    keep, back = call(carry_kernel, pair, parts, [flags], [dk])
    grad_key, grad_value = call(
        close_kernel,
        [(flat, BF16)] * 2,
        [key, value, dk, dv, keep, send(back, 1, 0)],
        [where],
        [done],
    )
    return mixed, grad_query, grad_key, grad_value


def near_and_far(attn, arrived, cotangent, mate_cotangent, weight, core, chip, colour, product):
    own, model = cotangent.shape
    wide = model // 2
    spots = jnp.stack([colour * wide, (1 - colour) * wide, core * DH])
    tokens = ((2 * own, DH), BF16)
    parts = [((own, wide), F32)] * 2
    all_arrays = [(cotangent, all_of, rows_at(0, own)), (mate_cotangent, all_of, rows_at(own, own))]
    whole = fetch((2 * own, model), *all_arrays)
    left = [
        fetch((2 * own, wide), *((a, columns(n, wide), put) for a, _, put in all_arrays))
        for n in range(2)
    ]

    def own_rows(ref, spots, *_):
        return ref.at[pl.ds(pl.multiple_of(spots[2], DH), DH)]

    def own_columns(n):
        return lambda ref, spots, *_: ref.at[
            pl.ds(pl.multiple_of(spots[2], DH), DH), pl.ds(pl.multiple_of(spots[n], DH), wide)
        ]

    def stacked(*arrays):
        return [(a, all_of, rows_at(n * DH, DH)) for n, a in enumerate(arrays)]

    arrived[2] = send(arrived[1], 0, 1)
    second = {1: send(arrived[1], 2, 0), 3: send(arrived[3], 4, 0)}
    mine, half = call(
        first_kernel,
        [tokens, ((2 * own, 2 * DH), F32)],
        [
            whole,
            fetch((DH, model), (weight, own_rows, all_of)),
            fetch((2 * DH, wide), *stacked(arrived[1], arrived[3])),
        ],
        [spots],
        room=24,
        flops=2 * product,
    )
    one, three, *cuts = call(
        second_kernel,
        [tokens] * 2 + [((DH, wide // 2), BF16)] * 2,
        [
            left[1],
            fetch((2 * DH, wide), *stacked(second[1], second[3])),
            half,
            fetch((DH, wide), (arrived[2], all_of, all_of)),
        ],
        [spots],
        attn[1:],
        room=16,
        flops=product,
    )
    second[2] = [send(cuts[0], 2, 0), send(cuts[1], 4, 0)]
    both = {0: mine, 1: send(one, 0, -1), 3: send(three, 0, -3)}
    across = {s: send(both[s], 1, 0) for s in (0, 1, 3)}
    half, part, mate_part = call(
        near_kernel,
        [((2 * own, DH), F32), *parts],
        [
            left[0],
            fetch(
                (4 * DH, wide),
                (weight, own_columns(0), rows_at(0, DH)),
                *((arrived[s], all_of, rows_at(s * DH, DH)) for s in (1, 2, 3)),
            ),
            *attn,
        ],
        [spots],
        room=24,
        flops=2 * product,
    )
    joins = [part, send(mate_part, 1, 0)]
    quarters = [(a, all_of, columns_at(n * wide // 2, wide // 2)) for n, a in enumerate(second[2])]
    (two,) = call(
        last_kernel,
        [tokens],
        [left[1], fetch((DH, wide), *quarters), half],
        [spots],
        [both[1], both[3]],
        room=16,
        flops=product // 2,
    )
    both[2] = send(two, 0, -2)

    def quarter(n):
        return lambda ref, *_: ref.at[2 * DH : 3 * DH, n * wide // 2 : (n + 1) * wide // 2]

    part, mate_part = call(
        far_kernel,
        parts,
        [
            fetch(
                (4 * DH, wide),
                (weight, own_columns(1), rows_at(0, DH)),
                (second[1], all_of, rows_at(DH, DH)),
                (second[3], all_of, rows_at(3 * DH, DH)),
                *((a, all_of, quarter(n)) for n, a in enumerate(second[2])),
            ),
            *attn,
        ],
        [spots],
        [both[2], across[0], across[1], across[3]],
        room=24,
        flops=2 * product,
    )
    joins += [part, send(mate_part, 1, 0)]
    across[2] = send(both[2], 1, 0)
    return [both[s] for s in range(4)], [across[s] for s in range(4)], joins, [spots[0], spots[1]]


def by_gathers(attn, arrived, cotangent, mate_cotangent, out_weight, core, chip, colour, product):
    own, model = cotangent.shape
    shards, count = lax.axis_size("ctx"), lax.axis_size("head")
    weight = lax.dynamic_slice_in_dim(out_weight, core * DH, DH, 0)
    zero = jnp.zeros((1,), jnp.int32)
    groups = [list(range(k, shards, 2)) for k in range(2)]
    for s in range(2, count - 1):
        arrived[s] = send(arrived[s - 1], 0, 1)
    chunks = [weight] + [
        lax.all_gather(arrived[s], "ctx", axis=1, tiled=True, axis_index_groups=groups)
        for s in range(1, count)
    ]
    both = []
    for s in range(count):
        (block,) = call(
            functools.partial(grad_kernel, True, 0),
            [((2 * own, DH), BF16)],
            [cotangent, mate_cotangent, chunks[s]],
            [zero],
            flops=product,
        )
        both.append(send(block, 0, -s) if s else block)
    part, mate_part = call(
        functools.partial(mixed_kernel, count, [1] * (count - 1)),
        [((own, model), F32)] * 2,
        [*attn, *chunks],
        [zero],
        room=16,
        flops=count * product,
    )
    return both, [send(b, 1, 0) for b in both], [part, send(mate_part, 1, 0)], [jnp.int32(0)]


def solution(mesh):
    return jax.shard_map(
        on_device,
        mesh=mesh,
        in_specs=(
            P("ctx", "head"),
            P("ctx", "head"),
            P("ctx", "head"),
            P("ctx", None),
            P("head", None),
            P(("ctx", "head"), None),
        ),
        out_specs=(P(("ctx", "head"), None), P("ctx", "head"), P("ctx", "head"), P("ctx", "head")),
        check_vma=False,
    )
```

```python
import functools
import math

import jax
import jax.numpy as jnp
from jax import lax
from jax.experimental import pallas as pl
from jax.experimental.pallas import tpu as pltpu
from jax.sharding import PartitionSpec as P

DH = 128
F32 = jnp.float32
BF16 = jnp.bfloat16
NN = ((1,), (0,))
NT = ((1,), (1,))
TN = ((0,), (0,))
MIB = 1 << 20


def dot(a, b, dims):
    return lax.dot_general(a, b, (dims, ((), ())), preferred_element_type=F32)


def dot_wide(a, b, dims):
    high = b.astype(BF16)
    low = (b - high.astype(F32)).astype(BF16)
    return dot(a, high, dims) + dot(a, low, dims)


def fetch(shape, *parts):
    return (shape, parts)


def all_of(ref, *_):
    return ref


def columns(spot, wide, rows=slice(None)):
    def view(ref, spots, *_):
        return ref.at[rows, pl.ds(pl.multiple_of(spots[spot], DH), wide)]

    return view


def rows_at(first, count):
    return lambda ref, *_: ref.at[first : first + count]


def columns_at(first, count):
    return lambda ref, *_: ref.at[:, first : first + count]


def call(body, outs, args, smem=(), after=(), room=8, flops=1):
    arrays, specs, scratch = [], [], []
    for arg in args:
        if isinstance(arg, tuple):
            arrays += [part[0] for part in arg[1]]
            specs += [pl.BlockSpec(memory_space=pltpu.HBM) for _ in arg[1]]
            scratch.append(pltpu.VMEM(arg[0], arg[1][0][0].dtype))
        else:
            arrays.append(arg)
            specs.append(pl.BlockSpec(memory_space=pltpu.VMEM))
    copies = sum(len(arg[1]) for arg in args if isinstance(arg, tuple))
    held = len(scratch)
    if copies:
        scratch.append(pltpu.SemaphoreType.DMA((copies,)))

    def kernel(*refs):
        scalars, refs = refs[: len(smem)], list(refs[len(smem) :])
        ins, refs = refs[: len(arrays)], refs[len(arrays) + len(after) :]
        results, slots = refs[: len(outs)], refs[len(outs) :]
        given, started, slot = [], [], 0
        for arg in args:
            if not isinstance(arg, tuple):
                given.append(ins.pop(0))
                continue
            for _, source, target in arg[1]:
                copy = pltpu.make_async_copy(
                    source(ins.pop(0), *scalars),
                    target(slots[slot], *scalars),
                    slots[held].at[len(started)],
                )
                copy.start()
                started.append(copy)
            given.append(slots[slot])
            slot += 1
        for copy in started:
            copy.wait()
        body(*scalars, *given, *results)

    moved = sum(a.size * a.dtype.itemsize for a in arrays)
    moved += sum(math.prod(s) * jnp.dtype(t).itemsize for s, t in outs)
    return pl.pallas_call(
        kernel,
        out_shape=[jax.ShapeDtypeStruct(s, t) for s, t in outs],
        in_specs=[pl.BlockSpec(memory_space=pltpu.SMEM) for _ in smem]
        + specs
        + [pl.BlockSpec(memory_space=pl.ANY) for _ in after],
        out_specs=[pl.BlockSpec(memory_space=pltpu.VMEM) for _ in outs],
        scratch_shapes=scratch,
        compiler_params=pltpu.CompilerParams(vmem_limit_bytes=room * MIB),
        cost_estimate=pl.CostEstimate(
            flops=int(flops), bytes_accessed=int(moved), transcendentals=0
        ),
    )(*smem, *arrays, *after)


def hold(arrays, after):
    held = len(arrays)
    return pl.pallas_call(
        lambda *refs: None,
        out_shape=[jax.ShapeDtypeStruct(a.shape, a.dtype) for a in arrays],
        in_specs=[pl.BlockSpec(memory_space=pl.ANY) for _ in (*arrays, *after)],
        out_specs=[pl.BlockSpec(memory_space=pl.ANY) for _ in arrays],
        input_output_aliases={n: n for n in range(held)},
        cost_estimate=pl.CostEstimate(flops=1, bytes_accessed=1, transcendentals=0),
    )(*arrays, *after)


def lower_triangle(blk):
    return lax.broadcasted_iota(jnp.int32, (blk, blk), 0) >= lax.broadcasted_iota(
        jnp.int32, (blk, blk), 1
    )


def forward_kernel(
    scale,
    mask,
    where,
    q_ref,
    k_ref,
    v_ref,
    probs_ref,
    inner_ref,
    soft_ref,
    mine_ref,
    other_ref,
    far_ref,
    mine_state_ref,
    other_state_ref,
):
    heads = [slice(h * DH, (h + 1) * DH) for h in range(2)]
    states = [dot(k_ref[:, cols], v_ref[:, cols], TN) for cols in heads]
    mine_state_ref[...], other_state_ref[...] = pick(where[2], states)
    rows, width = q_ref.shape
    count = mask.shape[0]
    blk = rows // count
    inv_root = 1.0 / math.sqrt(DH)
    triangle = lower_triangle(blk)
    for i in range(count):
        here = slice(i * blk, (i + 1) * blk)
        upto = slice(0, (i + 1) * blk)
        sums = []
        for h in range(2):
            cols = slice(h * DH, (h + 1) * DH)
            raw = dot(q_ref[here, cols], k_ref[upto, cols], NT)
            scores, inner = [], []
            for j in range(i + 1):
                part = raw[:, j * blk : (j + 1) * blk]
                keep = triangle if j == i else mask[i, j] > 0
                scores.append(jnp.where(keep, part * inv_root, -1e30))
                inner.append(jnp.where(triangle, part, 0.0) if j == i else part)
            scores = jnp.concatenate(scores, 1)
            inner = jnp.concatenate(inner, 1).astype(BF16)
            expo = jnp.exp(scores - jnp.max(scores, -1, keepdims=True))
            probs = (expo / jnp.sum(expo, -1, keepdims=True)).astype(BF16)
            v = v_ref[upto, cols]
            soft = dot(probs, v, NN)
            probs_ref[h, here, upto] = probs
            inner_ref[h, here, upto] = inner
            soft_ref[here, cols] = soft
            sums.append(soft + scale * dot(inner, v, NN))
        mine_ref[here], other_ref[here] = pick(where[2], sums)
    far_ref[...] = q_ref[:, pl.ds(pl.multiple_of((1 - where[2]) * DH, DH), DH)]


def pick(core, parts):
    return jnp.where(core == 0, parts[0], parts[1]), jnp.where(core == 0, parts[1], parts[0])


def both_heads(core, mine_ref, other_ref):
    mine, other = mine_ref[...], other_ref[...]
    return jnp.where(core == 0, mine, other), jnp.where(core == 0, other, mine)


def carry(flags, here_ref, got_ref, totals):
    carried = jnp.zeros(here_ref.shape, F32)
    for n, total in enumerate(totals):
        carried = carried + jnp.where(flags[n] > 0, total[...], 0.0)
    counts = flags[len(totals)] > 0
    keep = carried + jnp.where(counts, got_ref[...], 0.0)
    return keep, carried + jnp.where(counts, 0.0, here_ref[...])


def carry_kernel(flags, here_ref, got_ref, *refs):
    totals, (keep_ref, back_ref) = refs[:-2], refs[-2:]
    keep_ref[...], back_ref[...] = carry(flags, here_ref, got_ref, totals)


def attn_kernel(scale, count, flags, where, here_ref, got_ref, *refs):
    totals, refs = refs[: -count - 6], refs[-count - 6 :]
    q_ref, far_ref, pre_ref, far_pre_ref = refs[:4]
    out_refs, (keep_ref, back_ref) = refs[4:-2], refs[-2:]
    keep, back = carry(flags, here_ref, got_ref, totals)
    keep_ref[...], back_ref[...] = keep, back
    own = pre_ref.shape[0] // count
    cols = pl.ds(pl.multiple_of(where[2] * DH, DH), DH)
    for s, out_ref in enumerate(out_refs):
        block = lax.rem(where[0] + s, count)
        here = pl.ds(pl.multiple_of(block * own, own), own)
        mine = pre_ref[here] + scale * dot_wide(q_ref[here, cols], keep, NN)
        mate = far_pre_ref[here] + scale * dot_wide(far_ref[here], back, NN)
        out_ref[:own] = mine.astype(BF16)
        out_ref[own:] = mate.astype(BF16)


def first_kernel(spots, left_ref, weight_ref, right_ref, own_ref, half_ref):
    own_ref[...] = dot(left_ref[...], weight_ref[...], NT).astype(BF16)
    near = left_ref[:, pl.ds(pl.multiple_of(spots[0], DH), right_ref.shape[1])]
    half_ref[...] = dot(near, right_ref[...], NT)


def second_kernel(spots, left_ref, right_ref, half_ref, piece_ref, one_ref, three_ref, *cut_refs):
    wide = cut_refs[0].shape[1]
    for n, cut_ref in enumerate(cut_refs):
        cut_ref[...] = piece_ref[:, n * wide : (n + 1) * wide]
    total = (half_ref[...] + dot(left_ref[...], right_ref[...], NT)).astype(BF16)
    one_ref[...], three_ref[...] = total[:, :DH], total[:, DH:]


def last_kernel(spots, left_ref, right_ref, half_ref, out_ref):
    out_ref[...] = (half_ref[...] + dot(left_ref[...], right_ref[...], NT)).astype(BF16)


def near_kernel(spots, left_ref, right_ref, *refs):
    attn, (half_ref, own_out, mate_out) = refs[:-3], refs[-3:]
    half_ref[...] = dot(left_ref[...], right_ref[2 * DH : 3 * DH], NT)
    far_kernel(spots, right_ref, *attn, own_out, mate_out)


def far_kernel(spots, right_ref, *refs):
    attn, (own_out, mate_out) = refs[:-2], refs[-2:]
    own = own_out.shape[0]
    part = dot(jnp.concatenate([a[...] for a in attn], 1), right_ref[...], NN)
    own_out[...] = part[:own]
    mate_out[...] = part[own:]


def grad_kernel(whole, added, places, mine_ref, mate_ref, *refs):
    chunks, out_ref = refs[added:-1], refs[-1]
    total = refs[0][...] if added else None
    for j, chunk in enumerate(chunks):
        cols = slice(None) if whole else pl.ds(pl.multiple_of(places[j], DH), chunk.shape[1])
        left = jnp.concatenate([mine_ref[:, cols], mate_ref[:, cols]], 0)
        part = dot(left, chunk[...], NT)
        total = part if total is None else total + part
    out_ref[...] = total.astype(out_ref.dtype)


def mixed_kernel(count, each, places, *refs):
    attn, weight = refs[:count], refs[count]
    chunks, (own_out, mate_out) = list(refs[count + 1 : -2]), refs[-2:]
    own = own_out.shape[0]
    left = jnp.concatenate([a[...] for a in attn], 1)
    right = [weight[:, pl.ds(pl.multiple_of(places[0], DH), own_out.shape[1])]]
    for n in each:
        parts = [chunks.pop(0)[...] for _ in range(n)]
        right.append(jnp.concatenate(parts, 1) if n > 1 else parts[0])
    part = dot(left, jnp.concatenate(right, 0), NN)
    own_out[...] = part[:own]
    mate_out[...] = part[own:]


def join_kernel(places, *refs):
    out_ref, done_ref = refs[-2:]
    done_ref[...] = jnp.zeros(done_ref.shape, F32)
    for n in range(len(refs) // 2 - 1):
        wide = refs[2 * n].shape[1]
        there = pl.ds(pl.multiple_of(places[n], DH), wide)
        out_ref[:, there] = (refs[2 * n][...] + refs[2 * n + 1][...]).astype(BF16)


def collect_kernel(scale, count, where, q_ref, *refs):
    direct, across = refs[:count], refs[count : 2 * count]
    g_ref, mine_ref, other_ref = refs[2 * count :]
    own = g_ref.shape[0] // count
    mine = pl.ds(pl.multiple_of(where[2] * DH, DH), DH)
    mate = pl.ds(pl.multiple_of((1 - where[2]) * DH, DH), DH)
    for s in range(count):
        block = lax.rem(where[0] + s, count)
        here = pl.ds(pl.multiple_of(block * own, own), own)
        g_ref[here, mine] = direct[s][:own]
        g_ref[here, mate] = across[s][own:]
    heads = [slice(h * DH, (h + 1) * DH) for h in range(2)]
    parts = [scale * dot(q_ref[:, cols], g_ref[:, cols], TN) for cols in heads]
    mine_ref[...], other_ref[...] = pick(where[2], parts)


def backward_kernel(
    scale,
    count,
    where,
    q_ref,
    k_ref,
    v_ref,
    g_ref,
    probs_ref,
    inner_ref,
    soft_ref,
    mine_ref,
    other_ref,
    dq_ref,
    dk_ref,
    dv_ref,
):
    rows, width = q_ref.shape
    blk = rows // count
    inv_root = 1.0 / math.sqrt(DH)
    triangle = lower_triangle(blk)
    states = both_heads(where[2], mine_ref, other_ref)
    for h in range(width // DH):
        cols = slice(h * DH, (h + 1) * DH)
        for i in reversed(range(count)):
            here = slice(i * blk, (i + 1) * blk)
            upto = slice(0, (i + 1) * blk)
            q, g = q_ref[here, cols], g_ref[here, cols]
            k = k_ref[upto, cols]
            probs = probs_ref[h, here, upto]
            dprod = dot(g, v_ref[upto, cols], NT)
            delta = jnp.sum(g.astype(F32) * soft_ref[here, cols], -1, keepdims=True)
            dscore = (probs.astype(F32) * (dprod - delta) * inv_root).astype(BF16)
            last = jnp.where(triangle, dprod[:, i * blk :], 0.0)
            dinner = jnp.concatenate([dprod[:, : i * blk], last], 1) if i else last
            dinner = dinner.astype(BF16)
            dq_ref[here, cols] = (
                dot(dscore, k, NN)
                + scale * (dot(dinner, k, NN) + dot_wide(g, states[h], NT))
            ).astype(BF16)
            dk = dot(dscore, q, TN) + scale * dot(dinner, q, TN)
            dv = dot(probs, g, TN) + scale * dot(inner_ref[h, here, upto], g, TN)
            if i == count - 1:
                dk_ref[upto, cols] = dk
                dv_ref[upto, cols] = dv
            else:
                dk_ref[upto, cols] += dk
                dv_ref[upto, cols] += dv


def close_kernel(where, k_ref, v_ref, dk_ref, dv_ref, mine_ref, other_ref, gk_ref, gv_ref):
    states = both_heads(where[2], mine_ref, other_ref)
    for h in range(k_ref.shape[1] // DH):
        cols = slice(h * DH, (h + 1) * DH)
        state = states[h]
        gk_ref[:, cols] = (dk_ref[:, cols] + dot_wide(v_ref[:, cols], state, NT)).astype(BF16)
        gv_ref[:, cols] = (dv_ref[:, cols] + dot_wide(k_ref[:, cols], state, NN)).astype(BF16)


def send(x, flip, shift):
    shards, heads = lax.axis_size("ctx"), lax.axis_size("head")
    pairs = [
        (c * heads + z, (c ^ flip) * heads + (z + shift) % heads)
        for c in range(shards)
        for z in range(heads)
    ]
    return lax.ppermute(x, ("ctx", "head"), pairs)


def exchange(mine, other, core, chip, chips, later):
    got = send(other, 1, 0)
    own = total = mine + got
    totals, flags = [], []
    if chips == 4:
        for flip in (1, 2, 3):
            totals.append(send(total, 2 * flip, 0))
            flags.append(((chip ^ flip) > chip) == later)
    else:
        step = 1
        while step < chips:
            totals.append(send(total, 2 * step, 0))
            flags.append(((chip & step) == 0) == later)
            total = total + totals[-1]
            step *= 2
    flags.append((core == 0) == later)
    return jnp.stack(flags).astype(jnp.int32), [mine, got, *totals], own


def on_device(query, key, value, block_mask, out_weight, cotangent):
    rows, width = query.shape
    heads = width // DH
    shards, count = lax.axis_size("ctx"), lax.axis_size("head")
    model = out_weight.shape[1]
    own = rows // count
    scale = 1.0 / math.sqrt(DH * rows * shards)
    blocks = block_mask.shape[0]
    ctx, place = lax.axis_index("ctx"), lax.axis_index("head")
    core, chip, chips = ctx & 1, ctx >> 1, shards // 2
    where = jnp.stack([place, ctx, core])
    flat, square = (rows, width), rows * rows * DH * heads
    pair = [((DH, DH), F32)] * 2
    tokens = ((2 * own, DH), BF16)
    product = 4 * own * DH * model

    board = chips == 4 and count == 4
    wide = model // (2 if board else chips)
    colour = (chip & 1) ^ (chip >> 1) if board else chip
    piece = lax.dynamic_slice(out_weight, (core * DH, colour * wide), (DH, wide))
    arrived = {1: send(piece, 0, 1), count - 1: send(piece, 0, -1)}
    mate_cotangent = send(cotangent, 1, 0)

    probs, inner, soft, pre, other_pre, far, mine, other = call(
        functools.partial(forward_kernel, scale),
        [((heads, rows, rows), BF16)] * 2
        + [(flat, F32)]
        + [((rows, DH), F32)] * 2
        + [((rows, DH), BF16)]
        + pair,
        [query, key, value],
        [block_mask, where],
        [mate_cotangent],
        flops=7 * square,
    )
    far, other_pre = send(far, 1, 0), send(other_pre, 1, 0)
    (mine,) = hold([mine], [far, other_pre])
    flags, parts, total = exchange(mine, other, core, chip, chips, False)
    *attn, keep, back = call(
        functools.partial(attn_kernel, scale, count),
        [tokens] * count + pair,
        [*parts, query, far, pre, other_pre],
        [flags, where],
    )
    linear = [keep, send(back, 1, 0)]
    attn = [attn[0]] + [send(attn[s], 0, s) for s in range(1, count)]

    work = near_and_far if board else by_gathers
    both, across, joins, starts = work(
        attn, arrived, cotangent, mate_cotangent, out_weight, core, chip, colour, product
    )
    mixed, done = call(
        join_kernel, [((own, model), BF16), ((8, DH), F32)], joins, [jnp.stack(starts)]
    )

    g, mine, other = call(
        functools.partial(collect_kernel, scale, count),
        [(flat, BF16), *pair],
        [query, *both, *across],
        [where],
    )
    flags, parts, total = exchange(mine, other, core, chip, chips, True)
    grad_query, dk, dv = call(
        functools.partial(backward_kernel, scale, blocks),
        [(flat, BF16)] + [(flat, F32)] * 2,
        [query, key, value, g, probs, inner, soft, *linear],
        [where],
        [total],
        flops=14 * square,
    )
    keep, back = call(carry_kernel, pair, parts, [flags], [dk])
    grad_key, grad_value = call(
        close_kernel,
        [(flat, BF16)] * 2,
        [key, value, dk, dv, keep, send(back, 1, 0)],
        [where],
        [done],
    )
    return mixed, grad_query, grad_key, grad_value


def near_and_far(attn, arrived, cotangent, mate_cotangent, weight, core, chip, colour, product):
    own, model = cotangent.shape
    wide = model // 2
    spots = jnp.stack([colour * wide, (1 - colour) * wide, core * DH])
    tokens = ((2 * own, DH), BF16)
    parts = [((own, wide), F32)] * 2
    all_arrays = [(cotangent, all_of, rows_at(0, own)), (mate_cotangent, all_of, rows_at(own, own))]
    whole = fetch((2 * own, model), *all_arrays)
    left = [
        fetch((2 * own, wide), *((a, columns(n, wide), put) for a, _, put in all_arrays))
        for n in range(2)
    ]

    def own_rows(ref, spots, *_):
        return ref.at[pl.ds(pl.multiple_of(spots[2], DH), DH)]

    def own_columns(n):
        return lambda ref, spots, *_: ref.at[
            pl.ds(pl.multiple_of(spots[2], DH), DH), pl.ds(pl.multiple_of(spots[n], DH), wide)
        ]

    def stacked(*arrays):
        return [(a, all_of, rows_at(n * DH, DH)) for n, a in enumerate(arrays)]

    arrived[1], arrived[3] = hold([arrived[1], arrived[3]], attn[:1])
    arrived[2] = send(arrived[1], 0, 1)
    second = {1: send(arrived[1], 2, 0), 3: send(arrived[3], 4, 0)}
    mine, half = call(
        first_kernel,
        [tokens, ((2 * own, 2 * DH), F32)],
        [
            whole,
            fetch((DH, model), (weight, own_rows, all_of)),
            fetch((2 * DH, wide), *stacked(arrived[1], arrived[3])),
        ],
        [spots],
        room=24,
        flops=2 * product,
    )
    one, three, *cuts = call(
        second_kernel,
        [tokens] * 2 + [((DH, wide // 2), BF16)] * 2,
        [
            left[1],
            fetch((2 * DH, wide), *stacked(second[1], second[3])),
            half,
            fetch((DH, wide), (arrived[2], all_of, all_of)),
        ],
        [spots],
        room=16,
        flops=product,
    )
    second[2] = [send(cuts[0], 2, 0), send(cuts[1], 4, 0)]
    both = {0: mine, 1: send(one, 0, -1), 3: send(three, 0, -3)}
    across = {s: send(both[s], 1, 0) for s in (0, 1, 3)}
    half, part, mate_part = call(
        near_kernel,
        [((2 * own, DH), F32), *parts],
        [
            left[0],
            fetch(
                (4 * DH, wide),
                (weight, own_columns(0), rows_at(0, DH)),
                *((arrived[s], all_of, rows_at(s * DH, DH)) for s in (1, 2, 3)),
            ),
            *attn,
        ],
        [spots],
        room=24,
        flops=2 * product,
    )
    joins = [part, send(mate_part, 1, 0)]
    quarters = [(a, all_of, columns_at(n * wide // 2, wide // 2)) for n, a in enumerate(second[2])]
    (two,) = call(
        last_kernel,
        [tokens],
        [left[1], fetch((DH, wide), *quarters), half],
        [spots],
        [both[1], both[3]],
        room=16,
        flops=product // 2,
    )
    both[2] = send(two, 0, -2)

    def quarter(n):
        return lambda ref, *_: ref.at[2 * DH : 3 * DH, n * wide // 2 : (n + 1) * wide // 2]

    part, mate_part = call(
        far_kernel,
        parts,
        [
            fetch(
                (4 * DH, wide),
                (weight, own_columns(1), rows_at(0, DH)),
                (second[1], all_of, rows_at(DH, DH)),
                (second[3], all_of, rows_at(3 * DH, DH)),
                *((a, all_of, quarter(n)) for n, a in enumerate(second[2])),
            ),
            *attn,
        ],
        [spots],
        [both[2], across[0], across[1], across[3]],
        room=24,
        flops=2 * product,
    )
    joins += [part, send(mate_part, 1, 0)]
    across[2] = send(both[2], 1, 0)
    return [both[s] for s in range(4)], [across[s] for s in range(4)], joins, [spots[0], spots[1]]


def by_gathers(attn, arrived, cotangent, mate_cotangent, out_weight, core, chip, colour, product):
    own, model = cotangent.shape
    shards, count = lax.axis_size("ctx"), lax.axis_size("head")
    weight = lax.dynamic_slice_in_dim(out_weight, core * DH, DH, 0)
    zero = jnp.zeros((1,), jnp.int32)
    groups = [list(range(k, shards, 2)) for k in range(2)]
    for s in range(2, count - 1):
        arrived[s] = send(arrived[s - 1], 0, 1)
    chunks = [weight] + [
        lax.all_gather(arrived[s], "ctx", axis=1, tiled=True, axis_index_groups=groups)
        for s in range(1, count)
    ]
    both = []
    for s in range(count):
        (block,) = call(
            functools.partial(grad_kernel, True, 0),
            [((2 * own, DH), BF16)],
            [cotangent, mate_cotangent, chunks[s]],
            [zero],
            flops=product,
        )
        both.append(send(block, 0, -s) if s else block)
    part, mate_part = call(
        functools.partial(mixed_kernel, count, [1] * (count - 1)),
        [((own, model), F32)] * 2,
        [*attn, *chunks],
        [zero],
        room=16,
        flops=count * product,
    )
    return both, [send(b, 1, 0) for b in both], [part, send(mate_part, 1, 0)], [jnp.int32(0)]


def solution(mesh):
    return jax.shard_map(
        on_device,
        mesh=mesh,
        in_specs=(
            P("ctx", "head"),
            P("ctx", "head"),
            P("ctx", "head"),
            P("ctx", None),
            P("head", None),
            P(("ctx", "head"), None),
        ),
        out_specs=(P(("ctx", "head"), None), P("ctx", "head"), P("ctx", "head"), P("ctx", "head")),
        check_vma=False,
    )
```

```python
import functools
import math

import jax
import jax.numpy as jnp
from jax import lax
from jax.experimental import pallas as pl
from jax.experimental.pallas import tpu as pltpu
from jax.sharding import PartitionSpec as P

DH = 128
F32 = jnp.float32
BF16 = jnp.bfloat16
NN = ((1,), (0,))
NT = ((1,), (1,))
TN = ((0,), (0,))
MIB = 1 << 20


def dot(a, b, dims):
    return lax.dot_general(a, b, (dims, ((), ())), preferred_element_type=F32)


def dot_wide(a, b, dims):
    high = b.astype(BF16)
    low = (b - high.astype(F32)).astype(BF16)
    return dot(a, high, dims) + dot(a, low, dims)


def fetch(shape, *parts):
    return (shape, parts)


def all_of(ref, *_):
    return ref


def columns(spot, wide, rows=slice(None)):
    def view(ref, spots, *_):
        return ref.at[rows, pl.ds(pl.multiple_of(spots[spot], DH), wide)]

    return view


def rows_at(first, count):
    return lambda ref, *_: ref.at[first : first + count]


def columns_at(first, count):
    return lambda ref, *_: ref.at[:, first : first + count]


def call(body, outs, args, smem=(), after=(), room=2, flops=1):
    arrays, specs, scratch = [], [], []
    for arg in args:
        if isinstance(arg, tuple):
            arrays += [part[0] for part in arg[1]]
            specs += [pl.BlockSpec(memory_space=pltpu.HBM) for _ in arg[1]]
            scratch.append(pltpu.VMEM(arg[0], arg[1][0][0].dtype))
        else:
            arrays.append(arg)
            specs.append(pl.BlockSpec(memory_space=pltpu.VMEM))
    copies = sum(len(arg[1]) for arg in args if isinstance(arg, tuple))
    held = len(scratch)
    if copies:
        scratch.append(pltpu.SemaphoreType.DMA((copies,)))

    def kernel(*refs):
        scalars, refs = refs[: len(smem)], list(refs[len(smem) :])
        ins, refs = refs[: len(arrays)], refs[len(arrays) + len(after) :]
        results, slots = refs[: len(outs)], refs[len(outs) :]
        given, started, slot = [], [], 0
        for arg in args:
            if not isinstance(arg, tuple):
                given.append(ins.pop(0))
                continue
            for _, source, target in arg[1]:
                copy = pltpu.make_async_copy(
                    source(ins.pop(0), *scalars),
                    target(slots[slot], *scalars),
                    slots[held].at[len(started)],
                )
                copy.start()
                started.append(copy)
            given.append(slots[slot])
            slot += 1
        for copy in started:
            copy.wait()
        body(*scalars, *given, *results)

    moved = sum(a.size * a.dtype.itemsize for a in arrays)
    moved += sum(math.prod(s) * jnp.dtype(t).itemsize for s, t in outs)
    return pl.pallas_call(
        kernel,
        out_shape=[jax.ShapeDtypeStruct(s, t) for s, t in outs],
        in_specs=[pl.BlockSpec(memory_space=pltpu.SMEM) for _ in smem]
        + specs
        + [pl.BlockSpec(memory_space=pl.ANY) for _ in after],
        out_specs=[pl.BlockSpec(memory_space=pltpu.VMEM) for _ in outs],
        scratch_shapes=scratch,
        compiler_params=pltpu.CompilerParams(vmem_limit_bytes=room * MIB),
        cost_estimate=pl.CostEstimate(
            flops=int(flops), bytes_accessed=int(moved), transcendentals=0
        ),
    )(*smem, *arrays, *after)


def hold(arrays, after):
    held = len(arrays)
    return pl.pallas_call(
        lambda *refs: None,
        out_shape=[jax.ShapeDtypeStruct(a.shape, a.dtype) for a in arrays],
        in_specs=[pl.BlockSpec(memory_space=pl.ANY) for _ in (*arrays, *after)],
        out_specs=[pl.BlockSpec(memory_space=pl.ANY) for _ in arrays],
        input_output_aliases={n: n for n in range(held)},
        cost_estimate=pl.CostEstimate(flops=1, bytes_accessed=1, transcendentals=0),
    )(*arrays, *after)


def lower_triangle(blk):
    return lax.broadcasted_iota(jnp.int32, (blk, blk), 0) >= lax.broadcasted_iota(
        jnp.int32, (blk, blk), 1
    )


def forward_kernel(
    scale,
    mask,
    where,
    q_ref,
    k_ref,
    v_ref,
    probs_ref,
    inner_ref,
    soft_ref,
    mine_ref,
    other_ref,
    far_ref,
    mine_state_ref,
    other_state_ref,
):
    heads = [slice(h * DH, (h + 1) * DH) for h in range(2)]
    states = [dot(k_ref[:, cols], v_ref[:, cols], TN) for cols in heads]
    mine_state_ref[...], other_state_ref[...] = pick(where[2], states)
    rows, width = q_ref.shape
    count = mask.shape[0]
    blk = rows // count
    inv_root = 1.0 / math.sqrt(DH)
    triangle = lower_triangle(blk)
    for i in range(count):
        here = slice(i * blk, (i + 1) * blk)
        upto = slice(0, (i + 1) * blk)
        sums = []
        for h in range(2):
            cols = slice(h * DH, (h + 1) * DH)
            raw = dot(q_ref[here, cols], k_ref[upto, cols], NT)
            scores, inner = [], []
            for j in range(i + 1):
                part = raw[:, j * blk : (j + 1) * blk]
                keep = triangle if j == i else mask[i, j] > 0
                scores.append(jnp.where(keep, part * inv_root, -1e30))
                inner.append(jnp.where(triangle, part, 0.0) if j == i else part)
            scores = jnp.concatenate(scores, 1)
            inner = jnp.concatenate(inner, 1).astype(BF16)
            expo = jnp.exp(scores - jnp.max(scores, -1, keepdims=True))
            probs = (expo / jnp.sum(expo, -1, keepdims=True)).astype(BF16)
            v = v_ref[upto, cols]
            soft = dot(probs, v, NN)
            probs_ref[h, here, upto] = probs
            inner_ref[h, here, upto] = inner
            soft_ref[here, cols] = soft
            sums.append(soft + scale * dot(inner, v, NN))
        mine_ref[here], other_ref[here] = pick(where[2], sums)
    far_ref[...] = q_ref[:, pl.ds(pl.multiple_of((1 - where[2]) * DH, DH), DH)]


def pick(core, parts):
    return jnp.where(core == 0, parts[0], parts[1]), jnp.where(core == 0, parts[1], parts[0])


def both_heads(core, mine_ref, other_ref):
    mine, other = mine_ref[...], other_ref[...]
    return jnp.where(core == 0, mine, other), jnp.where(core == 0, other, mine)


def carry(flags, here_ref, got_ref, totals):
    carried = jnp.zeros(here_ref.shape, F32)
    for n, total in enumerate(totals):
        carried = carried + jnp.where(flags[n] > 0, total[...], 0.0)
    counts = flags[len(totals)] > 0
    keep = carried + jnp.where(counts, got_ref[...], 0.0)
    return keep, carried + jnp.where(counts, 0.0, here_ref[...])


def carry_kernel(flags, here_ref, got_ref, *refs):
    totals, (keep_ref, back_ref) = refs[:-2], refs[-2:]
    keep_ref[...], back_ref[...] = carry(flags, here_ref, got_ref, totals)


def attn_kernel(scale, count, flags, where, here_ref, got_ref, *refs):
    totals, refs = refs[: -count - 6], refs[-count - 6 :]
    q_ref, far_ref, pre_ref, far_pre_ref = refs[:4]
    out_refs, (keep_ref, back_ref) = refs[4:-2], refs[-2:]
    keep, back = carry(flags, here_ref, got_ref, totals)
    keep_ref[...], back_ref[...] = keep, back
    own = pre_ref.shape[0] // count
    cols = pl.ds(pl.multiple_of(where[2] * DH, DH), DH)
    for s, out_ref in enumerate(out_refs):
        block = lax.rem(where[0] + s, count)
        here = pl.ds(pl.multiple_of(block * own, own), own)
        mine = pre_ref[here] + scale * dot_wide(q_ref[here, cols], keep, NN)
        mate = far_pre_ref[here] + scale * dot_wide(far_ref[here], back, NN)
        out_ref[:own] = mine.astype(BF16)
        out_ref[own:] = mate.astype(BF16)


def first_kernel(spots, left_ref, weight_ref, right_ref, own_ref, half_ref):
    own_ref[...] = dot(left_ref[...], weight_ref[...], NT).astype(BF16)
    near = left_ref[:, pl.ds(pl.multiple_of(spots[0], DH), right_ref.shape[1])]
    half_ref[...] = dot(near, right_ref[...], NT)


def second_kernel(spots, left_ref, right_ref, half_ref, piece_ref, one_ref, three_ref, *cut_refs):
    wide = cut_refs[0].shape[1]
    for n, cut_ref in enumerate(cut_refs):
        cut_ref[...] = piece_ref[:, n * wide : (n + 1) * wide]
    total = (half_ref[...] + dot(left_ref[...], right_ref[...], NT)).astype(BF16)
    one_ref[...], three_ref[...] = total[:, :DH], total[:, DH:]


def last_kernel(spots, left_ref, right_ref, half_ref, out_ref):
    out_ref[...] = (half_ref[...] + dot(left_ref[...], right_ref[...], NT)).astype(BF16)


def near_kernel(spots, left_ref, right_ref, *refs):
    attn, (half_ref, own_out, mate_out) = refs[:-3], refs[-3:]
    half_ref[...] = dot(left_ref[...], right_ref[2 * DH : 3 * DH], NT)
    far_kernel(spots, right_ref, *attn, own_out, mate_out)


def far_kernel(spots, right_ref, *refs):
    attn, (own_out, mate_out) = refs[:-2], refs[-2:]
    own = own_out.shape[0]
    part = dot(jnp.concatenate([a[...] for a in attn], 1), right_ref[...], NN)
    own_out[...] = part[:own]
    mate_out[...] = part[own:]


def grad_kernel(whole, added, places, mine_ref, mate_ref, *refs):
    chunks, out_ref = refs[added:-1], refs[-1]
    total = refs[0][...] if added else None
    for j, chunk in enumerate(chunks):
        cols = slice(None) if whole else pl.ds(pl.multiple_of(places[j], DH), chunk.shape[1])
        left = jnp.concatenate([mine_ref[:, cols], mate_ref[:, cols]], 0)
        part = dot(left, chunk[...], NT)
        total = part if total is None else total + part
    out_ref[...] = total.astype(out_ref.dtype)


def mixed_kernel(count, each, places, *refs):
    attn, weight = refs[:count], refs[count]
    chunks, (own_out, mate_out) = list(refs[count + 1 : -2]), refs[-2:]
    own = own_out.shape[0]
    left = jnp.concatenate([a[...] for a in attn], 1)
    right = [weight[:, pl.ds(pl.multiple_of(places[0], DH), own_out.shape[1])]]
    for n in each:
        parts = [chunks.pop(0)[...] for _ in range(n)]
        right.append(jnp.concatenate(parts, 1) if n > 1 else parts[0])
    part = dot(left, jnp.concatenate(right, 0), NN)
    own_out[...] = part[:own]
    mate_out[...] = part[own:]


def join_kernel(places, *refs):
    out_ref, done_ref = refs[-2:]
    done_ref[...] = jnp.zeros(done_ref.shape, F32)
    for n in range(len(refs) // 2 - 1):
        wide = refs[2 * n].shape[1]
        there = pl.ds(pl.multiple_of(places[n], DH), wide)
        out_ref[:, there] = (refs[2 * n][...] + refs[2 * n + 1][...]).astype(BF16)


def collect_kernel(scale, count, where, q_ref, *refs):
    direct, across = refs[:count], refs[count : 2 * count]
    g_ref, mine_ref, other_ref = refs[2 * count :]
    own = g_ref.shape[0] // count
    mine = pl.ds(pl.multiple_of(where[2] * DH, DH), DH)
    mate = pl.ds(pl.multiple_of((1 - where[2]) * DH, DH), DH)
    for s in range(count):
        block = lax.rem(where[0] + s, count)
        here = pl.ds(pl.multiple_of(block * own, own), own)
        g_ref[here, mine] = direct[s][:own]
        g_ref[here, mate] = across[s][own:]
    heads = [slice(h * DH, (h + 1) * DH) for h in range(2)]
    parts = [scale * dot(q_ref[:, cols], g_ref[:, cols], TN) for cols in heads]
    mine_ref[...], other_ref[...] = pick(where[2], parts)


def backward_kernel(
    scale,
    count,
    where,
    q_ref,
    k_ref,
    v_ref,
    g_ref,
    probs_ref,
    inner_ref,
    soft_ref,
    mine_ref,
    other_ref,
    dq_ref,
    dk_ref,
    dv_ref,
):
    rows, width = q_ref.shape
    blk = rows // count
    inv_root = 1.0 / math.sqrt(DH)
    triangle = lower_triangle(blk)
    states = both_heads(where[2], mine_ref, other_ref)
    for h in range(width // DH):
        cols = slice(h * DH, (h + 1) * DH)
        for i in reversed(range(count)):
            here = slice(i * blk, (i + 1) * blk)
            upto = slice(0, (i + 1) * blk)
            q, g = q_ref[here, cols], g_ref[here, cols]
            k = k_ref[upto, cols]
            probs = probs_ref[h, here, upto]
            dprod = dot(g, v_ref[upto, cols], NT)
            delta = jnp.sum(g.astype(F32) * soft_ref[here, cols], -1, keepdims=True)
            dscore = (probs.astype(F32) * (dprod - delta) * inv_root).astype(BF16)
            last = jnp.where(triangle, dprod[:, i * blk :], 0.0)
            dinner = jnp.concatenate([dprod[:, : i * blk], last], 1) if i else last
            dinner = dinner.astype(BF16)
            dq_ref[here, cols] = (
                dot(dscore, k, NN)
                + scale * (dot(dinner, k, NN) + dot_wide(g, states[h], NT))
            ).astype(BF16)
            dk = dot(dscore, q, TN) + scale * dot(dinner, q, TN)
            dv = dot(probs, g, TN) + scale * dot(inner_ref[h, here, upto], g, TN)
            if i == count - 1:
                dk_ref[upto, cols] = dk
                dv_ref[upto, cols] = dv
            else:
                dk_ref[upto, cols] += dk
                dv_ref[upto, cols] += dv


def close_kernel(where, k_ref, v_ref, dk_ref, dv_ref, mine_ref, other_ref, gk_ref, gv_ref):
    states = both_heads(where[2], mine_ref, other_ref)
    for h in range(k_ref.shape[1] // DH):
        cols = slice(h * DH, (h + 1) * DH)
        state = states[h]
        gk_ref[:, cols] = (dk_ref[:, cols] + dot_wide(v_ref[:, cols], state, NT)).astype(BF16)
        gv_ref[:, cols] = (dv_ref[:, cols] + dot_wide(k_ref[:, cols], state, NN)).astype(BF16)


def send(x, flip, shift):
    shards, heads = lax.axis_size("ctx"), lax.axis_size("head")
    pairs = [
        (c * heads + z, (c ^ flip) * heads + (z + shift) % heads)
        for c in range(shards)
        for z in range(heads)
    ]
    return lax.ppermute(x, ("ctx", "head"), pairs)


def exchange(mine, other, core, chip, chips, later):
    got = send(other, 1, 0)
    own = total = mine + got
    totals, flags = [], []
    if chips == 4:
        for flip in (1, 2, 3):
            totals.append(send(total, 2 * flip, 0))
            flags.append(((chip ^ flip) > chip) == later)
    else:
        step = 1
        while step < chips:
            totals.append(send(total, 2 * step, 0))
            flags.append(((chip & step) == 0) == later)
            total = total + totals[-1]
            step *= 2
    flags.append((core == 0) == later)
    return jnp.stack(flags).astype(jnp.int32), [mine, got, *totals], own


def on_device(query, key, value, block_mask, out_weight, cotangent):
    rows, width = query.shape
    heads = width // DH
    shards, count = lax.axis_size("ctx"), lax.axis_size("head")
    model = out_weight.shape[1]
    own = rows // count
    scale = 1.0 / math.sqrt(DH * rows * shards)
    blocks = block_mask.shape[0]
    ctx, place = lax.axis_index("ctx"), lax.axis_index("head")
    core, chip, chips = ctx & 1, ctx >> 1, shards // 2
    where = jnp.stack([place, ctx, core])
    flat, square = (rows, width), rows * rows * DH * heads
    pair = [((DH, DH), F32)] * 2
    tokens = ((2 * own, DH), BF16)
    product = 4 * own * DH * model

    board = chips == 4 and count == 4
    wide = model // (2 if board else chips)
    colour = (chip & 1) ^ (chip >> 1) if board else chip
    piece = lax.dynamic_slice(out_weight, (core * DH, colour * wide), (DH, wide))
    arrived = {1: send(piece, 0, 1), count - 1: send(piece, 0, -1)}
    mate_cotangent = send(cotangent, 1, 0)

    probs, inner, soft, pre, other_pre, far, mine, other = call(
        functools.partial(forward_kernel, scale),
        [((heads, rows, rows), BF16)] * 2
        + [(flat, F32)]
        + [((rows, DH), F32)] * 2
        + [((rows, DH), BF16)]
        + pair,
        [query, key, value],
        [block_mask, where],
        [mate_cotangent],
        flops=7 * square,
    )
    far, other_pre = send(far, 1, 0), send(other_pre, 1, 0)
    (mine,) = hold([mine], [far, other_pre])
    flags, parts, total = exchange(mine, other, core, chip, chips, False)
    *attn, keep, back = call(
        functools.partial(attn_kernel, scale, count),
        [tokens] * count + pair,
        [*parts, query, far, pre, other_pre],
        [flags, where],
    )
    linear = [keep, send(back, 1, 0)]
    attn = [attn[0]] + [send(attn[s], 0, s) for s in range(1, count)]

    work = near_and_far if board else by_gathers
    both, across, joins, starts = work(
        attn, arrived, cotangent, mate_cotangent, out_weight, core, chip, colour, product
    )
    mixed, done = call(
        join_kernel, [((own, model), BF16), ((8, DH), F32)], joins, [jnp.stack(starts)]
    )

    g, mine, other = call(
        functools.partial(collect_kernel, scale, count),
        [(flat, BF16), *pair],
        [query, *both, *across],
        [where],
    )
    flags, parts, total = exchange(mine, other, core, chip, chips, True)
    grad_query, dk, dv = call(
        functools.partial(backward_kernel, scale, blocks),
        [(flat, BF16)] + [(flat, F32)] * 2,
        [query, key, value, g, probs, inner, soft, *linear],
        [where],
        [total],
        flops=14 * square,
    )
    keep, back = call(carry_kernel, pair, parts, [flags], [dk])
    grad_key, grad_value = call(
        close_kernel,
        [(flat, BF16)] * 2,
        [key, value, dk, dv, keep, send(back, 1, 0)],
        [where],
        [done],
    )
    return mixed, grad_query, grad_key, grad_value


def near_and_far(attn, arrived, cotangent, mate_cotangent, weight, core, chip, colour, product):
    own, model = cotangent.shape
    wide = model // 2
    spots = jnp.stack([colour * wide, (1 - colour) * wide, core * DH])
    tokens = ((2 * own, DH), BF16)
    parts = [((own, wide), F32)] * 2
    all_arrays = [(cotangent, all_of, rows_at(0, own)), (mate_cotangent, all_of, rows_at(own, own))]
    whole = fetch((2 * own, model), *all_arrays)
    left = [
        fetch((2 * own, wide), *((a, columns(n, wide), put) for a, _, put in all_arrays))
        for n in range(2)
    ]

    def own_rows(ref, spots, *_):
        return ref.at[pl.ds(pl.multiple_of(spots[2], DH), DH)]

    def own_columns(n):
        return lambda ref, spots, *_: ref.at[
            pl.ds(pl.multiple_of(spots[2], DH), DH), pl.ds(pl.multiple_of(spots[n], DH), wide)
        ]

    def stacked(*arrays):
        return [(a, all_of, rows_at(n * DH, DH)) for n, a in enumerate(arrays)]

    arrived[1], arrived[3] = hold([arrived[1], arrived[3]], attn[:1])
    arrived[2] = send(arrived[1], 0, 1)
    second = {1: send(arrived[1], 2, 0), 3: send(arrived[3], 4, 0)}
    mine, half = call(
        first_kernel,
        [tokens, ((2 * own, 2 * DH), F32)],
        [
            whole,
            fetch((DH, model), (weight, own_rows, all_of)),
            fetch((2 * DH, wide), *stacked(arrived[1], arrived[3])),
        ],
        [spots],
        room=6,
        flops=2 * product,
    )
    one, three, *cuts = call(
        second_kernel,
        [tokens] * 2 + [((DH, wide // 2), BF16)] * 2,
        [
            left[1],
            fetch((2 * DH, wide), *stacked(second[1], second[3])),
            half,
            fetch((DH, wide), (arrived[2], all_of, all_of)),
        ],
        [spots],
        room=6,
        flops=product,
    )
    second[2] = [send(cuts[0], 2, 0), send(cuts[1], 4, 0)]
    both = {0: mine, 1: send(one, 0, -1), 3: send(three, 0, -3)}
    across = {s: send(both[s], 1, 0) for s in (0, 1, 3)}
    half, part, mate_part = call(
        near_kernel,
        [((2 * own, DH), F32), *parts],
        [
            left[0],
            fetch(
                (4 * DH, wide),
                (weight, own_columns(0), rows_at(0, DH)),
                *((arrived[s], all_of, rows_at(s * DH, DH)) for s in (1, 2, 3)),
            ),
            *attn,
        ],
        [spots],
        room=6,
        flops=2 * product,
    )
    joins = [part, send(mate_part, 1, 0)]
    quarters = [(a, all_of, columns_at(n * wide // 2, wide // 2)) for n, a in enumerate(second[2])]
    (two,) = call(
        last_kernel,
        [tokens],
        [left[1], fetch((DH, wide), *quarters), half],
        [spots],
        [both[1], both[3]],
        room=6,
        flops=product // 2,
    )
    both[2] = send(two, 0, -2)

    def quarter(n):
        return lambda ref, *_: ref.at[2 * DH : 3 * DH, n * wide // 2 : (n + 1) * wide // 2]

    part, mate_part = call(
        far_kernel,
        parts,
        [
            fetch(
                (4 * DH, wide),
                (weight, own_columns(1), rows_at(0, DH)),
                (second[1], all_of, rows_at(DH, DH)),
                (second[3], all_of, rows_at(3 * DH, DH)),
                *((a, all_of, quarter(n)) for n, a in enumerate(second[2])),
            ),
            *attn,
        ],
        [spots],
        [both[2], across[0], across[1], across[3]],
        room=6,
        flops=2 * product,
    )
    joins += [part, send(mate_part, 1, 0)]
    across[2] = send(both[2], 1, 0)
    return [both[s] for s in range(4)], [across[s] for s in range(4)], joins, [spots[0], spots[1]]


def by_gathers(attn, arrived, cotangent, mate_cotangent, out_weight, core, chip, colour, product):
    own, model = cotangent.shape
    shards, count = lax.axis_size("ctx"), lax.axis_size("head")
    weight = lax.dynamic_slice_in_dim(out_weight, core * DH, DH, 0)
    zero = jnp.zeros((1,), jnp.int32)
    groups = [list(range(k, shards, 2)) for k in range(2)]
    for s in range(2, count - 1):
        arrived[s] = send(arrived[s - 1], 0, 1)
    chunks = [weight] + [
        lax.all_gather(arrived[s], "ctx", axis=1, tiled=True, axis_index_groups=groups)
        for s in range(1, count)
    ]
    both = []
    for s in range(count):
        (block,) = call(
            functools.partial(grad_kernel, True, 0),
            [((2 * own, DH), BF16)],
            [cotangent, mate_cotangent, chunks[s]],
            [zero],
            flops=product,
        )
        both.append(send(block, 0, -s) if s else block)
    part, mate_part = call(
        functools.partial(mixed_kernel, count, [1] * (count - 1)),
        [((own, model), F32)] * 2,
        [*attn, *chunks],
        [zero],
        room=6,
        flops=count * product,
    )
    return both, [send(b, 1, 0) for b in both], [part, send(mate_part, 1, 0)], [jnp.int32(0)]


def solution(mesh):
    return jax.shard_map(
        on_device,
        mesh=mesh,
        in_specs=(
            P("ctx", "head"),
            P("ctx", "head"),
            P("ctx", "head"),
            P("ctx", None),
            P("head", None),
            P(("ctx", "head"), None),
        ),
        out_specs=(P(("ctx", "head"), None), P("ctx", "head"), P("ctx", "head"), P("ctx", "head")),
        check_vma=False,
    )
```

```python
import functools
import math

import jax
import jax.numpy as jnp
from jax import lax
from jax.experimental import pallas as pl
from jax.experimental.pallas import tpu as pltpu
from jax.sharding import PartitionSpec as P

DH = 128
F32 = jnp.float32
BF16 = jnp.bfloat16
NN = ((1,), (0,))
NT = ((1,), (1,))
TN = ((0,), (0,))
MIB = 1 << 20


def dot(a, b, dims):
    return lax.dot_general(a, b, (dims, ((), ())), preferred_element_type=F32)


def dot_wide(a, b, dims):
    high = b.astype(BF16)
    low = (b - high.astype(F32)).astype(BF16)
    return dot(a, high, dims) + dot(a, low, dims)


def fetch(shape, *parts):
    return (shape, parts)


def all_of(ref, *_):
    return ref


def columns(spot, wide, rows=slice(None)):
    def view(ref, spots, *_):
        return ref.at[rows, pl.ds(pl.multiple_of(spots[spot], DH), wide)]

    return view


def rows_at(first, count):
    return lambda ref, *_: ref.at[first : first + count]


def columns_at(first, count):
    return lambda ref, *_: ref.at[:, first : first + count]


def call(body, outs, args, smem=(), after=(), room=2, flops=1):
    arrays, specs, scratch = [], [], []
    for arg in args:
        if isinstance(arg, tuple):
            arrays += [part[0] for part in arg[1]]
            specs += [pl.BlockSpec(memory_space=pltpu.HBM) for _ in arg[1]]
            scratch.append(pltpu.VMEM(arg[0], arg[1][0][0].dtype))
        else:
            arrays.append(arg)
            specs.append(pl.BlockSpec(memory_space=pltpu.VMEM))
    copies = sum(len(arg[1]) for arg in args if isinstance(arg, tuple))
    held = len(scratch)
    if copies:
        scratch.append(pltpu.SemaphoreType.DMA((copies,)))

    def kernel(*refs):
        scalars, refs = refs[: len(smem)], list(refs[len(smem) :])
        ins, refs = refs[: len(arrays)], refs[len(arrays) + len(after) :]
        results, slots = refs[: len(outs)], refs[len(outs) :]
        given, started, slot = [], [], 0
        for arg in args:
            if not isinstance(arg, tuple):
                given.append(ins.pop(0))
                continue
            for _, source, target in arg[1]:
                copy = pltpu.make_async_copy(
                    source(ins.pop(0), *scalars),
                    target(slots[slot], *scalars),
                    slots[held].at[len(started)],
                )
                copy.start()
                started.append(copy)
            given.append(slots[slot])
            slot += 1
        for copy in started:
            copy.wait()
        body(*scalars, *given, *results)

    moved = sum(a.size * a.dtype.itemsize for a in arrays)
    moved += sum(math.prod(s) * jnp.dtype(t).itemsize for s, t in outs)
    return pl.pallas_call(
        kernel,
        out_shape=[jax.ShapeDtypeStruct(s, t) for s, t in outs],
        in_specs=[pl.BlockSpec(memory_space=pltpu.SMEM) for _ in smem]
        + specs
        + [pl.BlockSpec(memory_space=pl.ANY) for _ in after],
        out_specs=[pl.BlockSpec(memory_space=pltpu.VMEM) for _ in outs],
        scratch_shapes=scratch,
        compiler_params=pltpu.CompilerParams(vmem_limit_bytes=room * MIB),
        cost_estimate=pl.CostEstimate(
            flops=int(flops), bytes_accessed=int(moved), transcendentals=0
        ),
    )(*smem, *arrays, *after)


def hold(arrays, after):
    held = len(arrays)
    return pl.pallas_call(
        lambda *refs: None,
        out_shape=[jax.ShapeDtypeStruct(a.shape, a.dtype) for a in arrays],
        in_specs=[pl.BlockSpec(memory_space=pl.ANY) for _ in (*arrays, *after)],
        out_specs=[pl.BlockSpec(memory_space=pl.ANY) for _ in arrays],
        input_output_aliases={n: n for n in range(held)},
        cost_estimate=pl.CostEstimate(flops=1, bytes_accessed=1, transcendentals=0),
    )(*arrays, *after)


def lower_triangle(blk):
    return lax.broadcasted_iota(jnp.int32, (blk, blk), 0) >= lax.broadcasted_iota(
        jnp.int32, (blk, blk), 1
    )


def forward_kernel(
    scale,
    mask,
    where,
    q_ref,
    k_ref,
    v_ref,
    store_ref,
    mine_ref,
    other_ref,
    far_ref,
    mine_state_ref,
    other_state_ref,
):
    heads = [slice(h * DH, (h + 1) * DH) for h in range(2)]
    states = [dot(k_ref[:, cols], v_ref[:, cols], TN) for cols in heads]
    mine_state_ref[...], other_state_ref[...] = pick(where[2], states)
    rows, width = q_ref.shape
    count = mask.shape[0]
    blk = rows // count
    inv_root = 1.0 / math.sqrt(DH)
    triangle = lower_triangle(blk)
    for i in range(count):
        here = slice(i * blk, (i + 1) * blk)
        upto = slice(0, (i + 1) * blk)
        sums = []
        for h in range(2):
            cols = slice(h * DH, (h + 1) * DH)
            raw = dot(q_ref[here, cols], k_ref[upto, cols], NT)
            scores, inner = [], []
            for j in range(i + 1):
                part = raw[:, j * blk : (j + 1) * blk]
                keep = triangle if j == i else mask[i, j] > 0
                scores.append(jnp.where(keep, part * inv_root, -1e30))
                inner.append(jnp.where(triangle, part, 0.0) if j == i else part)
            scores = jnp.concatenate(scores, 1)
            inner = jnp.concatenate(inner, 1).astype(BF16)
            expo = jnp.exp(scores - jnp.max(scores, -1, keepdims=True))
            probs = (expo / jnp.sum(expo, -1, keepdims=True)).astype(BF16)
            v = v_ref[upto, cols]
            soft = dot(probs, v, NN)
            store_ref[h, here, upto] = probs
            store_ref[2 + h, here, upto] = inner
            sums.append(soft + scale * dot(inner, v, NN))
        mine_ref[here], other_ref[here] = pick(where[2], sums)
    far_ref[...] = q_ref[:, pl.ds(pl.multiple_of((1 - where[2]) * DH, DH), DH)]


def pick(core, parts):
    return jnp.where(core == 0, parts[0], parts[1]), jnp.where(core == 0, parts[1], parts[0])


def both_heads(core, mine_ref, other_ref):
    mine, other = mine_ref[...], other_ref[...]
    return jnp.where(core == 0, mine, other), jnp.where(core == 0, other, mine)


def carry(flags, here_ref, got_ref, totals):
    carried = jnp.zeros(here_ref.shape, F32)
    for n, total in enumerate(totals):
        carried = carried + jnp.where(flags[n] > 0, total[...], 0.0)
    counts = flags[len(totals)] > 0
    keep = carried + jnp.where(counts, got_ref[...], 0.0)
    return keep, carried + jnp.where(counts, 0.0, here_ref[...])


def carry_kernel(flags, here_ref, got_ref, *refs):
    totals, (keep_ref, back_ref) = refs[:-2], refs[-2:]
    keep_ref[...], back_ref[...] = carry(flags, here_ref, got_ref, totals)


def attn_kernel(scale, flags, where, here_ref, got_ref, *refs):
    totals, refs = refs[:-7], refs[-7:]
    q_ref, far_ref, pre_ref, far_pre_ref, out_ref, keep_ref, back_ref = refs
    keep, back = carry(flags, here_ref, got_ref, totals)
    keep_ref[...], back_ref[...] = keep, back
    count = out_ref.shape[0]
    own = pre_ref.shape[0] // count
    cols = pl.ds(pl.multiple_of(where[2] * DH, DH), DH)
    mine = pre_ref[...] + scale * dot_wide(q_ref[:, cols], keep, NN)
    mate = far_pre_ref[...] + scale * dot_wide(far_ref[...], back, NN)
    for z in range(count):
        out_ref[z, :own] = mine[z * own : (z + 1) * own].astype(BF16)
        out_ref[z, own:] = mate[z * own : (z + 1) * own].astype(BF16)


def back_along(attn_ref, place):
    count = attn_ref.shape[0]
    return jnp.concatenate([attn_ref[lax.rem(place - s + count, count)] for s in range(count)], 1)


def first_kernel(spots, left_ref, weight_ref, right_ref, own_ref, half_ref):
    own_ref[...] = dot(left_ref[...], weight_ref[...], NT).astype(BF16)
    near = left_ref[:, pl.ds(pl.multiple_of(spots[0], DH), right_ref.shape[1])]
    half_ref[...] = dot(near, right_ref[...], NT)


def second_kernel(spots, left_ref, right_ref, half_ref, piece_ref, one_ref, three_ref, *cut_refs):
    wide = cut_refs[0].shape[1]
    for n, cut_ref in enumerate(cut_refs):
        cut_ref[...] = piece_ref[:, n * wide : (n + 1) * wide]
    total = (half_ref[...] + dot(left_ref[...], right_ref[...], NT)).astype(BF16)
    one_ref[...], three_ref[...] = total[:, :DH], total[:, DH:]


def last_kernel(spots, left_ref, right_ref, half_ref, out_ref):
    out_ref[...] = (half_ref[...] + dot(left_ref[...], right_ref[...], NT)).astype(BF16)


def near_kernel(spots, left_ref, right_ref, attn_ref, half_ref, own_out, mate_out):
    half_ref[...] = dot(left_ref[...], right_ref[2 * DH : 3 * DH], NT)
    far_kernel(spots, right_ref, attn_ref, own_out, mate_out)


def far_kernel(spots, right_ref, attn_ref, own_out, mate_out):
    own = own_out.shape[0]
    part = dot(back_along(attn_ref, spots[3]), right_ref[...], NN)
    own_out[...] = part[:own]
    mate_out[...] = part[own:]


def grad_kernel(whole, added, places, mine_ref, mate_ref, *refs):
    chunks, out_ref = refs[added:-1], refs[-1]
    total = refs[0][...] if added else None
    for j, chunk in enumerate(chunks):
        cols = slice(None) if whole else pl.ds(pl.multiple_of(places[j], DH), chunk.shape[1])
        left = jnp.concatenate([mine_ref[:, cols], mate_ref[:, cols]], 0)
        part = dot(left, chunk[...], NT)
        total = part if total is None else total + part
    out_ref[...] = total.astype(out_ref.dtype)


def mixed_kernel(where, attn_ref, *refs):
    chunks, (own_out, mate_out) = refs[:-2], refs[-2:]
    own = own_out.shape[0]
    right = jnp.concatenate([chunk[...] for chunk in chunks], 0)
    part = dot(back_along(attn_ref, where[0]), right, NN)
    own_out[...] = part[:own]
    mate_out[...] = part[own:]


def join_kernel(places, *refs):
    out_ref, done_ref = refs[-2:]
    done_ref[...] = jnp.zeros(done_ref.shape, F32)
    for n in range(len(refs) // 2 - 1):
        wide = refs[2 * n].shape[1]
        there = pl.ds(pl.multiple_of(places[n], DH), wide)
        out_ref[:, there] = (refs[2 * n][...] + refs[2 * n + 1][...]).astype(BF16)


def collect_kernel(scale, count, where, q_ref, *refs):
    direct, across = refs[:count], refs[count : 2 * count]
    g_ref, mine_ref, other_ref = refs[2 * count :]
    own = g_ref.shape[0] // count
    mine = pl.ds(pl.multiple_of(where[2] * DH, DH), DH)
    mate = pl.ds(pl.multiple_of((1 - where[2]) * DH, DH), DH)
    for s in range(count):
        block = lax.rem(where[0] + s, count)
        here = pl.ds(pl.multiple_of(block * own, own), own)
        g_ref[here, mine] = direct[s][:own]
        g_ref[here, mate] = across[s][own:]
    heads = [slice(h * DH, (h + 1) * DH) for h in range(2)]
    parts = [scale * dot(q_ref[:, cols], g_ref[:, cols], TN) for cols in heads]
    mine_ref[...], other_ref[...] = pick(where[2], parts)


def backward_kernel(
    scale,
    count,
    where,
    q_ref,
    k_ref,
    v_ref,
    g_ref,
    store_ref,
    mine_ref,
    other_ref,
    dq_ref,
    dk_ref,
    dv_ref,
):
    rows, width = q_ref.shape
    blk = rows // count
    inv_root = 1.0 / math.sqrt(DH)
    triangle = lower_triangle(blk)
    states = both_heads(where[2], mine_ref, other_ref)
    for h in range(width // DH):
        cols = slice(h * DH, (h + 1) * DH)
        for i in reversed(range(count)):
            here = slice(i * blk, (i + 1) * blk)
            upto = slice(0, (i + 1) * blk)
            q, g = q_ref[here, cols], g_ref[here, cols]
            k = k_ref[upto, cols]
            probs, v = store_ref[h, here, upto], v_ref[upto, cols]
            dprod = dot(g, v, NT)
            delta = jnp.sum(g.astype(F32) * dot(probs, v, NN), -1, keepdims=True)
            dscore = (probs.astype(F32) * (dprod - delta) * inv_root).astype(BF16)
            last = jnp.where(triangle, dprod[:, i * blk :], 0.0)
            dinner = jnp.concatenate([dprod[:, : i * blk], last], 1) if i else last
            dinner = dinner.astype(BF16)
            dq_ref[here, cols] = (
                dot(dscore, k, NN)
                + scale * (dot(dinner, k, NN) + dot_wide(g, states[h], NT))
            ).astype(BF16)
            dk = dot(dscore, q, TN) + scale * dot(dinner, q, TN)
            dv = dot(probs, g, TN) + scale * dot(store_ref[2 + h, here, upto], g, TN)
            if i == count - 1:
                dk_ref[upto, cols] = dk
                dv_ref[upto, cols] = dv
            else:
                dk_ref[upto, cols] += dk
                dv_ref[upto, cols] += dv


def close_kernel(where, k_ref, v_ref, dk_ref, dv_ref, mine_ref, other_ref, gk_ref, gv_ref):
    states = both_heads(where[2], mine_ref, other_ref)
    for h in range(k_ref.shape[1] // DH):
        cols = slice(h * DH, (h + 1) * DH)
        state = states[h]
        gk_ref[:, cols] = (dk_ref[:, cols] + dot_wide(v_ref[:, cols], state, NT)).astype(BF16)
        gv_ref[:, cols] = (dv_ref[:, cols] + dot_wide(k_ref[:, cols], state, NN)).astype(BF16)


def send(x, flip, shift):
    shards, heads = lax.axis_size("ctx"), lax.axis_size("head")
    pairs = [
        (c * heads + z, (c ^ flip) * heads + (z + shift) % heads)
        for c in range(shards)
        for z in range(heads)
    ]
    return lax.ppermute(x, ("ctx", "head"), pairs)


def exchange(mine, other, core, chip, chips, later):
    got = send(other, 1, 0)
    own = total = mine + got
    totals, flags = [], []
    if chips == 4:
        for flip in (1, 2, 3):
            totals.append(send(total, 2 * flip, 0))
            flags.append(((chip ^ flip) > chip) == later)
    else:
        step = 1
        while step < chips:
            totals.append(send(total, 2 * step, 0))
            flags.append(((chip & step) == 0) == later)
            total = total + totals[-1]
            step *= 2
    flags.append((core == 0) == later)
    return jnp.stack(flags).astype(jnp.int32), [mine, got, *totals], own


def on_device(query, key, value, block_mask, out_weight, cotangent):
    rows, width = query.shape
    heads = width // DH
    shards, count = lax.axis_size("ctx"), lax.axis_size("head")
    model = out_weight.shape[1]
    own = rows // count
    scale = 1.0 / math.sqrt(DH * rows * shards)
    blocks = block_mask.shape[0]
    ctx, place = lax.axis_index("ctx"), lax.axis_index("head")
    core, chip, chips = ctx & 1, ctx >> 1, shards // 2
    where = jnp.stack([place, ctx, core])
    flat, square = (rows, width), rows * rows * DH * heads
    pair = [((DH, DH), F32)] * 2
    tokens = ((2 * own, DH), BF16)
    product = 4 * own * DH * model

    board = chips == 4 and count == 4
    wide = model // (2 if board else chips)
    colour = (chip & 1) ^ (chip >> 1) if board else chip
    piece = lax.dynamic_slice(out_weight, (core * DH, colour * wide), (DH, wide))
    arrived = {1: send(piece, 0, 1), count - 1: send(piece, 0, -1)}
    mate_cotangent = send(cotangent, 1, 0)

    store, pre, other_pre, far, mine, other = call(
        functools.partial(forward_kernel, scale),
        [((2 * heads, rows, rows), BF16)]
        + [((rows, DH), F32)] * 2
        + [((rows, DH), BF16)]
        + pair,
        [query, key, value],
        [block_mask, where],
        [mate_cotangent],
        flops=7 * square,
    )
    far, other_pre = send(far, 1, 0), send(other_pre, 1, 0)
    (mine,) = hold([mine], [far, other_pre])
    flags, parts, total = exchange(mine, other, core, chip, chips, False)
    attn, keep, back = call(
        functools.partial(attn_kernel, scale),
        [((count, *tokens[0]), BF16), *pair],
        [*parts, query, far, pre, other_pre],
        [flags, where],
    )
    linear = [keep, send(back, 1, 0)]
    if board:
        arrived[1], arrived[3] = hold([arrived[1], arrived[3]], [keep])
    attn = lax.all_to_all(attn, "head", 0, 0, tiled=True)

    work = near_and_far if board else by_gathers
    both, across, joins, starts = work(
        attn, arrived, cotangent, mate_cotangent, out_weight, core, chip, colour, product
    )
    mixed, done = call(
        join_kernel, [((own, model), BF16), ((8, DH), F32)], joins, [jnp.stack(starts)]
    )

    g, mine, other = call(
        functools.partial(collect_kernel, scale, count),
        [(flat, BF16), *pair],
        [query, *both, *across],
        [where],
    )
    flags, parts, total = exchange(mine, other, core, chip, chips, True)
    grad_query, dk, dv = call(
        functools.partial(backward_kernel, scale, blocks),
        [(flat, BF16)] + [(flat, F32)] * 2,
        [query, key, value, g, store, *linear],
        [where],
        [total],
        flops=14 * square,
    )
    keep, back = call(carry_kernel, pair, parts, [flags], [dk])
    grad_key, grad_value = call(
        close_kernel,
        [(flat, BF16)] * 2,
        [key, value, dk, dv, keep, send(back, 1, 0)],
        [where],
        [done],
    )
    return mixed, grad_query, grad_key, grad_value


def near_and_far(attn, arrived, cotangent, mate_cotangent, weight, core, chip, colour, product):
    own, model = cotangent.shape
    wide = model // 2
    place = lax.axis_index("head")
    spots = jnp.stack([colour * wide, (1 - colour) * wide, core * DH, place])
    tokens = ((2 * own, DH), BF16)
    parts = [((own, wide), F32)] * 2
    all_arrays = [(cotangent, all_of, rows_at(0, own)), (mate_cotangent, all_of, rows_at(own, own))]
    whole = fetch((2 * own, model), *all_arrays)
    left = [
        fetch((2 * own, wide), *((a, columns(n, wide), put) for a, _, put in all_arrays))
        for n in range(2)
    ]

    def own_rows(ref, spots, *_):
        return ref.at[pl.ds(pl.multiple_of(spots[2], DH), DH)]

    def own_columns(n):
        return lambda ref, spots, *_: ref.at[
            pl.ds(pl.multiple_of(spots[2], DH), DH), pl.ds(pl.multiple_of(spots[n], DH), wide)
        ]

    def stacked(*arrays):
        return [(a, all_of, rows_at(n * DH, DH)) for n, a in enumerate(arrays)]

    arrived[2] = send(arrived[1], 0, 1)
    second = {1: send(arrived[1], 2, 0), 3: send(arrived[3], 4, 0)}
    mine, half = call(
        first_kernel,
        [tokens, ((2 * own, 2 * DH), F32)],
        [
            whole,
            fetch((DH, model), (weight, own_rows, all_of)),
            fetch((2 * DH, wide), *stacked(arrived[1], arrived[3])),
        ],
        [spots],
        room=6,
        flops=2 * product,
    )
    one, three, *cuts = call(
        second_kernel,
        [tokens] * 2 + [((DH, wide // 2), BF16)] * 2,
        [
            left[1],
            fetch((2 * DH, wide), *stacked(second[1], second[3])),
            half,
            fetch((DH, wide), (arrived[2], all_of, all_of)),
        ],
        [spots],
        room=6,
        flops=product,
    )
    second[2] = [send(cuts[0], 2, 0), send(cuts[1], 4, 0)]
    both = {0: mine, 1: send(one, 0, -1), 3: send(three, 0, -3)}
    across = {s: send(both[s], 1, 0) for s in (0, 1, 3)}
    half, part, mate_part = call(
        near_kernel,
        [((2 * own, DH), F32), *parts],
        [
            left[0],
            fetch(
                (4 * DH, wide),
                (weight, own_columns(0), rows_at(0, DH)),
                *((arrived[s], all_of, rows_at(s * DH, DH)) for s in (1, 2, 3)),
            ),
            attn,
        ],
        [spots],
        room=6,
        flops=2 * product,
    )
    joins = [part, send(mate_part, 1, 0)]
    quarters = [(a, all_of, columns_at(n * wide // 2, wide // 2)) for n, a in enumerate(second[2])]
    (two,) = call(
        last_kernel,
        [tokens],
        [left[1], fetch((DH, wide), *quarters), half],
        [spots],
        [both[1], both[3]],
        room=6,
        flops=product // 2,
    )
    both[2] = send(two, 0, -2)

    def quarter(n):
        return lambda ref, *_: ref.at[2 * DH : 3 * DH, n * wide // 2 : (n + 1) * wide // 2]

    part, mate_part = call(
        far_kernel,
        parts,
        [
            fetch(
                (4 * DH, wide),
                (weight, own_columns(1), rows_at(0, DH)),
                (second[1], all_of, rows_at(DH, DH)),
                (second[3], all_of, rows_at(3 * DH, DH)),
                *((a, all_of, quarter(n)) for n, a in enumerate(second[2])),
            ),
            attn,
        ],
        [spots],
        [both[2], across[0], across[1], across[3]],
        room=6,
        flops=2 * product,
    )
    joins += [part, send(mate_part, 1, 0)]
    across[2] = send(both[2], 1, 0)
    return [both[s] for s in range(4)], [across[s] for s in range(4)], joins, [spots[0], spots[1]]


def by_gathers(attn, arrived, cotangent, mate_cotangent, out_weight, core, chip, colour, product):
    own, model = cotangent.shape
    shards, count = lax.axis_size("ctx"), lax.axis_size("head")
    weight = lax.dynamic_slice_in_dim(out_weight, core * DH, DH, 0)
    zero = jnp.zeros((1,), jnp.int32)
    groups = [list(range(k, shards, 2)) for k in range(2)]
    for s in range(2, count - 1):
        arrived[s] = send(arrived[s - 1], 0, 1)
    chunks = [weight] + [
        lax.all_gather(arrived[s], "ctx", axis=1, tiled=True, axis_index_groups=groups)
        for s in range(1, count)
    ]
    both = []
    for s in range(count):
        (block,) = call(
            functools.partial(grad_kernel, True, 0),
            [((2 * own, DH), BF16)],
            [cotangent, mate_cotangent, chunks[s]],
            [zero],
            flops=product,
        )
        both.append(send(block, 0, -s) if s else block)
    part, mate_part = call(
        mixed_kernel,
        [((own, model), F32)] * 2,
        [attn, *chunks],
        [lax.axis_index("head").reshape(1)],
        room=6,
        flops=count * product,
    )
    return both, [send(b, 1, 0) for b in both], [part, send(mate_part, 1, 0)], [jnp.int32(0)]


def solution(mesh):
    return jax.shard_map(
        on_device,
        mesh=mesh,
        in_specs=(
            P("ctx", "head"),
            P("ctx", "head"),
            P("ctx", "head"),
            P("ctx", None),
            P("head", None),
            P(("ctx", "head"), None),
        ),
        out_specs=(P(("ctx", "head"), None), P("ctx", "head"), P("ctx", "head"), P("ctx", "head")),
        check_vma=False,
    )
```

```python
import functools
import math

import jax
import jax.numpy as jnp
from jax import lax
from jax.experimental import pallas as pl
from jax.experimental.pallas import tpu as pltpu
from jax.sharding import PartitionSpec as P

DH = 128
F32 = jnp.float32
BF16 = jnp.bfloat16
NN = ((1,), (0,))
NT = ((1,), (1,))
TN = ((0,), (0,))
MIB = 1 << 20


def dot(a, b, dims):
    return lax.dot_general(a, b, (dims, ((), ())), preferred_element_type=F32)


def dot_wide(a, b, dims):
    high = b.astype(BF16)
    low = (b - high.astype(F32)).astype(BF16)
    both = dot(a, jnp.concatenate([high, low], 1 - dims[1][0]), dims)
    return both[:, :DH] + both[:, DH:]


def fetch(shape, *parts):
    return (shape, parts)


def all_of(ref, *_):
    return ref


def columns(spot, wide, rows=slice(None)):
    def view(ref, spots, *_):
        return ref.at[rows, pl.ds(pl.multiple_of(spots[spot], DH), wide)]

    return view


def rows_at(first, count):
    return lambda ref, *_: ref.at[first : first + count]


def columns_at(first, count):
    return lambda ref, *_: ref.at[:, first : first + count]


def call(body, outs, args, smem=(), after=(), room=2, flops=1):
    arrays, specs, scratch = [], [], []
    for arg in args:
        if isinstance(arg, tuple):
            arrays += [part[0] for part in arg[1]]
            specs += [pl.BlockSpec(memory_space=pltpu.HBM) for _ in arg[1]]
            scratch.append(pltpu.VMEM(arg[0], arg[1][0][0].dtype))
        else:
            arrays.append(arg)
            specs.append(pl.BlockSpec(memory_space=pltpu.VMEM))
    copies = sum(len(arg[1]) for arg in args if isinstance(arg, tuple))
    held = len(scratch)
    if copies:
        scratch.append(pltpu.SemaphoreType.DMA((copies,)))

    def kernel(*refs):
        scalars, refs = refs[: len(smem)], list(refs[len(smem) :])
        ins, refs = refs[: len(arrays)], refs[len(arrays) + len(after) :]
        results, slots = refs[: len(outs)], refs[len(outs) :]
        given, started, slot = [], [], 0
        for arg in args:
            if not isinstance(arg, tuple):
                given.append(ins.pop(0))
                continue
            for _, source, target in arg[1]:
                copy = pltpu.make_async_copy(
                    source(ins.pop(0), *scalars),
                    target(slots[slot], *scalars),
                    slots[held].at[len(started)],
                )
                copy.start()
                started.append(copy)
            given.append(slots[slot])
            slot += 1
        for copy in started:
            copy.wait()
        body(*scalars, *given, *results)

    moved = sum(a.size * a.dtype.itemsize for a in arrays)
    moved += sum(math.prod(s) * jnp.dtype(t).itemsize for s, t in outs)
    return pl.pallas_call(
        kernel,
        out_shape=[jax.ShapeDtypeStruct(s, t) for s, t in outs],
        in_specs=[pl.BlockSpec(memory_space=pltpu.SMEM) for _ in smem]
        + specs
        + [pl.BlockSpec(memory_space=pl.ANY) for _ in after],
        out_specs=[pl.BlockSpec(memory_space=pltpu.VMEM) for _ in outs],
        scratch_shapes=scratch,
        compiler_params=pltpu.CompilerParams(vmem_limit_bytes=room * MIB),
        cost_estimate=pl.CostEstimate(
            flops=int(flops), bytes_accessed=int(moved), transcendentals=0
        ),
    )(*smem, *arrays, *after)


def hold(arrays, after):
    held = len(arrays)
    return pl.pallas_call(
        lambda *refs: None,
        out_shape=[jax.ShapeDtypeStruct(a.shape, a.dtype) for a in arrays],
        in_specs=[pl.BlockSpec(memory_space=pl.ANY) for _ in (*arrays, *after)],
        out_specs=[pl.BlockSpec(memory_space=pl.ANY) for _ in arrays],
        input_output_aliases={n: n for n in range(held)},
        cost_estimate=pl.CostEstimate(flops=1, bytes_accessed=1, transcendentals=0),
    )(*arrays, *after)


def lower_triangle(blk):
    return lax.broadcasted_iota(jnp.int32, (blk, blk), 0) >= lax.broadcasted_iota(
        jnp.int32, (blk, blk), 1
    )


def forward_kernel(
    scale,
    mask,
    where,
    all_ref,
    store_ref,
    mine_ref,
    other_ref,
    far_ref,
    mine_state_ref,
    other_state_ref,
):
    q_ref, k_ref, v_ref = (all_ref.at[n] for n in range(3))
    heads = [slice(h * DH, (h + 1) * DH) for h in range(2)]
    states = [dot(k_ref[:, cols], v_ref[:, cols], TN) for cols in heads]
    mine_state_ref[...], other_state_ref[...] = pick(where[2], states)
    rows, width = q_ref.shape
    count = mask.shape[0]
    blk = rows // count
    inv_root = 1.0 / math.sqrt(DH)
    triangle = lower_triangle(blk)
    for i in range(count):
        here = slice(i * blk, (i + 1) * blk)
        upto = slice(0, (i + 1) * blk)
        sums = []
        for h in range(2):
            cols = slice(h * DH, (h + 1) * DH)
            raw = dot(q_ref[here, cols], k_ref[upto, cols], NT)
            scores, inner = [], []
            for j in range(i + 1):
                part = raw[:, j * blk : (j + 1) * blk]
                keep = triangle if j == i else mask[i, j] > 0
                scores.append(jnp.where(keep, part * inv_root, -1e30))
                inner.append(jnp.where(triangle, part, 0.0) if j == i else part)
            scores = jnp.concatenate(scores, 1)
            inner = jnp.concatenate(inner, 1).astype(BF16)
            expo = jnp.exp(scores - jnp.max(scores, -1, keepdims=True))
            probs = (expo / jnp.sum(expo, -1, keepdims=True)).astype(BF16)
            store_ref[h, here, upto] = probs
            store_ref[2 + h, here, upto] = inner
            both = dot(jnp.concatenate([probs, inner], 0), v_ref[upto, cols], NN)
            sums.append(both[:blk] + scale * both[blk:])
        mine_ref[here], other_ref[here] = pick(where[2], sums)
    far_ref[...] = q_ref[:, pl.ds(pl.multiple_of((1 - where[2]) * DH, DH), DH)]


def pick(core, parts):
    return jnp.where(core == 0, parts[0], parts[1]), jnp.where(core == 0, parts[1], parts[0])


def both_heads(core, mine_ref, other_ref):
    mine, other = mine_ref[...], other_ref[...]
    return jnp.where(core == 0, mine, other), jnp.where(core == 0, other, mine)


def carry(flags, here_ref, got_ref, totals):
    carried = jnp.zeros(here_ref.shape, F32)
    for n, total in enumerate(totals):
        carried = carried + jnp.where(flags[n] > 0, total[...], 0.0)
    counts = flags[len(totals)] > 0
    keep = carried + jnp.where(counts, got_ref[...], 0.0)
    return keep, carried + jnp.where(counts, 0.0, here_ref[...])


def carry_kernel(flags, here_ref, got_ref, *refs):
    totals, (keep_ref, back_ref) = refs[:-2], refs[-2:]
    keep_ref[...], back_ref[...] = carry(flags, here_ref, got_ref, totals)


def attn_kernel(scale, flags, where, here_ref, got_ref, *refs):
    totals, refs = refs[:-7], refs[-7:]
    q_ref, far_ref, pre_ref, far_pre_ref, out_ref, keep_ref, back_ref = refs
    keep, back = carry(flags, here_ref, got_ref, totals)
    keep_ref[...], back_ref[...] = keep, back
    count = out_ref.shape[0]
    own = pre_ref.shape[0] // count
    cols = pl.ds(pl.multiple_of(where[2] * DH, DH), DH)
    mine = pre_ref[...] + scale * dot_wide(q_ref[:, cols], keep, NN)
    mate = far_pre_ref[...] + scale * dot_wide(far_ref[...], back, NN)
    for z in range(count):
        out_ref[z, :own] = mine[z * own : (z + 1) * own].astype(BF16)
        out_ref[z, own:] = mate[z * own : (z + 1) * own].astype(BF16)


def back_along(attn_ref, place):
    count = attn_ref.shape[0]
    return jnp.concatenate([attn_ref[lax.rem(place - s + count, count)] for s in range(count)], 1)


def first_kernel(spots, left_ref, weight_ref, right_ref, own_ref, half_ref):
    own_ref[...] = dot(left_ref[...], weight_ref[...], NT).astype(BF16)
    near = left_ref[:, pl.ds(pl.multiple_of(spots[0], DH), right_ref.shape[1])]
    half_ref[...] = dot(near, right_ref[...], NT)


def second_kernel(spots, left_ref, right_ref, half_ref, piece_ref, one_ref, three_ref, *cut_refs):
    wide = cut_refs[0].shape[1]
    for n, cut_ref in enumerate(cut_refs):
        cut_ref[...] = piece_ref[:, n * wide : (n + 1) * wide]
    total = (half_ref[...] + dot(left_ref[...], right_ref[...], NT)).astype(BF16)
    one_ref[...], three_ref[...] = total[:, :DH], total[:, DH:]


def last_kernel(spots, left_ref, right_ref, half_ref, out_ref):
    out_ref[...] = (half_ref[...] + dot(left_ref[...], right_ref[...], NT)).astype(BF16)


def near_kernel(spots, left_ref, right_ref, attn_ref, half_ref, own_out, mate_out):
    half_ref[...] = dot(left_ref[...], right_ref[2 * DH : 3 * DH], NT)
    far_kernel(spots, right_ref, attn_ref, own_out, mate_out)


def far_kernel(spots, right_ref, attn_ref, own_out, mate_out):
    own = own_out.shape[0]
    part = dot(back_along(attn_ref, spots[3]), right_ref[...], NN)
    own_out[...] = part[:own]
    mate_out[...] = part[own:]


def grad_kernel(whole, added, places, mine_ref, mate_ref, *refs):
    chunks, out_ref = refs[added:-1], refs[-1]
    total = refs[0][...] if added else None
    for j, chunk in enumerate(chunks):
        cols = slice(None) if whole else pl.ds(pl.multiple_of(places[j], DH), chunk.shape[1])
        left = jnp.concatenate([mine_ref[:, cols], mate_ref[:, cols]], 0)
        part = dot(left, chunk[...], NT)
        total = part if total is None else total + part
    out_ref[...] = total.astype(out_ref.dtype)


def mixed_kernel(where, attn_ref, *refs):
    chunks, (own_out, mate_out) = refs[:-2], refs[-2:]
    own = own_out.shape[0]
    right = jnp.concatenate([chunk[...] for chunk in chunks], 0)
    part = dot(back_along(attn_ref, where[0]), right, NN)
    own_out[...] = part[:own]
    mate_out[...] = part[own:]


def join_kernel(places, *refs):
    out_ref, done_ref = refs[-2:]
    done_ref[...] = jnp.zeros(done_ref.shape, F32)
    for n in range(len(refs) // 2 - 1):
        wide = refs[2 * n].shape[1]
        there = pl.ds(pl.multiple_of(places[n], DH), wide)
        out_ref[:, there] = (refs[2 * n][...] + refs[2 * n + 1][...]).astype(BF16)


def collect_kernel(scale, count, where, q_ref, *refs):
    direct, across = refs[:count], refs[count : 2 * count]
    g_ref, mine_ref, other_ref = refs[2 * count :]
    own = g_ref.shape[0] // count
    mine = pl.ds(pl.multiple_of(where[2] * DH, DH), DH)
    mate = pl.ds(pl.multiple_of((1 - where[2]) * DH, DH), DH)
    for s in range(count):
        block = lax.rem(where[0] + s, count)
        here = pl.ds(pl.multiple_of(block * own, own), own)
        g_ref[here, mine] = direct[s][:own]
        g_ref[here, mate] = across[s][own:]
    heads = [slice(h * DH, (h + 1) * DH) for h in range(2)]
    parts = [scale * dot(q_ref[:, cols], g_ref[:, cols], TN) for cols in heads]
    mine_ref[...], other_ref[...] = pick(where[2], parts)


def backward_kernel(
    scale,
    count,
    where,
    q_ref,
    k_ref,
    v_ref,
    g_ref,
    store_ref,
    mine_ref,
    other_ref,
    dq_ref,
    dk_ref,
    dv_ref,
):
    rows, width = q_ref.shape
    blk = rows // count
    inv_root = 1.0 / math.sqrt(DH)
    triangle = lower_triangle(blk)
    states = both_heads(where[2], mine_ref, other_ref)
    for h in range(width // DH):
        cols = slice(h * DH, (h + 1) * DH)
        for i in reversed(range(count)):
            here = slice(i * blk, (i + 1) * blk)
            upto = slice(0, (i + 1) * blk)
            q, g = q_ref[here, cols], g_ref[here, cols]
            k = k_ref[upto, cols]
            probs, v = store_ref[h, here, upto], v_ref[upto, cols]
            dprod = dot(g, v, NT)
            delta = jnp.sum(g.astype(F32) * dot(probs, v, NN), -1, keepdims=True)
            dscore = (probs.astype(F32) * (dprod - delta) * inv_root).astype(BF16)
            last = jnp.where(triangle, dprod[:, i * blk :], 0.0)
            dinner = jnp.concatenate([dprod[:, : i * blk], last], 1) if i else last
            dinner = dinner.astype(BF16)
            far = slice(upto.stop, 2 * upto.stop)
            inner = store_ref[2 + h, here, upto]
            left = dot(jnp.concatenate([dscore, dinner], 0), k, NN)
            linear = left[blk:] + dot_wide(g, states[h], NT)
            dq_ref[here, cols] = (left[:blk] + scale * linear).astype(BF16)
            dk = dot(jnp.concatenate([dscore, dinner], 1), q, TN)
            dk = dk[upto] + scale * dk[far]
            dv = dot(jnp.concatenate([probs, inner], 1), g, TN)
            dv = dv[upto] + scale * dv[far]
            if i == count - 1:
                dk_ref[upto, cols] = dk
                dv_ref[upto, cols] = dv
            else:
                dk_ref[upto, cols] += dk
                dv_ref[upto, cols] += dv


def close_kernel(where, k_ref, v_ref, dk_ref, dv_ref, mine_ref, other_ref, gk_ref, gv_ref):
    states = both_heads(where[2], mine_ref, other_ref)
    for h in range(k_ref.shape[1] // DH):
        cols = slice(h * DH, (h + 1) * DH)
        state = states[h]
        gk_ref[:, cols] = (dk_ref[:, cols] + dot_wide(v_ref[:, cols], state, NT)).astype(BF16)
        gv_ref[:, cols] = (dv_ref[:, cols] + dot_wide(k_ref[:, cols], state, NN)).astype(BF16)


def send(x, flip, shift):
    shards, heads = lax.axis_size("ctx"), lax.axis_size("head")
    pairs = [
        (c * heads + z, (c ^ flip) * heads + (z + shift) % heads)
        for c in range(shards)
        for z in range(heads)
    ]
    return lax.ppermute(x, ("ctx", "head"), pairs)


def exchange(mine, other, core, chip, chips, later):
    got = send(other, 1, 0)
    own = total = mine + got
    totals, flags = [], []
    if chips == 4:
        for flip in (1, 2, 3):
            totals.append(send(total, 2 * flip, 0))
            flags.append(((chip ^ flip) > chip) == later)
    else:
        step = 1
        while step < chips:
            totals.append(send(total, 2 * step, 0))
            flags.append(((chip & step) == 0) == later)
            total = total + totals[-1]
            step *= 2
    flags.append((core == 0) == later)
    return jnp.stack(flags).astype(jnp.int32), [mine, got, *totals], own


def on_device(query, key, value, block_mask, out_weight, cotangent):
    rows, width = query.shape
    heads = width // DH
    shards, count = lax.axis_size("ctx"), lax.axis_size("head")
    model = out_weight.shape[1]
    own = rows // count
    scale = 1.0 / math.sqrt(DH * rows * shards)
    blocks = block_mask.shape[0]
    ctx, place = lax.axis_index("ctx"), lax.axis_index("head")
    core, chip, chips = ctx & 1, ctx >> 1, shards // 2
    where = jnp.stack([place, ctx, core])
    flat, square = (rows, width), rows * rows * DH * heads
    pair = [((DH, DH), F32)] * 2
    tokens = ((2 * own, DH), BF16)
    product = 4 * own * DH * model

    board = chips == 4 and count == 4
    wide = model // (2 if board else chips)
    colour = (chip & 1) ^ (chip >> 1) if board else chip
    piece = lax.dynamic_slice(out_weight, (core * DH, colour * wide), (DH, wide))
    arrived = {1: send(piece, 0, 1), count - 1: send(piece, 0, -1)}
    mate_cotangent = send(cotangent, 1, 0)

    store, pre, other_pre, far, mine, other = call(
        functools.partial(forward_kernel, scale),
        [((2 * heads, rows, rows), BF16)]
        + [((rows, DH), F32)] * 2
        + [((rows, DH), BF16)]
        + pair,
        [jnp.stack([query, key, value])],
        [block_mask, where],
        [mate_cotangent],
        flops=7 * square,
    )
    far, other_pre = send(far, 1, 0), send(other_pre, 1, 0)
    (mine,) = hold([mine], [far, other_pre])
    flags, parts, total = exchange(mine, other, core, chip, chips, False)
    attn, keep, back = call(
        functools.partial(attn_kernel, scale),
        [((count, *tokens[0]), BF16), *pair],
        [*parts, query, far, pre, other_pre],
        [flags, where],
    )
    linear = [keep, send(back, 1, 0)]
    if board:
        arrived[1], arrived[3] = hold([arrived[1], arrived[3]], [keep])
    attn = lax.all_to_all(attn, "head", 0, 0, tiled=True)

    work = near_and_far if board else by_gathers
    both, across, joins, starts = work(
        attn, arrived, cotangent, mate_cotangent, out_weight, core, chip, colour, product
    )
    mixed, done = call(
        join_kernel, [((own, model), BF16), ((8, DH), F32)], joins, [jnp.stack(starts)]
    )

    g, mine, other = call(
        functools.partial(collect_kernel, scale, count),
        [(flat, BF16), *pair],
        [query, *both, *across],
        [where],
    )
    flags, parts, total = exchange(mine, other, core, chip, chips, True)
    grad_query, dk, dv = call(
        functools.partial(backward_kernel, scale, blocks),
        [(flat, BF16)] + [(flat, F32)] * 2,
        [query, key, value, g, store, *linear],
        [where],
        [total],
        flops=14 * square,
    )
    keep, back = call(carry_kernel, pair, parts, [flags], [dk])
    grad_key, grad_value = call(
        close_kernel,
        [(flat, BF16)] * 2,
        [key, value, dk, dv, keep, send(back, 1, 0)],
        [where],
        [done],
    )
    return mixed, grad_query, grad_key, grad_value


def near_and_far(attn, arrived, cotangent, mate_cotangent, weight, core, chip, colour, product):
    own, model = cotangent.shape
    wide = model // 2
    place = lax.axis_index("head")
    spots = jnp.stack([colour * wide, (1 - colour) * wide, core * DH, place])
    tokens = ((2 * own, DH), BF16)
    parts = [((own, wide), F32)] * 2
    all_arrays = [(cotangent, all_of, rows_at(0, own)), (mate_cotangent, all_of, rows_at(own, own))]
    whole = fetch((2 * own, model), *all_arrays)
    left = [
        fetch((2 * own, wide), *((a, columns(n, wide), put) for a, _, put in all_arrays))
        for n in range(2)
    ]

    def own_rows(ref, spots, *_):
        return ref.at[pl.ds(pl.multiple_of(spots[2], DH), DH)]

    def own_columns(n):
        return lambda ref, spots, *_: ref.at[
            pl.ds(pl.multiple_of(spots[2], DH), DH), pl.ds(pl.multiple_of(spots[n], DH), wide)
        ]

    def stacked(*arrays):
        return [(a, all_of, rows_at(n * DH, DH)) for n, a in enumerate(arrays)]

    arrived[2] = send(arrived[1], 0, 1)
    second = {1: send(arrived[1], 2, 0), 3: send(arrived[3], 4, 0)}
    mine, half = call(
        first_kernel,
        [tokens, ((2 * own, 2 * DH), F32)],
        [
            whole,
            fetch((DH, model), (weight, own_rows, all_of)),
            fetch((2 * DH, wide), *stacked(arrived[1], arrived[3])),
        ],
        [spots],
        room=6,
        flops=2 * product,
    )
    one, three, *cuts = call(
        second_kernel,
        [tokens] * 2 + [((DH, wide // 2), BF16)] * 2,
        [
            left[1],
            fetch((2 * DH, wide), *stacked(second[1], second[3])),
            half,
            fetch((DH, wide), (arrived[2], all_of, all_of)),
        ],
        [spots],
        room=6,
        flops=product,
    )
    second[2] = [send(cuts[0], 2, 0), send(cuts[1], 4, 0)]
    both = {0: mine, 1: send(one, 0, -1), 3: send(three, 0, -3)}
    across = {s: send(both[s], 1, 0) for s in (0, 1, 3)}
    half, part, mate_part = call(
        near_kernel,
        [((2 * own, DH), F32), *parts],
        [
            left[0],
            fetch(
                (4 * DH, wide),
                (weight, own_columns(0), rows_at(0, DH)),
                *((arrived[s], all_of, rows_at(s * DH, DH)) for s in (1, 2, 3)),
            ),
            attn,
        ],
        [spots],
        room=6,
        flops=2 * product,
    )
    joins = [part, send(mate_part, 1, 0)]
    quarters = [(a, all_of, columns_at(n * wide // 2, wide // 2)) for n, a in enumerate(second[2])]
    (two,) = call(
        last_kernel,
        [tokens],
        [left[1], fetch((DH, wide), *quarters), half],
        [spots],
        [both[1], both[3]],
        room=6,
        flops=product // 2,
    )
    both[2] = send(two, 0, -2)

    def quarter(n):
        return lambda ref, *_: ref.at[2 * DH : 3 * DH, n * wide // 2 : (n + 1) * wide // 2]

    part, mate_part = call(
        far_kernel,
        parts,
        [
            fetch(
                (4 * DH, wide),
                (weight, own_columns(1), rows_at(0, DH)),
                (second[1], all_of, rows_at(DH, DH)),
                (second[3], all_of, rows_at(3 * DH, DH)),
                *((a, all_of, quarter(n)) for n, a in enumerate(second[2])),
            ),
            attn,
        ],
        [spots],
        [both[2], across[0], across[1], across[3]],
        room=6,
        flops=2 * product,
    )
    joins += [part, send(mate_part, 1, 0)]
    across[2] = send(both[2], 1, 0)
    return [both[s] for s in range(4)], [across[s] for s in range(4)], joins, [spots[0], spots[1]]


def by_gathers(attn, arrived, cotangent, mate_cotangent, out_weight, core, chip, colour, product):
    own, model = cotangent.shape
    shards, count = lax.axis_size("ctx"), lax.axis_size("head")
    weight = lax.dynamic_slice_in_dim(out_weight, core * DH, DH, 0)
    zero = jnp.zeros((1,), jnp.int32)
    groups = [list(range(k, shards, 2)) for k in range(2)]
    for s in range(2, count - 1):
        arrived[s] = send(arrived[s - 1], 0, 1)
    chunks = [weight] + [
        lax.all_gather(arrived[s], "ctx", axis=1, tiled=True, axis_index_groups=groups)
        for s in range(1, count)
    ]
    both = []
    for s in range(count):
        (block,) = call(
            functools.partial(grad_kernel, True, 0),
            [((2 * own, DH), BF16)],
            [cotangent, mate_cotangent, chunks[s]],
            [zero],
            flops=product,
        )
        both.append(send(block, 0, -s) if s else block)
    part, mate_part = call(
        mixed_kernel,
        [((own, model), F32)] * 2,
        [attn, *chunks],
        [lax.axis_index("head").reshape(1)],
        room=6,
        flops=count * product,
    )
    return both, [send(b, 1, 0) for b in both], [part, send(mate_part, 1, 0)], [jnp.int32(0)]


def solution(mesh):
    return jax.shard_map(
        on_device,
        mesh=mesh,
        in_specs=(
            P("ctx", "head"),
            P("ctx", "head"),
            P("ctx", "head"),
            P("ctx", None),
            P("head", None),
            P(("ctx", "head"), None),
        ),
        out_specs=(P(("ctx", "head"), None), P("ctx", "head"), P("ctx", "head"), P("ctx", "head")),
        check_vma=False,
    )
```

```python
import functools
import math

import jax
import jax.numpy as jnp
from jax import lax
from jax.experimental import pallas as pl
from jax.experimental.pallas import tpu as pltpu
from jax.sharding import PartitionSpec as P

DH = 128
F32 = jnp.float32
BF16 = jnp.bfloat16
NN = ((1,), (0,))
NT = ((1,), (1,))
TN = ((0,), (0,))
MIB = 1 << 20


def dot(a, b, dims):
    return lax.dot_general(a, b, (dims, ((), ())), preferred_element_type=F32)


def dot_wide(a, b, dims):
    high = b.astype(BF16)
    low = (b - high.astype(F32)).astype(BF16)
    both = dot(a, jnp.concatenate([high, low], 1 - dims[1][0]), dims)
    return both[:, :DH] + both[:, DH:]


def fetch(shape, *parts):
    return (shape, parts)


def all_of(ref, *_):
    return ref


def columns(spot, wide, rows=slice(None)):
    def view(ref, spots, *_):
        return ref.at[rows, pl.ds(pl.multiple_of(spots[spot], DH), wide)]

    return view


def rows_at(first, count):
    return lambda ref, *_: ref.at[first : first + count]


def columns_at(first, count):
    return lambda ref, *_: ref.at[:, first : first + count]


def call(body, outs, args, smem=(), after=(), room=2, flops=1):
    arrays, specs, scratch = [], [], []
    for arg in args:
        if isinstance(arg, tuple):
            arrays += [part[0] for part in arg[1]]
            specs += [pl.BlockSpec(memory_space=pltpu.HBM) for _ in arg[1]]
            scratch.append(pltpu.VMEM(arg[0], arg[1][0][0].dtype))
        else:
            arrays.append(arg)
            specs.append(pl.BlockSpec(memory_space=pltpu.VMEM))
    copies = sum(len(arg[1]) for arg in args if isinstance(arg, tuple))
    held = len(scratch)
    if copies:
        scratch.append(pltpu.SemaphoreType.DMA((copies,)))

    def kernel(*refs):
        scalars, refs = refs[: len(smem)], list(refs[len(smem) :])
        ins, refs = refs[: len(arrays)], refs[len(arrays) + len(after) :]
        results, slots = refs[: len(outs)], refs[len(outs) :]
        given, started, slot = [], [], 0
        for arg in args:
            if not isinstance(arg, tuple):
                given.append(ins.pop(0))
                continue
            for _, source, target in arg[1]:
                copy = pltpu.make_async_copy(
                    source(ins.pop(0), *scalars),
                    target(slots[slot], *scalars),
                    slots[held].at[len(started)],
                )
                copy.start()
                started.append(copy)
            given.append(slots[slot])
            slot += 1
        for copy in started:
            copy.wait()
        body(*scalars, *given, *results)

    moved = sum(a.size * a.dtype.itemsize for a in arrays)
    moved += sum(math.prod(s) * jnp.dtype(t).itemsize for s, t in outs)
    return pl.pallas_call(
        kernel,
        out_shape=[jax.ShapeDtypeStruct(s, t) for s, t in outs],
        in_specs=[pl.BlockSpec(memory_space=pltpu.SMEM) for _ in smem]
        + specs
        + [pl.BlockSpec(memory_space=pl.ANY) for _ in after],
        out_specs=[pl.BlockSpec(memory_space=pltpu.VMEM) for _ in outs],
        scratch_shapes=scratch,
        compiler_params=pltpu.CompilerParams(vmem_limit_bytes=room * MIB),
        cost_estimate=pl.CostEstimate(
            flops=int(flops), bytes_accessed=int(moved), transcendentals=0
        ),
    )(*smem, *arrays, *after)


def hold(arrays, after):
    held = len(arrays)
    return pl.pallas_call(
        lambda *refs: None,
        out_shape=[jax.ShapeDtypeStruct(a.shape, a.dtype) for a in arrays],
        in_specs=[pl.BlockSpec(memory_space=pl.ANY) for _ in (*arrays, *after)],
        out_specs=[pl.BlockSpec(memory_space=pl.ANY) for _ in arrays],
        input_output_aliases={n: n for n in range(held)},
        cost_estimate=pl.CostEstimate(flops=1, bytes_accessed=1, transcendentals=0),
    )(*arrays, *after)


def lower_triangle(blk):
    return lax.broadcasted_iota(jnp.int32, (blk, blk), 0) >= lax.broadcasted_iota(
        jnp.int32, (blk, blk), 1
    )


def forward_kernel(
    scale,
    mask,
    where,
    all_ref,
    store_ref,
    mine_ref,
    other_ref,
    far_ref,
    mine_state_ref,
    other_state_ref,
):
    q_ref, k_ref, v_ref = (all_ref.at[n] for n in range(3))
    heads = [slice(h * DH, (h + 1) * DH) for h in range(2)]
    states = [dot(k_ref[:, cols], v_ref[:, cols], TN) for cols in heads]
    mine_state_ref[...], other_state_ref[...] = pick(where[2], states)
    rows, width = q_ref.shape
    count = mask.shape[0]
    blk = rows // count
    inv_root = 1.0 / math.sqrt(DH)
    triangle = lower_triangle(blk)
    sums = []
    for h in range(2):
        raw = dot(q_ref[:, heads[h]], k_ref[:, heads[h]], NT)
        probs, inner = [], []
        for i in range(count):
            own = raw[i * blk : (i + 1) * blk]
            scores, linear = [], []
            for j in range(i + 1):
                part = own[:, j * blk : (j + 1) * blk]
                keep = triangle if j == i else mask[i, j] > 0
                scores.append(jnp.where(keep, part * inv_root, -1e30))
                linear.append(jnp.where(triangle, part, 0.0) if j == i else part)
            empty = [jnp.zeros((blk, blk), F32)] * (count - 1 - i)
            scores = jnp.concatenate(scores, 1)
            expo = jnp.exp(scores - jnp.max(scores, -1, keepdims=True))
            share = expo / jnp.sum(expo, -1, keepdims=True)
            probs.append(jnp.concatenate([share, *empty], 1).astype(BF16))
            inner.append(jnp.concatenate([*linear, *empty], 1).astype(BF16))
        stacked = jnp.concatenate(probs + inner, 0)
        store_ref[h], store_ref[2 + h] = stacked[:rows], stacked[rows:]
        both = dot(stacked, v_ref[:, heads[h]], NN)
        sums.append(both[:rows] + scale * both[rows:])
    mine_ref[...], other_ref[...] = pick(where[2], sums)
    far_ref[...] = q_ref[:, pl.ds(pl.multiple_of((1 - where[2]) * DH, DH), DH)]


def pick(core, parts):
    return jnp.where(core == 0, parts[0], parts[1]), jnp.where(core == 0, parts[1], parts[0])


def both_heads(core, mine_ref, other_ref):
    mine, other = mine_ref[...], other_ref[...]
    return jnp.where(core == 0, mine, other), jnp.where(core == 0, other, mine)


def carry(flags, here_ref, got_ref, totals):
    carried = jnp.zeros(here_ref.shape, F32)
    for n, total in enumerate(totals):
        carried = carried + jnp.where(flags[n] > 0, total[...], 0.0)
    counts = flags[len(totals)] > 0
    keep = carried + jnp.where(counts, got_ref[...], 0.0)
    return keep, carried + jnp.where(counts, 0.0, here_ref[...])


def carry_kernel(flags, here_ref, got_ref, *refs):
    totals, (keep_ref, back_ref) = refs[:-2], refs[-2:]
    keep_ref[...], back_ref[...] = carry(flags, here_ref, got_ref, totals)


def attn_kernel(scale, flags, where, here_ref, got_ref, *refs):
    totals, refs = refs[:-7], refs[-7:]
    q_ref, far_ref, pre_ref, far_pre_ref, out_ref, keep_ref, back_ref = refs
    keep, back = carry(flags, here_ref, got_ref, totals)
    keep_ref[...], back_ref[...] = keep, back
    count = out_ref.shape[0]
    own = pre_ref.shape[0] // count
    cols = pl.ds(pl.multiple_of(where[2] * DH, DH), DH)
    mine = pre_ref[...] + scale * dot_wide(q_ref[:, cols], keep, NN)
    mate = far_pre_ref[...] + scale * dot_wide(far_ref[...], back, NN)
    for z in range(count):
        out_ref[z, :own] = mine[z * own : (z + 1) * own].astype(BF16)
        out_ref[z, own:] = mate[z * own : (z + 1) * own].astype(BF16)


def back_along(attn_ref, place):
    count = attn_ref.shape[0]
    return jnp.concatenate([attn_ref[lax.rem(place - s + count, count)] for s in range(count)], 1)


def first_kernel(spots, left_ref, weight_ref, right_ref, own_ref, half_ref):
    own_ref[...] = dot(left_ref[...], weight_ref[...], NT).astype(BF16)
    near = left_ref[:, pl.ds(pl.multiple_of(spots[0], DH), right_ref.shape[1])]
    half_ref[...] = dot(near, right_ref[...], NT)


def second_kernel(spots, left_ref, right_ref, half_ref, piece_ref, one_ref, three_ref, *cut_refs):
    wide = cut_refs[0].shape[1]
    for n, cut_ref in enumerate(cut_refs):
        cut_ref[...] = piece_ref[:, n * wide : (n + 1) * wide]
    total = (half_ref[...] + dot(left_ref[...], right_ref[...], NT)).astype(BF16)
    one_ref[...], three_ref[...] = total[:, :DH], total[:, DH:]


def last_kernel(spots, left_ref, right_ref, half_ref, out_ref):
    out_ref[...] = (half_ref[...] + dot(left_ref[...], right_ref[...], NT)).astype(BF16)


def near_kernel(spots, left_ref, right_ref, attn_ref, half_ref, own_out, mate_out):
    half_ref[...] = dot(left_ref[...], right_ref[2 * DH : 3 * DH], NT)
    far_kernel(spots, right_ref, attn_ref, own_out, mate_out)


def far_kernel(spots, right_ref, attn_ref, own_out, mate_out):
    own = own_out.shape[0]
    part = dot(back_along(attn_ref, spots[3]), right_ref[...], NN)
    own_out[...] = part[:own]
    mate_out[...] = part[own:]


def grad_kernel(whole, added, places, mine_ref, mate_ref, *refs):
    chunks, out_ref = refs[added:-1], refs[-1]
    total = refs[0][...] if added else None
    for j, chunk in enumerate(chunks):
        cols = slice(None) if whole else pl.ds(pl.multiple_of(places[j], DH), chunk.shape[1])
        left = jnp.concatenate([mine_ref[:, cols], mate_ref[:, cols]], 0)
        part = dot(left, chunk[...], NT)
        total = part if total is None else total + part
    out_ref[...] = total.astype(out_ref.dtype)


def mixed_kernel(where, attn_ref, *refs):
    chunks, (own_out, mate_out) = refs[:-2], refs[-2:]
    own = own_out.shape[0]
    right = jnp.concatenate([chunk[...] for chunk in chunks], 0)
    part = dot(back_along(attn_ref, where[0]), right, NN)
    own_out[...] = part[:own]
    mate_out[...] = part[own:]


def join_kernel(places, *refs):
    out_ref, done_ref = refs[-2:]
    done_ref[...] = jnp.zeros(done_ref.shape, F32)
    for n in range(len(refs) // 2 - 1):
        wide = refs[2 * n].shape[1]
        there = pl.ds(pl.multiple_of(places[n], DH), wide)
        out_ref[:, there] = (refs[2 * n][...] + refs[2 * n + 1][...]).astype(BF16)


def collect_kernel(scale, count, where, q_ref, *refs):
    direct, across = refs[:count], refs[count : 2 * count]
    g_ref, mine_ref, other_ref = refs[2 * count :]
    own = g_ref.shape[0] // count
    mine = pl.ds(pl.multiple_of(where[2] * DH, DH), DH)
    mate = pl.ds(pl.multiple_of((1 - where[2]) * DH, DH), DH)
    for s in range(count):
        block = lax.rem(where[0] + s, count)
        here = pl.ds(pl.multiple_of(block * own, own), own)
        g_ref[here, mine] = direct[s][:own]
        g_ref[here, mate] = across[s][own:]
    heads = [slice(h * DH, (h + 1) * DH) for h in range(2)]
    parts = [scale * dot(q_ref[:, cols], g_ref[:, cols], TN) for cols in heads]
    mine_ref[...], other_ref[...] = pick(where[2], parts)


def backward_kernel(
    scale, where, q_ref, k_ref, v_ref, g_ref, store_ref, mine_ref, other_ref, dq_ref, dk_ref, dv_ref
):
    rows, width = q_ref.shape
    inv_root = 1.0 / math.sqrt(DH)
    triangle = lower_triangle(rows)
    states = both_heads(where[2], mine_ref, other_ref)
    for h in range(width // DH):
        cols = slice(h * DH, (h + 1) * DH)
        q, k, v, g = q_ref[:, cols], k_ref[:, cols], v_ref[:, cols], g_ref[:, cols]
        probs, inner = store_ref[h], store_ref[2 + h]
        dprod = dot(g, v, NT)
        delta = jnp.sum(g.astype(F32) * dot(probs, v, NN), -1, keepdims=True)
        dscore = (probs.astype(F32) * (dprod - delta) * inv_root).astype(BF16)
        dinner = jnp.where(triangle, dprod, 0.0).astype(BF16)
        left = dot(jnp.concatenate([dscore, dinner], 0), k, NN)
        linear = left[rows:] + dot_wide(g, states[h], NT)
        dq_ref[:, cols] = (left[:rows] + scale * linear).astype(BF16)
        dk = dot(jnp.concatenate([dscore, dinner], 1), q, TN)
        dk_ref[:, cols] = dk[:rows] + scale * dk[rows:]
        dv = dot(jnp.concatenate([probs, inner], 1), g, TN)
        dv_ref[:, cols] = dv[:rows] + scale * dv[rows:]


def close_kernel(where, k_ref, v_ref, dk_ref, dv_ref, mine_ref, other_ref, gk_ref, gv_ref):
    states = both_heads(where[2], mine_ref, other_ref)
    for h in range(k_ref.shape[1] // DH):
        cols = slice(h * DH, (h + 1) * DH)
        state = states[h]
        gk_ref[:, cols] = (dk_ref[:, cols] + dot_wide(v_ref[:, cols], state, NT)).astype(BF16)
        gv_ref[:, cols] = (dv_ref[:, cols] + dot_wide(k_ref[:, cols], state, NN)).astype(BF16)


def send(x, flip, shift):
    shards, heads = lax.axis_size("ctx"), lax.axis_size("head")
    pairs = [
        (c * heads + z, (c ^ flip) * heads + (z + shift) % heads)
        for c in range(shards)
        for z in range(heads)
    ]
    return lax.ppermute(x, ("ctx", "head"), pairs)


def exchange(mine, other, core, chip, chips, later):
    got = send(other, 1, 0)
    own = total = mine + got
    totals, flags = [], []
    if chips == 4:
        for flip in (1, 2, 3):
            totals.append(send(total, 2 * flip, 0))
            flags.append(((chip ^ flip) > chip) == later)
    else:
        step = 1
        while step < chips:
            totals.append(send(total, 2 * step, 0))
            flags.append(((chip & step) == 0) == later)
            total = total + totals[-1]
            step *= 2
    flags.append((core == 0) == later)
    return jnp.stack(flags).astype(jnp.int32), [mine, got, *totals], own


def on_device(query, key, value, block_mask, out_weight, cotangent):
    rows, width = query.shape
    heads = width // DH
    shards, count = lax.axis_size("ctx"), lax.axis_size("head")
    model = out_weight.shape[1]
    own = rows // count
    scale = 1.0 / math.sqrt(DH * rows * shards)
    ctx, place = lax.axis_index("ctx"), lax.axis_index("head")
    core, chip, chips = ctx & 1, ctx >> 1, shards // 2
    where = jnp.stack([place, ctx, core])
    flat, square = (rows, width), rows * rows * DH * heads
    pair = [((DH, DH), F32)] * 2
    tokens = ((2 * own, DH), BF16)
    product = 4 * own * DH * model

    board = chips == 4 and count == 4
    wide = model // (2 if board else chips)
    colour = (chip & 1) ^ (chip >> 1) if board else chip
    piece = lax.dynamic_slice(out_weight, (core * DH, colour * wide), (DH, wide))
    arrived = {1: send(piece, 0, 1), count - 1: send(piece, 0, -1)}
    mate_cotangent = send(cotangent, 1, 0)

    store, pre, other_pre, far, mine, other = call(
        functools.partial(forward_kernel, scale),
        [((2 * heads, rows, rows), BF16)]
        + [((rows, DH), F32)] * 2
        + [((rows, DH), BF16)]
        + pair,
        [jnp.stack([query, key, value])],
        [block_mask, where],
        [mate_cotangent],
        flops=7 * square,
    )
    far, other_pre = send(far, 1, 0), send(other_pre, 1, 0)
    (mine,) = hold([mine], [far, other_pre])
    flags, parts, total = exchange(mine, other, core, chip, chips, False)
    attn, keep, back = call(
        functools.partial(attn_kernel, scale),
        [((count, *tokens[0]), BF16), *pair],
        [*parts, query, far, pre, other_pre],
        [flags, where],
    )
    linear = [keep, send(back, 1, 0)]
    if board:
        arrived[1], arrived[3] = hold([arrived[1], arrived[3]], [keep])
    attn = lax.all_to_all(attn, "head", 0, 0, tiled=True)

    work = near_and_far if board else by_gathers
    both, across, joins, starts = work(
        attn, arrived, cotangent, mate_cotangent, out_weight, core, chip, colour, product
    )
    mixed, done = call(
        join_kernel, [((own, model), BF16), ((8, DH), F32)], joins, [jnp.stack(starts)]
    )

    g, mine, other = call(
        functools.partial(collect_kernel, scale, count),
        [(flat, BF16), *pair],
        [query, *both, *across],
        [where],
    )
    flags, parts, total = exchange(mine, other, core, chip, chips, True)
    grad_query, dk, dv = call(
        functools.partial(backward_kernel, scale),
        [(flat, BF16)] + [(flat, F32)] * 2,
        [query, key, value, g, store, *linear],
        [where],
        [total],
        flops=14 * square,
    )
    keep, back = call(carry_kernel, pair, parts, [flags], [dk])
    grad_key, grad_value = call(
        close_kernel,
        [(flat, BF16)] * 2,
        [key, value, dk, dv, keep, send(back, 1, 0)],
        [where],
        [done],
    )
    return mixed, grad_query, grad_key, grad_value


def near_and_far(attn, arrived, cotangent, mate_cotangent, weight, core, chip, colour, product):
    own, model = cotangent.shape
    wide = model // 2
    place = lax.axis_index("head")
    spots = jnp.stack([colour * wide, (1 - colour) * wide, core * DH, place])
    tokens = ((2 * own, DH), BF16)
    parts = [((own, wide), F32)] * 2
    all_arrays = [(cotangent, all_of, rows_at(0, own)), (mate_cotangent, all_of, rows_at(own, own))]
    whole = fetch((2 * own, model), *all_arrays)
    left = [
        fetch((2 * own, wide), *((a, columns(n, wide), put) for a, _, put in all_arrays))
        for n in range(2)
    ]

    def own_rows(ref, spots, *_):
        return ref.at[pl.ds(pl.multiple_of(spots[2], DH), DH)]

    def own_columns(n):
        return lambda ref, spots, *_: ref.at[
            pl.ds(pl.multiple_of(spots[2], DH), DH), pl.ds(pl.multiple_of(spots[n], DH), wide)
        ]

    def stacked(*arrays):
        return [(a, all_of, rows_at(n * DH, DH)) for n, a in enumerate(arrays)]

    arrived[2] = send(arrived[1], 0, 1)
    second = {1: send(arrived[1], 2, 0), 3: send(arrived[3], 4, 0)}
    mine, half = call(
        first_kernel,
        [tokens, ((2 * own, 2 * DH), F32)],
        [
            whole,
            fetch((DH, model), (weight, own_rows, all_of)),
            fetch((2 * DH, wide), *stacked(arrived[1], arrived[3])),
        ],
        [spots],
        room=6,
        flops=2 * product,
    )
    one, three, *cuts = call(
        second_kernel,
        [tokens] * 2 + [((DH, wide // 2), BF16)] * 2,
        [
            left[1],
            fetch((2 * DH, wide), *stacked(second[1], second[3])),
            half,
            fetch((DH, wide), (arrived[2], all_of, all_of)),
        ],
        [spots],
        room=6,
        flops=product,
    )
    second[2] = [send(cuts[0], 2, 0), send(cuts[1], 4, 0)]
    both = {0: mine, 1: send(one, 0, -1), 3: send(three, 0, -3)}
    across = {s: send(both[s], 1, 0) for s in (0, 1, 3)}
    half, part, mate_part = call(
        near_kernel,
        [((2 * own, DH), F32), *parts],
        [
            left[0],
            fetch(
                (4 * DH, wide),
                (weight, own_columns(0), rows_at(0, DH)),
                *((arrived[s], all_of, rows_at(s * DH, DH)) for s in (1, 2, 3)),
            ),
            attn,
        ],
        [spots],
        room=6,
        flops=2 * product,
    )
    joins = [part, send(mate_part, 1, 0)]
    quarters = [(a, all_of, columns_at(n * wide // 2, wide // 2)) for n, a in enumerate(second[2])]
    (two,) = call(
        last_kernel,
        [tokens],
        [left[1], fetch((DH, wide), *quarters), half],
        [spots],
        [both[1], both[3]],
        room=6,
        flops=product // 2,
    )
    both[2] = send(two, 0, -2)

    def quarter(n):
        return lambda ref, *_: ref.at[2 * DH : 3 * DH, n * wide // 2 : (n + 1) * wide // 2]

    part, mate_part = call(
        far_kernel,
        parts,
        [
            fetch(
                (4 * DH, wide),
                (weight, own_columns(1), rows_at(0, DH)),
                (second[1], all_of, rows_at(DH, DH)),
                (second[3], all_of, rows_at(3 * DH, DH)),
                *((a, all_of, quarter(n)) for n, a in enumerate(second[2])),
            ),
            attn,
        ],
        [spots],
        [both[2], across[0], across[1], across[3]],
        room=6,
        flops=2 * product,
    )
    joins += [part, send(mate_part, 1, 0)]
    across[2] = send(both[2], 1, 0)
    return [both[s] for s in range(4)], [across[s] for s in range(4)], joins, [spots[0], spots[1]]


def by_gathers(attn, arrived, cotangent, mate_cotangent, out_weight, core, chip, colour, product):
    own, model = cotangent.shape
    shards, count = lax.axis_size("ctx"), lax.axis_size("head")
    weight = lax.dynamic_slice_in_dim(out_weight, core * DH, DH, 0)
    zero = jnp.zeros((1,), jnp.int32)
    groups = [list(range(k, shards, 2)) for k in range(2)]
    for s in range(2, count - 1):
        arrived[s] = send(arrived[s - 1], 0, 1)
    chunks = [weight] + [
        lax.all_gather(arrived[s], "ctx", axis=1, tiled=True, axis_index_groups=groups)
        for s in range(1, count)
    ]
    both = []
    for s in range(count):
        (block,) = call(
            functools.partial(grad_kernel, True, 0),
            [((2 * own, DH), BF16)],
            [cotangent, mate_cotangent, chunks[s]],
            [zero],
            flops=product,
        )
        both.append(send(block, 0, -s) if s else block)
    part, mate_part = call(
        mixed_kernel,
        [((own, model), F32)] * 2,
        [attn, *chunks],
        [lax.axis_index("head").reshape(1)],
        room=6,
        flops=count * product,
    )
    return both, [send(b, 1, 0) for b in both], [part, send(mate_part, 1, 0)], [jnp.int32(0)]


def solution(mesh):
    return jax.shard_map(
        on_device,
        mesh=mesh,
        in_specs=(
            P("ctx", "head"),
            P("ctx", "head"),
            P("ctx", "head"),
            P("ctx", None),
            P("head", None),
            P(("ctx", "head"), None),
        ),
        out_specs=(P(("ctx", "head"), None), P("ctx", "head"), P("ctx", "head"), P("ctx", "head")),
        check_vma=False,
    )
```

```python
import functools
import math

import jax
import jax.numpy as jnp
from jax import lax
from jax.experimental import pallas as pl
from jax.experimental.pallas import tpu as pltpu
from jax.sharding import PartitionSpec as P

DH = 128
F32 = jnp.float32
BF16 = jnp.bfloat16
NN = ((1,), (0,))
NT = ((1,), (1,))
TN = ((0,), (0,))
MIB = 1 << 20


def dot(a, b, dims):
    return lax.dot_general(a, b, (dims, ((), ())), preferred_element_type=F32)


def dot_wide(a, b, dims):
    high = b.astype(BF16)
    low = (b - high.astype(F32)).astype(BF16)
    both = dot(a, jnp.concatenate([high, low], 1 - dims[1][0]), dims)
    return both[:, :DH] + both[:, DH:]


def fetch(shape, *parts):
    return (shape, parts)


def all_of(ref, *_):
    return ref


def columns(spot, wide, rows=slice(None)):
    def view(ref, spots, *_):
        return ref.at[rows, pl.ds(pl.multiple_of(spots[spot], DH), wide)]

    return view


def rows_at(first, count):
    return lambda ref, *_: ref.at[first : first + count]


def columns_at(first, count):
    return lambda ref, *_: ref.at[:, first : first + count]


def call(body, outs, args, smem=(), after=(), room=2, flops=1, lazy=False):
    arrays, specs, scratch = [], [], []
    for arg in args:
        if isinstance(arg, tuple):
            arrays += [part[0] for part in arg[1]]
            specs += [pl.BlockSpec(memory_space=pltpu.HBM) for _ in arg[1]]
            scratch.append(pltpu.VMEM(arg[0], arg[1][0][0].dtype))
        else:
            arrays.append(arg)
            specs.append(pl.BlockSpec(memory_space=pltpu.VMEM))
    copies = sum(len(arg[1]) for arg in args if isinstance(arg, tuple))
    held = len(scratch)
    if copies:
        scratch.append(pltpu.SemaphoreType.DMA((copies,)))

    def kernel(*refs):
        scalars, refs = refs[: len(smem)], list(refs[len(smem) :])
        ins, refs = refs[: len(arrays)], refs[len(arrays) + len(after) :]
        results, slots = refs[: len(outs)], refs[len(outs) :]
        given, started, slot, groups = [], [], 0, []
        for arg in args:
            if not isinstance(arg, tuple):
                given.append(ins.pop(0))
                continue
            for _, source, target in arg[1]:
                copy = pltpu.make_async_copy(
                    source(ins.pop(0), *scalars),
                    target(slots[slot], *scalars),
                    slots[held].at[len(started)],
                )
                copy.start()
                started.append(copy)
            given.append(slots[slot])
            groups.append(started[sum(len(group) for group in groups) :])
            slot += 1

        def ready(n):
            for copy in groups[n]:
                copy.wait()

        if lazy:
            body(ready, *scalars, *given, *results)
            return
        for n in range(len(groups)):
            ready(n)
        body(*scalars, *given, *results)

    moved = sum(a.size * a.dtype.itemsize for a in arrays)
    moved += sum(math.prod(s) * jnp.dtype(t).itemsize for s, t in outs)
    return pl.pallas_call(
        kernel,
        out_shape=[jax.ShapeDtypeStruct(s, t) for s, t in outs],
        in_specs=[pl.BlockSpec(memory_space=pltpu.SMEM) for _ in smem]
        + specs
        + [pl.BlockSpec(memory_space=pl.ANY) for _ in after],
        out_specs=[pl.BlockSpec(memory_space=pltpu.VMEM) for _ in outs],
        scratch_shapes=scratch,
        compiler_params=pltpu.CompilerParams(vmem_limit_bytes=room * MIB),
        cost_estimate=pl.CostEstimate(
            flops=int(flops), bytes_accessed=int(moved), transcendentals=0
        ),
    )(*smem, *arrays, *after)


def hold(arrays, after):
    held = len(arrays)
    return pl.pallas_call(
        lambda *refs: None,
        out_shape=[jax.ShapeDtypeStruct(a.shape, a.dtype) for a in arrays],
        in_specs=[pl.BlockSpec(memory_space=pl.ANY) for _ in (*arrays, *after)],
        out_specs=[pl.BlockSpec(memory_space=pl.ANY) for _ in arrays],
        input_output_aliases={n: n for n in range(held)},
        cost_estimate=pl.CostEstimate(flops=1, bytes_accessed=1, transcendentals=0),
    )(*arrays, *after)


def lower_triangle(blk):
    return lax.broadcasted_iota(jnp.int32, (blk, blk), 0) >= lax.broadcasted_iota(
        jnp.int32, (blk, blk), 1
    )


def forward_kernel(
    scale,
    mask,
    where,
    all_ref,
    store_ref,
    mine_ref,
    other_ref,
    far_ref,
    mine_state_ref,
    other_state_ref,
):
    q_ref, k_ref, v_ref = (all_ref.at[n] for n in range(3))
    heads = [slice(h * DH, (h + 1) * DH) for h in range(2)]
    states = [dot(k_ref[:, cols], v_ref[:, cols], TN) for cols in heads]
    mine_state_ref[...], other_state_ref[...] = pick(where[2], states)
    rows, width = q_ref.shape
    count = mask.shape[0]
    blk = rows // count
    inv_root = 1.0 / math.sqrt(DH)
    triangle = lower_triangle(blk)
    sums = []
    for h in range(2):
        raw = dot(q_ref[:, heads[h]], k_ref[:, heads[h]], NT)
        probs, inner = [], []
        for i in range(count):
            own = raw[i * blk : (i + 1) * blk]
            scores, linear = [], []
            for j in range(i + 1):
                part = own[:, j * blk : (j + 1) * blk]
                keep = triangle if j == i else mask[i, j] > 0
                scores.append(jnp.where(keep, part * inv_root, -1e30))
                linear.append(jnp.where(triangle, part, 0.0) if j == i else part)
            empty = [jnp.zeros((blk, blk), F32)] * (count - 1 - i)
            scores = jnp.concatenate(scores, 1)
            expo = jnp.exp(scores - jnp.max(scores, -1, keepdims=True))
            share = expo / jnp.sum(expo, -1, keepdims=True)
            probs.append(jnp.concatenate([share, *empty], 1).astype(BF16))
            inner.append(jnp.concatenate([*linear, *empty], 1).astype(BF16))
        stacked = jnp.concatenate(probs + inner, 0)
        store_ref[h], store_ref[2 + h] = stacked[:rows], stacked[rows:]
        both = dot(stacked, v_ref[:, heads[h]], NN)
        sums.append(both[:rows] + scale * both[rows:])
    mine_ref[...], other_ref[...] = pick(where[2], sums)
    far_ref[...] = q_ref[:, pl.ds(pl.multiple_of((1 - where[2]) * DH, DH), DH)]


def pick(core, parts):
    return jnp.where(core == 0, parts[0], parts[1]), jnp.where(core == 0, parts[1], parts[0])


def both_heads(core, mine_ref, other_ref):
    mine, other = mine_ref[...], other_ref[...]
    return jnp.where(core == 0, mine, other), jnp.where(core == 0, other, mine)


def carry(flags, here_ref, got_ref, totals):
    carried = jnp.zeros(here_ref.shape, F32)
    for n, total in enumerate(totals):
        carried = carried + jnp.where(flags[n] > 0, total[...], 0.0)
    counts = flags[len(totals)] > 0
    keep = carried + jnp.where(counts, got_ref[...], 0.0)
    return keep, carried + jnp.where(counts, 0.0, here_ref[...])


def carry_kernel(flags, here_ref, got_ref, *refs):
    totals, (keep_ref, back_ref) = refs[:-2], refs[-2:]
    keep_ref[...], back_ref[...] = carry(flags, here_ref, got_ref, totals)


def attn_kernel(scale, flags, where, here_ref, got_ref, *refs):
    totals, refs = refs[:-7], refs[-7:]
    q_ref, far_ref, pre_ref, far_pre_ref, out_ref, keep_ref, back_ref = refs
    keep, back = carry(flags, here_ref, got_ref, totals)
    keep_ref[...], back_ref[...] = keep, back
    count = out_ref.shape[0]
    own = pre_ref.shape[0] // count
    cols = pl.ds(pl.multiple_of(where[2] * DH, DH), DH)
    mine = pre_ref[...] + scale * dot_wide(q_ref[:, cols], keep, NN)
    mate = far_pre_ref[...] + scale * dot_wide(far_ref[...], back, NN)
    for z in range(count):
        out_ref[z, :own] = mine[z * own : (z + 1) * own].astype(BF16)
        out_ref[z, own:] = mate[z * own : (z + 1) * own].astype(BF16)


def back_along(attn_ref, place):
    count = attn_ref.shape[0]
    return jnp.concatenate([attn_ref[lax.rem(place - s + count, count)] for s in range(count)], 1)


def first_kernel(ready, spots, left_ref, weight_ref, right_ref, own_ref, half_ref):
    ready(0)
    ready(1)
    own_ref[...] = dot(left_ref[...], weight_ref[...], NT).astype(BF16)
    ready(2)
    near = left_ref[:, pl.ds(pl.multiple_of(spots[0], DH), right_ref.shape[1])]
    half_ref[...] = dot(near, right_ref[...], NT)


def second_kernel(spots, left_ref, right_ref, half_ref, piece_ref, one_ref, three_ref, *cut_refs):
    wide = cut_refs[0].shape[1]
    for n, cut_ref in enumerate(cut_refs):
        cut_ref[...] = piece_ref[:, n * wide : (n + 1) * wide]
    total = (half_ref[...] + dot(left_ref[...], right_ref[...], NT)).astype(BF16)
    one_ref[...], three_ref[...] = total[:, :DH], total[:, DH:]


def last_kernel(spots, left_ref, right_ref, half_ref, out_ref):
    out_ref[...] = (half_ref[...] + dot(left_ref[...], right_ref[...], NT)).astype(BF16)


def half_kernel(spots, left_ref, right_ref, half_ref):
    half_ref[...] = dot(left_ref[...], right_ref[...], NT)


def halves_kernel(ready, spots, attn_ref, *refs):
    rights, outs = refs[:2], refs[2:]
    own = outs[0].shape[0]
    ready(0)
    left = back_along(attn_ref, spots[3])
    for n, right_ref in enumerate(rights):
        ready(1 + n)
        part = dot(left, right_ref[...], NN)
        outs[2 * n][...] = part[:own]
        outs[2 * n + 1][...] = part[own:]


def grad_kernel(whole, added, places, mine_ref, mate_ref, *refs):
    chunks, out_ref = refs[added:-1], refs[-1]
    total = refs[0][...] if added else None
    for j, chunk in enumerate(chunks):
        cols = slice(None) if whole else pl.ds(pl.multiple_of(places[j], DH), chunk.shape[1])
        left = jnp.concatenate([mine_ref[:, cols], mate_ref[:, cols]], 0)
        part = dot(left, chunk[...], NT)
        total = part if total is None else total + part
    out_ref[...] = total.astype(out_ref.dtype)


def mixed_kernel(where, attn_ref, *refs):
    chunks, (own_out, mate_out) = refs[:-2], refs[-2:]
    own = own_out.shape[0]
    right = jnp.concatenate([chunk[...] for chunk in chunks], 0)
    part = dot(back_along(attn_ref, where[0]), right, NN)
    own_out[...] = part[:own]
    mate_out[...] = part[own:]


def join_kernel(places, *refs):
    out_ref, done_ref = refs[-2:]
    done_ref[...] = jnp.zeros(done_ref.shape, F32)
    for n in range(len(refs) // 2 - 1):
        wide = refs[2 * n].shape[1]
        there = pl.ds(pl.multiple_of(places[n], DH), wide)
        out_ref[:, there] = (refs[2 * n][...] + refs[2 * n + 1][...]).astype(BF16)


def collect_kernel(scale, count, where, q_ref, *refs):
    direct, across = refs[:count], refs[count : 2 * count]
    g_ref, mine_ref, other_ref = refs[2 * count :]
    own = g_ref.shape[0] // count
    mine = pl.ds(pl.multiple_of(where[2] * DH, DH), DH)
    mate = pl.ds(pl.multiple_of((1 - where[2]) * DH, DH), DH)
    for s in range(count):
        block = lax.rem(where[0] + s, count)
        here = pl.ds(pl.multiple_of(block * own, own), own)
        g_ref[here, mine] = direct[s][:own]
        g_ref[here, mate] = across[s][own:]
    heads = [slice(h * DH, (h + 1) * DH) for h in range(2)]
    parts = [scale * dot(q_ref[:, cols], g_ref[:, cols], TN) for cols in heads]
    mine_ref[...], other_ref[...] = pick(where[2], parts)


def backward_kernel(
    scale, where, q_ref, k_ref, v_ref, g_ref, store_ref, mine_ref, other_ref, dq_ref, dk_ref, dv_ref
):
    rows, width = q_ref.shape
    inv_root = 1.0 / math.sqrt(DH)
    triangle = lower_triangle(rows)
    states = both_heads(where[2], mine_ref, other_ref)
    for h in range(width // DH):
        cols = slice(h * DH, (h + 1) * DH)
        q, k, v, g = q_ref[:, cols], k_ref[:, cols], v_ref[:, cols], g_ref[:, cols]
        probs, inner = store_ref[h], store_ref[2 + h]
        dprod = dot(g, v, NT)
        delta = jnp.sum(g.astype(F32) * dot(probs, v, NN), -1, keepdims=True)
        dscore = (probs.astype(F32) * (dprod - delta) * inv_root).astype(BF16)
        dinner = jnp.where(triangle, dprod, 0.0).astype(BF16)
        left = dot(jnp.concatenate([dscore, dinner], 0), k, NN)
        linear = left[rows:] + dot_wide(g, states[h], NT)
        dq_ref[:, cols] = (left[:rows] + scale * linear).astype(BF16)
        dk = dot(jnp.concatenate([dscore, dinner], 1), q, TN)
        dk_ref[:, cols] = dk[:rows] + scale * dk[rows:]
        dv = dot(jnp.concatenate([probs, inner], 1), g, TN)
        dv_ref[:, cols] = dv[:rows] + scale * dv[rows:]


def close_kernel(where, k_ref, v_ref, dk_ref, dv_ref, mine_ref, other_ref, gk_ref, gv_ref):
    states = both_heads(where[2], mine_ref, other_ref)
    for h in range(k_ref.shape[1] // DH):
        cols = slice(h * DH, (h + 1) * DH)
        state = states[h]
        gk_ref[:, cols] = (dk_ref[:, cols] + dot_wide(v_ref[:, cols], state, NT)).astype(BF16)
        gv_ref[:, cols] = (dv_ref[:, cols] + dot_wide(k_ref[:, cols], state, NN)).astype(BF16)


def send(x, flip, shift):
    shards, heads = lax.axis_size("ctx"), lax.axis_size("head")
    pairs = [
        (c * heads + z, (c ^ flip) * heads + (z + shift) % heads)
        for c in range(shards)
        for z in range(heads)
    ]
    return lax.ppermute(x, ("ctx", "head"), pairs)


def exchange(mine, other, core, chip, chips, later):
    got = send(other, 1, 0)
    own = total = mine + got
    totals, flags = [], []
    if chips == 4:
        for flip in (1, 2, 3):
            totals.append(send(total, 2 * flip, 0))
            flags.append(((chip ^ flip) > chip) == later)
    else:
        step = 1
        while step < chips:
            totals.append(send(total, 2 * step, 0))
            flags.append(((chip & step) == 0) == later)
            total = total + totals[-1]
            step *= 2
    flags.append((core == 0) == later)
    return jnp.stack(flags).astype(jnp.int32), [mine, got, *totals], own


def on_device(query, key, value, block_mask, out_weight, cotangent):
    rows, width = query.shape
    heads = width // DH
    shards, count = lax.axis_size("ctx"), lax.axis_size("head")
    model = out_weight.shape[1]
    own = rows // count
    scale = 1.0 / math.sqrt(DH * rows * shards)
    ctx, place = lax.axis_index("ctx"), lax.axis_index("head")
    core, chip, chips = ctx & 1, ctx >> 1, shards // 2
    where = jnp.stack([place, ctx, core])
    flat, square = (rows, width), rows * rows * DH * heads
    pair = [((DH, DH), F32)] * 2
    tokens = ((2 * own, DH), BF16)
    product = 4 * own * DH * model

    board = chips == 4 and count == 4
    wide = model // (2 if board else chips)
    colour = (chip & 1) ^ (chip >> 1) if board else chip
    piece = lax.dynamic_slice(out_weight, (core * DH, colour * wide), (DH, wide))
    arrived = {1: send(piece, 0, 1), count - 1: send(piece, 0, -1)}
    mate_cotangent = send(cotangent, 1, 0)

    store, pre, other_pre, far, mine, other = call(
        functools.partial(forward_kernel, scale),
        [((2 * heads, rows, rows), BF16)]
        + [((rows, DH), F32)] * 2
        + [((rows, DH), BF16)]
        + pair,
        [jnp.stack([query, key, value])],
        [block_mask, where],
        [mate_cotangent],
        flops=7 * square,
    )
    far, other_pre = send(far, 1, 0), send(other_pre, 1, 0)
    (mine,) = hold([mine], [far, other_pre])
    flags, parts, total = exchange(mine, other, core, chip, chips, False)
    attn, keep, back = call(
        functools.partial(attn_kernel, scale),
        [((count, *tokens[0]), BF16), *pair],
        [*parts, query, far, pre, other_pre],
        [flags, where],
    )
    linear = [keep, send(back, 1, 0)]
    if board:
        arrived[1], arrived[3] = hold([arrived[1], arrived[3]], [keep])
    work = near_and_far if board else by_gathers
    both, across, joins, starts = work(
        attn, arrived, cotangent, mate_cotangent, out_weight, core, chip, colour, product
    )
    mixed, done = call(
        join_kernel, [((own, model), BF16), ((8, DH), F32)], joins, [jnp.stack(starts)]
    )

    g, mine, other = call(
        functools.partial(collect_kernel, scale, count),
        [(flat, BF16), *pair],
        [query, *both, *across],
        [where],
    )
    flags, parts, total = exchange(mine, other, core, chip, chips, True)
    grad_query, dk, dv = call(
        functools.partial(backward_kernel, scale),
        [(flat, BF16)] + [(flat, F32)] * 2,
        [query, key, value, g, store, *linear],
        [where],
        [total],
        flops=14 * square,
    )
    keep, back = call(carry_kernel, pair, parts, [flags], [dk])
    grad_key, grad_value = call(
        close_kernel,
        [(flat, BF16)] * 2,
        [key, value, dk, dv, keep, send(back, 1, 0)],
        [where],
        [done],
    )
    return mixed, grad_query, grad_key, grad_value


def near_and_far(attn, arrived, cotangent, mate_cotangent, weight, core, chip, colour, product):
    own, model = cotangent.shape
    wide = model // 2
    place = lax.axis_index("head")
    spots = jnp.stack([colour * wide, (1 - colour) * wide, core * DH, place])
    tokens = ((2 * own, DH), BF16)
    parts = [((own, wide), F32)] * 2
    all_arrays = [(cotangent, all_of, rows_at(0, own)), (mate_cotangent, all_of, rows_at(own, own))]
    whole = fetch((2 * own, model), *all_arrays)
    left = [
        fetch((2 * own, wide), *((a, columns(n, wide), put) for a, _, put in all_arrays))
        for n in range(2)
    ]

    def own_rows(ref, spots, *_):
        return ref.at[pl.ds(pl.multiple_of(spots[2], DH), DH)]

    def own_columns(n):
        return lambda ref, spots, *_: ref.at[
            pl.ds(pl.multiple_of(spots[2], DH), DH), pl.ds(pl.multiple_of(spots[n], DH), wide)
        ]

    def stacked(*arrays):
        return [(a, all_of, rows_at(n * DH, DH)) for n, a in enumerate(arrays)]

    arrived[2] = send(arrived[1], 0, 1)
    second = {1: send(arrived[1], 2, 0), 3: send(arrived[3], 4, 0)}
    mine, half = call(
        first_kernel,
        [tokens, ((2 * own, 2 * DH), F32)],
        [
            whole,
            fetch((DH, model), (weight, own_rows, all_of)),
            fetch((2 * DH, wide), *stacked(arrived[1], arrived[3])),
        ],
        [spots],
        lazy=True,
        room=6,
        flops=2 * product,
    )
    one, three, *cuts = call(
        second_kernel,
        [tokens] * 2 + [((DH, wide // 2), BF16)] * 2,
        [
            left[1],
            fetch((2 * DH, wide), *stacked(second[1], second[3])),
            half,
            fetch((DH, wide), (arrived[2], all_of, all_of)),
        ],
        [spots],
        room=6,
        flops=product,
    )
    second[2] = [send(cuts[0], 2, 0), send(cuts[1], 4, 0)]
    both = {0: mine, 1: send(one, 0, -1), 3: send(three, 0, -3)}
    across = {s: send(both[s], 1, 0) for s in (0, 1, 3)}
    attn = lax.all_to_all(*hold([attn], [both[1], both[3]]), "head", 0, 0, tiled=True)
    (half,) = call(
        half_kernel,
        [((2 * own, DH), F32)],
        [left[0], fetch((DH, wide), (arrived[2], all_of, all_of))],
        [spots],
        room=6,
        flops=product // 2,
    )
    quarters = [(a, all_of, columns_at(n * wide // 2, wide // 2)) for n, a in enumerate(second[2])]
    (two,) = call(
        last_kernel,
        [tokens],
        [left[1], fetch((DH, wide), *quarters), half],
        [spots],
        [both[1], both[3]],
        room=6,
        flops=product // 2,
    )
    both[2] = send(two, 0, -2)

    def quarter(n):
        return lambda ref, *_: ref.at[2 * DH : 3 * DH, n * wide // 2 : (n + 1) * wide // 2]

    parts = call(
        halves_kernel,
        parts * 2,
        [
            fetch(attn.shape, (attn, all_of, all_of)),
            fetch(
                (4 * DH, wide),
                (weight, own_columns(0), rows_at(0, DH)),
                *((arrived[s], all_of, rows_at(s * DH, DH)) for s in (1, 2, 3)),
            ),
            fetch(
                (4 * DH, wide),
                (weight, own_columns(1), rows_at(0, DH)),
                (second[1], all_of, rows_at(DH, DH)),
                (second[3], all_of, rows_at(3 * DH, DH)),
                *((a, all_of, quarter(n)) for n, a in enumerate(second[2])),
            ),
        ],
        [spots],
        [both[2], across[0], across[1], across[3]],
        room=16,
        flops=4 * product,
        lazy=True,
    )
    joins = [parts[0], send(parts[1], 1, 0), parts[2], send(parts[3], 1, 0)]
    across[2] = send(both[2], 1, 0)
    return [both[s] for s in range(4)], [across[s] for s in range(4)], joins, [spots[0], spots[1]]


def by_gathers(attn, arrived, cotangent, mate_cotangent, out_weight, core, chip, colour, product):
    own, model = cotangent.shape
    shards, count = lax.axis_size("ctx"), lax.axis_size("head")
    attn = lax.all_to_all(attn, "head", 0, 0, tiled=True)
    weight = lax.dynamic_slice_in_dim(out_weight, core * DH, DH, 0)
    zero = jnp.zeros((1,), jnp.int32)
    groups = [list(range(k, shards, 2)) for k in range(2)]
    for s in range(2, count - 1):
        arrived[s] = send(arrived[s - 1], 0, 1)
    chunks = [weight] + [
        lax.all_gather(arrived[s], "ctx", axis=1, tiled=True, axis_index_groups=groups)
        for s in range(1, count)
    ]
    both = []
    for s in range(count):
        (block,) = call(
            functools.partial(grad_kernel, True, 0),
            [((2 * own, DH), BF16)],
            [cotangent, mate_cotangent, chunks[s]],
            [zero],
            flops=product,
        )
        both.append(send(block, 0, -s) if s else block)
    part, mate_part = call(
        mixed_kernel,
        [((own, model), F32)] * 2,
        [attn, *chunks],
        [lax.axis_index("head").reshape(1)],
        room=6,
        flops=count * product,
    )
    return both, [send(b, 1, 0) for b in both], [part, send(mate_part, 1, 0)], [jnp.int32(0)]


def solution(mesh):
    return jax.shard_map(
        on_device,
        mesh=mesh,
        in_specs=(
            P("ctx", "head"),
            P("ctx", "head"),
            P("ctx", "head"),
            P("ctx", None),
            P("head", None),
            P(("ctx", "head"), None),
        ),
        out_specs=(P(("ctx", "head"), None), P("ctx", "head"), P("ctx", "head"), P("ctx", "head")),
        check_vma=False,
    )
```

```python
import functools
import math

import jax
import jax.numpy as jnp
from jax import lax
from jax.experimental import pallas as pl
from jax.experimental.pallas import tpu as pltpu
from jax.sharding import PartitionSpec as P

DH = 128
F32 = jnp.float32
BF16 = jnp.bfloat16
NN = ((1,), (0,))
NT = ((1,), (1,))
TN = ((0,), (0,))
MIB = 1 << 20


def dot(a, b, dims):
    return lax.dot_general(a, b, (dims, ((), ())), preferred_element_type=F32)


def dot_wide(a, b, dims):
    high = b.astype(BF16)
    low = (b - high.astype(F32)).astype(BF16)
    both = dot(a, jnp.concatenate([high, low], 1 - dims[1][0]), dims)
    return both[:, :DH] + both[:, DH:]


def fetch(shape, *parts):
    return (shape, parts)


def all_of(ref, *_):
    return ref


def columns(spot, wide, rows=slice(None)):
    def view(ref, spots, *_):
        return ref.at[rows, pl.ds(pl.multiple_of(spots[spot], DH), wide)]

    return view


def rows_at(first, count):
    return lambda ref, *_: ref.at[first : first + count]


def columns_at(first, count):
    return lambda ref, *_: ref.at[:, first : first + count]


def call(body, outs, args, smem=(), after=(), room=2, flops=1, lazy=False):
    arrays, specs, scratch = [], [], []
    for arg in args:
        if isinstance(arg, tuple):
            arrays += [part[0] for part in arg[1]]
            specs += [pl.BlockSpec(memory_space=pltpu.HBM) for _ in arg[1]]
            scratch.append(pltpu.VMEM(arg[0], arg[1][0][0].dtype))
        else:
            arrays.append(arg)
            specs.append(pl.BlockSpec(memory_space=pltpu.VMEM))
    copies = sum(len(arg[1]) for arg in args if isinstance(arg, tuple))
    held = len(scratch)
    if copies:
        scratch.append(pltpu.SemaphoreType.DMA((copies,)))

    def kernel(*refs):
        scalars, refs = refs[: len(smem)], list(refs[len(smem) :])
        ins, refs = refs[: len(arrays)], refs[len(arrays) + len(after) :]
        results, slots = refs[: len(outs)], refs[len(outs) :]
        given, started, slot, groups = [], [], 0, []
        for arg in args:
            if not isinstance(arg, tuple):
                given.append(ins.pop(0))
                continue
            for _, source, target in arg[1]:
                copy = pltpu.make_async_copy(
                    source(ins.pop(0), *scalars),
                    target(slots[slot], *scalars),
                    slots[held].at[len(started)],
                )
                copy.start()
                started.append(copy)
            given.append(slots[slot])
            groups.append(started[sum(len(group) for group in groups) :])
            slot += 1

        def ready(n):
            for copy in groups[n]:
                copy.wait()

        if lazy:
            body(ready, *scalars, *given, *results)
            return
        for n in range(len(groups)):
            ready(n)
        body(*scalars, *given, *results)

    moved = sum(a.size * a.dtype.itemsize for a in arrays)
    moved += sum(math.prod(s) * jnp.dtype(t).itemsize for s, t in outs)
    return pl.pallas_call(
        kernel,
        out_shape=[jax.ShapeDtypeStruct(s, t) for s, t in outs],
        in_specs=[pl.BlockSpec(memory_space=pltpu.SMEM) for _ in smem]
        + specs
        + [pl.BlockSpec(memory_space=pl.ANY) for _ in after],
        out_specs=[pl.BlockSpec(memory_space=pltpu.VMEM) for _ in outs],
        scratch_shapes=scratch,
        compiler_params=pltpu.CompilerParams(vmem_limit_bytes=room * MIB),
        cost_estimate=pl.CostEstimate(
            flops=int(flops), bytes_accessed=int(moved), transcendentals=0
        ),
    )(*smem, *arrays, *after)


def hold(arrays, after):
    held = len(arrays)
    return pl.pallas_call(
        lambda *refs: None,
        out_shape=[jax.ShapeDtypeStruct(a.shape, a.dtype) for a in arrays],
        in_specs=[pl.BlockSpec(memory_space=pl.ANY) for _ in (*arrays, *after)],
        out_specs=[pl.BlockSpec(memory_space=pl.ANY) for _ in arrays],
        input_output_aliases={n: n for n in range(held)},
        cost_estimate=pl.CostEstimate(flops=1, bytes_accessed=1, transcendentals=0),
    )(*arrays, *after)


def lower_triangle(blk):
    return lax.broadcasted_iota(jnp.int32, (blk, blk), 0) >= lax.broadcasted_iota(
        jnp.int32, (blk, blk), 1
    )


def forward_kernel(
    scale,
    mask,
    where,
    all_ref,
    store_ref,
    mine_ref,
    other_ref,
    far_ref,
    mine_state_ref,
    other_state_ref,
):
    q_ref, k_ref, v_ref = (all_ref.at[n] for n in range(3))
    heads = [slice(h * DH, (h + 1) * DH) for h in range(2)]
    states = [dot(k_ref[:, cols], v_ref[:, cols], TN) for cols in heads]
    mine_state_ref[...], other_state_ref[...] = pick(where[2], states)
    rows, width = q_ref.shape
    count = mask.shape[0]
    blk = rows // count
    inv_root = 1.0 / math.sqrt(DH)
    triangle = lower_triangle(blk)
    sums = []
    for h in range(2):
        raw = dot(q_ref[:, heads[h]], k_ref[:, heads[h]], NT)
        probs, inner = [], []
        for i in range(count):
            own = raw[i * blk : (i + 1) * blk]
            scores, linear = [], []
            for j in range(i + 1):
                part = own[:, j * blk : (j + 1) * blk]
                keep = triangle if j == i else mask[i, j] > 0
                scores.append(jnp.where(keep, part * inv_root, -1e30))
                linear.append(jnp.where(triangle, part, 0.0) if j == i else part)
            empty = [jnp.zeros((blk, blk), F32)] * (count - 1 - i)
            scores = jnp.concatenate(scores, 1)
            expo = jnp.exp(scores - jnp.max(scores, -1, keepdims=True))
            share = expo / jnp.sum(expo, -1, keepdims=True)
            probs.append(jnp.concatenate([share, *empty], 1).astype(BF16))
            inner.append(jnp.concatenate([*linear, *empty], 1).astype(BF16))
        stacked = jnp.concatenate(probs + inner, 0)
        store_ref[h], store_ref[2 + h] = stacked[:rows], stacked[rows:]
        both = dot(stacked, v_ref[:, heads[h]], NN)
        sums.append(both[:rows] + scale * both[rows:])
    mine_ref[...], other_ref[...] = pick(where[2], sums)
    far_ref[...] = q_ref[:, pl.ds(pl.multiple_of((1 - where[2]) * DH, DH), DH)]


def pick(core, parts):
    return jnp.where(core == 0, parts[0], parts[1]), jnp.where(core == 0, parts[1], parts[0])


def both_heads(core, mine_ref, other_ref):
    mine, other = mine_ref[...], other_ref[...]
    return jnp.where(core == 0, mine, other), jnp.where(core == 0, other, mine)


def carry(flags, here_ref, got_ref, totals):
    carried = jnp.zeros(here_ref.shape, F32)
    for n, total in enumerate(totals):
        carried = carried + jnp.where(flags[n] > 0, total[...], 0.0)
    counts = flags[len(totals)] > 0
    keep = carried + jnp.where(counts, got_ref[...], 0.0)
    return keep, carried + jnp.where(counts, 0.0, here_ref[...])


def carry_kernel(flags, here_ref, got_ref, *refs):
    totals, (keep_ref, back_ref) = refs[:-2], refs[-2:]
    keep_ref[...], back_ref[...] = carry(flags, here_ref, got_ref, totals)


def attn_kernel(scale, flags, where, here_ref, got_ref, *refs):
    totals, refs = refs[:-7], refs[-7:]
    q_ref, far_ref, pre_ref, far_pre_ref, out_ref, keep_ref, back_ref = refs
    keep, back = carry(flags, here_ref, got_ref, totals)
    keep_ref[...], back_ref[...] = keep, back
    count = out_ref.shape[0]
    own = pre_ref.shape[0] // count
    cols = pl.ds(pl.multiple_of(where[2] * DH, DH), DH)
    mine = pre_ref[...] + scale * dot_wide(q_ref[:, cols], keep, NN)
    mate = far_pre_ref[...] + scale * dot_wide(far_ref[...], back, NN)
    for z in range(count):
        out_ref[z, :own] = mine[z * own : (z + 1) * own].astype(BF16)
        out_ref[z, own:] = mate[z * own : (z + 1) * own].astype(BF16)


def back_along(attn_ref, place):
    count = attn_ref.shape[0]
    return jnp.concatenate([attn_ref[lax.rem(place - s + count, count)] for s in range(count)], 1)


def first_kernel(ready, spots, left_ref, weight_ref, right_ref, own_ref, half_ref):
    ready(0)
    ready(1)
    own_ref[...] = dot(left_ref[...], weight_ref[...], NT).astype(BF16)
    ready(2)
    near = left_ref[:, pl.ds(pl.multiple_of(spots[0], DH), right_ref.shape[1])]
    half_ref[...] = dot(near, right_ref[...], NT)


def second_kernel(spots, left_ref, right_ref, half_ref, piece_ref, one_ref, three_ref, *cut_refs):
    wide = cut_refs[0].shape[1]
    for n, cut_ref in enumerate(cut_refs):
        cut_ref[...] = piece_ref[:, n * wide : (n + 1) * wide]
    total = (half_ref[...] + dot(left_ref[...], right_ref[...], NT)).astype(BF16)
    one_ref[...], three_ref[...] = total[:, :DH], total[:, DH:]


def last_kernel(spots, left_ref, right_ref, half_ref, out_ref):
    out_ref[...] = (half_ref[...] + dot(left_ref[...], right_ref[...], NT)).astype(BF16)


def half_kernel(spots, left_ref, right_ref, half_ref):
    half_ref[...] = dot(left_ref[...], right_ref[...], NT)


def halves_kernel(ready, spots, attn_ref, *refs):
    rights, outs = refs[:2], refs[2:]
    own = outs[0].shape[0]
    ready(0)
    left = back_along(attn_ref, spots[3])
    for n, right_ref in enumerate(rights):
        ready(1 + n)
        part = dot(left, right_ref[...], NN)
        outs[2 * n][...] = part[:own]
        outs[2 * n + 1][...] = part[own:]


def grad_kernel(whole, added, places, mine_ref, mate_ref, *refs):
    chunks, out_ref = refs[added:-1], refs[-1]
    total = refs[0][...] if added else None
    for j, chunk in enumerate(chunks):
        cols = slice(None) if whole else pl.ds(pl.multiple_of(places[j], DH), chunk.shape[1])
        left = jnp.concatenate([mine_ref[:, cols], mate_ref[:, cols]], 0)
        part = dot(left, chunk[...], NT)
        total = part if total is None else total + part
    out_ref[...] = total.astype(out_ref.dtype)


def mixed_kernel(where, attn_ref, *refs):
    chunks, (own_out, mate_out) = refs[:-2], refs[-2:]
    own = own_out.shape[0]
    right = jnp.concatenate([chunk[...] for chunk in chunks], 0)
    part = dot(back_along(attn_ref, where[0]), right, NN)
    own_out[...] = part[:own]
    mate_out[...] = part[own:]


def join_kernel(places, *refs):
    out_ref, done_ref = refs[-2:]
    done_ref[...] = jnp.zeros(done_ref.shape, F32)
    for n in range(len(refs) // 2 - 1):
        wide = refs[2 * n].shape[1]
        there = pl.ds(pl.multiple_of(places[n], DH), wide)
        out_ref[:, there] = (refs[2 * n][...] + refs[2 * n + 1][...]).astype(BF16)


def collect_kernel(scale, count, where, q_ref, *refs):
    direct, across = refs[:count], refs[count : 2 * count]
    g_ref, mine_ref, other_ref = refs[2 * count :]
    own = g_ref.shape[0] // count
    mine = pl.ds(pl.multiple_of(where[2] * DH, DH), DH)
    mate = pl.ds(pl.multiple_of((1 - where[2]) * DH, DH), DH)
    for s in range(count):
        block = lax.rem(where[0] + s, count)
        here = pl.ds(pl.multiple_of(block * own, own), own)
        g_ref[here, mine] = direct[s][:own]
        g_ref[here, mate] = across[s][own:]
    heads = [slice(h * DH, (h + 1) * DH) for h in range(2)]
    parts = [scale * dot(q_ref[:, cols], g_ref[:, cols], TN) for cols in heads]
    mine_ref[...], other_ref[...] = pick(where[2], parts)


def backward_kernel(
    scale, where, q_ref, k_ref, v_ref, g_ref, store_ref, mine_ref, other_ref, dq_ref, dk_ref, dv_ref
):
    rows, width = q_ref.shape
    inv_root = 1.0 / math.sqrt(DH)
    triangle = lower_triangle(rows)
    states = both_heads(where[2], mine_ref, other_ref)
    for h in range(width // DH):
        cols = slice(h * DH, (h + 1) * DH)
        q, k, v, g = q_ref[:, cols], k_ref[:, cols], v_ref[:, cols], g_ref[:, cols]
        probs, inner = store_ref[h], store_ref[2 + h]
        dprod = dot(g, v, NT)
        delta = jnp.sum(g.astype(F32) * dot(probs, v, NN), -1, keepdims=True)
        dscore = (probs.astype(F32) * (dprod - delta) * inv_root).astype(BF16)
        dinner = jnp.where(triangle, dprod, 0.0).astype(BF16)
        left = dot(jnp.concatenate([dscore, dinner], 0), k, NN)
        linear = left[rows:] + dot_wide(g, states[h], NT)
        dq_ref[:, cols] = (left[:rows] + scale * linear).astype(BF16)
        dk = dot(jnp.concatenate([dscore, dinner], 1), q, TN)
        dk_ref[:, cols] = dk[:rows] + scale * dk[rows:]
        dv = dot(jnp.concatenate([probs, inner], 1), g, TN)
        dv_ref[:, cols] = dv[:rows] + scale * dv[rows:]


def close_kernel(where, k_ref, v_ref, dk_ref, dv_ref, mine_ref, other_ref, gk_ref, gv_ref):
    states = both_heads(where[2], mine_ref, other_ref)
    for h in range(k_ref.shape[1] // DH):
        cols = slice(h * DH, (h + 1) * DH)
        state = states[h]
        gk_ref[:, cols] = (dk_ref[:, cols] + dot_wide(v_ref[:, cols], state, NT)).astype(BF16)
        gv_ref[:, cols] = (dv_ref[:, cols] + dot_wide(k_ref[:, cols], state, NN)).astype(BF16)


def send(x, flip, shift):
    shards, heads = lax.axis_size("ctx"), lax.axis_size("head")
    pairs = [
        (c * heads + z, (c ^ flip) * heads + (z + shift) % heads)
        for c in range(shards)
        for z in range(heads)
    ]
    return lax.ppermute(x, ("ctx", "head"), pairs)


def exchange(mine, other, core, chip, chips, later):
    got = send(other, 1, 0)
    own = total = mine + got
    totals, flags = [], []
    if chips == 4:
        for flip in (1, 2, 3):
            totals.append(send(total, 2 * flip, 0))
            flags.append(((chip ^ flip) > chip) == later)
    else:
        step = 1
        while step < chips:
            totals.append(send(total, 2 * step, 0))
            flags.append(((chip & step) == 0) == later)
            total = total + totals[-1]
            step *= 2
    flags.append((core == 0) == later)
    return jnp.stack(flags).astype(jnp.int32), [mine, got, *totals], own


def on_device(query, key, value, block_mask, out_weight, cotangent):
    rows, width = query.shape
    heads = width // DH
    shards, count = lax.axis_size("ctx"), lax.axis_size("head")
    model = out_weight.shape[1]
    own = rows // count
    scale = 1.0 / math.sqrt(DH * rows * shards)
    ctx, place = lax.axis_index("ctx"), lax.axis_index("head")
    core, chip, chips = ctx & 1, ctx >> 1, shards // 2
    where = jnp.stack([place, ctx, core])
    flat, square = (rows, width), rows * rows * DH * heads
    pair = [((DH, DH), F32)] * 2
    tokens = ((2 * own, DH), BF16)
    product = 4 * own * DH * model

    board = chips == 4 and count == 4
    wide = model // (2 if board else chips)
    colour = (chip & 1) ^ (chip >> 1) if board else chip
    piece = lax.dynamic_slice(out_weight, (core * DH, colour * wide), (DH, wide))
    arrived = {1: send(piece, 0, 1), count - 1: send(piece, 0, -1)}
    mate_cotangent = send(cotangent, 1, 0)

    store, pre, other_pre, far, mine, other = call(
        functools.partial(forward_kernel, scale),
        [((2 * heads, rows, rows), BF16)]
        + [((rows, DH), F32)] * 2
        + [((rows, DH), BF16)]
        + pair,
        [jnp.stack([query, key, value])],
        [block_mask, where],
        [mate_cotangent],
        flops=7 * square,
    )
    far, other_pre = send(far, 1, 0), send(other_pre, 1, 0)
    (mine,) = hold([mine], [far, other_pre])
    flags, parts, total = exchange(mine, other, core, chip, chips, False)
    attn, keep, back = call(
        functools.partial(attn_kernel, scale),
        [((count, *tokens[0]), BF16), *pair],
        [*parts, query, far, pre, other_pre],
        [flags, where],
    )
    linear = [keep, send(back, 1, 0)]
    if board:
        arrived[1], arrived[3] = hold([arrived[1], arrived[3]], [keep])
    attn = lax.all_to_all(attn, "head", 0, 0, tiled=True)

    work = near_and_far if board else by_gathers
    both, across, joins, starts = work(
        attn, arrived, cotangent, mate_cotangent, out_weight, core, chip, colour, product
    )
    mixed, done = call(
        join_kernel, [((own, model), BF16), ((8, DH), F32)], joins, [jnp.stack(starts)]
    )

    g, mine, other = call(
        functools.partial(collect_kernel, scale, count),
        [(flat, BF16), *pair],
        [query, *both, *across],
        [where],
    )
    flags, parts, total = exchange(mine, other, core, chip, chips, True)
    grad_query, dk, dv = call(
        functools.partial(backward_kernel, scale),
        [(flat, BF16)] + [(flat, F32)] * 2,
        [query, key, value, g, store, *linear],
        [where],
        [total],
        flops=14 * square,
    )
    keep, back = call(carry_kernel, pair, parts, [flags], [dk])
    grad_key, grad_value = call(
        close_kernel,
        [(flat, BF16)] * 2,
        [key, value, dk, dv, keep, send(back, 1, 0)],
        [where],
        [done],
    )
    return mixed, grad_query, grad_key, grad_value


def near_and_far(attn, arrived, cotangent, mate_cotangent, weight, core, chip, colour, product):
    own, model = cotangent.shape
    wide = model // 2
    place = lax.axis_index("head")
    spots = jnp.stack([colour * wide, (1 - colour) * wide, core * DH, place])
    tokens = ((2 * own, DH), BF16)
    parts = [((own, wide), F32)] * 2
    all_arrays = [(cotangent, all_of, rows_at(0, own)), (mate_cotangent, all_of, rows_at(own, own))]
    whole = fetch((2 * own, model), *all_arrays)
    left = [
        fetch((2 * own, wide), *((a, columns(n, wide), put) for a, _, put in all_arrays))
        for n in range(2)
    ]

    def own_rows(ref, spots, *_):
        return ref.at[pl.ds(pl.multiple_of(spots[2], DH), DH)]

    def own_columns(n):
        return lambda ref, spots, *_: ref.at[
            pl.ds(pl.multiple_of(spots[2], DH), DH), pl.ds(pl.multiple_of(spots[n], DH), wide)
        ]

    def stacked(*arrays):
        return [(a, all_of, rows_at(n * DH, DH)) for n, a in enumerate(arrays)]

    arrived[2] = send(arrived[1], 0, 1)
    second = {1: send(arrived[1], 2, 0), 3: send(arrived[3], 4, 0)}
    mine, half = call(
        first_kernel,
        [tokens, ((2 * own, 2 * DH), F32)],
        [
            whole,
            fetch((DH, model), (weight, own_rows, all_of)),
            fetch((2 * DH, wide), *stacked(arrived[1], arrived[3])),
        ],
        [spots],
        lazy=True,
        room=6,
        flops=2 * product,
    )
    one, three, *cuts = call(
        second_kernel,
        [tokens] * 2 + [((DH, wide // 2), BF16)] * 2,
        [
            left[1],
            fetch((2 * DH, wide), *stacked(second[1], second[3])),
            half,
            fetch((DH, wide), (arrived[2], all_of, all_of)),
        ],
        [spots],
        room=6,
        flops=product,
    )
    second[2] = [send(cuts[0], 2, 0), send(cuts[1], 4, 0)]
    both = {0: mine, 1: send(one, 0, -1), 3: send(three, 0, -3)}
    across = {s: send(both[s], 1, 0) for s in (0, 1, 3)}
    (half,) = call(
        half_kernel,
        [((2 * own, DH), F32)],
        [left[0], fetch((DH, wide), (arrived[2], all_of, all_of))],
        [spots],
        [attn],
        room=6,
        flops=product // 2,
    )
    quarters = [(a, all_of, columns_at(n * wide // 2, wide // 2)) for n, a in enumerate(second[2])]
    (two,) = call(
        last_kernel,
        [tokens],
        [left[1], fetch((DH, wide), *quarters), half],
        [spots],
        [both[1], both[3]],
        room=6,
        flops=product // 2,
    )
    both[2] = send(two, 0, -2)

    def quarter(n):
        return lambda ref, *_: ref.at[2 * DH : 3 * DH, n * wide // 2 : (n + 1) * wide // 2]

    parts = call(
        halves_kernel,
        parts * 2,
        [
            fetch(attn.shape, (attn, all_of, all_of)),
            fetch(
                (4 * DH, wide),
                (weight, own_columns(0), rows_at(0, DH)),
                *((arrived[s], all_of, rows_at(s * DH, DH)) for s in (1, 2, 3)),
            ),
            fetch(
                (4 * DH, wide),
                (weight, own_columns(1), rows_at(0, DH)),
                (second[1], all_of, rows_at(DH, DH)),
                (second[3], all_of, rows_at(3 * DH, DH)),
                *((a, all_of, quarter(n)) for n, a in enumerate(second[2])),
            ),
        ],
        [spots],
        [both[2], across[0], across[1], across[3]],
        room=8,
        flops=4 * product,
        lazy=True,
    )
    joins = [parts[0], send(parts[1], 1, 0), parts[2], send(parts[3], 1, 0)]
    across[2] = send(both[2], 1, 0)
    return [both[s] for s in range(4)], [across[s] for s in range(4)], joins, [spots[0], spots[1]]


def by_gathers(attn, arrived, cotangent, mate_cotangent, out_weight, core, chip, colour, product):
    own, model = cotangent.shape
    shards, count = lax.axis_size("ctx"), lax.axis_size("head")
    weight = lax.dynamic_slice_in_dim(out_weight, core * DH, DH, 0)
    zero = jnp.zeros((1,), jnp.int32)
    groups = [list(range(k, shards, 2)) for k in range(2)]
    for s in range(2, count - 1):
        arrived[s] = send(arrived[s - 1], 0, 1)
    chunks = [weight] + [
        lax.all_gather(arrived[s], "ctx", axis=1, tiled=True, axis_index_groups=groups)
        for s in range(1, count)
    ]
    both = []
    for s in range(count):
        (block,) = call(
            functools.partial(grad_kernel, True, 0),
            [((2 * own, DH), BF16)],
            [cotangent, mate_cotangent, chunks[s]],
            [zero],
            flops=product,
        )
        both.append(send(block, 0, -s) if s else block)
    part, mate_part = call(
        mixed_kernel,
        [((own, model), F32)] * 2,
        [attn, *chunks],
        [lax.axis_index("head").reshape(1)],
        room=6,
        flops=count * product,
    )
    return both, [send(b, 1, 0) for b in both], [part, send(mate_part, 1, 0)], [jnp.int32(0)]


def solution(mesh):
    return jax.shard_map(
        on_device,
        mesh=mesh,
        in_specs=(
            P("ctx", "head"),
            P("ctx", "head"),
            P("ctx", "head"),
            P("ctx", None),
            P("head", None),
            P(("ctx", "head"), None),
        ),
        out_specs=(P(("ctx", "head"), None), P("ctx", "head"), P("ctx", "head"), P("ctx", "head")),
        check_vma=False,
    )
```

```python
import functools
import math

import jax
import jax.numpy as jnp
from jax import lax
from jax.experimental import pallas as pl
from jax.experimental.pallas import tpu as pltpu
from jax.sharding import PartitionSpec as P

DH = 128
F32 = jnp.float32
BF16 = jnp.bfloat16
NN = ((1,), (0,))
NT = ((1,), (1,))
TN = ((0,), (0,))
MIB = 1 << 20


def dot(a, b, dims):
    return lax.dot_general(a, b, (dims, ((), ())), preferred_element_type=F32)


def dot_wide(a, b, dims):
    high = b.astype(BF16)
    low = (b - high.astype(F32)).astype(BF16)
    both = dot(a, jnp.concatenate([high, low], 1 - dims[1][0]), dims)
    return both[:, :DH] + both[:, DH:]


def fetch(shape, *parts):
    return (shape, parts)


def all_of(ref, *_):
    return ref


def columns(spot, wide, rows=slice(None)):
    def view(ref, spots, *_):
        return ref.at[rows, pl.ds(pl.multiple_of(spots[spot], DH), wide)]

    return view


def rows_at(first, count):
    return lambda ref, *_: ref.at[first : first + count]


def columns_at(first, count):
    return lambda ref, *_: ref.at[:, first : first + count]


def call(body, outs, args, smem=(), after=(), room=2, flops=1, lazy=False):
    arrays, specs, scratch = [], [], []
    for arg in args:
        if isinstance(arg, tuple):
            arrays += [part[0] for part in arg[1]]
            specs += [pl.BlockSpec(memory_space=pltpu.HBM) for _ in arg[1]]
            scratch.append(pltpu.VMEM(arg[0], arg[1][0][0].dtype))
        else:
            arrays.append(arg)
            specs.append(pl.BlockSpec(memory_space=pltpu.VMEM))
    copies = sum(len(arg[1]) for arg in args if isinstance(arg, tuple))
    held = len(scratch)
    if copies:
        scratch.append(pltpu.SemaphoreType.DMA((copies,)))

    def kernel(*refs):
        scalars, refs = refs[: len(smem)], list(refs[len(smem) :])
        ins, refs = refs[: len(arrays)], refs[len(arrays) + len(after) :]
        results, slots = refs[: len(outs)], refs[len(outs) :]
        given, started, slot, groups = [], [], 0, []
        for arg in args:
            if not isinstance(arg, tuple):
                given.append(ins.pop(0))
                continue
            for _, source, target in arg[1]:
                copy = pltpu.make_async_copy(
                    source(ins.pop(0), *scalars),
                    target(slots[slot], *scalars),
                    slots[held].at[len(started)],
                )
                copy.start()
                started.append(copy)
            given.append(slots[slot])
            groups.append(started[sum(len(group) for group in groups) :])
            slot += 1

        def ready(n):
            for copy in groups[n]:
                copy.wait()

        if lazy:
            body(ready, *scalars, *given, *results)
            return
        for n in range(len(groups)):
            ready(n)
        body(*scalars, *given, *results)

    moved = sum(a.size * a.dtype.itemsize for a in arrays)
    moved += sum(math.prod(s) * jnp.dtype(t).itemsize for s, t in outs)
    return pl.pallas_call(
        kernel,
        out_shape=[jax.ShapeDtypeStruct(s, t) for s, t in outs],
        in_specs=[pl.BlockSpec(memory_space=pltpu.SMEM) for _ in smem]
        + specs
        + [pl.BlockSpec(memory_space=pl.ANY) for _ in after],
        out_specs=[pl.BlockSpec(memory_space=pltpu.VMEM) for _ in outs],
        scratch_shapes=scratch,
        compiler_params=pltpu.CompilerParams(vmem_limit_bytes=room * MIB),
        cost_estimate=pl.CostEstimate(
            flops=int(flops), bytes_accessed=int(moved), transcendentals=0
        ),
    )(*smem, *arrays, *after)


def hold(arrays, after):
    held = len(arrays)
    return pl.pallas_call(
        lambda *refs: None,
        out_shape=[jax.ShapeDtypeStruct(a.shape, a.dtype) for a in arrays],
        in_specs=[pl.BlockSpec(memory_space=pl.ANY) for _ in (*arrays, *after)],
        out_specs=[pl.BlockSpec(memory_space=pl.ANY) for _ in arrays],
        input_output_aliases={n: n for n in range(held)},
        cost_estimate=pl.CostEstimate(flops=1, bytes_accessed=1, transcendentals=0),
    )(*arrays, *after)


def lower_triangle(blk):
    return lax.broadcasted_iota(jnp.int32, (blk, blk), 0) >= lax.broadcasted_iota(
        jnp.int32, (blk, blk), 1
    )


def forward_kernel(
    scale,
    mask,
    where,
    all_ref,
    store_ref,
    mine_ref,
    other_ref,
    far_ref,
    mine_state_ref,
    other_state_ref,
):
    q_ref, k_ref, v_ref = (all_ref.at[n] for n in range(3))
    heads = [slice(h * DH, (h + 1) * DH) for h in range(2)]
    states = [dot(k_ref[:, cols], v_ref[:, cols], TN) for cols in heads]
    mine_state_ref[...], other_state_ref[...] = pick(where[2], states)
    rows, width = q_ref.shape
    count = mask.shape[0]
    blk = rows // count
    inv_root = 1.0 / math.sqrt(DH)
    triangle = lower_triangle(blk)
    sums = []
    for h in range(2):
        raw = dot(q_ref[:, heads[h]], k_ref[:, heads[h]], NT)
        probs, inner = [], []
        for i in range(count):
            own = raw[i * blk : (i + 1) * blk]
            scores, linear = [], []
            for j in range(i + 1):
                part = own[:, j * blk : (j + 1) * blk]
                keep = triangle if j == i else mask[i, j] > 0
                scores.append(jnp.where(keep, part * inv_root, -1e30))
                linear.append(jnp.where(triangle, part, 0.0) if j == i else part)
            empty = [jnp.zeros((blk, blk), F32)] * (count - 1 - i)
            scores = jnp.concatenate(scores, 1)
            expo = jnp.exp(scores - jnp.max(scores, -1, keepdims=True))
            share = expo / jnp.sum(expo, -1, keepdims=True)
            probs.append(jnp.concatenate([share, *empty], 1).astype(BF16))
            inner.append(jnp.concatenate([*linear, *empty], 1).astype(BF16))
        stacked = jnp.concatenate(probs + inner, 0)
        store_ref[h], store_ref[2 + h] = stacked[:rows], stacked[rows:]
        both = dot(stacked, v_ref[:, heads[h]], NN)
        sums.append(both[:rows] + scale * both[rows:])
    mine_ref[...], other_ref[...] = pick(where[2], sums)
    far_ref[...] = q_ref[:, pl.ds(pl.multiple_of((1 - where[2]) * DH, DH), DH)]


def pick(core, parts):
    return jnp.where(core == 0, parts[0], parts[1]), jnp.where(core == 0, parts[1], parts[0])


def both_heads(core, mine_ref, other_ref):
    mine, other = mine_ref[...], other_ref[...]
    return jnp.where(core == 0, mine, other), jnp.where(core == 0, other, mine)


def carry(flags, here_ref, got_ref, totals):
    carried = jnp.zeros(here_ref.shape, F32)
    for n, total in enumerate(totals):
        carried = carried + jnp.where(flags[n] > 0, total[...], 0.0)
    counts = flags[len(totals)] > 0
    keep = carried + jnp.where(counts, got_ref[...], 0.0)
    return keep, carried + jnp.where(counts, 0.0, here_ref[...])


def carry_kernel(flags, here_ref, got_ref, *refs):
    totals, (keep_ref, back_ref) = refs[:-2], refs[-2:]
    keep_ref[...], back_ref[...] = carry(flags, here_ref, got_ref, totals)


def attn_kernel(scale, flags, where, here_ref, got_ref, *refs):
    totals, refs = refs[:-7], refs[-7:]
    q_ref, far_ref, pre_ref, far_pre_ref, out_ref, keep_ref, back_ref = refs
    keep, back = carry(flags, here_ref, got_ref, totals)
    keep_ref[...], back_ref[...] = keep, back
    count = out_ref.shape[0]
    own = pre_ref.shape[0] // count
    cols = pl.ds(pl.multiple_of(where[2] * DH, DH), DH)
    mine = pre_ref[...] + scale * dot_wide(q_ref[:, cols], keep, NN)
    mate = far_pre_ref[...] + scale * dot_wide(far_ref[...], back, NN)
    for z in range(count):
        out_ref[z, :own] = mine[z * own : (z + 1) * own].astype(BF16)
        out_ref[z, own:] = mate[z * own : (z + 1) * own].astype(BF16)


def back_along(attn_ref, place):
    count = attn_ref.shape[0]
    return jnp.concatenate([attn_ref[lax.rem(place - s + count, count)] for s in range(count)], 1)


def first_kernel(ready, spots, left_ref, weight_ref, right_ref, own_ref, half_ref):
    ready(0)
    ready(1)
    own_ref[...] = dot(left_ref[...], weight_ref[...], NT).astype(BF16)
    ready(2)
    near = left_ref[:, pl.ds(pl.multiple_of(spots[0], DH), right_ref.shape[1])]
    half_ref[...] = dot(near, right_ref[...], NT)


def second_kernel(spots, left_ref, right_ref, half_ref, piece_ref, one_ref, three_ref, *cut_refs):
    wide = cut_refs[0].shape[1]
    for n, cut_ref in enumerate(cut_refs):
        cut_ref[...] = piece_ref[:, n * wide : (n + 1) * wide]
    total = (half_ref[...] + dot(left_ref[...], right_ref[...], NT)).astype(BF16)
    one_ref[...], three_ref[...] = total[:, :DH], total[:, DH:]


def last_kernel(spots, left_ref, right_ref, half_ref, out_ref):
    out_ref[...] = (half_ref[...] + dot(left_ref[...], right_ref[...], NT)).astype(BF16)


def half_kernel(spots, left_ref, right_ref, half_ref):
    half_ref[...] = dot(left_ref[...], right_ref[...], NT)


def halves_kernel(ready, spots, attn_ref, *refs):
    rights, outs = refs[:2], refs[2:]
    own = outs[0].shape[0]
    ready(0)
    left = back_along(attn_ref, spots[3])
    for n, right_ref in enumerate(rights):
        ready(1 + n)
        part = dot(left, right_ref[...], NN)
        outs[2 * n][...] = part[:own]
        outs[2 * n + 1][...] = part[own:]


def grad_kernel(whole, added, places, mine_ref, mate_ref, *refs):
    chunks, out_ref = refs[added:-1], refs[-1]
    total = refs[0][...] if added else None
    for j, chunk in enumerate(chunks):
        cols = slice(None) if whole else pl.ds(pl.multiple_of(places[j], DH), chunk.shape[1])
        left = jnp.concatenate([mine_ref[:, cols], mate_ref[:, cols]], 0)
        part = dot(left, chunk[...], NT)
        total = part if total is None else total + part
    out_ref[...] = total.astype(out_ref.dtype)


def mixed_kernel(where, attn_ref, *refs):
    chunks, (own_out, mate_out) = refs[:-2], refs[-2:]
    own = own_out.shape[0]
    right = jnp.concatenate([chunk[...] for chunk in chunks], 0)
    part = dot(back_along(attn_ref, where[0]), right, NN)
    own_out[...] = part[:own]
    mate_out[...] = part[own:]


def join_kernel(places, *refs):
    out_ref, done_ref = refs[-2:]
    done_ref[...] = jnp.zeros(done_ref.shape, F32)
    for n in range(len(refs) // 2 - 1):
        wide = refs[2 * n].shape[1]
        there = pl.ds(pl.multiple_of(places[n], DH), wide)
        out_ref[:, there] = (refs[2 * n][...] + refs[2 * n + 1][...]).astype(BF16)


def collect_kernel(scale, count, where, q_ref, *refs):
    direct, across = refs[:count], refs[count : 2 * count]
    g_ref, mine_ref, other_ref = refs[2 * count :]
    own = g_ref.shape[0] // count
    mine = pl.ds(pl.multiple_of(where[2] * DH, DH), DH)
    mate = pl.ds(pl.multiple_of((1 - where[2]) * DH, DH), DH)
    for s in range(count):
        block = lax.rem(where[0] + s, count)
        here = pl.ds(pl.multiple_of(block * own, own), own)
        g_ref[here, mine] = direct[s][:own]
        g_ref[here, mate] = across[s][own:]
    heads = [slice(h * DH, (h + 1) * DH) for h in range(2)]
    parts = [scale * dot(q_ref[:, cols], g_ref[:, cols], TN) for cols in heads]
    mine_ref[...], other_ref[...] = pick(where[2], parts)


def backward_kernel(
    scale, where, q_ref, k_ref, v_ref, g_ref, store_ref, mine_ref, other_ref, dq_ref, dk_ref, dv_ref
):
    rows, width = q_ref.shape
    inv_root = 1.0 / math.sqrt(DH)
    triangle = lower_triangle(rows)
    states = both_heads(where[2], mine_ref, other_ref)
    for h in range(width // DH):
        cols = slice(h * DH, (h + 1) * DH)
        q, k, v, g = q_ref[:, cols], k_ref[:, cols], v_ref[:, cols], g_ref[:, cols]
        probs, inner = store_ref[h], store_ref[2 + h]
        dprod = dot(g, v, NT)
        delta = jnp.sum(g.astype(F32) * dot(probs, v, NN), -1, keepdims=True)
        dscore = (probs.astype(F32) * (dprod - delta) * inv_root).astype(BF16)
        dinner = jnp.where(triangle, dprod, 0.0).astype(BF16)
        left = dot(jnp.concatenate([dscore, dinner], 0), k, NN)
        linear = left[rows:] + dot_wide(g, states[h], NT)
        dq_ref[:, cols] = (left[:rows] + scale * linear).astype(BF16)
        dk = dot(jnp.concatenate([dscore, dinner], 1), q, TN)
        dk_ref[:, cols] = dk[:rows] + scale * dk[rows:]
        dv = dot(jnp.concatenate([probs, inner], 1), g, TN)
        dv_ref[:, cols] = dv[:rows] + scale * dv[rows:]


def close_kernel(where, k_ref, v_ref, dk_ref, dv_ref, mine_ref, other_ref, gk_ref, gv_ref):
    states = both_heads(where[2], mine_ref, other_ref)
    for h in range(k_ref.shape[1] // DH):
        cols = slice(h * DH, (h + 1) * DH)
        state = states[h]
        gk_ref[:, cols] = (dk_ref[:, cols] + dot_wide(v_ref[:, cols], state, NT)).astype(BF16)
        gv_ref[:, cols] = (dv_ref[:, cols] + dot_wide(k_ref[:, cols], state, NN)).astype(BF16)


def send(x, flip, shift):
    shards, heads = lax.axis_size("ctx"), lax.axis_size("head")
    pairs = [
        (c * heads + z, (c ^ flip) * heads + (z + shift) % heads)
        for c in range(shards)
        for z in range(heads)
    ]
    return lax.ppermute(x, ("ctx", "head"), pairs)


def exchange(mine, other, core, chip, chips, later):
    got = send(other, 1, 0)
    own = total = mine + got
    totals, flags = [], []
    if chips == 4:
        for flip in (1, 2, 3):
            totals.append(send(total, 2 * flip, 0))
            flags.append(((chip ^ flip) > chip) == later)
    else:
        step = 1
        while step < chips:
            totals.append(send(total, 2 * step, 0))
            flags.append(((chip & step) == 0) == later)
            total = total + totals[-1]
            step *= 2
    flags.append((core == 0) == later)
    return jnp.stack(flags).astype(jnp.int32), [mine, got, *totals], own


def on_device(query, key, value, block_mask, out_weight, cotangent):
    rows, width = query.shape
    heads = width // DH
    shards, count = lax.axis_size("ctx"), lax.axis_size("head")
    model = out_weight.shape[1]
    own = rows // count
    scale = 1.0 / math.sqrt(DH * rows * shards)
    ctx, place = lax.axis_index("ctx"), lax.axis_index("head")
    core, chip, chips = ctx & 1, ctx >> 1, shards // 2
    where = jnp.stack([place, ctx, core])
    flat, square = (rows, width), rows * rows * DH * heads
    pair = [((DH, DH), F32)] * 2
    tokens = ((2 * own, DH), BF16)
    product = 4 * own * DH * model

    board = chips == 4 and count == 4
    wide = model // (2 if board else chips)
    colour = (chip & 1) ^ (chip >> 1) if board else chip
    piece = lax.dynamic_slice(out_weight, (core * DH, colour * wide), (DH, wide))
    arrived = {1: send(piece, 0, 1), count - 1: send(piece, 0, -1)}
    mate_cotangent = send(cotangent, 1, 0)

    store, pre, other_pre, far, mine, other = call(
        functools.partial(forward_kernel, scale),
        [((2 * heads, rows, rows), BF16)]
        + [((rows, DH), F32)] * 2
        + [((rows, DH), BF16)]
        + pair,
        [jnp.stack([query, key, value])],
        [block_mask, where],
        [mate_cotangent],
        flops=7 * square,
    )
    far, other_pre = send(far, 1, 0), send(other_pre, 1, 0)
    (mine,) = hold([mine], [far, other_pre])
    flags, parts, total = exchange(mine, other, core, chip, chips, False)
    attn, keep, back = call(
        functools.partial(attn_kernel, scale),
        [((count, *tokens[0]), BF16), *pair],
        [*parts, query, far, pre, other_pre],
        [flags, where],
    )
    linear = [keep, send(back, 1, 0)]
    if board:
        arrived[1], arrived[3] = hold([arrived[1], arrived[3]], [keep])
    attn = lax.all_to_all(attn, "head", 0, 0, tiled=True)

    work = near_and_far if board else by_gathers
    both, across, mix = work(
        attn, arrived, cotangent, mate_cotangent, out_weight, core, chip, colour, product
    )
    g, mine, other = call(
        functools.partial(collect_kernel, scale, count),
        [(flat, BF16), *pair],
        [query, *both, *across],
        [where],
        linear[1:],
    )
    flags, parts, total = exchange(mine, other, core, chip, chips, True)
    joins, starts = mix([total])
    mixed, done = call(
        join_kernel, [((own, model), BF16), ((8, DH), F32)], joins, [jnp.stack(starts)]
    )

    grad_query, dk, dv = call(
        functools.partial(backward_kernel, scale),
        [(flat, BF16)] + [(flat, F32)] * 2,
        [query, key, value, g, store, *linear],
        [where],
        [total],
        flops=14 * square,
    )
    keep, back = call(carry_kernel, pair, parts, [flags], [dk])
    grad_key, grad_value = call(
        close_kernel,
        [(flat, BF16)] * 2,
        [key, value, dk, dv, keep, send(back, 1, 0)],
        [where],
        [done],
    )
    return mixed, grad_query, grad_key, grad_value


def near_and_far(attn, arrived, cotangent, mate_cotangent, weight, core, chip, colour, product):
    own, model = cotangent.shape
    wide = model // 2
    place = lax.axis_index("head")
    spots = jnp.stack([colour * wide, (1 - colour) * wide, core * DH, place])
    tokens = ((2 * own, DH), BF16)
    parts = [((own, wide), F32)] * 2
    all_arrays = [(cotangent, all_of, rows_at(0, own)), (mate_cotangent, all_of, rows_at(own, own))]
    whole = fetch((2 * own, model), *all_arrays)
    left = [
        fetch((2 * own, wide), *((a, columns(n, wide), put) for a, _, put in all_arrays))
        for n in range(2)
    ]

    def own_rows(ref, spots, *_):
        return ref.at[pl.ds(pl.multiple_of(spots[2], DH), DH)]

    def own_columns(n):
        return lambda ref, spots, *_: ref.at[
            pl.ds(pl.multiple_of(spots[2], DH), DH), pl.ds(pl.multiple_of(spots[n], DH), wide)
        ]

    def stacked(*arrays):
        return [(a, all_of, rows_at(n * DH, DH)) for n, a in enumerate(arrays)]

    arrived[2] = send(arrived[1], 0, 1)
    second = {1: send(arrived[1], 2, 0), 3: send(arrived[3], 4, 0)}
    mine, half = call(
        first_kernel,
        [tokens, ((2 * own, 2 * DH), F32)],
        [
            whole,
            fetch((DH, model), (weight, own_rows, all_of)),
            fetch((2 * DH, wide), *stacked(arrived[1], arrived[3])),
        ],
        [spots],
        lazy=True,
        room=6,
        flops=2 * product,
    )
    one, three, *cuts = call(
        second_kernel,
        [tokens] * 2 + [((DH, wide // 2), BF16)] * 2,
        [
            left[1],
            fetch((2 * DH, wide), *stacked(second[1], second[3])),
            half,
            fetch((DH, wide), (arrived[2], all_of, all_of)),
        ],
        [spots],
        room=6,
        flops=product,
    )
    second[2] = [send(cuts[0], 2, 0), send(cuts[1], 4, 0)]
    both = {0: mine, 1: send(one, 0, -1), 3: send(three, 0, -3)}
    across = {s: send(both[s], 1, 0) for s in (0, 1, 3)}
    (half,) = call(
        half_kernel,
        [((2 * own, DH), F32)],
        [left[0], fetch((DH, wide), (arrived[2], all_of, all_of))],
        [spots],
        [attn],
        room=6,
        flops=product // 2,
    )
    quarters = [(a, all_of, columns_at(n * wide // 2, wide // 2)) for n, a in enumerate(second[2])]
    (two,) = call(
        last_kernel,
        [tokens],
        [left[1], fetch((DH, wide), *quarters), half],
        [spots],
        [both[1], both[3]],
        room=6,
        flops=product // 2,
    )
    both[2] = send(two, 0, -2)
    across[2] = send(both[2], 1, 0)

    def quarter(n):
        return lambda ref, *_: ref.at[2 * DH : 3 * DH, n * wide // 2 : (n + 1) * wide // 2]

    def mix(after):
        outs = call(
            halves_kernel,
            parts * 2,
            [
                fetch(attn.shape, (attn, all_of, all_of)),
                fetch(
                    (4 * DH, wide),
                    (weight, own_columns(0), rows_at(0, DH)),
                    *((arrived[s], all_of, rows_at(s * DH, DH)) for s in (1, 2, 3)),
                ),
                fetch(
                    (4 * DH, wide),
                    (weight, own_columns(1), rows_at(0, DH)),
                    (second[1], all_of, rows_at(DH, DH)),
                    (second[3], all_of, rows_at(3 * DH, DH)),
                    *((a, all_of, quarter(n)) for n, a in enumerate(second[2])),
                ),
            ],
            [spots],
            after,
            room=8,
            flops=4 * product,
            lazy=True,
        )
        joins = [outs[0], send(outs[1], 1, 0), outs[2], send(outs[3], 1, 0)]
        return joins, [spots[0], spots[1]]

    return [both[s] for s in range(4)], [across[s] for s in range(4)], mix


def by_gathers(attn, arrived, cotangent, mate_cotangent, out_weight, core, chip, colour, product):
    own, model = cotangent.shape
    shards, count = lax.axis_size("ctx"), lax.axis_size("head")
    weight = lax.dynamic_slice_in_dim(out_weight, core * DH, DH, 0)
    zero = jnp.zeros((1,), jnp.int32)
    groups = [list(range(k, shards, 2)) for k in range(2)]
    for s in range(2, count - 1):
        arrived[s] = send(arrived[s - 1], 0, 1)
    chunks = [weight] + [
        lax.all_gather(arrived[s], "ctx", axis=1, tiled=True, axis_index_groups=groups)
        for s in range(1, count)
    ]
    both = []
    for s in range(count):
        (block,) = call(
            functools.partial(grad_kernel, True, 0),
            [((2 * own, DH), BF16)],
            [cotangent, mate_cotangent, chunks[s]],
            [zero],
            flops=product,
        )
        both.append(send(block, 0, -s) if s else block)
    def mix(after):
        part, mate_part = call(
            mixed_kernel,
            [((own, model), F32)] * 2,
            [attn, *chunks],
            [lax.axis_index("head").reshape(1)],
            after,
            room=16,
            flops=count * product,
        )
        return [part, send(mate_part, 1, 0)], [jnp.int32(0)]

    return both, [send(b, 1, 0) for b in both], mix


def solution(mesh):
    return jax.shard_map(
        on_device,
        mesh=mesh,
        in_specs=(
            P("ctx", "head"),
            P("ctx", "head"),
            P("ctx", "head"),
            P("ctx", None),
            P("head", None),
            P(("ctx", "head"), None),
        ),
        out_specs=(P(("ctx", "head"), None), P("ctx", "head"), P("ctx", "head"), P("ctx", "head")),
        check_vma=False,
    )
```

```python
import functools
import math

import jax
import jax.numpy as jnp
from jax import lax
from jax.experimental import pallas as pl
from jax.experimental.pallas import tpu as pltpu
from jax.sharding import PartitionSpec as P

DH = 128
F32 = jnp.float32
BF16 = jnp.bfloat16
NN = ((1,), (0,))
NT = ((1,), (1,))
TN = ((0,), (0,))
MIB = 1 << 20


def dot(a, b, dims):
    return lax.dot_general(a, b, (dims, ((), ())), preferred_element_type=F32)


def dot_wide(a, b, dims):
    high = b.astype(BF16)
    low = (b - high.astype(F32)).astype(BF16)
    both = dot(a, jnp.concatenate([high, low], 1 - dims[1][0]), dims)
    return both[:, :DH] + both[:, DH:]


def fetch(shape, *parts):
    return (shape, parts)


def all_of(ref, *_):
    return ref


def columns(spot, wide, rows=slice(None)):
    def view(ref, spots, *_):
        return ref.at[rows, pl.ds(pl.multiple_of(spots[spot], DH), wide)]

    return view


def rows_at(first, count):
    return lambda ref, *_: ref.at[first : first + count]


def columns_at(first, count):
    return lambda ref, *_: ref.at[:, first : first + count]


def call(body, outs, args, smem=(), after=(), room=2, flops=1, lazy=False):
    arrays, specs, scratch = [], [], []
    for arg in args:
        if isinstance(arg, tuple):
            arrays += [part[0] for part in arg[1]]
            specs += [pl.BlockSpec(memory_space=pltpu.HBM) for _ in arg[1]]
            scratch.append(pltpu.VMEM(arg[0], arg[1][0][0].dtype))
        else:
            arrays.append(arg)
            specs.append(pl.BlockSpec(memory_space=pltpu.VMEM))
    copies = sum(len(arg[1]) for arg in args if isinstance(arg, tuple))
    held = len(scratch)
    if copies:
        scratch.append(pltpu.SemaphoreType.DMA((copies,)))

    def kernel(*refs):
        scalars, refs = refs[: len(smem)], list(refs[len(smem) :])
        ins, refs = refs[: len(arrays)], refs[len(arrays) + len(after) :]
        results, slots = refs[: len(outs)], refs[len(outs) :]
        given, started, slot, groups = [], [], 0, []
        for arg in args:
            if not isinstance(arg, tuple):
                given.append(ins.pop(0))
                continue
            for _, source, target in arg[1]:
                copy = pltpu.make_async_copy(
                    source(ins.pop(0), *scalars),
                    target(slots[slot], *scalars),
                    slots[held].at[len(started)],
                )
                copy.start()
                started.append(copy)
            given.append(slots[slot])
            groups.append(started[sum(len(group) for group in groups) :])
            slot += 1

        def ready(n):
            for copy in groups[n]:
                copy.wait()

        if lazy:
            body(ready, *scalars, *given, *results)
            return
        for n in range(len(groups)):
            ready(n)
        body(*scalars, *given, *results)

    moved = sum(a.size * a.dtype.itemsize for a in arrays)
    moved += sum(math.prod(s) * jnp.dtype(t).itemsize for s, t in outs)
    return pl.pallas_call(
        kernel,
        out_shape=[jax.ShapeDtypeStruct(s, t) for s, t in outs],
        in_specs=[pl.BlockSpec(memory_space=pltpu.SMEM) for _ in smem]
        + specs
        + [pl.BlockSpec(memory_space=pl.ANY) for _ in after],
        out_specs=[pl.BlockSpec(memory_space=pltpu.VMEM) for _ in outs],
        scratch_shapes=scratch,
        compiler_params=pltpu.CompilerParams(vmem_limit_bytes=room * MIB),
        cost_estimate=pl.CostEstimate(
            flops=int(flops), bytes_accessed=int(moved), transcendentals=0
        ),
    )(*smem, *arrays, *after)


def hold(arrays, after):
    held = len(arrays)
    return pl.pallas_call(
        lambda *refs: None,
        out_shape=[jax.ShapeDtypeStruct(a.shape, a.dtype) for a in arrays],
        in_specs=[pl.BlockSpec(memory_space=pl.ANY) for _ in (*arrays, *after)],
        out_specs=[pl.BlockSpec(memory_space=pl.ANY) for _ in arrays],
        input_output_aliases={n: n for n in range(held)},
        cost_estimate=pl.CostEstimate(flops=1, bytes_accessed=1, transcendentals=0),
    )(*arrays, *after)


def lower_triangle(blk):
    return lax.broadcasted_iota(jnp.int32, (blk, blk), 0) >= lax.broadcasted_iota(
        jnp.int32, (blk, blk), 1
    )


def forward_kernel(
    scale,
    mask,
    where,
    all_ref,
    store_ref,
    mine_ref,
    other_ref,
    far_ref,
    mine_state_ref,
    other_state_ref,
):
    q_ref, k_ref, v_ref = (all_ref.at[n] for n in range(3))
    heads = [slice(h * DH, (h + 1) * DH) for h in range(2)]
    states = [dot(k_ref[:, cols], v_ref[:, cols], TN) for cols in heads]
    mine_state_ref[...], other_state_ref[...] = pick(where[2], states)
    rows, width = q_ref.shape
    count = mask.shape[0]
    blk = rows // count
    inv_root = 1.0 / math.sqrt(DH)
    triangle = lower_triangle(blk)
    sums = []
    for h in range(2):
        raw = dot(q_ref[:, heads[h]], k_ref[:, heads[h]], NT)
        probs, inner = [], []
        for i in range(count):
            own = raw[i * blk : (i + 1) * blk]
            scores, linear = [], []
            for j in range(i + 1):
                part = own[:, j * blk : (j + 1) * blk]
                keep = triangle if j == i else mask[i, j] > 0
                scores.append(jnp.where(keep, part * inv_root, -1e30))
                linear.append(jnp.where(triangle, part, 0.0) if j == i else part)
            empty = [jnp.zeros((blk, blk), F32)] * (count - 1 - i)
            scores = jnp.concatenate(scores, 1)
            expo = jnp.exp(scores - jnp.max(scores, -1, keepdims=True))
            share = expo / jnp.sum(expo, -1, keepdims=True)
            probs.append(jnp.concatenate([share, *empty], 1).astype(BF16))
            inner.append(jnp.concatenate([*linear, *empty], 1).astype(BF16))
        stacked = jnp.concatenate(probs + inner, 0)
        store_ref[h], store_ref[2 + h] = stacked[:rows], stacked[rows:]
        both = dot(stacked, v_ref[:, heads[h]], NN)
        sums.append(both[:rows] + scale * both[rows:])
    mine_ref[...], other_ref[...] = pick(where[2], sums)
    far_ref[...] = q_ref[:, pl.ds(pl.multiple_of((1 - where[2]) * DH, DH), DH)]


def pick(core, parts):
    return jnp.where(core == 0, parts[0], parts[1]), jnp.where(core == 0, parts[1], parts[0])


def both_heads(core, mine_ref, other_ref):
    mine, other = mine_ref[...], other_ref[...]
    return jnp.where(core == 0, mine, other), jnp.where(core == 0, other, mine)


def carry(flags, here_ref, got_ref, totals):
    carried = jnp.zeros(here_ref.shape, F32)
    for n, total in enumerate(totals):
        carried = carried + jnp.where(flags[n] > 0, total[...], 0.0)
    counts = flags[len(totals)] > 0
    keep = carried + jnp.where(counts, got_ref[...], 0.0)
    return keep, carried + jnp.where(counts, 0.0, here_ref[...])


def carry_kernel(flags, here_ref, got_ref, *refs):
    totals, (keep_ref, back_ref) = refs[:-2], refs[-2:]
    keep_ref[...], back_ref[...] = carry(flags, here_ref, got_ref, totals)


def attn_kernel(scale, flags, where, here_ref, got_ref, *refs):
    totals, refs = refs[:-7], refs[-7:]
    q_ref, far_ref, pre_ref, far_pre_ref, out_ref, keep_ref, back_ref = refs
    keep, back = carry(flags, here_ref, got_ref, totals)
    keep_ref[...], back_ref[...] = keep, back
    count = out_ref.shape[0]
    own = pre_ref.shape[0] // count
    cols = pl.ds(pl.multiple_of(where[2] * DH, DH), DH)
    mine = pre_ref[...] + scale * dot_wide(q_ref[:, cols], keep, NN)
    mate = far_pre_ref[...] + scale * dot_wide(far_ref[...], back, NN)
    for z in range(count):
        out_ref[z, :own] = mine[z * own : (z + 1) * own].astype(BF16)
        out_ref[z, own:] = mate[z * own : (z + 1) * own].astype(BF16)


def back_along(attn_ref, place):
    count = attn_ref.shape[0]
    return jnp.concatenate([attn_ref[lax.rem(place - s + count, count)] for s in range(count)], 1)


def first_kernel(ready, spots, left_ref, weight_ref, right_ref, own_ref, half_ref):
    ready(0)
    ready(1)
    own_ref[...] = dot(left_ref[...], weight_ref[...], NT).astype(BF16)
    ready(2)
    near = left_ref[:, pl.ds(pl.multiple_of(spots[0], DH), right_ref.shape[1])]
    half_ref[...] = dot(near, right_ref[...], NT)


def second_kernel(spots, left_ref, right_ref, half_ref, piece_ref, one_ref, three_ref, *cut_refs):
    wide = cut_refs[0].shape[1]
    for n, cut_ref in enumerate(cut_refs):
        cut_ref[...] = piece_ref[:, n * wide : (n + 1) * wide]
    total = (half_ref[...] + dot(left_ref[...], right_ref[...], NT)).astype(BF16)
    one_ref[...], three_ref[...] = total[:, :DH], total[:, DH:]


def last_kernel(spots, left_ref, right_ref, half_ref, out_ref):
    out_ref[...] = (half_ref[...] + dot(left_ref[...], right_ref[...], NT)).astype(BF16)


def half_kernel(spots, left_ref, right_ref, half_ref):
    half_ref[...] = dot(left_ref[...], right_ref[...], NT)


def halves_kernel(ready, spots, attn_ref, *refs):
    rights, outs = refs[:2], refs[2:]
    own = outs[0].shape[0]
    ready(0)
    left = back_along(attn_ref, spots[3])
    for n, right_ref in enumerate(rights):
        ready(1 + n)
        part = dot(left, right_ref[...], NN)
        outs[2 * n][...] = part[:own]
        outs[2 * n + 1][...] = part[own:]


def grad_kernel(whole, added, places, mine_ref, mate_ref, *refs):
    chunks, out_ref = refs[added:-1], refs[-1]
    total = refs[0][...] if added else None
    for j, chunk in enumerate(chunks):
        cols = slice(None) if whole else pl.ds(pl.multiple_of(places[j], DH), chunk.shape[1])
        left = jnp.concatenate([mine_ref[:, cols], mate_ref[:, cols]], 0)
        part = dot(left, chunk[...], NT)
        total = part if total is None else total + part
    out_ref[...] = total.astype(out_ref.dtype)


def mixed_kernel(where, attn_ref, *refs):
    chunks, (own_out, mate_out) = refs[:-2], refs[-2:]
    own = own_out.shape[0]
    right = jnp.concatenate([chunk[...] for chunk in chunks], 0)
    part = dot(back_along(attn_ref, where[0]), right, NN)
    own_out[...] = part[:own]
    mate_out[...] = part[own:]


def join_kernel(places, *refs):
    out_ref, done_ref = refs[-2:]
    done_ref[...] = jnp.zeros(done_ref.shape, F32)
    for n in range(len(refs) // 2 - 1):
        wide = refs[2 * n].shape[1]
        there = pl.ds(pl.multiple_of(places[n], DH), wide)
        out_ref[:, there] = (refs[2 * n][...] + refs[2 * n + 1][...]).astype(BF16)


def collect_kernel(scale, count, where, q_ref, *refs):
    direct, across = refs[:count], refs[count : 2 * count]
    g_ref, mine_ref, other_ref = refs[2 * count :]
    own = g_ref.shape[0] // count
    mine = pl.ds(pl.multiple_of(where[2] * DH, DH), DH)
    mate = pl.ds(pl.multiple_of((1 - where[2]) * DH, DH), DH)
    for s in range(count):
        block = lax.rem(where[0] + s, count)
        here = pl.ds(pl.multiple_of(block * own, own), own)
        g_ref[here, mine] = direct[s][:own]
        g_ref[here, mate] = across[s][own:]
    heads = [slice(h * DH, (h + 1) * DH) for h in range(2)]
    parts = [scale * dot(q_ref[:, cols], g_ref[:, cols], TN) for cols in heads]
    mine_ref[...], other_ref[...] = pick(where[2], parts)


def backward_kernel(
    scale, where, q_ref, k_ref, v_ref, g_ref, store_ref, mine_ref, other_ref, dq_ref, dk_ref, dv_ref
):
    rows, width = q_ref.shape
    inv_root = 1.0 / math.sqrt(DH)
    triangle = lower_triangle(rows)
    states = both_heads(where[2], mine_ref, other_ref)
    for h in range(width // DH):
        cols = slice(h * DH, (h + 1) * DH)
        q, k, v, g = q_ref[:, cols], k_ref[:, cols], v_ref[:, cols], g_ref[:, cols]
        probs, inner = store_ref[h], store_ref[2 + h]
        dprod = dot(g, v, NT)
        delta = jnp.sum(g.astype(F32) * dot(probs, v, NN), -1, keepdims=True)
        dscore = (probs.astype(F32) * (dprod - delta) * inv_root).astype(BF16)
        dinner = jnp.where(triangle, dprod, 0.0).astype(BF16)
        left = dot(jnp.concatenate([dscore, dinner], 0), k, NN)
        linear = left[rows:] + dot_wide(g, states[h], NT)
        dq_ref[:, cols] = (left[:rows] + scale * linear).astype(BF16)
        dk = dot(jnp.concatenate([dscore, dinner], 1), q, TN)
        dk_ref[:, cols] = dk[:rows] + scale * dk[rows:]
        dv = dot(jnp.concatenate([probs, inner], 1), g, TN)
        dv_ref[:, cols] = dv[:rows] + scale * dv[rows:]


def close_kernel(where, k_ref, v_ref, dk_ref, dv_ref, mine_ref, other_ref, gk_ref, gv_ref):
    states = both_heads(where[2], mine_ref, other_ref)
    for h in range(k_ref.shape[1] // DH):
        cols = slice(h * DH, (h + 1) * DH)
        state = states[h]
        gk_ref[:, cols] = (dk_ref[:, cols] + dot_wide(v_ref[:, cols], state, NT)).astype(BF16)
        gv_ref[:, cols] = (dv_ref[:, cols] + dot_wide(k_ref[:, cols], state, NN)).astype(BF16)


def send(x, flip, shift):
    shards, heads = lax.axis_size("ctx"), lax.axis_size("head")
    pairs = [
        (c * heads + z, (c ^ flip) * heads + (z + shift) % heads)
        for c in range(shards)
        for z in range(heads)
    ]
    return lax.ppermute(x, ("ctx", "head"), pairs)


def exchange(mine, other, core, chip, chips, later):
    got = send(other, 1, 0)
    own = total = mine + got
    totals, flags = [], []
    if chips == 4:
        for flip in (1, 2, 3):
            totals.append(send(total, 2 * flip, 0))
            flags.append(((chip ^ flip) > chip) == later)
    else:
        step = 1
        while step < chips:
            totals.append(send(total, 2 * step, 0))
            flags.append(((chip & step) == 0) == later)
            total = total + totals[-1]
            step *= 2
    flags.append((core == 0) == later)
    return jnp.stack(flags).astype(jnp.int32), [mine, got, *totals], own


def on_device(query, key, value, block_mask, out_weight, cotangent):
    rows, width = query.shape
    heads = width // DH
    shards, count = lax.axis_size("ctx"), lax.axis_size("head")
    model = out_weight.shape[1]
    own = rows // count
    scale = 1.0 / math.sqrt(DH * rows * shards)
    ctx, place = lax.axis_index("ctx"), lax.axis_index("head")
    core, chip, chips = ctx & 1, ctx >> 1, shards // 2
    where = jnp.stack([place, ctx, core])
    flat, square = (rows, width), rows * rows * DH * heads
    pair = [((DH, DH), F32)] * 2
    tokens = ((2 * own, DH), BF16)
    product = 4 * own * DH * model

    board = chips == 4 and count == 4
    wide = model // (2 if board else chips)
    colour = (chip & 1) ^ (chip >> 1) if board else chip
    piece = lax.dynamic_slice(out_weight, (core * DH, colour * wide), (DH, wide))
    arrived = {1: send(piece, 0, 1), count - 1: send(piece, 0, -1)}
    mate_cotangent = send(cotangent, 1, 0)

    store, pre, other_pre, far, mine, other = call(
        functools.partial(forward_kernel, scale),
        [((2 * heads, rows, rows), BF16)]
        + [((rows, DH), F32)] * 2
        + [((rows, DH), BF16)]
        + pair,
        [jnp.stack([query, key, value])],
        [block_mask, where],
        [mate_cotangent],
        flops=7 * square,
    )
    far, other_pre = send(far, 1, 0), send(other_pre, 1, 0)
    (mine,) = hold([mine], [far, other_pre])
    flags, parts, total = exchange(mine, other, core, chip, chips, False)
    attn, keep, back = call(
        functools.partial(attn_kernel, scale),
        [((count, *tokens[0]), BF16), *pair],
        [*parts, query, far, pre, other_pre],
        [flags, where],
    )
    linear = [keep, send(back, 1, 0)]
    if board:
        arrived[1], arrived[3] = hold([arrived[1], arrived[3]], [keep])
    attn = lax.all_to_all(attn, "head", 0, 0, tiled=True)

    work = near_and_far if board else by_gathers
    both, across, mix = work(
        attn, arrived, cotangent, mate_cotangent, out_weight, core, chip, colour, product
    )
    g, mine, other = call(
        functools.partial(collect_kernel, scale, count),
        [(flat, BF16), *pair],
        [query, *both, *across],
        [where],
        linear[1:],
    )
    flags, parts, total = exchange(mine, other, core, chip, chips, True)
    joins, starts = mix([total])
    mixed, done = call(
        join_kernel, [((own, model), BF16), ((8, DH), F32)], joins, [jnp.stack(starts)]
    )

    grad_query, dk, dv = call(
        functools.partial(backward_kernel, scale),
        [(flat, BF16)] + [(flat, F32)] * 2,
        [query, key, value, g, store, *linear],
        [where],
        [total],
        flops=14 * square,
    )
    keep, back = call(carry_kernel, pair, parts, [flags], [dk])
    grad_key, grad_value = call(
        close_kernel,
        [(flat, BF16)] * 2,
        [key, value, dk, dv, keep, send(back, 1, 0)],
        [where],
        [done],
    )
    return mixed, grad_query, grad_key, grad_value


def near_and_far(attn, arrived, cotangent, mate_cotangent, weight, core, chip, colour, product):
    own, model = cotangent.shape
    wide = model // 2
    place = lax.axis_index("head")
    spots = jnp.stack([colour * wide, (1 - colour) * wide, core * DH, place])
    tokens = ((2 * own, DH), BF16)
    parts = [((own, wide), F32)] * 2
    all_arrays = [(cotangent, all_of, rows_at(0, own)), (mate_cotangent, all_of, rows_at(own, own))]
    whole = fetch((2 * own, model), *all_arrays)
    left = [
        fetch((2 * own, wide), *((a, columns(n, wide), put) for a, _, put in all_arrays))
        for n in range(2)
    ]

    def own_rows(ref, spots, *_):
        return ref.at[pl.ds(pl.multiple_of(spots[2], DH), DH)]

    def own_columns(n):
        return lambda ref, spots, *_: ref.at[
            pl.ds(pl.multiple_of(spots[2], DH), DH), pl.ds(pl.multiple_of(spots[n], DH), wide)
        ]

    def stacked(*arrays):
        return [(a, all_of, rows_at(n * DH, DH)) for n, a in enumerate(arrays)]

    arrived[2] = send(arrived[1], 0, 1)
    second = {1: send(arrived[1], 2, 0), 3: send(arrived[3], 4, 0)}
    mine, half = call(
        first_kernel,
        [tokens, ((2 * own, 2 * DH), F32)],
        [
            whole,
            fetch((DH, model), (weight, own_rows, all_of)),
            fetch((2 * DH, wide), *stacked(arrived[1], arrived[3])),
        ],
        [spots],
        lazy=True,
        room=6,
        flops=2 * product,
    )
    (half,) = hold([half], [arrived[2]])
    one, three, *cuts = call(
        second_kernel,
        [tokens] * 2 + [((DH, wide // 2), BF16)] * 2,
        [
            left[1],
            fetch((2 * DH, wide), *stacked(second[1], second[3])),
            half,
            fetch((DH, wide), (arrived[2], all_of, all_of)),
        ],
        [spots],
        room=6,
        flops=product,
    )
    second[2] = [send(cuts[0], 2, 0), send(cuts[1], 4, 0)]
    both = {0: mine, 1: send(one, 0, -1), 3: send(three, 0, -3)}
    across = {s: send(both[s], 1, 0) for s in (0, 1, 3)}
    (half,) = call(
        half_kernel,
        [((2 * own, DH), F32)],
        [left[0], fetch((DH, wide), (arrived[2], all_of, all_of))],
        [spots],
        [attn],
        room=6,
        flops=product // 2,
    )
    quarters = [(a, all_of, columns_at(n * wide // 2, wide // 2)) for n, a in enumerate(second[2])]
    (two,) = call(
        last_kernel,
        [tokens],
        [left[1], fetch((DH, wide), *quarters), half],
        [spots],
        [both[1], both[3]],
        room=6,
        flops=product // 2,
    )
    both[2] = send(two, 0, -2)
    across[2] = send(both[2], 1, 0)

    def quarter(n):
        return lambda ref, *_: ref.at[2 * DH : 3 * DH, n * wide // 2 : (n + 1) * wide // 2]

    def mix(after):
        outs = call(
            halves_kernel,
            parts * 2,
            [
                fetch(attn.shape, (attn, all_of, all_of)),
                fetch(
                    (4 * DH, wide),
                    (weight, own_columns(0), rows_at(0, DH)),
                    *((arrived[s], all_of, rows_at(s * DH, DH)) for s in (1, 2, 3)),
                ),
                fetch(
                    (4 * DH, wide),
                    (weight, own_columns(1), rows_at(0, DH)),
                    (second[1], all_of, rows_at(DH, DH)),
                    (second[3], all_of, rows_at(3 * DH, DH)),
                    *((a, all_of, quarter(n)) for n, a in enumerate(second[2])),
                ),
            ],
            [spots],
            after,
            room=8,
            flops=4 * product,
            lazy=True,
        )
        joins = [outs[0], send(outs[1], 1, 0), outs[2], send(outs[3], 1, 0)]
        return joins, [spots[0], spots[1]]

    return [both[s] for s in range(4)], [across[s] for s in range(4)], mix


def by_gathers(attn, arrived, cotangent, mate_cotangent, out_weight, core, chip, colour, product):
    own, model = cotangent.shape
    shards, count = lax.axis_size("ctx"), lax.axis_size("head")
    weight = lax.dynamic_slice_in_dim(out_weight, core * DH, DH, 0)
    zero = jnp.zeros((1,), jnp.int32)
    groups = [list(range(k, shards, 2)) for k in range(2)]
    for s in range(2, count - 1):
        arrived[s] = send(arrived[s - 1], 0, 1)
    chunks = [weight] + [
        lax.all_gather(arrived[s], "ctx", axis=1, tiled=True, axis_index_groups=groups)
        for s in range(1, count)
    ]
    both = []
    for s in range(count):
        (block,) = call(
            functools.partial(grad_kernel, True, 0),
            [((2 * own, DH), BF16)],
            [cotangent, mate_cotangent, chunks[s]],
            [zero],
            flops=product,
        )
        both.append(send(block, 0, -s) if s else block)
    def mix(after):
        part, mate_part = call(
            mixed_kernel,
            [((own, model), F32)] * 2,
            [attn, *chunks],
            [lax.axis_index("head").reshape(1)],
            after,
            room=16,
            flops=count * product,
        )
        return [part, send(mate_part, 1, 0)], [jnp.int32(0)]

    return both, [send(b, 1, 0) for b in both], mix


def solution(mesh):
    return jax.shard_map(
        on_device,
        mesh=mesh,
        in_specs=(
            P("ctx", "head"),
            P("ctx", "head"),
            P("ctx", "head"),
            P("ctx", None),
            P("head", None),
            P(("ctx", "head"), None),
        ),
        out_specs=(P(("ctx", "head"), None), P("ctx", "head"), P("ctx", "head"), P("ctx", "head")),
        check_vma=False,
    )
```

```python
import functools
import math

import jax
import jax.numpy as jnp
from jax import lax
from jax.experimental import pallas as pl
from jax.experimental.pallas import tpu as pltpu
from jax.sharding import PartitionSpec as P

DH = 128
F32 = jnp.float32
BF16 = jnp.bfloat16
NN = ((1,), (0,))
NT = ((1,), (1,))
TN = ((0,), (0,))
MIB = 1 << 20


def dot(a, b, dims):
    return lax.dot_general(a, b, (dims, ((), ())), preferred_element_type=F32)


def dot_wide(a, b, dims):
    high = b.astype(BF16)
    low = (b - high.astype(F32)).astype(BF16)
    both = dot(a, jnp.concatenate([high, low], 1 - dims[1][0]), dims)
    return both[:, :DH] + both[:, DH:]


def fetch(shape, *parts):
    return (shape, parts)


def all_of(ref, *_):
    return ref


def columns(spot, wide, rows=slice(None)):
    def view(ref, spots, *_):
        return ref.at[rows, pl.ds(pl.multiple_of(spots[spot], DH), wide)]

    return view


def rows_at(first, count):
    return lambda ref, *_: ref.at[first : first + count]


def columns_at(first, count):
    return lambda ref, *_: ref.at[:, first : first + count]


def call(body, outs, args, smem=(), after=(), room=2, flops=1, lazy=False):
    arrays, specs, scratch = [], [], []
    for arg in args:
        if isinstance(arg, tuple):
            arrays += [part[0] for part in arg[1]]
            specs += [pl.BlockSpec(memory_space=pltpu.HBM) for _ in arg[1]]
            scratch.append(pltpu.VMEM(arg[0], arg[1][0][0].dtype))
        else:
            arrays.append(arg)
            specs.append(pl.BlockSpec(memory_space=pltpu.VMEM))
    copies = sum(len(arg[1]) for arg in args if isinstance(arg, tuple))
    held = len(scratch)
    if copies:
        scratch.append(pltpu.SemaphoreType.DMA((copies,)))

    def kernel(*refs):
        scalars, refs = refs[: len(smem)], list(refs[len(smem) :])
        ins, refs = refs[: len(arrays)], refs[len(arrays) + len(after) :]
        results, slots = refs[: len(outs)], refs[len(outs) :]
        given, started, slot, groups = [], [], 0, []
        for arg in args:
            if not isinstance(arg, tuple):
                given.append(ins.pop(0))
                continue
            for _, source, target in arg[1]:
                copy = pltpu.make_async_copy(
                    source(ins.pop(0), *scalars),
                    target(slots[slot], *scalars),
                    slots[held].at[len(started)],
                )
                copy.start()
                started.append(copy)
            given.append(slots[slot])
            groups.append(started[sum(len(group) for group in groups) :])
            slot += 1

        def ready(n):
            for copy in groups[n]:
                copy.wait()

        if lazy:
            body(ready, *scalars, *given, *results)
            return
        for n in range(len(groups)):
            ready(n)
        body(*scalars, *given, *results)

    moved = sum(a.size * a.dtype.itemsize for a in arrays)
    moved += sum(math.prod(s) * jnp.dtype(t).itemsize for s, t in outs)
    return pl.pallas_call(
        kernel,
        out_shape=[jax.ShapeDtypeStruct(s, t) for s, t in outs],
        in_specs=[pl.BlockSpec(memory_space=pltpu.SMEM) for _ in smem]
        + specs
        + [pl.BlockSpec(memory_space=pl.ANY) for _ in after],
        out_specs=[pl.BlockSpec(memory_space=pltpu.VMEM) for _ in outs],
        scratch_shapes=scratch,
        compiler_params=pltpu.CompilerParams(vmem_limit_bytes=room * MIB),
        cost_estimate=pl.CostEstimate(
            flops=int(flops), bytes_accessed=int(moved), transcendentals=0
        ),
    )(*smem, *arrays, *after)


def hold(arrays, after):
    held = len(arrays)
    return pl.pallas_call(
        lambda *refs: None,
        out_shape=[jax.ShapeDtypeStruct(a.shape, a.dtype) for a in arrays],
        in_specs=[pl.BlockSpec(memory_space=pl.ANY) for _ in (*arrays, *after)],
        out_specs=[pl.BlockSpec(memory_space=pl.ANY) for _ in arrays],
        input_output_aliases={n: n for n in range(held)},
        cost_estimate=pl.CostEstimate(flops=1, bytes_accessed=1, transcendentals=0),
    )(*arrays, *after)


def lower_triangle(blk):
    return lax.broadcasted_iota(jnp.int32, (blk, blk), 0) >= lax.broadcasted_iota(
        jnp.int32, (blk, blk), 1
    )


def forward_kernel(
    scale,
    mask,
    where,
    all_ref,
    store_ref,
    mine_ref,
    other_ref,
    far_ref,
    mine_state_ref,
    other_state_ref,
):
    q_ref, k_ref, v_ref = (all_ref.at[n] for n in range(3))
    heads = [slice(h * DH, (h + 1) * DH) for h in range(2)]
    states = [dot(k_ref[:, cols], v_ref[:, cols], TN) for cols in heads]
    mine_state_ref[...], other_state_ref[...] = pick(where[2], states)
    rows, width = q_ref.shape
    count = mask.shape[0]
    blk = rows // count
    inv_root = 1.0 / math.sqrt(DH)
    triangle = lower_triangle(blk)
    sums = []
    for h in range(2):
        raw = dot(q_ref[:, heads[h]], k_ref[:, heads[h]], NT)
        probs, inner = [], []
        for i in range(count):
            own = raw[i * blk : (i + 1) * blk]
            scores, linear = [], []
            for j in range(i + 1):
                part = own[:, j * blk : (j + 1) * blk]
                keep = triangle if j == i else mask[i, j] > 0
                scores.append(jnp.where(keep, part * inv_root, -1e30))
                linear.append(jnp.where(triangle, part, 0.0) if j == i else part)
            empty = [jnp.zeros((blk, blk), F32)] * (count - 1 - i)
            scores = jnp.concatenate(scores, 1)
            expo = jnp.exp(scores - jnp.max(scores, -1, keepdims=True))
            share = expo / jnp.sum(expo, -1, keepdims=True)
            probs.append(jnp.concatenate([share, *empty], 1).astype(BF16))
            inner.append(jnp.concatenate([*linear, *empty], 1).astype(BF16))
        stacked = jnp.concatenate(probs + inner, 0)
        store_ref[h], store_ref[2 + h] = stacked[:rows], stacked[rows:]
        both = dot(stacked, v_ref[:, heads[h]], NN)
        sums.append(both[:rows] + scale * both[rows:])
    mine_ref[...], other_ref[...] = pick(where[2], sums)
    far_ref[...] = q_ref[:, pl.ds(pl.multiple_of((1 - where[2]) * DH, DH), DH)]


def pick(core, parts):
    return jnp.where(core == 0, parts[0], parts[1]), jnp.where(core == 0, parts[1], parts[0])


def both_heads(core, mine_ref, other_ref):
    mine, other = mine_ref[...], other_ref[...]
    return jnp.where(core == 0, mine, other), jnp.where(core == 0, other, mine)


def carry(flags, here_ref, got_ref, totals):
    carried = jnp.zeros(here_ref.shape, F32)
    for n, total in enumerate(totals):
        carried = carried + jnp.where(flags[n] > 0, total[...], 0.0)
    counts = flags[len(totals)] > 0
    keep = carried + jnp.where(counts, got_ref[...], 0.0)
    return keep, carried + jnp.where(counts, 0.0, here_ref[...])


def carry_kernel(flags, here_ref, got_ref, *refs):
    totals, (keep_ref, back_ref) = refs[:-2], refs[-2:]
    keep_ref[...], back_ref[...] = carry(flags, here_ref, got_ref, totals)


def attn_kernel(scale, flags, where, here_ref, got_ref, *refs):
    totals, refs = refs[:-7], refs[-7:]
    q_ref, far_ref, pre_ref, far_pre_ref, out_ref, keep_ref, back_ref = refs
    keep, back = carry(flags, here_ref, got_ref, totals)
    keep_ref[...], back_ref[...] = keep, back
    count = out_ref.shape[0]
    own = pre_ref.shape[0] // count
    cols = pl.ds(pl.multiple_of(where[2] * DH, DH), DH)
    mine = pre_ref[...] + scale * dot_wide(q_ref[:, cols], keep, NN)
    mate = far_pre_ref[...] + scale * dot_wide(far_ref[...], back, NN)
    for z in range(count):
        out_ref[z, :own] = mine[z * own : (z + 1) * own].astype(BF16)
        out_ref[z, own:] = mate[z * own : (z + 1) * own].astype(BF16)


def back_along(attn_ref, place):
    count = attn_ref.shape[0]
    return jnp.concatenate([attn_ref[lax.rem(place - s + count, count)] for s in range(count)], 1)


def first_kernel(ready, spots, left_ref, weight_ref, right_ref, own_ref, half_ref):
    ready(0)
    ready(1)
    own_ref[...] = dot(left_ref[...], weight_ref[...], NT).astype(BF16)
    ready(2)
    near = left_ref[:, pl.ds(pl.multiple_of(spots[0], DH), right_ref.shape[1])]
    half_ref[...] = dot(near, right_ref[...], NT)


def second_kernel(spots, left_ref, right_ref, half_ref, piece_ref, one_ref, three_ref, *cut_refs):
    wide = cut_refs[0].shape[1]
    for n, cut_ref in enumerate(cut_refs):
        cut_ref[...] = piece_ref[:, n * wide : (n + 1) * wide]
    total = (half_ref[...] + dot(left_ref[...], right_ref[...], NT)).astype(BF16)
    one_ref[...], three_ref[...] = total[:, :DH], total[:, DH:]


def last_kernel(spots, left_ref, right_ref, half_ref, out_ref):
    out_ref[...] = (half_ref[...] + dot(left_ref[...], right_ref[...], NT)).astype(BF16)


def half_kernel(spots, left_ref, right_ref, half_ref):
    half_ref[...] = dot(left_ref[...], right_ref[...], NT)


def halves_kernel(ready, spots, attn_ref, *refs):
    rights, outs = refs[:2], refs[2:]
    own = outs[0].shape[0]
    ready(0)
    left = back_along(attn_ref, spots[3])
    for n, right_ref in enumerate(rights):
        ready(1 + n)
        part = dot(left, right_ref[...], NN)
        outs[2 * n][...] = part[:own]
        outs[2 * n + 1][...] = part[own:]


def grad_kernel(whole, added, places, mine_ref, mate_ref, *refs):
    chunks, out_ref = refs[added:-1], refs[-1]
    total = refs[0][...] if added else None
    for j, chunk in enumerate(chunks):
        cols = slice(None) if whole else pl.ds(pl.multiple_of(places[j], DH), chunk.shape[1])
        left = jnp.concatenate([mine_ref[:, cols], mate_ref[:, cols]], 0)
        part = dot(left, chunk[...], NT)
        total = part if total is None else total + part
    out_ref[...] = total.astype(out_ref.dtype)


def mixed_kernel(where, attn_ref, *refs):
    chunks, (own_out, mate_out) = refs[:-2], refs[-2:]
    own = own_out.shape[0]
    right = jnp.concatenate([chunk[...] for chunk in chunks], 0)
    part = dot(back_along(attn_ref, where[0]), right, NN)
    own_out[...] = part[:own]
    mate_out[...] = part[own:]


def join_kernel(places, *refs):
    out_ref, done_ref = refs[-2:]
    done_ref[...] = jnp.zeros(done_ref.shape, F32)
    for n in range(len(refs) // 2 - 1):
        wide = refs[2 * n].shape[1]
        there = pl.ds(pl.multiple_of(places[n], DH), wide)
        out_ref[:, there] = (refs[2 * n][...] + refs[2 * n + 1][...]).astype(BF16)


def collect_kernel(scale, count, where, q_ref, *refs):
    direct, across = refs[:count], refs[count : 2 * count]
    g_ref, mine_ref, other_ref = refs[2 * count :]
    own = g_ref.shape[0] // count
    mine = pl.ds(pl.multiple_of(where[2] * DH, DH), DH)
    mate = pl.ds(pl.multiple_of((1 - where[2]) * DH, DH), DH)
    for s in range(count):
        block = lax.rem(where[0] + s, count)
        here = pl.ds(pl.multiple_of(block * own, own), own)
        g_ref[here, mine] = direct[s][:own]
        g_ref[here, mate] = across[s][own:]
    heads = [slice(h * DH, (h + 1) * DH) for h in range(2)]
    parts = [scale * dot(q_ref[:, cols], g_ref[:, cols], TN) for cols in heads]
    mine_ref[...], other_ref[...] = pick(where[2], parts)


def backward_kernel(
    scale, where, q_ref, k_ref, v_ref, g_ref, store_ref, mine_ref, other_ref, dq_ref, dk_ref, dv_ref
):
    rows, width = q_ref.shape
    inv_root = 1.0 / math.sqrt(DH)
    triangle = lower_triangle(rows)
    states = both_heads(where[2], mine_ref, other_ref)
    for h in range(width // DH):
        cols = slice(h * DH, (h + 1) * DH)
        q, k, v, g = q_ref[:, cols], k_ref[:, cols], v_ref[:, cols], g_ref[:, cols]
        probs, inner = store_ref[h], store_ref[2 + h]
        dprod = dot(g, v, NT)
        delta = jnp.sum(g.astype(F32) * dot(probs, v, NN), -1, keepdims=True)
        dscore = (probs.astype(F32) * (dprod - delta) * inv_root).astype(BF16)
        dinner = jnp.where(triangle, dprod, 0.0).astype(BF16)
        left = dot(jnp.concatenate([dscore, dinner], 0), k, NN)
        linear = left[rows:] + dot_wide(g, states[h], NT)
        dq_ref[:, cols] = (left[:rows] + scale * linear).astype(BF16)
        dk = dot(jnp.concatenate([dscore, dinner], 1), q, TN)
        dk_ref[:, cols] = dk[:rows] + scale * dk[rows:]
        dv = dot(jnp.concatenate([probs, inner], 1), g, TN)
        dv_ref[:, cols] = dv[:rows] + scale * dv[rows:]


def close_kernel(where, k_ref, v_ref, dk_ref, dv_ref, mine_ref, other_ref, gk_ref, gv_ref):
    states = both_heads(where[2], mine_ref, other_ref)
    for h in range(k_ref.shape[1] // DH):
        cols = slice(h * DH, (h + 1) * DH)
        state = states[h]
        gk_ref[:, cols] = (dk_ref[:, cols] + dot_wide(v_ref[:, cols], state, NT)).astype(BF16)
        gv_ref[:, cols] = (dv_ref[:, cols] + dot_wide(k_ref[:, cols], state, NN)).astype(BF16)


def send(x, flip, shift):
    shards, heads = lax.axis_size("ctx"), lax.axis_size("head")
    pairs = [
        (c * heads + z, (c ^ flip) * heads + (z + shift) % heads)
        for c in range(shards)
        for z in range(heads)
    ]
    return lax.ppermute(x, ("ctx", "head"), pairs)


def exchange(mine, other, core, chip, chips, later):
    got = send(other, 1, 0)
    own = total = mine + got
    totals, flags = [], []
    if chips == 4:
        for flip in (1, 2, 3):
            totals.append(send(total, 2 * flip, 0))
            flags.append(((chip ^ flip) > chip) == later)
    else:
        step = 1
        while step < chips:
            totals.append(send(total, 2 * step, 0))
            flags.append(((chip & step) == 0) == later)
            total = total + totals[-1]
            step *= 2
    flags.append((core == 0) == later)
    return jnp.stack(flags).astype(jnp.int32), [mine, got, *totals], own


def on_device(query, key, value, block_mask, out_weight, cotangent):
    rows, width = query.shape
    heads = width // DH
    shards, count = lax.axis_size("ctx"), lax.axis_size("head")
    model = out_weight.shape[1]
    own = rows // count
    scale = 1.0 / math.sqrt(DH * rows * shards)
    ctx, place = lax.axis_index("ctx"), lax.axis_index("head")
    core, chip, chips = ctx & 1, ctx >> 1, shards // 2
    where = jnp.stack([place, ctx, core])
    flat, square = (rows, width), rows * rows * DH * heads
    pair = [((DH, DH), F32)] * 2
    tokens = ((2 * own, DH), BF16)
    product = 4 * own * DH * model

    board = chips == 4 and count == 4
    wide = model // (2 if board else chips)
    colour = (chip & 1) ^ (chip >> 1) if board else chip
    piece = lax.dynamic_slice(out_weight, (core * DH, colour * wide), (DH, wide))
    arrived = {1: send(piece, 0, 1), count - 1: send(piece, 0, -1)}
    mate_cotangent = send(cotangent, 1, 0)

    store, pre, other_pre, far, mine, other = call(
        functools.partial(forward_kernel, scale),
        [((2 * heads, rows, rows), BF16)]
        + [((rows, DH), F32)] * 2
        + [((rows, DH), BF16)]
        + pair,
        [jnp.stack([query, key, value])],
        [block_mask, where],
        [mate_cotangent],
        flops=7 * square,
    )
    far, other_pre = send(far, 1, 0), send(other_pre, 1, 0)
    (mine,) = hold([mine], [far, other_pre])
    flags, parts, total = exchange(mine, other, core, chip, chips, False)
    attn, keep, back = call(
        functools.partial(attn_kernel, scale),
        [((count, *tokens[0]), BF16), *pair],
        [*parts, query, far, pre, other_pre],
        [flags, where],
    )
    linear = [keep, send(back, 1, 0)]
    if board:
        arrived[1], arrived[3] = hold([arrived[1], arrived[3]], [keep])
    attn = lax.all_to_all(attn, "head", 0, 0, tiled=True)

    work = near_and_far if board else by_gathers
    both, across, mix = work(
        attn, arrived, cotangent, mate_cotangent, out_weight, core, chip, colour, product
    )
    g, mine, other = call(
        functools.partial(collect_kernel, scale, count),
        [(flat, BF16), *pair],
        [query, *both, *across],
        [where],
        linear[1:],
    )
    flags, parts, total = exchange(mine, other, core, chip, chips, True)
    joins, starts = mix([total])
    mixed, done = call(
        join_kernel, [((own, model), BF16), ((8, DH), F32)], joins, [jnp.stack(starts)]
    )

    grad_query, dk, dv = call(
        functools.partial(backward_kernel, scale),
        [(flat, BF16)] + [(flat, F32)] * 2,
        [query, key, value, g, store, *linear],
        [where],
        [total],
        flops=14 * square,
    )
    keep, back = call(carry_kernel, pair, parts, [flags], [dk])
    grad_key, grad_value = call(
        close_kernel,
        [(flat, BF16)] * 2,
        [key, value, dk, dv, keep, send(back, 1, 0)],
        [where],
        [done],
    )
    return mixed, grad_query, grad_key, grad_value


def near_and_far(attn, arrived, cotangent, mate_cotangent, weight, core, chip, colour, product):
    own, model = cotangent.shape
    wide = model // 2
    place = lax.axis_index("head")
    spots = jnp.stack([colour * wide, (1 - colour) * wide, core * DH, place])
    tokens = ((2 * own, DH), BF16)
    parts = [((own, wide), F32)] * 2
    all_arrays = [(cotangent, all_of, rows_at(0, own)), (mate_cotangent, all_of, rows_at(own, own))]
    whole = fetch((2 * own, model), *all_arrays)
    left = [
        fetch((2 * own, wide), *((a, columns(n, wide), put) for a, _, put in all_arrays))
        for n in range(2)
    ]

    def own_rows(ref, spots, *_):
        return ref.at[pl.ds(pl.multiple_of(spots[2], DH), DH)]

    def own_columns(n):
        return lambda ref, spots, *_: ref.at[
            pl.ds(pl.multiple_of(spots[2], DH), DH), pl.ds(pl.multiple_of(spots[n], DH), wide)
        ]

    def stacked(*arrays):
        return [(a, all_of, rows_at(n * DH, DH)) for n, a in enumerate(arrays)]

    arrived[2] = send(arrived[1], 0, 1)
    second = {1: send(arrived[1], 2, 0), 3: send(arrived[3], 4, 0)}
    mine, half = call(
        first_kernel,
        [tokens, ((2 * own, 2 * DH), F32)],
        [
            whole,
            fetch((DH, model), (weight, own_rows, all_of)),
            fetch((2 * DH, wide), *stacked(arrived[1], arrived[3])),
        ],
        [spots],
        lazy=True,
        room=6,
        flops=2 * product,
    )
    one, three, *cuts = call(
        second_kernel,
        [tokens] * 2 + [((DH, wide // 2), BF16)] * 2,
        [
            left[1],
            fetch((2 * DH, wide), *stacked(second[1], second[3])),
            half,
            fetch((DH, wide), (arrived[2], all_of, all_of)),
        ],
        [spots],
        room=6,
        flops=product,
    )
    second[2] = [send(cuts[0], 2, 0), send(cuts[1], 4, 0)]
    both = {0: mine, 1: send(one, 0, -1), 3: send(three, 0, -3)}
    across = {s: send(both[s], 1, 0) for s in (0, 1, 3)}
    (half,) = call(
        half_kernel,
        [((2 * own, DH), F32)],
        [left[0], fetch((DH, wide), (arrived[2], all_of, all_of))],
        [spots],
        [attn],
        room=6,
        flops=product // 2,
    )
    quarters = [(a, all_of, columns_at(n * wide // 2, wide // 2)) for n, a in enumerate(second[2])]
    (two,) = call(
        last_kernel,
        [tokens],
        [left[1], fetch((DH, wide), *quarters), half],
        [spots],
        [both[1], both[3]],
        room=6,
        flops=product // 2,
    )
    both[2] = send(two, 0, -2)
    across[2] = send(both[2], 1, 0)

    def quarter(n):
        return lambda ref, *_: ref.at[2 * DH : 3 * DH, n * wide // 2 : (n + 1) * wide // 2]

    def mix(after):
        outs = call(
            halves_kernel,
            parts * 2,
            [
                fetch(attn.shape, (attn, all_of, all_of)),
                fetch(
                    (4 * DH, wide),
                    (weight, own_columns(1), rows_at(0, DH)),
                    (second[1], all_of, rows_at(DH, DH)),
                    (second[3], all_of, rows_at(3 * DH, DH)),
                    *((a, all_of, quarter(n)) for n, a in enumerate(second[2])),
                ),
                fetch(
                    (4 * DH, wide),
                    (weight, own_columns(0), rows_at(0, DH)),
                    *((arrived[s], all_of, rows_at(s * DH, DH)) for s in (1, 2, 3)),
                ),
            ],
            [spots],
            after,
            room=8,
            flops=4 * product,
            lazy=True,
        )
        joins = [outs[0], send(outs[1], 1, 0), outs[2], send(outs[3], 1, 0)]
        return joins, [spots[1], spots[0]]

    return [both[s] for s in range(4)], [across[s] for s in range(4)], mix


def by_gathers(attn, arrived, cotangent, mate_cotangent, out_weight, core, chip, colour, product):
    own, model = cotangent.shape
    shards, count = lax.axis_size("ctx"), lax.axis_size("head")
    weight = lax.dynamic_slice_in_dim(out_weight, core * DH, DH, 0)
    zero = jnp.zeros((1,), jnp.int32)
    groups = [list(range(k, shards, 2)) for k in range(2)]
    for s in range(2, count - 1):
        arrived[s] = send(arrived[s - 1], 0, 1)
    chunks = [weight] + [
        lax.all_gather(arrived[s], "ctx", axis=1, tiled=True, axis_index_groups=groups)
        for s in range(1, count)
    ]
    both = []
    for s in range(count):
        (block,) = call(
            functools.partial(grad_kernel, True, 0),
            [((2 * own, DH), BF16)],
            [cotangent, mate_cotangent, chunks[s]],
            [zero],
            flops=product,
        )
        both.append(send(block, 0, -s) if s else block)
    def mix(after):
        part, mate_part = call(
            mixed_kernel,
            [((own, model), F32)] * 2,
            [attn, *chunks],
            [lax.axis_index("head").reshape(1)],
            after,
            room=16,
            flops=count * product,
        )
        return [part, send(mate_part, 1, 0)], [jnp.int32(0)]

    return both, [send(b, 1, 0) for b in both], mix


def solution(mesh):
    return jax.shard_map(
        on_device,
        mesh=mesh,
        in_specs=(
            P("ctx", "head"),
            P("ctx", "head"),
            P("ctx", "head"),
            P("ctx", None),
            P("head", None),
            P(("ctx", "head"), None),
        ),
        out_specs=(P(("ctx", "head"), None), P("ctx", "head"), P("ctx", "head"), P("ctx", "head")),
        check_vma=False,
    )
```

```python
import functools
import math

import jax
import jax.numpy as jnp
from jax import lax
from jax.experimental import pallas as pl
from jax.experimental.pallas import tpu as pltpu
from jax.sharding import PartitionSpec as P

DH = 128
F32 = jnp.float32
BF16 = jnp.bfloat16
NN = ((1,), (0,))
NT = ((1,), (1,))
TN = ((0,), (0,))
MIB = 1 << 20


def dot(a, b, dims):
    return lax.dot_general(a, b, (dims, ((), ())), preferred_element_type=F32)


def dot_wide(a, b, dims):
    high = b.astype(BF16)
    low = (b - high.astype(F32)).astype(BF16)
    both = dot(a, jnp.concatenate([high, low], 1 - dims[1][0]), dims)
    return both[:, :DH] + both[:, DH:]


def fetch(shape, *parts):
    return (shape, parts)


def all_of(ref, *_):
    return ref


def columns(spot, wide, rows=slice(None)):
    def view(ref, spots, *_):
        return ref.at[rows, pl.ds(pl.multiple_of(spots[spot], DH), wide)]

    return view


def rows_at(first, count):
    return lambda ref, *_: ref.at[first : first + count]


def columns_at(first, count):
    return lambda ref, *_: ref.at[:, first : first + count]


def call(body, outs, args, smem=(), after=(), room=2, flops=1, lazy=False):
    arrays, specs, scratch = [], [], []
    for arg in args:
        if isinstance(arg, tuple):
            arrays += [part[0] for part in arg[1]]
            specs += [pl.BlockSpec(memory_space=pltpu.HBM) for _ in arg[1]]
            scratch.append(pltpu.VMEM(arg[0], arg[1][0][0].dtype))
        else:
            arrays.append(arg)
            specs.append(pl.BlockSpec(memory_space=pltpu.VMEM))
    copies = sum(len(arg[1]) for arg in args if isinstance(arg, tuple))
    held = len(scratch)
    if copies:
        scratch.append(pltpu.SemaphoreType.DMA((copies,)))

    def kernel(*refs):
        scalars, refs = refs[: len(smem)], list(refs[len(smem) :])
        ins, refs = refs[: len(arrays)], refs[len(arrays) + len(after) :]
        results, slots = refs[: len(outs)], refs[len(outs) :]
        given, started, slot, groups = [], [], 0, []
        for arg in args:
            if not isinstance(arg, tuple):
                given.append(ins.pop(0))
                continue
            for _, source, target in arg[1]:
                copy = pltpu.make_async_copy(
                    source(ins.pop(0), *scalars),
                    target(slots[slot], *scalars),
                    slots[held].at[len(started)],
                )
                copy.start()
                started.append(copy)
            given.append(slots[slot])
            groups.append(started[sum(len(group) for group in groups) :])
            slot += 1

        def ready(n):
            for copy in groups[n]:
                copy.wait()

        if lazy:
            body(ready, *scalars, *given, *results)
            return
        for n in range(len(groups)):
            ready(n)
        body(*scalars, *given, *results)

    moved = sum(a.size * a.dtype.itemsize for a in arrays)
    moved += sum(math.prod(s) * jnp.dtype(t).itemsize for s, t in outs)
    return pl.pallas_call(
        kernel,
        out_shape=[jax.ShapeDtypeStruct(s, t) for s, t in outs],
        in_specs=[pl.BlockSpec(memory_space=pltpu.SMEM) for _ in smem]
        + specs
        + [pl.BlockSpec(memory_space=pl.ANY) for _ in after],
        out_specs=[pl.BlockSpec(memory_space=pltpu.VMEM) for _ in outs],
        scratch_shapes=scratch,
        compiler_params=pltpu.CompilerParams(vmem_limit_bytes=room * MIB),
        cost_estimate=pl.CostEstimate(
            flops=int(flops), bytes_accessed=int(moved), transcendentals=0
        ),
    )(*smem, *arrays, *after)


def hold(arrays, after):
    held = len(arrays)
    return pl.pallas_call(
        lambda *refs: None,
        out_shape=[jax.ShapeDtypeStruct(a.shape, a.dtype) for a in arrays],
        in_specs=[pl.BlockSpec(memory_space=pl.ANY) for _ in (*arrays, *after)],
        out_specs=[pl.BlockSpec(memory_space=pl.ANY) for _ in arrays],
        input_output_aliases={n: n for n in range(held)},
        cost_estimate=pl.CostEstimate(flops=1, bytes_accessed=1, transcendentals=0),
    )(*arrays, *after)


def lower_triangle(blk):
    return lax.broadcasted_iota(jnp.int32, (blk, blk), 0) >= lax.broadcasted_iota(
        jnp.int32, (blk, blk), 1
    )


def forward_kernel(
    scale,
    mask,
    where,
    all_ref,
    store_ref,
    mine_ref,
    other_ref,
    far_ref,
    mine_state_ref,
    other_state_ref,
):
    q_ref, k_ref, v_ref = (all_ref.at[n] for n in range(3))
    heads = [slice(h * DH, (h + 1) * DH) for h in range(2)]
    states = [dot(k_ref[:, cols], v_ref[:, cols], TN) for cols in heads]
    mine_state_ref[...], other_state_ref[...] = pick(where[2], states)
    rows, width = q_ref.shape
    count = mask.shape[0]
    blk = rows // count
    inv_root = 1.0 / math.sqrt(DH)
    triangle = lower_triangle(blk)
    sums = []
    for h in range(2):
        raw = dot(q_ref[:, heads[h]], k_ref[:, heads[h]], NT)
        probs, inner = [], []
        for i in range(count):
            own = raw[i * blk : (i + 1) * blk]
            scores, linear = [], []
            for j in range(i + 1):
                part = own[:, j * blk : (j + 1) * blk]
                keep = triangle if j == i else mask[i, j] > 0
                scores.append(jnp.where(keep, part * inv_root, -1e30))
                linear.append(jnp.where(triangle, part, 0.0) if j == i else part)
            empty = [jnp.zeros((blk, blk), F32)] * (count - 1 - i)
            scores = jnp.concatenate(scores, 1)
            expo = jnp.exp(scores - jnp.max(scores, -1, keepdims=True))
            share = expo / jnp.sum(expo, -1, keepdims=True)
            probs.append(jnp.concatenate([share, *empty], 1).astype(BF16))
            inner.append(jnp.concatenate([*linear, *empty], 1).astype(BF16))
        stacked = jnp.concatenate(probs + inner, 0)
        store_ref[h], store_ref[2 + h] = stacked[:rows], stacked[rows:]
        both = dot(stacked, v_ref[:, heads[h]], NN)
        sums.append(both[:rows] + scale * both[rows:])
    mine_ref[...], other_ref[...] = pick(where[2], sums)
    far_ref[...] = q_ref[:, pl.ds(pl.multiple_of((1 - where[2]) * DH, DH), DH)]


def pick(core, parts):
    return jnp.where(core == 0, parts[0], parts[1]), jnp.where(core == 0, parts[1], parts[0])


def both_heads(core, mine_ref, other_ref):
    mine, other = mine_ref[...], other_ref[...]
    return jnp.where(core == 0, mine, other), jnp.where(core == 0, other, mine)


def carry(flags, here_ref, got_ref, totals):
    carried = jnp.zeros(here_ref.shape, F32)
    for n, total in enumerate(totals):
        carried = carried + jnp.where(flags[n] > 0, total[...], 0.0)
    counts = flags[len(totals)] > 0
    keep = carried + jnp.where(counts, got_ref[...], 0.0)
    return keep, carried + jnp.where(counts, 0.0, here_ref[...])


def carry_kernel(flags, here_ref, got_ref, *refs):
    totals, (keep_ref, back_ref) = refs[:-2], refs[-2:]
    keep_ref[...], back_ref[...] = carry(flags, here_ref, got_ref, totals)


def attn_kernel(scale, flags, where, here_ref, got_ref, *refs):
    totals, refs = refs[:-7], refs[-7:]
    q_ref, far_ref, pre_ref, far_pre_ref, out_ref, keep_ref, back_ref = refs
    keep, back = carry(flags, here_ref, got_ref, totals)
    keep_ref[...], back_ref[...] = keep, back
    count = out_ref.shape[0]
    own = pre_ref.shape[0] // count
    cols = pl.ds(pl.multiple_of(where[2] * DH, DH), DH)
    mine = pre_ref[...] + scale * dot_wide(q_ref[:, cols], keep, NN)
    mate = far_pre_ref[...] + scale * dot_wide(far_ref[...], back, NN)
    for z in range(count):
        out_ref[z, :own] = mine[z * own : (z + 1) * own].astype(BF16)
        out_ref[z, own:] = mate[z * own : (z + 1) * own].astype(BF16)


def back_along(attn_ref, place):
    count = attn_ref.shape[0]
    return jnp.concatenate([attn_ref[lax.rem(place - s + count, count)] for s in range(count)], 1)


def first_kernel(ready, spots, left_ref, weight_ref, right_ref, own_ref, half_ref):
    ready(0)
    ready(1)
    own_ref[...] = dot(left_ref[...], weight_ref[...], NT).astype(BF16)
    ready(2)
    near = left_ref[:, pl.ds(pl.multiple_of(spots[0], DH), right_ref.shape[1])]
    half_ref[...] = dot(near, right_ref[...], NT)


def second_kernel(spots, left_ref, right_ref, half_ref, piece_ref, one_ref, three_ref, *cut_refs):
    wide = cut_refs[0].shape[1]
    for n, cut_ref in enumerate(cut_refs):
        cut_ref[...] = piece_ref[:, n * wide : (n + 1) * wide]
    total = (half_ref[...] + dot(left_ref[...], right_ref[...], NT)).astype(BF16)
    one_ref[...], three_ref[...] = total[:, :DH], total[:, DH:]


def last_kernel(spots, left_ref, right_ref, half_ref, out_ref):
    out_ref[...] = (half_ref[...] + dot(left_ref[...], right_ref[...], NT)).astype(BF16)


def half_kernel(spots, left_ref, right_ref, half_ref):
    half_ref[...] = dot(left_ref[...], right_ref[...], NT)


def halves_kernel(ready, spots, attn_ref, *refs):
    rights, outs = refs[:2], refs[2:]
    own = outs[0].shape[0]
    ready(0)
    left = back_along(attn_ref, spots[3])
    for n, right_ref in enumerate(rights):
        ready(1 + n)
        part = dot(left, right_ref[...], NN)
        outs[2 * n][...] = part[:own]
        outs[2 * n + 1][...] = part[own:]


def grad_kernel(whole, added, places, mine_ref, mate_ref, *refs):
    chunks, out_ref = refs[added:-1], refs[-1]
    total = refs[0][...] if added else None
    for j, chunk in enumerate(chunks):
        cols = slice(None) if whole else pl.ds(pl.multiple_of(places[j], DH), chunk.shape[1])
        left = jnp.concatenate([mine_ref[:, cols], mate_ref[:, cols]], 0)
        part = dot(left, chunk[...], NT)
        total = part if total is None else total + part
    out_ref[...] = total.astype(out_ref.dtype)


def mixed_kernel(where, attn_ref, *refs):
    chunks, (own_out, mate_out) = refs[:-2], refs[-2:]
    own = own_out.shape[0]
    right = jnp.concatenate([chunk[...] for chunk in chunks], 0)
    part = dot(back_along(attn_ref, where[0]), right, NN)
    own_out[...] = part[:own]
    mate_out[...] = part[own:]


def join_kernel(places, *refs):
    out_ref, done_ref = refs[-2:]
    done_ref[...] = jnp.zeros(done_ref.shape, F32)
    for n in range(len(refs) // 2 - 1):
        wide = refs[2 * n].shape[1]
        there = pl.ds(pl.multiple_of(places[n], DH), wide)
        out_ref[:, there] = (refs[2 * n][...] + refs[2 * n + 1][...]).astype(BF16)


def collect_kernel(scale, count, where, q_ref, *refs):
    direct, across = refs[:count], refs[count : 2 * count]
    g_ref, mine_ref, other_ref = refs[2 * count :]
    own = g_ref.shape[0] // count
    mine = pl.ds(pl.multiple_of(where[2] * DH, DH), DH)
    mate = pl.ds(pl.multiple_of((1 - where[2]) * DH, DH), DH)
    for s in range(count):
        block = lax.rem(where[0] + s, count)
        here = pl.ds(pl.multiple_of(block * own, own), own)
        g_ref[here, mine] = direct[s][:own]
        g_ref[here, mate] = across[s][own:]
    heads = [slice(h * DH, (h + 1) * DH) for h in range(2)]
    parts = [scale * dot(q_ref[:, cols], g_ref[:, cols], TN) for cols in heads]
    mine_ref[...], other_ref[...] = pick(where[2], parts)


def backward_kernel(
    scale, where, q_ref, k_ref, v_ref, g_ref, store_ref, mine_ref, other_ref, dq_ref, dk_ref, dv_ref
):
    rows, width = q_ref.shape
    inv_root = 1.0 / math.sqrt(DH)
    triangle = lower_triangle(rows)
    states = both_heads(where[2], mine_ref, other_ref)
    for h in range(width // DH):
        cols = slice(h * DH, (h + 1) * DH)
        q, k, v, g = q_ref[:, cols], k_ref[:, cols], v_ref[:, cols], g_ref[:, cols]
        probs, inner = store_ref[h], store_ref[2 + h]
        dprod = dot(g, v, NT)
        delta = jnp.sum(g.astype(F32) * dot(probs, v, NN), -1, keepdims=True)
        dscore = (probs.astype(F32) * (dprod - delta) * inv_root).astype(BF16)
        dinner = jnp.where(triangle, dprod, 0.0).astype(BF16)
        left = dot(jnp.concatenate([dscore, dinner], 0), k, NN)
        linear = left[rows:] + dot_wide(g, states[h], NT)
        dq_ref[:, cols] = (left[:rows] + scale * linear).astype(BF16)
        dk = dot(jnp.concatenate([dscore, dinner], 1), q, TN)
        dk_ref[:, cols] = dk[:rows] + scale * dk[rows:]
        dv = dot(jnp.concatenate([probs, inner], 1), g, TN)
        dv_ref[:, cols] = dv[:rows] + scale * dv[rows:]


def close_kernel(where, k_ref, v_ref, dk_ref, dv_ref, mine_ref, other_ref, gk_ref, gv_ref):
    states = both_heads(where[2], mine_ref, other_ref)
    for h in range(k_ref.shape[1] // DH):
        cols = slice(h * DH, (h + 1) * DH)
        state = states[h]
        gk_ref[:, cols] = (dk_ref[:, cols] + dot_wide(v_ref[:, cols], state, NT)).astype(BF16)
        gv_ref[:, cols] = (dv_ref[:, cols] + dot_wide(k_ref[:, cols], state, NN)).astype(BF16)


def send(x, flip, shift):
    shards, heads = lax.axis_size("ctx"), lax.axis_size("head")
    pairs = [
        (c * heads + z, (c ^ flip) * heads + (z + shift) % heads)
        for c in range(shards)
        for z in range(heads)
    ]
    return lax.ppermute(x, ("ctx", "head"), pairs)


def exchange(mine, other, core, chip, chips, later):
    got = send(other, 1, 0)
    own = total = mine + got
    totals, flags = [], []
    if chips == 4:
        for flip in (1, 2, 3):
            totals.append(send(total, 2 * flip, 0))
            flags.append(((chip ^ flip) > chip) == later)
    else:
        step = 1
        while step < chips:
            totals.append(send(total, 2 * step, 0))
            flags.append(((chip & step) == 0) == later)
            total = total + totals[-1]
            step *= 2
    flags.append((core == 0) == later)
    return jnp.stack(flags).astype(jnp.int32), [mine, got, *totals], own


def on_device(query, key, value, block_mask, out_weight, cotangent):
    rows, width = query.shape
    heads = width // DH
    shards, count = lax.axis_size("ctx"), lax.axis_size("head")
    model = out_weight.shape[1]
    own = rows // count
    scale = 1.0 / math.sqrt(DH * rows * shards)
    ctx, place = lax.axis_index("ctx"), lax.axis_index("head")
    core, chip, chips = ctx & 1, ctx >> 1, shards // 2
    where = jnp.stack([place, ctx, core])
    flat, square = (rows, width), rows * rows * DH * heads
    pair = [((DH, DH), F32)] * 2
    tokens = ((2 * own, DH), BF16)
    product = 4 * own * DH * model

    board = chips == 4 and count == 4
    wide = model // (2 if board else chips)
    colour = (chip & 1) ^ (chip >> 1) if board else chip
    piece = lax.dynamic_slice(out_weight, (core * DH, colour * wide), (DH, wide))
    arrived = {1: send(piece, 0, 1), count - 1: send(piece, 0, -1)}
    mate_cotangent = send(cotangent, 1, 0)

    store, pre, other_pre, far, mine, other = call(
        functools.partial(forward_kernel, scale),
        [((2 * heads, rows, rows), BF16)]
        + [((rows, DH), F32)] * 2
        + [((rows, DH), BF16)]
        + pair,
        [jnp.stack([query, key, value])],
        [block_mask, where],
        [mate_cotangent],
        flops=7 * square,
    )
    far, other_pre = send(far, 1, 0), send(other_pre, 1, 0)
    (mine,) = hold([mine], [far, other_pre])
    flags, parts, total = exchange(mine, other, core, chip, chips, False)
    attn, keep, back = call(
        functools.partial(attn_kernel, scale),
        [((count, *tokens[0]), BF16), *pair],
        [*parts, query, far, pre, other_pre],
        [flags, where],
    )
    linear = [keep, send(back, 1, 0)]
    if board:
        arrived[1], arrived[3] = hold([arrived[1], arrived[3]], [keep])
    attn = lax.all_to_all(attn, "head", 0, 0, tiled=True)

    work = near_and_far if board else by_gathers
    both, across, mix = work(
        attn, arrived, cotangent, mate_cotangent, out_weight, core, chip, colour, product
    )
    g, mine, other = call(
        functools.partial(collect_kernel, scale, count),
        [(flat, BF16), *pair],
        [query, *both, *across],
        [where],
        linear[1:],
    )
    flags, parts, total = exchange(mine, other, core, chip, chips, True)
    joins, starts = mix([total])
    mixed, done = call(
        join_kernel, [((own, model), BF16), ((8, DH), F32)], joins, [jnp.stack(starts)]
    )

    grad_query, dk, dv = call(
        functools.partial(backward_kernel, scale),
        [(flat, BF16)] + [(flat, F32)] * 2,
        [query, key, value, g, store, *linear],
        [where],
        [total],
        flops=14 * square,
    )
    keep, back = call(carry_kernel, pair, parts, [flags], [dk])
    grad_key, grad_value = call(
        close_kernel,
        [(flat, BF16)] * 2,
        [key, value, dk, dv, keep, send(back, 1, 0)],
        [where],
        [done],
    )
    return mixed, grad_query, grad_key, grad_value


def near_and_far(attn, arrived, cotangent, mate_cotangent, weight, core, chip, colour, product):
    own, model = cotangent.shape
    wide = model // 2
    place = lax.axis_index("head")
    spots = jnp.stack([colour * wide, (1 - colour) * wide, core * DH, place])
    tokens = ((2 * own, DH), BF16)
    parts = [((own, wide), F32)] * 2
    all_arrays = [(cotangent, all_of, rows_at(0, own)), (mate_cotangent, all_of, rows_at(own, own))]
    whole = fetch((2 * own, model), *all_arrays)
    left = [
        fetch((2 * own, wide), *((a, columns(n, wide), put) for a, _, put in all_arrays))
        for n in range(2)
    ]

    def own_rows(ref, spots, *_):
        return ref.at[pl.ds(pl.multiple_of(spots[2], DH), DH)]

    def own_columns(n):
        return lambda ref, spots, *_: ref.at[
            pl.ds(pl.multiple_of(spots[2], DH), DH), pl.ds(pl.multiple_of(spots[n], DH), wide)
        ]

    def stacked(*arrays):
        return [(a, all_of, rows_at(n * DH, DH)) for n, a in enumerate(arrays)]

    arrived[2] = send(arrived[1], 0, 1)
    second = {1: send(arrived[1], 2, 0), 3: send(arrived[3], 4, 0)}
    mine, half = call(
        first_kernel,
        [tokens, ((2 * own, 2 * DH), F32)],
        [
            whole,
            fetch((DH, model), (weight, own_rows, all_of)),
            fetch((2 * DH, wide), *stacked(arrived[1], arrived[3])),
        ],
        [spots],
        lazy=True,
        room=6,
        flops=2 * product,
    )
    one, three, *cuts = call(
        second_kernel,
        [tokens] * 2 + [((DH, wide // 2), BF16)] * 2,
        [
            left[1],
            fetch((2 * DH, wide), *stacked(second[1], second[3])),
            half,
            fetch((DH, wide), (arrived[2], all_of, all_of)),
        ],
        [spots],
        room=6,
        flops=product,
    )
    second[2] = [send(cuts[0], 2, 0), send(cuts[1], 4, 0)]
    both = {0: mine, 1: send(one, 0, -1), 3: send(three, 0, -3)}
    across = {s: send(both[s], 1, 0) for s in (0, 1, 3)}
    (half,) = call(
        half_kernel,
        [((2 * own, DH), F32)],
        [left[0], fetch((DH, wide), (arrived[2], all_of, all_of))],
        [spots],
        [attn],
        room=6,
        flops=product // 2,
    )
    quarters = [(a, all_of, columns_at(n * wide // 2, wide // 2)) for n, a in enumerate(second[2])]
    (two,) = call(
        last_kernel,
        [tokens],
        [left[1], fetch((DH, wide), *quarters), half],
        [spots],
        [both[1]],
        room=6,
        flops=product // 2,
    )
    both[2] = send(two, 0, -2)
    across[2] = send(both[2], 1, 0)

    def quarter(n):
        return lambda ref, *_: ref.at[2 * DH : 3 * DH, n * wide // 2 : (n + 1) * wide // 2]

    def mix(after):
        outs = call(
            halves_kernel,
            parts * 2,
            [
                fetch(attn.shape, (attn, all_of, all_of)),
                fetch(
                    (4 * DH, wide),
                    (weight, own_columns(1), rows_at(0, DH)),
                    (second[1], all_of, rows_at(DH, DH)),
                    (second[3], all_of, rows_at(3 * DH, DH)),
                    *((a, all_of, quarter(n)) for n, a in enumerate(second[2])),
                ),
                fetch(
                    (4 * DH, wide),
                    (weight, own_columns(0), rows_at(0, DH)),
                    *((arrived[s], all_of, rows_at(s * DH, DH)) for s in (1, 2, 3)),
                ),
            ],
            [spots],
            after,
            room=8,
            flops=4 * product,
            lazy=True,
        )
        joins = [outs[0], send(outs[1], 1, 0), outs[2], send(outs[3], 1, 0)]
        return joins, [spots[1], spots[0]]

    return [both[s] for s in range(4)], [across[s] for s in range(4)], mix


def by_gathers(attn, arrived, cotangent, mate_cotangent, out_weight, core, chip, colour, product):
    own, model = cotangent.shape
    shards, count = lax.axis_size("ctx"), lax.axis_size("head")
    weight = lax.dynamic_slice_in_dim(out_weight, core * DH, DH, 0)
    zero = jnp.zeros((1,), jnp.int32)
    groups = [list(range(k, shards, 2)) for k in range(2)]
    for s in range(2, count - 1):
        arrived[s] = send(arrived[s - 1], 0, 1)
    chunks = [weight] + [
        lax.all_gather(arrived[s], "ctx", axis=1, tiled=True, axis_index_groups=groups)
        for s in range(1, count)
    ]
    both = []
    for s in range(count):
        (block,) = call(
            functools.partial(grad_kernel, True, 0),
            [((2 * own, DH), BF16)],
            [cotangent, mate_cotangent, chunks[s]],
            [zero],
            flops=product,
        )
        both.append(send(block, 0, -s) if s else block)
    def mix(after):
        part, mate_part = call(
            mixed_kernel,
            [((own, model), F32)] * 2,
            [attn, *chunks],
            [lax.axis_index("head").reshape(1)],
            after,
            room=16,
            flops=count * product,
        )
        return [part, send(mate_part, 1, 0)], [jnp.int32(0)]

    return both, [send(b, 1, 0) for b in both], mix


def solution(mesh):
    return jax.shard_map(
        on_device,
        mesh=mesh,
        in_specs=(
            P("ctx", "head"),
            P("ctx", "head"),
            P("ctx", "head"),
            P("ctx", None),
            P("head", None),
            P(("ctx", "head"), None),
        ),
        out_specs=(P(("ctx", "head"), None), P("ctx", "head"), P("ctx", "head"), P("ctx", "head")),
        check_vma=False,
    )
```
